32 devices in a mesh: section: 2 (over core), seq: 16 (over z, y, x).
Axes of the slice: x: 2, y: 2, z: 4, core: 2. Of those that a mesh axis runs over, the one named last changes fastest.
Arguments:
- tokens: bfloat16 [4, 1024, 768], P(None, 'seq'), may hold values from -6 to 6
- starts: int32 [4, 1024], P(None, 'seq'), may hold values from 0 to 1, as said below
- norm_gain: float32 [2, 768], P('section'), may hold values from 0.1 to 1.9
- in_weight: bfloat16 [2, 768, 3072], P('section'), may hold values from -0.21875 to 0.21875
- conv_weight: float32 [2, 4, 1536], P('section'), may hold values from -3 to 3
- conv_bias: float32 [2, 1536], P('section'), may hold values from -3 to 3
- xproj_weight: bfloat16 [2, 1536, 80], P('section'), may hold values from -0.15625 to 0.15625
- dtproj_weight: bfloat16 [2, 48, 1536], P('section'), may hold values from -0.875 to 0.875
- dt_bias: float32 [2, 1536], P('section'), may hold values from -6 to -3
- decay_rate: float32 [2, 1536, 16], P('section'), may hold values from 0.0009765625 to 4
- skip_gain: float32 [2, 1536], P('section'), may hold values from 0.5 to 1.5
- out_weight: bfloat16 [2, 1536, 768], P('section'), may hold values from -0.4375 to 0.4375
- cotangent: bfloat16 [4, 1024, 768], P(None, 'seq'), may hold values from -6 to 6
Outputs:
- boundary: bfloat16 [2, 4, 1024, 768], P('section', None, 'seq')
- grad_norm_gain: float32 [2, 768], P('section', 'seq')
- grad_in_weight: float32 [2, 768, 3072], P('section', None, 'seq')
- grad_conv_weight: float32 [2, 4, 1536], P('section', None, 'seq')
- grad_conv_bias: float32 [2, 1536], P('section', 'seq')
- grad_xproj_weight: float32 [2, 1536, 80], P('section', 'seq')
- grad_dtproj_weight: float32 [2, 48, 1536], P('section', None, 'seq')
- grad_dt_bias: float32 [2, 1536], P('section', 'seq')
- grad_decay_rate: float32 [2, 1536, 16], P('section', 'seq')
- grad_skip_gain: float32 [2, 1536], P('section', 'seq')
- grad_out_weight: float32 [2, 1536, 768], P('section', 'seq')
The draws below stay inside these ranges and needn't reach their ends.
Inputs may be any that keep to these rules, and one draw needn't show every extreme that they name: starts[b, t] = 1 where a packed document begins at position t of micro-batch b; in one micro-batch, drawn from the seed, it is 0 at every position, so that its single document spans the whole sequence.
All inputs are finite; a program needn't handle non-finite values.
Results may differ from the reference program's by a relative error of at most 0.035.
Values may be sent and summed in bfloat16 or wider, within the bound.
No kernel may reach another device: no remote copies, remote signals or barrier semaphores. Data moves between devices by JAX's collectives and lax.ppermute only.
A program may use at most 256 MiB of HBM per device.

```python
import math
import jax
import jax.numpy as jnp
from jax import lax

D = 768
DI = 1536
NS = 16
RANK = 48
KCONV = 4
GROUP = 64
MB = 4
LAYERS = 2
LENGTH = 1024


def draw_starts(key, part):
    key = jax.random.fold_in(key, 11)
    first_key, second_key = jax.random.split(key)
    marks = (jax.random.randint(first_key, (MB, LENGTH), 0, 4 * GROUP) == 0).astype(jnp.int32)
    whole = jax.random.randint(second_key, (), 0, MB)
    row_ids = jnp.arange(MB, dtype=jnp.int32)[:, None]
    return jnp.where(row_ids == whole, 0, marks).astype(jnp.int32)


def levels(key, dims, shards, low, largest):
    level, own = 1.0, jax.random.fold_in(key, 6)
    for position, parts in shards:
        heights = jnp.exp(jax.random.uniform(jax.random.fold_in(own, position), (parts,), jnp.float32, low / len(shards), largest / len(shards)))
        level = level * jnp.repeat(heights, dims[position] // parts).reshape([-1 if axis == position else 1 for axis in range(len(dims))])
    return level


def noise(rng, dims, scale, bound, cuts=(), kind=jnp.bfloat16):
    entries = scale * jax.random.normal(rng, dims, jnp.float32)
    if cuts:
        entries = entries * levels(rng, dims, cuts, -0.22, 0.18)
    return jnp.clip(entries, -bound, bound).astype(kind)


def setup_inputs(seed: int = 0) -> dict:
    splits = jax.random.split(jax.random.key(seed), 14)
    tokens = noise(splits[0], (MB, LENGTH, D), 1.0, 6.0, ((1, 16),))
    starts = draw_starts(jax.random.fold_in(splits[13], 71), 0)
    norm_gain = jnp.clip(1.0 + 0.18 * jax.random.normal(splits[2], (LAYERS, D), jnp.float32), 0.1, 1.9)
    in_weight = noise(splits[3], (LAYERS, D, 2 * DI), D ** -0.5, 0.21875, ((0, 2),))
    conv_weight = noise(splits[4], (LAYERS, KCONV, DI), KCONV ** -0.5, 3.0, ((0, 2),), jnp.float32)
    conv_bias = noise(splits[5], (LAYERS, DI), 0.5, 3.0, ((0, 2),), jnp.float32)
    xproj_weight = noise(splits[6], (LAYERS, DI, RANK + 2 * NS), DI ** -0.5, 0.15625, ((0, 2),))
    dtproj_weight = noise(splits[7], (LAYERS, RANK, DI), RANK ** -0.5, 0.875, ((0, 2),))
    dt_bias = jnp.clip(-6.0 + 3.0 * jax.random.uniform(splits[8], (LAYERS, DI), jnp.float32) ** levels(splits[8], (LAYERS, DI), ((0, 2),), -0.2, 0.2), -6.0, -3.0)
    decay_rate = jnp.clip(jnp.exp(math.log(4.0) - 8.317766 * jax.random.uniform(splits[9], (LAYERS, DI, NS), jnp.float32) ** levels(splits[9], (LAYERS, DI, NS), ((0, 2),), -0.2, 0.2)), 0.0009765625, 4.0)
    skip_gain = jnp.clip(0.5 + 1.0 * jax.random.uniform(splits[10], (LAYERS, DI), jnp.float32) ** levels(splits[10], (LAYERS, DI), ((0, 2),), -0.2, 0.2), 0.5, 1.5)
    out_weight = noise(splits[11], (LAYERS, DI, D), (DI // 8) ** -0.5, 0.4375, ((0, 2),))
    cotangent = noise(splits[12], (MB, LENGTH, D), 1.0, 6.0, ((1, 16),))
    return dict(tokens=tokens, starts=starts, norm_gain=norm_gain, in_weight=in_weight, conv_weight=conv_weight, conv_bias=conv_bias, xproj_weight=xproj_weight, dtproj_weight=dtproj_weight, dt_bias=dt_bias, decay_rate=decay_rate, skip_gain=skip_gain, out_weight=out_weight, cotangent=cotangent)


EPS = 1e-05

@jax.custom_vjp
def low(v):
    return lax.optimization_barrier(v.astype(jnp.bfloat16)).astype(jnp.float32)

@jax.custom_vjp
def low_back(v):
    return v

def low_keep(v):
    return (low(v), None)

def low_pass(kept, grad):
    return (grad,)

def back_keep(v):
    return (v, None)

def back_low(kept, grad):
    return (low(grad),)
low.defvjp(low_keep, low_pass)
low_back.defvjp(back_keep, back_low)

def matmul(left, right):
    return jnp.dot(left, right, precision=lax.Precision.HIGHEST, preferred_element_type=jnp.float32)

def norm_rows(source, gain_row):
    return source * lax.rsqrt(lax.optimization_barrier(jnp.mean(source * source, axis=-1, keepdims=True)) + EPS) * gain_row

def conv_mix(extended, start_ext, kernel, offset):
    free_one = 1.0 - start_ext[3:]
    free_two = free_one * (1.0 - start_ext[2:-1])
    free_three = free_two * (1.0 - start_ext[1:-2])
    summed = offset + kernel[3] * extended[3:]
    summed = summed + kernel[2] * (free_one[:, None] * extended[2:-1])
    summed = summed + kernel[1] * (free_two[:, None] * extended[1:-2])
    summed = summed + kernel[0] * (free_three[:, None] * extended[:-3])
    return jax.nn.silu(summed)

def combine(earlier, later):
    return (earlier[0] * later[0], later[0] * earlier[1] + later[1])

def layer(source, start_rows, params):
    gain_row, weight_in, weight_conv, bias_conv, weight_x, weight_dt, bias_dt, rate_table, skip_row, weight_out = params
    inner_width = weight_conv.shape[1]
    rank_width = weight_dt.shape[0]
    state_width = rate_table.shape[1]
    row_count = source.shape[0]
    normed = low(norm_rows(source, gain_row))
    mixed = low_back(low(matmul(normed, weight_in)))
    inner_in = mixed[:, :inner_width]
    gate_in = mixed[:, inner_width:]
    extended = jnp.concatenate([jnp.zeros((3, inner_width), jnp.float32), inner_in], 0)
    start_ext = jnp.concatenate([jnp.zeros((3,), jnp.float32), start_rows], 0)
    convolved = low(conv_mix(extended, start_ext, weight_conv, bias_conv))
    projected = low_back(low(matmul(convolved, weight_x)))
    step_size = jax.nn.softplus(low_back(matmul(projected[:, :rank_width], weight_dt)) + bias_dt)
    in_b = projected[:, rank_width:rank_width + state_width]
    out_c = projected[:, rank_width + state_width:]
    kept_mask = 1.0 - start_rows

    def block_scan(state, pieces):
        steps_here, in_here, out_here, conv_here, mask_here = pieces
        decays = mask_here[:, None, None] * jnp.exp(-steps_here[:, :, None] * rate_table[None])
        drives = (steps_here * conv_here)[:, :, None] * in_here[:, None, :]
        cumulative, local_states = lax.associative_scan(combine, (decays, drives))
        states = local_states + cumulative * state[None]
        return (states[-1], jnp.einsum('tdn,tn->td', states, out_here, precision=lax.Precision.HIGHEST))
    blocks = row_count // GROUP
    pieces = tuple((member.reshape((blocks, GROUP) + member.shape[1:]) for member in (step_size, in_b, out_c, convolved, kept_mask)))
    closing, outputs = lax.scan(jax.checkpoint(block_scan), jnp.zeros((inner_width, state_width), jnp.float32), pieces)
    scanned = outputs.reshape(row_count, inner_width) + skip_row * convolved
    gated = low(scanned * jax.nn.silu(gate_in))
    return source + low_back(matmul(gated, weight_out))

def reference(tokens, starts, norm_gain, in_weight, conv_weight, conv_bias, xproj_weight, dtproj_weight, dt_bias, decay_rate, skip_gain, out_weight, cotangent):
    params = tuple((member.astype(jnp.float32) for member in (norm_gain, in_weight, conv_weight, conv_bias, xproj_weight, dtproj_weight, dt_bias, decay_rate, skip_gain, out_weight)))
    start_rows = starts.astype(jnp.float32)

    def forward(source, weights):

        def sequence(pair):
            rows_now, marks = pair
            for level in range(LAYERS):
                rows_now = layer(rows_now, marks, tuple((member[level] for member in weights)))
                if level < LAYERS - 1:
                    rows_now = low_back(low(rows_now))
            return rows_now
        return lax.map(jax.checkpoint(sequence), (source, start_rows))
    outputs, pullback = jax.vjp(forward, tokens.astype(jnp.float32), params)
    grad_tokens, grads = pullback(cotangent.astype(jnp.float32))
    boundary = jnp.stack([grad_tokens, outputs]).astype(jnp.bfloat16)
    return (boundary, grads[0], grads[1], grads[2], grads[3], grads[4], grads[5], grads[6], grads[7], grads[8], grads[9])
```

```python
import functools
import jax
import jax.numpy as jnp
from jax import lax
from jax.experimental import pallas as pl
from jax.experimental.pallas import tpu as pltpu
from jax.sharding import PartitionSpec as P

EPS = 1e-05
LOG2E = 1.4426950408889634
STOP = 1e7
LANES = 128
BLOCK = 256
TILES = BLOCK // LANES
F32 = jnp.float32
BF16 = jnp.bfloat16
VMEM_LIMIT = 56 * 1024 * 1024


def dot(left, right):
    return jnp.dot(left, right, preferred_element_type=F32)


def across(left, right):
    return lax.dot_general(left, right, (((0,), (0,)), ((), ())), preferred_element_type=F32)


def against(left, right):
    return lax.dot_general(left, right, (((1,), (1,)), ((), ())), preferred_element_type=F32)


def norm_rows(source, gain_row):
    return source * lax.rsqrt(jnp.mean(source * source, axis=-1, keepdims=True) + EPS) * gain_row


def softplus(v):
    return jnp.maximum(v, 0.0) + jnp.log1p(jnp.exp(-jnp.abs(v)))


def silu_slope(v):
    gate = jax.nn.sigmoid(v)
    return gate * (1.0 + v * (1.0 - gate))


def pair_up(left, right, row_ids, width):
    mask = (row_ids % (2 * width)) < width
    kept = jnp.where(mask, left, right)
    moved = jnp.where(mask, right, left)
    return kept + pltpu.roll(moved, 8 - width, 0)


def fold_rows(parts, row_ids):
    width = 1
    while len(parts) > 1:
        parts = [
            pair_up(parts[i], parts[i + 1], row_ids, width) for i in range(0, len(parts), 2)
        ]
        width *= 2
    return parts[0]


def halves(v):
    return v[:8] + v[8:]


def spread_columns(table, first, target):
    width = target.shape[1]
    for t in range(target.shape[0]):
        column = table[first : first + width, t : t + 1]
        target[t] = jnp.broadcast_to(column, (width, LANES))


def block_at(i):
    return pl.ds(pl.multiple_of(i * BLOCK, BLOCK), BLOCK)


def tile_at(i, lt):
    return pl.ds(pl.multiple_of(i * BLOCK + lt * LANES, LANES), LANES)


def local_scan(batches, span, blocks, seff, x, bx, at, final):
    def over_block(i, carry):
        rate = [at[:, tile_at(i, lt)] for lt in range(TILES)]

        def chunk(tc, states):
            states = list(states)
            for b in range(batches):
                rows = pl.ds(pl.multiple_of(b * span + tc * 8, 8), 8)
                for lt in range(TILES):
                    s8 = seff[rows, tile_at(i, lt)]
                    x8 = x[rows, tile_at(i, lt)]
                    h = states[b * TILES + lt]
                    for j in range(8):
                        decay = jnp.exp2(s8[j : j + 1] * rate[lt])
                        h = decay * h + x8[j : j + 1] * bx[b * span + tc * 8 + j]
                    states[b * TILES + lt] = h
            return tuple(states)

        zero = jnp.zeros((at.shape[0], LANES), F32)
        states = lax.fori_loop(0, span // 8, chunk, (zero,) * (batches * TILES))
        for b in range(batches):
            for lt in range(TILES):
                final[b, :, tile_at(i, lt)] = states[b * TILES + lt]
        return carry

    lax.fori_loop(0, blocks, over_block, 0)


def front_kernel(
    batches, span, width, rank, states_n,
    mixed, rim, marks, cw, cb, xw, dw, db, at,
    pre_o, conv_o, proj_o, spre_o, bx_o, cx_o, final_o, total_o,
    ext, seff, x,
):
    m = marks[...]
    for b in range(batches):
        lo, hi = b * span, (b + 1) * span
        ext[b, 0:8] = rim[b]
        ext[b, 8:] = mixed[lo:hi, :width].astype(F32)
        v = cb[...] + cw[3:4] * ext[b, 8 : 8 + span]
        for k in (1, 2, 3):
            v = v + cw[3 - k : 4 - k] * (m[lo:hi, k : k + 1] * ext[b, 8 - k : 8 - k + span])
        pre_o[lo:hi] = v
    conv = jax.nn.silu(pre_o[...]).astype(BF16)
    conv_o[...] = conv
    proj = dot(conv, xw[...])
    proj_o[...] = proj.astype(BF16)
    spre = dot(proj_o[...], dw[...]) + db[...]
    spre_o[...] = spre
    step = softplus(spre)
    seff[...] = step + m[:, 0:1] * STOP
    x[...] = step * conv.astype(F32)
    for b in range(batches):
        total_o[b] = jnp.sum(seff[b * span : (b + 1) * span], axis=0, keepdims=True)
    table = proj.astype(BF16).astype(F32).T
    spread_columns(table, rank, bx_o)
    spread_columns(table, rank + states_n, cx_o)
    local_scan(batches, span, width // BLOCK, seff, x, bx_o, at, final_o)


def out_kernel(
    batches, span, width,
    mixed, conv, spre, marks, bx, cx, state_in, at, skip,
    scanned_o, gated_o,
    seff, x,
):
    blocks = width // BLOCK
    step = softplus(spre[...])
    seff[...] = step + marks[:, 0:1] * STOP
    x[...] = step * conv[...].astype(F32)
    row_ids = lax.broadcasted_iota(jnp.int32, (8, LANES), 0)

    def over_block(i, carry):
        rate = [at[:, tile_at(i, lt)] for lt in range(TILES)]

        def chunk(tc, states):
            states = list(states)
            for b in range(batches):
                rows = pl.ds(pl.multiple_of(b * span + tc * 8, 8), 8)
                for lt in range(TILES):
                    s8 = seff[rows, tile_at(i, lt)]
                    x8 = x[rows, tile_at(i, lt)]
                    h = states[b * TILES + lt]
                    parts = []
                    for j in range(8):
                        t = b * span + tc * 8 + j
                        decay = jnp.exp2(s8[j : j + 1] * rate[lt])
                        h = decay * h + x8[j : j + 1] * bx[t]
                        parts.append(halves(h * cx[t]))
                    states[b * TILES + lt] = h
                    scanned_o[rows, tile_at(i, lt)] = fold_rows(parts, row_ids)
            return tuple(states)

        start = tuple(
            state_in[b, :, tile_at(i, lt)] for b in range(batches) for lt in range(TILES)
        )
        lax.fori_loop(0, span // 8, chunk, start)
        return carry

    lax.fori_loop(0, blocks, over_block, 0)
    scanned = scanned_o[...] + skip[...] * conv[...].astype(F32)
    scanned_o[...] = scanned
    gated_o[...] = (scanned * jax.nn.silu(mixed[:, width:].astype(F32))).astype(BF16)


def back_local_kernel(
    batches, span, width,
    sg, spre, marks, cx, at,
    first_o,
    seff,
):
    blocks = width // BLOCK
    seff[...] = softplus(spre[...]) + marks[:, 0:1] * STOP
    chunks = span // 8

    def over_block(i, carry):
        rate = [at[:, tile_at(i, lt)] for lt in range(TILES)]

        def chunk(k, states):
            states = list(states)
            tc = chunks - 1 - k
            for b in range(batches):
                rows = pl.ds(pl.multiple_of(b * span + tc * 8, 8), 8)
                for lt in range(TILES):
                    s8 = seff[rows, tile_at(i, lt)]
                    g8 = sg[rows, tile_at(i, lt)]
                    q = states[b * TILES + lt]
                    for j in range(7, -1, -1):
                        decay = jnp.exp2(s8[j : j + 1] * rate[lt])
                        q = decay * (q + g8[j : j + 1] * cx[b * span + tc * 8 + j])
                    states[b * TILES + lt] = q
            return tuple(states)

        zero = jnp.zeros((at.shape[0], LANES), F32)
        states = lax.fori_loop(0, chunks, chunk, (zero,) * (batches * TILES))
        for b in range(batches):
            for lt in range(TILES):
                first_o[b, :, tile_at(i, lt)] = states[b * TILES + lt]
        return carry

    lax.fori_loop(0, blocks, over_block, 0)


def back_kernel(
    batches, span, width, rank, states_n,
    sg, spre, pre, conv, mixed, rim, marks, bx, cx, state_in, grad_in, at, skip, cw, xw, dw,
    low_o, pgrad_o, inner_o, spill_o, vec_o,
    seff, x, hist, decays, drive, zsum, acc_b, acc_c, ext,
):
    blocks = width // BLOCK
    rows_n = batches * span
    chunks = span // 8
    m = marks[...]
    step = softplus(spre[...])
    seff[...] = step + m[:, 0:1] * STOP
    x[...] = step * conv[...].astype(F32)
    acc_b[...] = jnp.zeros_like(acc_b)
    acc_c[...] = jnp.zeros_like(acc_c)
    row_ids = lax.broadcasted_iota(jnp.int32, (8, LANES), 0)

    def over_block(i, carry):
        rate = [at[:, tile_at(i, lt)] for lt in range(TILES)]

        def again(tc, states):
            states = list(states)
            for b in range(batches):
                rows = pl.ds(pl.multiple_of(b * span + tc * 8, 8), 8)
                for lt in range(TILES):
                    s8 = seff[rows, tile_at(i, lt)]
                    x8 = x[rows, tile_at(i, lt)]
                    h = states[b * TILES + lt]
                    lanes = pl.ds(lt * LANES, LANES)
                    for j in range(8):
                        t = tc * 8 + j
                        decay = jnp.exp2(s8[j : j + 1] * rate[lt])
                        h = decay * h + x8[j : j + 1] * bx[b * span + t]
                        decays[b, t, :, lanes] = decay
                        hist[b, t + 1, :, lanes] = h
                    states[b * TILES + lt] = h
            return tuple(states)

        for b in range(batches):
            hist[b, 0] = state_in[b, :, block_at(i)]
        start = tuple(
            state_in[b, :, tile_at(i, lt)] for b in range(batches) for lt in range(TILES)
        )
        lax.fori_loop(0, chunks, again, start)

        sums = tuple(jnp.zeros((states_n, LANES), F32) for _ in range(TILES))
        for b in range(batches):

            def chunk(k, held):
                held = list(held)
                tc = chunks - 1 - k
                rows = pl.ds(pl.multiple_of(b * span + tc * 8, 8), 8)
                s8, x8, g8 = [], [], []
                for lt in range(TILES):
                    s8.append(seff[rows, tile_at(i, lt)])
                    x8.append(x[rows, tile_at(i, lt)])
                    g8.append(sg[rows, tile_at(i, lt)])
                drives = [[None] * 8 for _ in range(TILES)]
                zs = [[None] * 8 for _ in range(TILES)]
                for j in range(7, -1, -1):
                    t = tc * 8 + j
                    part_b, part_c = [], []
                    for lt in range(TILES):
                        lanes = pl.ds(lt * LANES, LANES)
                        total = held[lt] + g8[lt][j : j + 1] * cx[b * span + t]
                        q = decays[b, t, :, lanes] * total
                        log_grad = q * hist[b, t, :, lanes]
                        held[TILES + lt] = held[TILES + lt] + log_grad * s8[lt][j : j + 1]
                        zs[lt][j] = halves(log_grad * rate[lt])
                        drives[lt][j] = halves(total * bx[b * span + t])
                        part_b.append(total * x8[lt][j : j + 1])
                        part_c.append(g8[lt][j : j + 1] * hist[b, t + 1, :, lanes])
                        held[lt] = q
                    acc_b[b * span + t] += sum(part_b[1:], part_b[0])
                    acc_c[b * span + t] += sum(part_c[1:], part_c[0])
                for lt in range(TILES):
                    drive[rows, tile_at(i, lt)] = fold_rows(drives[lt], row_ids)
                    zsum[rows, tile_at(i, lt)] = fold_rows(zs[lt], row_ids)
                return tuple(held)

            start = tuple(grad_in[b, :, tile_at(i, lt)] for lt in range(TILES)) + sums
            sums = lax.fori_loop(0, chunks, chunk, start)[TILES:]
        for lt in range(TILES):
            vec_o[0:states_n, tile_at(i, lt)] = -sums[lt]
        return carry

    lax.fori_loop(0, blocks, over_block, 0)

    column_ids = lax.broadcasted_iota(jnp.int32, (states_n, rows_n), 1)

    def gather_column(t, pair):
        now = []
        for held, acc in zip(pair, (acc_b, acc_c)):
            column = jnp.sum(acc[t], axis=1, keepdims=True)
            now.append(jnp.where(column_ids == t, column, held))
        return tuple(now)

    zero = jnp.zeros((states_n, rows_n), F32)
    b_grad, c_grad = lax.fori_loop(0, rows_n, gather_column, (zero, zero), unroll=8)
    placed = jnp.concatenate(
        [
            jnp.zeros((rank, rows_n), F32),
            b_grad,
            c_grad,
            jnp.zeros((LANES - rank - 2 * states_n, rows_n), F32),
        ],
        0,
    ).T
    conv_f = conv[...].astype(F32)
    step = softplus(spre[...])
    step_grad = zsum[...] * (1.0 / LOG2E) + drive[...] * conv_f
    pre_g = step_grad * jax.nn.sigmoid(spre[...])
    low = pre_g.astype(BF16)
    low_o[...] = low
    pgrad = (against(low, dw[...]) + placed).astype(BF16)
    pgrad_o[...] = pgrad
    conv_grad = sg[...] * skip[...] + step * drive[...] + against(pgrad, xw[...])
    pre_grad = conv_grad * silu_slope(pre[...])
    vec_o[states_n + 4 : states_n + 5] = jnp.sum(pre_grad, axis=0, keepdims=True)
    vec_o[states_n + 5 : states_n + 6] = jnp.sum(pre_g, axis=0, keepdims=True)
    vec_o[states_n + 6 : states_n + 7] = jnp.sum(sg[...] * conv_f, axis=0, keepdims=True)
    vec_o[states_n + 7 : states_n + 8] = jnp.zeros((1, width), F32)
    taps = [jnp.zeros((1, width), F32) for _ in range(4)]
    for b in range(batches):
        lo, hi = b * span, (b + 1) * span
        ext[0:8] = rim[b]
        ext[8 : 8 + span] = mixed[lo:hi, :width].astype(F32)
        grad_b = pre_grad[lo:hi]
        taps[3] = taps[3] + jnp.sum(grad_b * ext[8 : 8 + span], axis=0, keepdims=True)
        for k in (1, 2, 3):
            taps[3 - k] = taps[3 - k] + jnp.sum(
                grad_b * (m[lo:hi, k : k + 1] * ext[8 - k : 8 - k + span]),
                axis=0, keepdims=True,
            )
        back = cw[3:4] * grad_b
        spill = jnp.zeros((8, width), F32)
        for k in (1, 2, 3):
            ext[0:8] = jnp.zeros((8, width), F32)
            ext[8 : 8 + span] = cw[3 - k : 4 - k] * (m[lo:hi, k : k + 1] * grad_b)
            ext[8 + span : 16 + span] = jnp.zeros((8, width), F32)
            back = back + ext[8 + k : 8 + k + span]
            spill = spill + ext[k : 8 + k]
        inner_o[lo:hi] = back
        spill_o[b] = spill
    for k in range(4):
        vec_o[states_n + k : states_n + k + 1] = taps[k]


def run(kernel, outs, scratch, *args, flops=0):
    return pl.pallas_call(
        kernel,
        out_shape=[jax.ShapeDtypeStruct(*o) for o in outs],
        in_specs=[pl.BlockSpec(memory_space=pltpu.VMEM)] * len(args),
        out_specs=[pl.BlockSpec(memory_space=pltpu.VMEM)] * len(outs),
        scratch_shapes=[pltpu.VMEM(*s) for s in scratch],
        compiler_params=pltpu.CompilerParams(vmem_limit_bytes=VMEM_LIMIT),
    )(*args)


def flip(array, axis, bit):
    count = lax.axis_size(axis)
    return lax.ppermute(array, axis, [(i, i ^ bit) for i in range(count)])


def shifted(array, by):
    count = lax.axis_size("seq")
    pairs = [(i, i + by) for i in range(count) if 0 <= i + by < count]
    return lax.ppermute(array, "seq", pairs)


def bits_of(count):
    bits = [1 << k for k in range(count.bit_length() - 1)]
    assert 1 << len(bits) == count
    return bits


def pack_total(total):
    one = total.astype(BF16)
    rest = total - one.astype(F32)
    two = rest.astype(BF16)
    three = (rest - two.astype(F32)).astype(BF16)
    return jnp.concatenate([one, two, three], 1)


def carry_forward(final, total, at):
    place = lax.axis_index("seq")
    before = jnp.zeros_like(final)
    span = jnp.zeros_like(total)
    spans = []
    for bit in bits_of(lax.axis_size("seq")):
        upper = (place & bit) != 0
        sent = jnp.concatenate([final.astype(BF16), pack_total(total)], 1)
        got = flip(sent, "seq", bit).astype(F32)
        n = at.shape[0]
        their, their_total = got[:, :n], got[:, n : n + 1] + got[:, n + 1 : n + 2] + got[:, n + 2 :]
        spans.append(their_total)
        before = jnp.where(upper, jnp.exp2(span * at) * their + before, before)
        span = jnp.where(upper, span + their_total, span)
        early, late = jnp.where(upper, their, final), jnp.where(upper, final, their)
        late_total = jnp.where(upper, total, their_total)
        final = jnp.exp2(late_total * at) * early + late
        total = total + their_total
    return before, spans


def carry_backward(first, total, spans, at):
    place = lax.axis_index("seq")
    after = jnp.zeros_like(first)
    span = jnp.zeros_like(total)
    for bit, their_total in zip(bits_of(lax.axis_size("seq")), spans):
        lower = (place & bit) == 0
        their = flip(first.astype(BF16), "seq", bit).astype(F32)
        after = jnp.where(lower, jnp.exp2(span * at) * their + after, after)
        span = jnp.where(lower, span + their_total, span)
        early, late = jnp.where(lower, first, their), jnp.where(lower, their, first)
        early_total = jnp.where(lower, total, their_total)
        first = jnp.exp2(early_total * at) * late + early
        total = total + their_total
    return after


def pick(array, index, axis):
    return lax.dynamic_index_in_dim(array, index, axis, keepdims=False)


def scatter_sum(parts):
    core, place = lax.axis_index("section"), lax.axis_index("seq")
    got = flip(pick(parts, 1 - core, 1), "section", 1)
    total = pick(parts, core, 1).astype(F32) + got.astype(F32)
    bits = bits_of(lax.axis_size("seq"))
    total = total.astype(BF16).reshape((2,) * len(bits) + total.shape[1:])
    left = len(bits)
    for k, bit in enumerate(bits):
        axis = left - 1
        mine = (place // bit) % 2
        got = flip(pick(total, 1 - mine, axis), "seq", bit)
        total = pick(total, mine, axis).astype(F32) + got.astype(F32)
        if k < len(bits) - 1:
            total = total.astype(BF16)
        left -= 1
    return total


def all_sum(parts):
    parts = parts + flip(parts, "section", 1)
    for bit in bits_of(lax.axis_size("seq")):
        parts = parts + flip(parts, "seq", bit)
    return parts


def local(
    tokens, starts, norm_gain, in_weight, conv_weight, conv_bias, xproj_weight,
    dtproj_weight, dt_bias, decay_rate, skip_gain, out_weight, cotangent,
):
    core = lax.axis_index("section")
    place = lax.axis_index("seq")
    cores = lax.axis_size("section")
    count = lax.axis_size("seq")
    batch_count, span, model = tokens.shape
    width = conv_weight.shape[2]
    states_n = decay_rate.shape[2]
    rank = dtproj_weight.shape[1]
    batches = batch_count // cores
    rows_n = batches * span
    low_core = core == 0

    own = (
        norm_gain[0][None], in_weight[0], conv_weight[0], conv_bias[0][None],
        jnp.pad(xproj_weight[0], ((0, 0), (0, LANES - xproj_weight.shape[2]))),
        jnp.pad(dtproj_weight[0], ((0, LANES - rank), (0, 0))),
        dt_bias[0][None], decay_rate[0].T * -LOG2E, skip_gain[0][None], out_weight[0],
    )
    other = tuple(flip(w, "section", 1) for w in own)
    layer_w = (
        tuple(jnp.where(low_core, a, b) for a, b in zip(own, other)),
        tuple(jnp.where(low_core, b, a) for a, b in zip(own, other)),
    )

    def mine(array):
        return lax.dynamic_slice_in_dim(array, core * batches, batches, 0).reshape(
            (rows_n,) + array.shape[2:]
        )

    rows0 = mine(tokens)
    top = mine(cotangent)
    r = lax.dynamic_slice_in_dim(starts, core * batches, batches, 0).astype(F32)
    r_ext = jnp.concatenate([shifted(r[:, -3:].astype(BF16), 1).astype(F32), r], 1)
    free = 1.0 - r_ext
    m1 = free[:, 3:]
    m2 = m1 * free[:, 2:-1]
    m3 = m2 * free[:, 1:-2]
    marks = jnp.stack([r, m1, m2, m3], -1).reshape(rows_n, 4)

    def front(rows, w):
        normed = norm_rows(rows.astype(F32), w[0]).astype(BF16)
        mixed = dot(normed, w[1]).astype(BF16)
        tail = mixed.reshape(batches, span, 2 * width)[:, -3:, :width]
        rim = jnp.pad(shifted(tail, 1).astype(F32), ((0, 0), (5, 0), (0, 0)))
        pre, conv, proj, spre, bx, cx, final, total = run(
            functools.partial(front_kernel, batches, span, width, rank, states_n),
            [
                ((rows_n, width), F32), ((rows_n, width), BF16), ((rows_n, LANES), BF16),
                ((rows_n, width), F32), ((rows_n, states_n, LANES), F32),
                ((rows_n, states_n, LANES), F32), ((batches, states_n, width), F32),
                ((batches, 1, width), F32),
            ],
            [
                ((batches, span + 8, width), F32), ((rows_n, width), F32),
                ((rows_n, width), F32),
            ],
            mixed, rim, marks, w[2], w[3], w[4], w[5], w[6], w[7],
        )
        before, spans = carry_forward(final, total, w[7])
        scanned, gated = run(
            functools.partial(out_kernel, batches, span, width),
            [((rows_n, width), F32), ((rows_n, width), BF16)],
            [((rows_n, width), F32), ((rows_n, width), F32)],
            mixed, conv, spre, marks, bx, cx, before, w[7], w[8],
        )
        result = (rows.astype(F32) + dot(gated, w[9])).astype(BF16)
        kept = (rows, normed, mixed, rim, pre, conv, proj, spre, bx, cx, before, total, spans,
                scanned, gated)
        return result, kept

    def back(g, w, kept):
        (rows, normed, mixed, rim, pre, conv, proj, spre, bx, cx, before, total, spans,
         scanned, gated) = kept
        gated_grad = against(g, w[9])
        gate = mixed[:, width:].astype(F32)
        sg = gated_grad * jax.nn.silu(gate)
        gate_grad = gated_grad * scanned * silu_slope(gate)
        first, = run(
            functools.partial(back_local_kernel, batches, span, width),
            [((batches, states_n, width), F32)],
            [((rows_n, width), F32)],
            sg, spre, marks, cx, w[7],
        )
        after = carry_backward(first, total, spans, w[7])
        low, pgrad, inner, spill, vec = run(
            functools.partial(back_kernel, batches, span, width, rank, states_n),
            [
                ((rows_n, width), BF16), ((rows_n, LANES), BF16), ((rows_n, width), F32),
                ((batches, 8, width), F32), ((states_n + 8, width), F32),
            ],
            [
                ((rows_n, width), F32), ((rows_n, width), F32),
                ((batches, span + 1, states_n, BLOCK), F32),
                ((batches, span, states_n, BLOCK), F32),
                ((rows_n, width), F32), ((rows_n, width), F32),
                ((rows_n, states_n, LANES), F32), ((rows_n, states_n, LANES), F32),
                ((span + 16, width), F32),
            ],
            sg, spre, pre, conv, mixed, rim, marks, bx, cx, before, after, w[7], w[8], w[2],
            w[4], w[5],
        )
        got = shifted(spill[:, 5:], -1)
        inner = inner.reshape(batches, span, width) + jnp.pad(
            got, ((0, 0), (span - 3, 0), (0, 0))
        )
        mixed_grad = jnp.concatenate(
            [inner.reshape(rows_n, width).astype(BF16), gate_grad.astype(BF16)], 1
        )
        normed_grad = against(mixed_grad, w[1])
        source = rows.astype(F32)
        input_grad, grad_gain = jax.vjp(norm_rows, source, w[0])[1](normed_grad)
        low_rows = (g.astype(F32) + input_grad).astype(BF16)
        half = lambda a: a.reshape(count, 2, a.shape[0] // (2 * count), a.shape[1])
        grad_in = half(across(mixed_grad, normed).astype(BF16))
        grad_out = half(across(gated, g).astype(BF16))
        grad_x = across(conv, pgrad)
        grad_dt = across(low, proj)
        columns = lax.broadcasted_iota(jnp.int32, (1, LANES), 1)
        small = jnp.where(
            columns < xproj_weight.shape[2], grad_x, jnp.roll(grad_dt, LANES - rank, 1)
        ).astype(BF16)
        small = small.reshape(count, 2, -1, LANES)
        grad_gain = jnp.pad(grad_gain, ((0, 0), (0, width - model)))
        vec = jnp.concatenate([vec[: states_n + 7], grad_gain], 0)
        return low_rows, (grad_in, grad_out, small, vec)

    def reduce(parts):
        grad_in, grad_out, small, vec = parts
        return scatter_sum(grad_in), scatter_sum(grad_out), scatter_sum(small), all_sum(vec)

    rows1, kept0 = front(rows0, layer_w[0])
    out1, kept1 = front(rows1, layer_w[1])
    g0, parts1 = back(top, layer_w[1], kept1)
    sums1 = reduce(parts1)
    dx, parts0 = back(g0, layer_w[0], kept0)
    sums0 = reduce(parts0)

    def settle(zero, one):
        got = flip(jnp.where(low_core, one, zero), "section", 1)
        own = jnp.where(low_core, zero, one)
        both = jnp.where(low_core, jnp.stack([own, got]), jnp.stack([got, own]))
        return both.reshape((-1,) + own.shape[1:])

    grad_in, grad_out, small = (settle(a, b) for a, b in zip(sums0[:3], sums1[:3]))
    vec = jnp.where(low_core, sums0[3], sums1[3])
    part = width // count
    vec_own = lax.dynamic_slice_in_dim(vec, place * part, part, 1)
    gain_part = model // count
    gain = lax.dynamic_slice_in_dim(vec[states_n + 7], place * gain_part, gain_part, 0)

    got = flip(jnp.where(low_core, out1, dx), "section", 1)
    boundary = jnp.where(
        low_core, jnp.concatenate([dx, got], 0), jnp.concatenate([got, out1], 0)
    ).reshape(1, batch_count, span, model)
    x_width = xproj_weight.shape[2]
    return (
        boundary,
        gain[None],
        grad_in.T[None],
        vec_own[states_n : states_n + 4][None],
        vec_own[states_n + 4][None],
        small[:, :x_width][None],
        small[:, x_width:].T[None],
        vec_own[states_n + 5][None],
        vec_own[:states_n].T[None],
        vec_own[states_n + 6][None],
        grad_out[None],
    )


def solution(mesh):
    in_specs = (
        P(None, "seq", None), P(None, "seq"), P("section", None), P("section", None, None),
        P("section", None, None), P("section", None), P("section", None, None),
        P("section", None, None), P("section", None), P("section", None, None),
        P("section", None), P("section", None, None), P(None, "seq", None),
    )
    out_specs = (
        P("section", None, "seq", None), P("section", "seq"), P("section", None, "seq"),
        P("section", None, "seq"), P("section", "seq"), P("section", "seq", None),
        P("section", None, "seq"), P("section", "seq"), P("section", "seq", None),
        P("section", "seq"), P("section", "seq", None),
    )
    return jax.shard_map(local, mesh=mesh, in_specs=in_specs, out_specs=out_specs, check_vma=False)
```

```python
import functools
import jax
import jax.numpy as jnp
from jax import lax
from jax.experimental import pallas as pl
from jax.experimental.pallas import tpu as pltpu
from jax.sharding import PartitionSpec as P

EPS = 1e-05
LOG2E = 1.4426950408889634
STOP = 1e7
LANES = 128
BLOCK = 256
TILES = BLOCK // LANES
F32 = jnp.float32
BF16 = jnp.bfloat16
SLACK = 8 * 1024 * 1024
HOP_LIMIT = 6 * 1024 * 1024


def dot(left, right):
    return jnp.dot(left, right, preferred_element_type=F32)


def across(left, right):
    return lax.dot_general(left, right, (((0,), (0,)), ((), ())), preferred_element_type=F32)


def against(left, right):
    return lax.dot_general(left, right, (((1,), (1,)), ((), ())), preferred_element_type=F32)


def norm_rows(source, gain_row):
    return source * lax.rsqrt(jnp.mean(source * source, axis=-1, keepdims=True) + EPS) * gain_row


def softplus(v):
    return jnp.maximum(v, 0.0) + jnp.log1p(jnp.exp(-jnp.abs(v)))


def silu_slope(v):
    gate = jax.nn.sigmoid(v)
    return gate * (1.0 + v * (1.0 - gate))


def pair_up(left, right, row_ids, width):
    mask = (row_ids % (2 * width)) < width
    kept = jnp.where(mask, left, right)
    moved = jnp.where(mask, right, left)
    return kept + pltpu.roll(moved, 8 - width, 0)


def fold_rows(parts, row_ids):
    width = 1
    while len(parts) > 1:
        parts = [
            pair_up(parts[i], parts[i + 1], row_ids, width) for i in range(0, len(parts), 2)
        ]
        width *= 2
    return parts[0]


def halves(v):
    return v[:8] + v[8:]


def spread_columns(table, first, target):
    width = target.shape[1]
    for t in range(target.shape[0]):
        column = table[first : first + width, t : t + 1]
        target[t] = jnp.broadcast_to(column, (width, LANES))


def block_at(i):
    return pl.ds(pl.multiple_of(i * BLOCK, BLOCK), BLOCK)


def tile_at(i, lt):
    return pl.ds(pl.multiple_of(i * BLOCK + lt * LANES, LANES), LANES)


def local_scan(batches, span, blocks, seff, x, bx, at, final):
    def over_block(i, carry):
        rate = [at[:, tile_at(i, lt)] for lt in range(TILES)]

        def chunk(tc, states):
            states = list(states)
            for b in range(batches):
                rows = pl.ds(pl.multiple_of(b * span + tc * 8, 8), 8)
                for lt in range(TILES):
                    s8 = seff[rows, tile_at(i, lt)]
                    x8 = x[rows, tile_at(i, lt)]
                    h = states[b * TILES + lt]
                    for j in range(8):
                        decay = jnp.exp2(s8[j : j + 1] * rate[lt])
                        h = decay * h + x8[j : j + 1] * bx[b * span + tc * 8 + j]
                    states[b * TILES + lt] = h
            return tuple(states)

        zero = jnp.zeros((at.shape[0], LANES), F32)
        states = lax.fori_loop(0, span // 8, chunk, (zero,) * (batches * TILES))
        for b in range(batches):
            for lt in range(TILES):
                final[b, :, tile_at(i, lt)] = states[b * TILES + lt]
        return carry

    lax.fori_loop(0, blocks, over_block, 0)


def back_scan(batches, span, blocks, seff, sg, cx, at, first):
    chunks = span // 8

    def over_block(i, carry):
        rate = [at[:, tile_at(i, lt)] for lt in range(TILES)]

        def chunk(k, states):
            states = list(states)
            tc = chunks - 1 - k
            for b in range(batches):
                rows = pl.ds(pl.multiple_of(b * span + tc * 8, 8), 8)
                for lt in range(TILES):
                    s8 = seff[rows, tile_at(i, lt)]
                    g8 = sg[rows, tile_at(i, lt)]
                    q = states[b * TILES + lt]
                    for j in range(7, -1, -1):
                        decay = jnp.exp2(s8[j : j + 1] * rate[lt])
                        q = decay * (q + g8[j : j + 1] * cx[b * span + tc * 8 + j])
                    states[b * TILES + lt] = q
            return tuple(states)

        zero = jnp.zeros((at.shape[0], LANES), F32)
        states = lax.fori_loop(0, chunks, chunk, (zero,) * (batches * TILES))
        for b in range(batches):
            for lt in range(TILES):
                first[b, :, tile_at(i, lt)] = states[b * TILES + lt]
        return carry

    lax.fori_loop(0, blocks, over_block, 0)


def fetch(layer, own, other, held, sem):
    mine = lax.axis_index("section") == layer

    @pl.when(mine)
    def _():
        pltpu.make_async_copy(own, held, sem).start()

    @pl.when(jnp.logical_not(mine))
    def _():
        pltpu.make_async_copy(other, held, sem).start()

    return pltpu.make_async_copy(own, held, sem)


def split_total(totals):
    width = totals[0].shape[1]
    row_ids = lax.broadcasted_iota(jnp.int32, (16, width), 0)
    block = jnp.zeros((16, width), F32)
    for b, total in enumerate(totals):
        rest = total
        for k in range(3):
            part = rest.astype(BF16).astype(F32)
            block = jnp.where(row_ids == 3 * b + k, part, block)
            rest = rest - part
    return block.astype(BF16)


def join_total(block, b):
    block = block.astype(F32)
    return block[3 * b : 3 * b + 1] + block[3 * b + 1 : 3 * b + 2] + block[3 * b + 2 : 3 * b + 3]


def tap_rows(ext, rim, mixed, width, span):
    ext[5:8] = rim.astype(F32)
    ext[8 : 8 + span] = mixed.astype(F32)


def conv_sum(ext, m, vec, n, span):
    v = vec[n + 4 : n + 5] + vec[n + 3 : n + 4] * ext[8 : 8 + span]
    for k in (1, 2, 3):
        v = v + vec[n + 3 - k : n + 4 - k] * (m[:, k : k + 1] * ext[8 - k : 8 - k + span])
    return v


def step_sum(proj, low_w, vec, rank, n):
    return dot(proj[:, :rank], low_w[rank + 2 * n :]) + vec[n + 5 : n + 6]


def front_kernel(
    batches, span, width, rank, states_n, with_back,
    *refs,
):
    refs = list(refs)
    mixed, rim, marks, vec, low_w = refs[:5]
    del refs[:5]
    if with_back:
        g, own_w, other_w = refs[:3]
        del refs[:3]
    conv_o, proj_o, final_o, total_o, send_o = refs[:5]
    del refs[:5]
    if with_back:
        first_o, send_back_o = refs[:2]
        del refs[:2]
    ext, seff, x, bx, cx = refs[:5]
    if with_back:
        sg, out_w, sem = refs[5:]
        arrival = fetch(1, own_w, other_w, out_w, sem)
    n = states_n
    m = marks[...]
    at = vec.at[0:n]
    for b in range(batches):
        lo, hi = b * span, (b + 1) * span
        tap_rows(ext, rim[b], mixed[lo:hi, :width], width, span)
        x[lo:hi] = jax.nn.silu(conv_sum(ext, m[lo:hi], vec, n, span))
    conv = x[...].astype(BF16)
    conv_o[...] = conv
    proj = against(conv, low_w[...]).astype(BF16)
    proj_o[...] = proj
    step = softplus(step_sum(proj, low_w, vec, rank, n))
    seff[...] = step + m[:, 0:1] * STOP
    x[...] = step * conv.astype(F32)
    totals = [
        jnp.sum(seff[b * span : (b + 1) * span], axis=0, keepdims=True) for b in range(batches)
    ]
    for b in range(batches):
        total_o[b] = totals[b]
    table = proj.astype(F32).T
    spread_columns(table, rank, bx)
    local_scan(batches, span, width // BLOCK, seff, x, bx, at, final_o)
    for b in range(batches):
        send_o[b * n : (b + 1) * n] = final_o[b].astype(BF16)
    send_o[batches * n :] = split_total(totals)
    if with_back:
        arrival.wait()
        spread_columns(table, rank + n, cx)
        gg = against(g[...], out_w[...])
        sg[...] = gg * jax.nn.silu(mixed[:, width:].astype(F32))
        back_scan(batches, span, width // BLOCK, seff, sg, cx, at, first_o)
        for b in range(batches):
            send_back_o[b * n : (b + 1) * n] = first_o[b].astype(BF16)


def hop_kernel(batches, n, forward, backward, last, *refs):
    refs = list(refs)
    take = lambda k: [refs.pop(0) for _ in range(k)]
    upper_ref, at_ref, total = take(3)
    upper = upper_ref[0] != 0
    at = at_ref[...]
    if forward:
        got, final, before, span = take(4)
    else:
        (their_total,) = take(1)
    if backward:
        got_b, first, after, span_b = take(4)
    total_o, = take(1)
    if forward:
        final_o, before_o, span_o, theirs_o, send_o = take(5)
    if backward:
        first_o, after_o, span_b_o, send_b_o = take(4)
    totals = []
    for b in range(batches):
        mine_t = total[b]
        if forward:
            their_t = join_total(got[batches * n :], b)
            theirs_o[b] = their_t
        else:
            their_t = their_total[b]
        if forward:
            their = got[b * n : (b + 1) * n].astype(F32)
            mine = final[b]
            held = before[b]
            before_o[b] = jnp.where(upper, jnp.exp2(span[b] * at) * their + held, held)
            span_o[b] = jnp.where(upper, span[b] + their_t, span[b])
            if not last:
                early = jnp.where(upper, their, mine)
                late = jnp.where(upper, mine, their)
                now = jnp.exp2(jnp.where(upper, mine_t, their_t) * at) * early + late
                final_o[b] = now
                send_o[b * n : (b + 1) * n] = now.astype(BF16)
        if backward:
            their = got_b[b * n : (b + 1) * n].astype(F32)
            mine = first[b]
            held = after[b]
            after_o[b] = jnp.where(upper, held, jnp.exp2(span_b[b] * at) * their + held)
            span_b_o[b] = jnp.where(upper, span_b[b], span_b[b] + their_t)
            if not last:
                early = jnp.where(upper, their, mine)
                late = jnp.where(upper, mine, their)
                now = jnp.exp2(jnp.where(upper, their_t, mine_t) * at) * late + early
                first_o[b] = now
                send_b_o[b * n : (b + 1) * n] = now.astype(BF16)
        totals.append(mine_t + their_t)
        total_o[b] = totals[-1]
    if forward and not last:
        send_o[batches * n :] = split_total(totals)


def prepare(step, marks, conv, seff, x):
    seff[...] = step + marks * STOP
    x[...] = step * conv.astype(F32)


def end_kernel(
    batches, span, width, rank, n,
    mixed, conv, proj, marks, state_in, vec, low_w, rows, gain, gain_before,
    own_out, other_out, own_in, other_in,
    scanned_o, gated_t_o, rows_o, normed_before_o, normed_o, mixed_o,
    seff, x, bx, cx, out_w, in_w, sems,
):
    arrivals = [
        fetch(0, own_out, other_out, out_w, sems.at[0]),
        fetch(1, own_in, other_in, in_w, sems.at[1]),
    ]
    blocks = width // BLOCK
    at = vec.at[0:n]
    normed_before_o[...] = norm_rows(rows[...].astype(F32), gain_before[...]).astype(BF16)
    step = softplus(step_sum(proj[...], low_w, vec, rank, n))
    prepare(step, marks[:, 0:1], conv[...], seff, x)
    table = proj[...].astype(F32).T
    spread_columns(table, rank, bx)
    spread_columns(table, rank + n, cx)
    row_ids = lax.broadcasted_iota(jnp.int32, (8, LANES), 0)

    def over_block(i, carry):
        rate = [at[:, tile_at(i, lt)] for lt in range(TILES)]

        def chunk(tc, states):
            states = list(states)
            for b in range(batches):
                rows8 = pl.ds(pl.multiple_of(b * span + tc * 8, 8), 8)
                for lt in range(TILES):
                    s8 = seff[rows8, tile_at(i, lt)]
                    x8 = x[rows8, tile_at(i, lt)]
                    h = states[b * TILES + lt]
                    parts = []
                    for j in range(8):
                        t = b * span + tc * 8 + j
                        decay = jnp.exp2(s8[j : j + 1] * rate[lt])
                        h = decay * h + x8[j : j + 1] * bx[t]
                        parts.append(halves(h * cx[t]))
                    states[b * TILES + lt] = h
                    scanned_o[rows8, tile_at(i, lt)] = fold_rows(parts, row_ids)
            return tuple(states)

        start = tuple(
            state_in[b, :, tile_at(i, lt)] for b in range(batches) for lt in range(TILES)
        )
        lax.fori_loop(0, span // 8, chunk, start)
        return carry

    lax.fori_loop(0, blocks, over_block, 0)
    scanned = scanned_o[...] + vec[n + 6 : n + 7] * conv[...].astype(F32)
    scanned_o[...] = scanned
    gated_f = scanned * jax.nn.silu(mixed[:, width:].astype(F32))
    gated = gated_f.astype(BF16)
    gated_t_o[...] = gated_f.T.astype(BF16)
    arrivals[0].wait()
    result = (rows[...].astype(F32) + dot(gated, out_w[...])).astype(BF16)
    rows_o[...] = result
    normed_o[...] = norm_rows(result.astype(F32), gain[...]).astype(BF16)
    arrivals[1].wait()

    def columns(i, carry):
        at_i = pl.ds(pl.multiple_of(i * 512, 512), 512)
        mixed_o[:, at_i] = dot(normed_o[...], in_w[:, at_i]).astype(BF16)
        return carry

    lax.fori_loop(0, 2 * width // 512, columns, 0)


def back_kernel(
    batches, span, width, rank, n, x_width, with_out,
    *refs,
):
    refs = list(refs)
    take = lambda k: [refs.pop(0) for _ in range(k)]
    gg, conv, mixed, rim, marks, state_in, grad_in, vec, low_w, proj = take(10)
    if with_out:
        rows, own_out, other_out = take(3)
    inner_o, spill_o, small_o = take(3)
    if with_out:
        gate_o, gated_t_o, out_o = take(3)
    seff, x, hist, decays, drive, zsum, acc_b, acc_c, ext, sg, vec_o, bx, cx, pre_grad = take(14)
    if with_out:
        scanned_ref, gg_s, out_w, sem = take(4)
        arrival = fetch(1, own_out, other_out, out_w, sem)
    blocks = width // BLOCK
    rows_n = batches * span
    chunks = span // 8
    m = marks[...]
    at = vec.at[0:n]
    spre = step_sum(proj[...], low_w, vec, rank, n)
    prepare(softplus(spre), m[:, 0:1], conv[...], seff, x)
    table = proj[...].astype(F32).T
    spread_columns(table, rank, bx)
    spread_columns(table, rank + n, cx)
    if with_out:
        arrival.wait()
        gg_s[...] = against(gg[...], out_w[...])
        gg = gg_s
    sg[...] = gg[...] * jax.nn.silu(mixed[:, width:].astype(F32))
    acc_b[...] = jnp.zeros_like(acc_b)
    acc_c[...] = jnp.zeros_like(acc_c)
    vec_o[...] = jnp.zeros_like(vec_o)
    row_ids = lax.broadcasted_iota(jnp.int32, (8, LANES), 0)

    def over_block(i, carry):
        rate = [at[:, tile_at(i, lt)] for lt in range(TILES)]

        def again(tc, states):
            states = list(states)
            for b in range(batches):
                rows8 = pl.ds(pl.multiple_of(b * span + tc * 8, 8), 8)
                for lt in range(TILES):
                    s8 = seff[rows8, tile_at(i, lt)]
                    x8 = x[rows8, tile_at(i, lt)]
                    h = states[b * TILES + lt]
                    lanes = pl.ds(lt * LANES, LANES)
                    parts = []
                    for j in range(8):
                        t = tc * 8 + j
                        decay = jnp.exp2(s8[j : j + 1] * rate[lt])
                        h = decay * h + x8[j : j + 1] * bx[b * span + t]
                        decays[b, t, :, lanes] = decay
                        hist[b, t + 1, :, lanes] = h
                        if with_out:
                            parts.append(halves(h * cx[b * span + t]))
                    states[b * TILES + lt] = h
                    if with_out:
                        scanned_ref[rows8, tile_at(i, lt)] = fold_rows(parts, row_ids)
            return tuple(states)

        for b in range(batches):
            hist[b, 0] = state_in[b, :, block_at(i)]
        start = tuple(
            state_in[b, :, tile_at(i, lt)] for b in range(batches) for lt in range(TILES)
        )
        lax.fori_loop(0, chunks, again, start)

        sums = tuple(jnp.zeros((n, LANES), F32) for _ in range(TILES))
        for b in range(batches):

            def chunk(k, held):
                held = list(held)
                tc = chunks - 1 - k
                rows8 = pl.ds(pl.multiple_of(b * span + tc * 8, 8), 8)
                s8, x8, g8 = [], [], []
                for lt in range(TILES):
                    s8.append(seff[rows8, tile_at(i, lt)])
                    x8.append(x[rows8, tile_at(i, lt)])
                    g8.append(sg[rows8, tile_at(i, lt)])
                drives = [[None] * 8 for _ in range(TILES)]
                zs = [[None] * 8 for _ in range(TILES)]
                for j in range(7, -1, -1):
                    t = tc * 8 + j
                    part_b, part_c = [], []
                    for lt in range(TILES):
                        lanes = pl.ds(lt * LANES, LANES)
                        total = held[lt] + g8[lt][j : j + 1] * cx[b * span + t]
                        q = decays[b, t, :, lanes] * total
                        log_grad = q * hist[b, t, :, lanes]
                        held[TILES + lt] = held[TILES + lt] + log_grad * s8[lt][j : j + 1]
                        zs[lt][j] = halves(log_grad * rate[lt])
                        drives[lt][j] = halves(total * bx[b * span + t])
                        part_b.append(total * x8[lt][j : j + 1])
                        part_c.append(g8[lt][j : j + 1] * hist[b, t + 1, :, lanes])
                        held[lt] = q
                    acc_b[b * span + t] += sum(part_b[1:], part_b[0])
                    acc_c[b * span + t] += sum(part_c[1:], part_c[0])
                for lt in range(TILES):
                    drive[rows8, tile_at(i, lt)] = fold_rows(drives[lt], row_ids)
                    zsum[rows8, tile_at(i, lt)] = fold_rows(zs[lt], row_ids)
                return tuple(held)

            start = tuple(grad_in[b, :, tile_at(i, lt)] for lt in range(TILES)) + sums
            sums = lax.fori_loop(0, chunks, chunk, start)[TILES:]
        for lt in range(TILES):
            vec_o[0:n, tile_at(i, lt)] = -sums[lt]
        return carry

    lax.fori_loop(0, blocks, over_block, 0)

    conv_f = conv[...].astype(F32)
    gate = mixed[:, width:].astype(F32)
    if with_out:
        scanned = scanned_ref[...] + vec[n + 6 : n + 7] * conv_f
        gated_f = scanned * jax.nn.silu(gate)
        gated_t_o[...] = gated_f.T.astype(BF16)
        out_o[...] = (rows[...].astype(F32) + dot(gated_f.astype(BF16), out_w[...])).astype(BF16)
        gate_o[...] = gg_s[...] * scanned * silu_slope(gate)

    column_ids = lax.broadcasted_iota(jnp.int32, (n, rows_n), 1)

    def gather_column(t, pair):
        now = []
        for held, acc in zip(pair, (acc_b, acc_c)):
            column = jnp.sum(acc[t], axis=1, keepdims=True)
            now.append(jnp.where(column_ids == t, column, held))
        return tuple(now)

    zero = jnp.zeros((n, rows_n), F32)
    b_grad, c_grad = lax.fori_loop(0, rows_n, gather_column, (zero, zero), unroll=8)
    rest = LANES - rank - 2 * n
    placed = jnp.concatenate(
        [jnp.zeros((rank, rows_n), F32), b_grad, c_grad, jnp.zeros((rest, rows_n), F32)], 0
    ).T
    spre = step_sum(proj[...], low_w, vec, rank, n)
    step = softplus(spre)
    step_grad = zsum[...] * (1.0 / LOG2E) + drive[...] * conv_f
    pre_g = step_grad * jax.nn.sigmoid(spre)
    low = pre_g.astype(BF16)
    low_grad = against(low, low_w[rank + 2 * n :])
    pgrad = (
        jnp.concatenate([low_grad, jnp.zeros((rows_n, LANES - rank), F32)], 1) + placed
    ).astype(BF16)
    small = dot(conv_f.T.astype(BF16), pgrad)
    lows = pltpu.roll(dot(pre_g.T.astype(BF16), proj[...]), x_width, 1)
    columns = lax.broadcasted_iota(jnp.int32, (1, LANES), 1)
    small_o[:, :LANES] = jnp.where(columns < x_width, small, lows).astype(BF16)
    conv_grad = (
        sg[...] * vec[n + 6 : n + 7] + step * drive[...]
        + dot(pgrad[:, : rank + 2 * n], low_w[: rank + 2 * n])
    )
    pre_grad[...] = conv_grad
    vec_o[n + 5 : n + 6] = jnp.sum(pre_g, axis=0, keepdims=True)
    vec_o[n + 6 : n + 7] = jnp.sum(sg[...] * conv_f, axis=0, keepdims=True)
    taps = [jnp.zeros((1, width), F32) for _ in range(4)]
    bias = jnp.zeros((1, width), F32)
    for b in range(batches):
        lo, hi = b * span, (b + 1) * span
        tap_rows(ext, rim[b], mixed[lo:hi, :width], width, span)
        grad_b = pre_grad[lo:hi] * silu_slope(conv_sum(ext, m[lo:hi], vec, n, span))
        bias = bias + jnp.sum(grad_b, axis=0, keepdims=True)
        taps[3] = taps[3] + jnp.sum(grad_b * ext[8 : 8 + span], axis=0, keepdims=True)
        for k in (1, 2, 3):
            taps[3 - k] = taps[3 - k] + jnp.sum(
                grad_b * (m[lo:hi, k : k + 1] * ext[8 - k : 8 - k + span]),
                axis=0, keepdims=True,
            )
        back = vec[n + 3 : n + 4] * grad_b
        spill = jnp.zeros((8, width), F32)
        for k in (1, 2, 3):
            ext[0:8] = jnp.zeros((8, width), F32)
            ext[8 : 8 + span] = vec[n + 3 - k : n + 4 - k] * (m[lo:hi, k : k + 1] * grad_b)
            ext[8 + span : 16 + span] = jnp.zeros((8, width), F32)
            back = back + ext[8 + k : 8 + k + span]
            spill = spill + ext[k : 8 + k]
        inner_o[lo:hi] = back
        spill_o[b] = spill[5:8]
    for k in range(4):
        vec_o[n + k : n + k + 1] = taps[k]
    vec_o[n + 4 : n + 5] = bias
    small_o[:, LANES:] = vec_o[...].T.astype(BF16)


def norm_back(source, gain, grad):
    scale = lax.rsqrt(jnp.mean(source * source, axis=-1, keepdims=True) + EPS)
    unit = source * scale
    scaled = grad * gain
    along = jnp.mean(scaled * unit, axis=-1, keepdims=True)
    return scale * (scaled - unit * along), jnp.sum(grad * unit, axis=0, keepdims=True)


def turn_kernel(
    batches, span, width, rank, n, targets, layer,
    *refs,
):
    refs = list(refs)
    take = lambda k: [refs.pop(0) for _ in range(k)]
    inner, spill, gate_grad, rows, gain, g, own_in, other_in = take(8)
    if layer:
        own_out, other_out, mixed, proj, marks, low_w, vec, scanned = take(8)
    grad_o, g_o = take(2)
    if layer:
        gain_o, gg_o, first_o, send_o, gate_o = take(5)
    in_w, sem_in, mixed_grad = take(3)
    rows_n = batches * span
    if layer:
        seff, sg, cx, out_w, sem_out = take(5)
    arrival = fetch(layer, own_in, other_in, in_w, sem_in)
    if layer:
        arrival_out = fetch(0, own_out, other_out, out_w, sem_out)
    for b in range(batches):
        inner[(b + 1) * span - 3 : (b + 1) * span] += spill[b]
    mixed_grad[:, :width] = inner[...].astype(BF16)
    mixed_grad[:, width:] = gate_grad[...].astype(BF16)
    if layer:
        grad_o[:width] = inner[...].T.astype(BF16)
        grad_o[width:] = gate_grad[...].T.astype(BF16)
    else:
        grad_o[:rows_n] = mixed_grad[...]
    arrival.wait()
    normed_grad = against(mixed_grad[...], in_w[...])
    input_grad, gain_grad = norm_back(rows[...].astype(F32), gain[...], normed_grad)
    if layer:
        gain_o[...] = gain_grad
    else:
        part = gain_grad.shape[1] // targets
        block = 2 * width // targets
        spot = lax.broadcasted_iota(jnp.int32, (16, 2 * width), 1)
        row = lax.broadcasted_iota(jnp.int32, (16, 2 * width), 0)
        wide = jnp.concatenate(
            [gain_grad, jnp.zeros((1, 2 * width - gain_grad.shape[1]), F32)], 1
        )
        riding = jnp.zeros((1, 2 * width), F32)
        for j in range(targets):
            moved = pltpu.roll(wide, j * (block - part), 1)
            at_j = (spot[:1] >= j * block) & (spot[:1] < j * block + part)
            riding = jnp.where(at_j, moved, riding)
        grad_o[rows_n:] = jnp.where(row == 0, riding, 0.0).astype(BF16)
    g_new = (g[...].astype(F32) + input_grad).astype(BF16)
    g_o[...] = g_new
    if layer:
        arrival_out.wait()
        gg = against(g_new, out_w[...])
        gg_o[...] = gg
        gate = mixed[:, width:].astype(F32)
        sg[...] = gg * jax.nn.silu(gate)
        step = softplus(step_sum(proj[...], low_w, vec, rank, n))
        seff[...] = step + marks[:, 0:1] * STOP
        spread_columns(proj[...].astype(F32).T, rank + n, cx)
        gate_new = gg * scanned[...] * silu_slope(gate)
        gate_o[...] = gate_new
        back_scan(batches, span, width // BLOCK, seff, sg, cx, vec.at[0:n], first_o)
        for b in range(batches):
            send_o[b * n : (b + 1) * n] = first_o[b].astype(BF16)


DMA = pltpu.SemaphoreType.DMA


def size_of(shape, dtype):
    rows = 1
    for extent in shape[:-1]:
        rows *= extent
    return rows * shape[-1] * jnp.dtype(dtype).itemsize


def expected(us):
    return pl.CostEstimate(
        flops=int(us * 1e9), bytes_accessed=int(us * 3e6), transcendentals=0
    )


def run(kernel, us, outs, scratch, args, elsewhere=()):
    held = [(a.shape, a.dtype) for i, a in enumerate(args) if i not in elsewhere]
    held += outs + [s for s in scratch if isinstance(s, tuple)]
    return pl.pallas_call(
        kernel,
        out_shape=[jax.ShapeDtypeStruct(*o) for o in outs],
        in_specs=[
            pl.BlockSpec(memory_space=pl.ANY if i in elsewhere else pltpu.VMEM)
            for i in range(len(args))
        ],
        out_specs=[pl.BlockSpec(memory_space=pltpu.VMEM)] * len(outs),
        scratch_shapes=[s if not isinstance(s, tuple) else pltpu.VMEM(*s) for s in scratch],
        compiler_params=pltpu.CompilerParams(
            vmem_limit_bytes=sum(size_of(*h) for h in held) + SLACK
        ),
        cost_estimate=expected(us),
    )(*args)


def hop(batches, n, upper, at, total, forward=None, backward=None, their=None, last=False):
    args = [upper, at, total]
    state = (total.shape, F32)
    wide = ((batches, n, at.shape[1]), F32)
    outs = [state]
    if forward is not None:
        args += forward
        outs += [wide, wide, state, state, (forward[0].shape, BF16)]
    else:
        args.append(their)
    if backward is not None:
        args += backward
        outs += [wide, wide, state, (backward[0].shape, BF16)]
    return pl.pallas_call(
        functools.partial(
            hop_kernel, batches, n, forward is not None, backward is not None, last
        ),
        out_shape=[jax.ShapeDtypeStruct(*o) for o in outs],
        in_specs=[pl.BlockSpec(memory_space=pltpu.SMEM)]
        + [pl.BlockSpec(memory_space=pltpu.VMEM)] * (len(args) - 1),
        out_specs=[pl.BlockSpec(memory_space=pltpu.VMEM)] * len(outs),
        compiler_params=pltpu.CompilerParams(vmem_limit_bytes=HOP_LIMIT),
        cost_estimate=expected(1),
    )(*args)


def flip(array, axis, bit):
    count = lax.axis_size(axis)
    return lax.ppermute(array, axis, [(i, i ^ bit) for i in range(count)])


def shifted(array, by):
    count = lax.axis_size("seq")
    pairs = [(i, i + by) for i in range(count) if 0 <= i + by < count]
    return lax.ppermute(array, "seq", pairs)


def bits_of(count):
    bits = [1 << k for k in range(count.bit_length() - 1)]
    assert 1 << len(bits) == count
    return bits


def pick(array, index, axis):
    return lax.dynamic_index_in_dim(array, index, axis, keepdims=False)


def local(
    tokens, starts, norm_gain, in_weight, conv_weight, conv_bias, xproj_weight,
    dtproj_weight, dt_bias, decay_rate, skip_gain, out_weight, cotangent,
):
    core = lax.axis_index("section")
    place = lax.axis_index("seq")
    cores = lax.axis_size("section")
    count = lax.axis_size("seq")
    bits = bits_of(count)
    batch_count, span, model = tokens.shape
    width = conv_weight.shape[2]
    n = decay_rate.shape[2]
    rank = dtproj_weight.shape[1]
    x_width = xproj_weight.shape[2]
    batches = batch_count // cores
    rows_n = batches * span
    half_model = model // 2
    low_core = core == 0
    uppers = [((place // bit) % 2).astype(jnp.int32).reshape(1) for bit in bits]

    def mine(array):
        return lax.dynamic_slice_in_dim(array, core * batches, batches, 0).reshape(
            (rows_n,) + array.shape[2:]
        )

    rows0 = mine(tokens)
    top = mine(cotangent)
    r = lax.dynamic_slice_in_dim(starts, core * batches, batches, 0).astype(F32)
    r_ext = jnp.concatenate([shifted(r[:, -3:].astype(BF16), 1).astype(F32), r], 1)
    free = 1.0 - r_ext
    m1 = free[:, 3:]
    m2 = m1 * free[:, 2:-1]
    m3 = m2 * free[:, 1:-2]
    marks = jnp.stack([r, m1, m2, m3], -1).reshape(rows_n, 4)

    own_gain = norm_gain[0][None]
    in_own, out_own = in_weight[0], out_weight[0]
    all_rows = tokens.reshape(batch_count * span, model).astype(F32)
    all_mixed = dot(norm_rows(all_rows, own_gain).astype(BF16), in_own).astype(BF16)
    sent = lax.ppermute(all_mixed[rows_n:], "section", [(0, 1)])
    mixed0 = jnp.where(low_core, all_mixed[:rows_n], sent)

    vec_own = jnp.concatenate(
        [
            decay_rate[0].T * -LOG2E, conv_weight[0], conv_bias[0][None], dt_bias[0][None],
            skip_gain[0][None], jnp.pad(own_gain, ((0, 0), (0, width - model))),
        ],
        0,
    )
    low_own = jnp.concatenate([xproj_weight[0].T, dtproj_weight[0]], 0)
    vec_other, low_other = flip(vec_own, "section", 1), flip(low_own, "section", 1)
    out_now, in_now, mixed0 = lax.optimization_barrier((out_own, in_own, mixed0))
    out_other, in_other = flip(out_now, "section", 1), flip(in_now, "section", 1)
    vecs = [jnp.where(low_core == (l == 0), vec_own, vec_other) for l in range(2)]
    lows = [jnp.where(low_core == (l == 0), low_own, low_other) for l in range(2)]
    gains = [v[n + 7 :, :model] for v in vecs]

    tall = ((rows_n, width), F32)
    low_tall = ((rows_n, width), BF16)
    spread = ((rows_n, n, LANES), F32)
    state = ((batches, n, width), F32)
    total_s = ((batches, 1, width), F32)
    flat_in = ((model, 2 * width), BF16)
    flat_out = ((width, model), BF16)
    send_s = ((batches * n + 16, width), BF16)
    send_back_s = ((batches * n, width), BF16)
    tall_t = ((width, rows_n), BF16)
    narrow = ((rows_n, model), BF16)

    def rim_of(mixed):
        return shifted(mixed.reshape(batches, span, 2 * width)[:, -3:, :width], 1)

    def front(layer, mixed, rim):
        outs = [low_tall, ((rows_n, LANES), BF16), state, total_s, send_s]
        scratch = [((span + 8, width), F32), tall, tall, spread, spread]
        args = [mixed, rim, marks, vecs[layer], lows[layer]]
        if layer:
            args += [top, out_own, out_other]
            outs += [state, send_back_s]
            scratch += [tall, flat_out, DMA]
        return run(
            functools.partial(front_kernel, batches, span, width, rank, n, bool(layer)),
            9 if layer else 5, outs, scratch, args, elsewhere=(6, 7),
        )

    zero = jnp.zeros(state[0], F32)
    zero_t = jnp.zeros(total_s[0], F32)

    rim0 = rim_of(mixed0)
    conv0, proj0, final, total0, send = front(0, mixed0, rim0)
    before, ahead, total = zero, zero_t, total0
    theirs = []
    at0, at1 = vecs[0][:n], vecs[1][:n]
    for k, bit in enumerate(bits):
        got = flip(send, "seq", bit)
        total, final, before, ahead, their, send = hop(
            batches, n, uppers[k], at0, total, [got, final, before, ahead],
            last=k == len(bits) - 1,
        )
        theirs.append(their)
    before0 = before
    scanned0, gated_t0, rows1, normed0, normed1, mixed1 = run(
        functools.partial(end_kernel, batches, span, width, rank, n), 9,
        [tall, tall_t, narrow, narrow, narrow, ((rows_n, 2 * width), BF16)],
        [tall, tall, spread, spread, flat_out, flat_in, DMA((2,))],
        [mixed0, conv0, proj0, marks, before, vecs[0], lows[0], rows0, gains[1], gains[0],
         out_own, out_other, in_own, in_other],
        elsewhere=(10, 11, 12, 13),
    )

    rim1 = rim_of(mixed1)
    conv1, proj1, final, total, send, first, send_b = front(1, mixed1, rim1)
    before, ahead, after, behind = zero, zero_t, zero, zero_t
    for k, bit in enumerate(bits):
        got, got_b = flip(send, "seq", bit), flip(send_b, "seq", bit)
        total, final, before, ahead, _, send, first, after, behind, send_b = hop(
            batches, n, uppers[k], at1, total, [got, final, before, ahead],
            [got_b, first, after, behind], last=k == len(bits) - 1,
        )

    def back(layer, gg, conv, mixed, rim, before, after, proj, *rest):
        outs = [tall, ((batches, 3, width), F32), ((width, 2 * LANES), BF16)]
        scratch = [
            tall, tall, ((batches, span + 1, n, BLOCK), F32), ((batches, span, n, BLOCK), F32),
            tall, tall, spread, spread, ((span + 16, width), F32), tall,
            ((LANES, width), F32), spread, spread, tall,
        ]
        if layer:
            outs += [tall, tall_t, narrow]
            scratch += [tall, tall, flat_out, DMA]
        return run(
            functools.partial(
                back_kernel, batches, span, width, rank, n, x_width, bool(layer)
            ),
            20 if layer else 18, outs, scratch,
            [gg, conv, mixed, rim, marks, before, after, vecs[layer], lows[layer], proj, *rest],
            elsewhere=(11, 12),
        )

    inner1, spill1, small1, gate1, gated_t1, out1 = back(
        1, top, conv1, mixed1, rim1, before, after, proj1, rows1, out_own, out_other
    )
    got1 = shifted(spill1, -1)

    def turn(layer, inner, spill, gate, rows, g, *rest):
        outs = [
            (((2 * width, rows_n) if layer else (rows_n + 16, 2 * width)), BF16), narrow,
        ]
        scratch = [flat_in, DMA, ((rows_n, 2 * width), BF16)]
        args = [inner, spill, gate, rows, gains[layer], g, in_own, in_other, *rest]
        elsewhere = [6, 7]
        if layer:
            outs += [((1, model), F32), tall, state, send_back_s, tall]
            scratch += [tall, tall, spread, flat_out, DMA]
            elsewhere += [8, 9]
        return run(
            functools.partial(turn_kernel, batches, span, width, rank, n, count, layer),
            11 if layer else 3, outs, scratch, args, elsewhere=elsewhere,
        )

    grad_t1, g0, gain1, gg0, first, send_b, gate0 = turn(
        1, inner1, got1, gate1, rows1, top, out_own, out_other, mixed0, proj0, marks, lows[0],
        vecs[0], scanned0,
    )
    all_normed0 = lax.all_gather(normed0, "seq", axis=0, tiled=True)

    def half(array, which):
        return lax.dynamic_slice_in_dim(array, which * half_model, half_model, 1)

    def parted(array, bit, targets):
        low = min(bit, targets // 2)
        array = array.reshape(
            targets // (2 * low), 2, low, array.shape[0] // targets, array.shape[1]
        )
        mine = (place // bit) % 2
        flat = lambda a: a.reshape(-1, a.shape[-1])
        return flat(pick(array, 1 - mine, 1)), flat(pick(array, mine, 1))

    def core_start(left, right, bit, targets):
        goes, stays = parted(left, bit, targets)
        sent = dot(jnp.concatenate([goes, stays], 0), half(right, 1 - core)).astype(BF16)
        return goes, stays, half(right, core), flip(sent, "section", 1)

    def core_end(started):
        goes, stays, right, got = started
        middle = goes.shape[0]
        return (
            (dot(goes, right) + got[:middle].astype(F32)).astype(BF16),
            dot(stays, right) + got[middle:].astype(F32),
        )

    def add(kept, got):
        return kept + got.astype(F32)

    def finish(total, used, left_bits, targets):
        order = sorted(left_bits)
        total = total.reshape((2,) * len(order) + (-1, total.shape[-1]))
        for bit in left_bits:
            axis = len(order) - 1 - order.index(bit)
            order.remove(bit)
            mine = (place // bit) % 2
            got = flip(pick(total, 1 - mine, axis).astype(BF16), "seq", bit)
            total = add(pick(total, mine, axis), got)
        return total

    x_bit, y_bit = bits[0], bits[1]
    a = core_start(grad_t1, normed1, x_bit, count)
    left_own = jnp.where(low_core, gated_t0, gated_t1)
    left_other = jnp.where(low_core, gated_t1, gated_t0)
    right_own = jnp.where(low_core, g0, top)
    right_other = jnp.where(low_core, top, g0)
    goes, stays = parted(left_other, y_bit, count)
    sent = dot(jnp.concatenate([goes, stays], 0), right_other).astype(BF16)
    goes, stays = parted(left_own, y_bit, count)
    b = (goes, stays, right_own, flip(sent, "section", 1))

    after, behind, total = zero, zero_t, total0
    for k, bit in enumerate(bits):
        got_b = flip(send_b, "seq", bit)
        if k == 2:
            a_goes, a_stays = core_end(a)
            b_goes, b_stays = core_end(b)
            first, a_goes, b_goes = lax.optimization_barrier((first, a_goes, b_goes))
            a_got = flip(a_goes, "seq", x_bit)
            b_got = flip(b_goes, "seq", y_bit)
        total, first, after, behind, send_b = hop(
            batches, n, uppers[k], at0, total, None, [got_b, first, after, behind],
            their=theirs[k], last=k == len(bits) - 1,
        )
    inner0, spill0, small0 = back(0, gg0, conv0, mixed0, rim0, before0, after, proj0)
    inner0, spill0, small0, a_got, b_got = lax.optimization_barrier(
        (inner0, spill0, small0, a_got, b_got)
    )
    got0 = shifted(spill0, -1)
    in_sum1 = finish(add(a_stays, a_got), x_bit, bits[1:], count)
    out_sum = finish(add(b_stays, b_got), y_bit, [x_bit] + bits[2:], count)
    mixed_grad0, dx = turn(0, inner0, got0, gate0, rows0, g0)

    columns = lax.all_to_all(
        mixed_grad0.reshape(rows_n + 16, count, -1), "seq", 1, 0, tiled=False
    )
    gain0 = jnp.sum(columns[:, rows_n, : model // count].astype(F32), 0, keepdims=True)
    in_sum0 = across(
        columns[:, :rows_n].reshape(count * rows_n, -1), all_normed0
    )
    got = lax.ppermute(in_sum0.astype(BF16), "section", [(1, 0)])
    in_sum0 = add(in_sum0, got)

    got = flip(jnp.where(low_core, small1, small0), "section", 1)
    small = add(jnp.where(low_core, small0, small1).astype(F32), got)
    small = finish(small, None, bits, count)

    gain1 = gain1.reshape(count, 1, model // count)
    for bit in reversed(bits):
        left = gain1.reshape(2, -1, 1, model // count)
        mine = (place // bit) % 2
        gain1 = add(pick(left, mine, 0), flip(pick(left, 1 - mine, 0), "seq", bit))
    got = flip(jnp.where(low_core, gain1[0], gain0), "section", 1)
    gain = jnp.where(low_core, gain0, gain1[0]) + got

    got = lax.ppermute(in_sum1, "section", [(0, 1)])
    grad_in = jnp.where(low_core, in_sum0, jnp.concatenate([got, in_sum1], 1))
    got = flip(jnp.where(low_core, out1, dx), "section", 1)
    boundary = jnp.where(
        low_core, jnp.concatenate([dx, got], 0), jnp.concatenate([got, out1], 0)
    ).reshape(1, batch_count, span, model)
    vec_sum = small[:, LANES:]
    return (
        boundary,
        gain,
        grad_in.T[None],
        vec_sum[:, n : n + 4].T[None],
        vec_sum[:, n + 4][None],
        small[:, :x_width][None],
        small[:, x_width:LANES].T[None],
        vec_sum[:, n + 5][None],
        vec_sum[:, :n][None],
        vec_sum[:, n + 6][None],
        out_sum[None],
    )


def solution(mesh):
    in_specs = (
        P(None, "seq", None), P(None, "seq"), P("section", None), P("section", None, None),
        P("section", None, None), P("section", None), P("section", None, None),
        P("section", None, None), P("section", None), P("section", None, None),
        P("section", None), P("section", None, None), P(None, "seq", None),
    )
    out_specs = (
        P("section", None, "seq", None), P("section", "seq"), P("section", None, "seq"),
        P("section", None, "seq"), P("section", "seq"), P("section", "seq", None),
        P("section", None, "seq"), P("section", "seq"), P("section", "seq", None),
        P("section", "seq"), P("section", "seq", None),
    )
    return jax.shard_map(local, mesh=mesh, in_specs=in_specs, out_specs=out_specs, check_vma=False)
```

```python
import functools
import jax
import jax.numpy as jnp
from jax import lax
from jax.experimental import pallas as pl
from jax.experimental.pallas import tpu as pltpu
from jax.sharding import PartitionSpec as P

EPS = 1e-05
LOG2E = 1.4426950408889634
STOP = 1e7
LANES = 128
BLOCK = 256
TILES = BLOCK // LANES
F32 = jnp.float32
BF16 = jnp.bfloat16
VMEM_LIMIT = 58 * 1024 * 1024
HOP_LIMIT = 6 * 1024 * 1024


def dot(left, right):
    return jnp.dot(left, right, preferred_element_type=F32)


def across(left, right):
    return lax.dot_general(left, right, (((0,), (0,)), ((), ())), preferred_element_type=F32)


def against(left, right):
    return lax.dot_general(left, right, (((1,), (1,)), ((), ())), preferred_element_type=F32)


def norm_rows(source, gain_row):
    return source * lax.rsqrt(jnp.mean(source * source, axis=-1, keepdims=True) + EPS) * gain_row


def softplus(v):
    return jnp.maximum(v, 0.0) + jnp.log1p(jnp.exp(-jnp.abs(v)))


def silu_slope(v):
    gate = jax.nn.sigmoid(v)
    return gate * (1.0 + v * (1.0 - gate))


def pair_up(left, right, row_ids, width):
    mask = (row_ids % (2 * width)) < width
    kept = jnp.where(mask, left, right)
    moved = jnp.where(mask, right, left)
    return kept + pltpu.roll(moved, 8 - width, 0)


def fold_rows(parts, row_ids):
    width = 1
    while len(parts) > 1:
        parts = [
            pair_up(parts[i], parts[i + 1], row_ids, width) for i in range(0, len(parts), 2)
        ]
        width *= 2
    return parts[0]


def halves(v):
    return v[:8] + v[8:]


def spread_columns(table, first, target):
    width = target.shape[1]
    for t in range(target.shape[0]):
        column = table[first : first + width, t : t + 1]
        target[t] = jnp.broadcast_to(column, (width, LANES))


def block_at(i):
    return pl.ds(pl.multiple_of(i * BLOCK, BLOCK), BLOCK)


def tile_at(i, lt):
    return pl.ds(pl.multiple_of(i * BLOCK + lt * LANES, LANES), LANES)


def local_scan(batches, span, blocks, seff, x, bx, at, final):
    def over_block(i, carry):
        rate = [at[:, tile_at(i, lt)] for lt in range(TILES)]

        def chunk(tc, states):
            states = list(states)
            for b in range(batches):
                rows = pl.ds(pl.multiple_of(b * span + tc * 8, 8), 8)
                for lt in range(TILES):
                    s8 = seff[rows, tile_at(i, lt)]
                    x8 = x[rows, tile_at(i, lt)]
                    h = states[b * TILES + lt]
                    for j in range(8):
                        decay = jnp.exp2(s8[j : j + 1] * rate[lt])
                        h = decay * h + x8[j : j + 1] * bx[b * span + tc * 8 + j]
                    states[b * TILES + lt] = h
            return tuple(states)

        zero = jnp.zeros((at.shape[0], LANES), F32)
        states = lax.fori_loop(0, span // 8, chunk, (zero,) * (batches * TILES))
        for b in range(batches):
            for lt in range(TILES):
                final[b, :, tile_at(i, lt)] = states[b * TILES + lt]
        return carry

    lax.fori_loop(0, blocks, over_block, 0)


def back_scan(batches, span, blocks, seff, sg, cx, at, first):
    chunks = span // 8

    def over_block(i, carry):
        rate = [at[:, tile_at(i, lt)] for lt in range(TILES)]

        def chunk(k, states):
            states = list(states)
            tc = chunks - 1 - k
            for b in range(batches):
                rows = pl.ds(pl.multiple_of(b * span + tc * 8, 8), 8)
                for lt in range(TILES):
                    s8 = seff[rows, tile_at(i, lt)]
                    g8 = sg[rows, tile_at(i, lt)]
                    q = states[b * TILES + lt]
                    for j in range(7, -1, -1):
                        decay = jnp.exp2(s8[j : j + 1] * rate[lt])
                        q = decay * (q + g8[j : j + 1] * cx[b * span + tc * 8 + j])
                    states[b * TILES + lt] = q
            return tuple(states)

        zero = jnp.zeros((at.shape[0], LANES), F32)
        states = lax.fori_loop(0, chunks, chunk, (zero,) * (batches * TILES))
        for b in range(batches):
            for lt in range(TILES):
                first[b, :, tile_at(i, lt)] = states[b * TILES + lt]
        return carry

    lax.fori_loop(0, blocks, over_block, 0)


class Arriving:
    def __init__(self, source, held, sem, other=None):
        self.held, self.waited = held, False
        if other is None:
            self.copy = pltpu.make_async_copy(source, held, sem)
            self.copy.start()
        else:
            self.copy = fetch(0, source, other, held, sem)

    def __getitem__(self, where):
        assert self.waited
        return self.held[where]

    def __setitem__(self, where, value):
        assert self.waited
        self.held[where] = value

    @property
    def at(self):
        return self.held.at


class Leaving:
    def __init__(self, target, held, sem):
        self.copy, self.held, self.started = pltpu.make_async_copy(held, target, sem), held, False

    def __getitem__(self, where):
        return self.held[where]

    def __setitem__(self, where, value):
        self.held[where] = value


def uppers_of(steps):
    place = lax.axis_index("seq")
    return [(place // (1 << k)) % 2 != 0 for k in range(steps)]


def ready(*refs):
    for ref in refs:
        if isinstance(ref, Arriving) and not ref.waited:
            ref.copy.wait()
            ref.waited = True


def leave(*refs):
    for ref in refs:
        if isinstance(ref, Leaving) and not ref.started:
            ref.copy.start()
            ref.started = True


def fetch(layer, own, other, held, sem):
    mine = lax.axis_index("section") == layer

    @pl.when(mine)
    def _():
        pltpu.make_async_copy(own, held, sem).start()

    @pl.when(jnp.logical_not(mine))
    def _():
        pltpu.make_async_copy(other, held, sem).start()

    return pltpu.make_async_copy(own, held, sem)


def split_total(totals):
    width = totals[0].shape[1]
    row_ids = lax.broadcasted_iota(jnp.int32, (16, width), 0)
    block = jnp.zeros((16, width), F32)
    for b, total in enumerate(totals):
        rest = total
        for k in range(3):
            part = rest.astype(BF16).astype(F32)
            block = jnp.where(row_ids == 3 * b + k, part, block)
            rest = rest - part
    return block.astype(BF16)


def join_total(block, b):
    block = block.astype(F32)
    return block[3 * b : 3 * b + 1] + block[3 * b + 1 : 3 * b + 2] + block[3 * b + 2 : 3 * b + 3]


def enter_kernel(
    batches, span, width,
    rows, gain, in_w,
    in_a_o, in_b_o, gate_a_o, gate_b_o, tail_a_o, tail_b_o,
    normed, held, sems,
):
    chunk = held.shape[2]
    copies = [
        pltpu.make_async_copy(in_w.at[:, pl.ds(c * chunk, chunk)], held.at[c], sems.at[c])
        for c in range(held.shape[0])
    ]
    for copy in copies:
        copy.start()
    ready(rows, gain)
    normed[...] = norm_rows(rows[...].astype(F32), gain[...]).astype(BF16)
    half = batches * span
    for c, copy in enumerate(copies):
        copy.wait()
        mixed = dot(normed[...], held[c])
        outs = (in_a_o, in_b_o) if c * chunk < width else (gate_a_o, gate_b_o)
        lanes = slice(c * chunk % width, c * chunk % width + chunk)
        for k, out in enumerate(outs):
            out[:, lanes] = mixed[k * half : (k + 1) * half].astype(BF16)
        if c * chunk < width:
            for k, tail in enumerate((tail_a_o, tail_b_o)):
                for b in range(batches):
                    last = k * half + (b + 1) * span
                    tail[b, :, lanes] = mixed[last - 3 : last].astype(BF16).astype(F32)
        if (c + 1) * chunk == width:
            leave(in_a_o, in_b_o, tail_a_o, tail_b_o)


def tap_rows(ext, rim, mixed, width, span):
    ext[5:8] = rim
    ext[8 : 8 + span] = mixed.astype(F32)


def conv_sum(ext, m, vec, n, span):
    v = vec[n + 4 : n + 5] + vec[n + 3 : n + 4] * ext[8 : 8 + span]
    for k in (1, 2, 3):
        v = v + vec[n + 3 - k : n + 4 - k] * (m[:, k : k + 1] * ext[8 - k : 8 - k + span])
    return v


def step_sum(proj, low_w, vec, rank, n):
    return dot(proj[:, :rank], low_w[rank + 2 * n :]) + vec[n + 5 : n + 6]


def front_kernel(
    batches, span, width, rank, states_n, with_back,
    *refs,
):
    refs = list(refs)
    mixed, rim, marks, vec, low_w = refs[:5]
    del refs[:5]
    if with_back:
        gate, g, own_w, other_w = refs[:4]
        del refs[:4]
    conv_o, proj_o, send_o = refs[:3]
    del refs[:3]
    if with_back:
        (send_back_o,) = refs[:1]
        del refs[:1]
    ext, seff, x, bx, cx, final = refs[:6]
    if with_back:
        sg, out_w, sem = refs[6:]
        arrival = fetch(1, own_w, other_w, out_w, sem)
    n = states_n
    ready(rim, marks, vec)
    m = marks[...]
    at = vec.at[0:n]
    ready(mixed)
    for b in range(batches):
        lo, hi = b * span, (b + 1) * span
        tap_rows(ext, rim[b], mixed[lo:hi], width, span)
        x[lo:hi] = jax.nn.silu(conv_sum(ext, m[lo:hi], vec, n, span))
    conv = x[...].astype(BF16)
    conv_o[...] = conv
    leave(conv_o)
    ready(low_w)
    proj = against(conv, low_w[...]).astype(BF16)
    proj_o[...] = proj
    leave(proj_o)
    step = softplus(step_sum(proj, low_w, vec, rank, n))
    seff[...] = step + m[:, 0:1] * STOP
    x[...] = step * conv.astype(F32)
    totals = [
        jnp.sum(seff[b * span : (b + 1) * span], axis=0, keepdims=True) for b in range(batches)
    ]
    send_o[batches * n :] = split_total(totals)
    table = proj.astype(F32).T
    spread_columns(table, rank, bx)
    local_scan(batches, span, width // BLOCK, seff, x, bx, at, final)
    for b in range(batches):
        send_o[b * n : (b + 1) * n] = final[b].astype(BF16)
    leave(send_o)
    if with_back:
        arrival.wait()
        spread_columns(table, rank + n, cx)
        ready(g, gate)
        gg = against(g[...], out_w[...])
        sg[...] = gg * jax.nn.silu(gate[...].astype(F32))
        back_scan(batches, span, width // BLOCK, seff, sg, cx, at, final)
        for b in range(batches):
            send_back_o[b * n : (b + 1) * n] = final[b].astype(BF16)


def merge(at, upper, mine, theirs, mine_total, their_total, backward):
    early, late = jnp.where(upper, theirs, mine), jnp.where(upper, mine, theirs)
    if backward:
        return jnp.exp2(jnp.where(upper, their_total, mine_total) * at) * late + early
    return jnp.exp2(jnp.where(upper, mine_total, their_total) * at) * early + late


def reach(at, n, b, uppers, gots, totals, backward):
    carry = jnp.zeros(at.shape, F32)
    span = jnp.zeros((1, at.shape[1]), F32)
    for upper, got, their_total in zip(uppers, gots, totals):
        comes = jnp.logical_not(upper) if backward else upper
        theirs = got[b * n : (b + 1) * n].astype(F32)
        carry = jnp.where(comes, jnp.exp2(span * at) * theirs + carry, carry)
        span = jnp.where(comes, span + their_total, span)
    return carry


def hop_kernel(batches, n, steps, forward, backward, *refs):
    refs = list(refs)
    take = lambda k: [refs.pop(0) for _ in range(k)]
    (at,) = take(1)
    at = at[...]
    if forward:
        own, *gots = take(1 + steps)
    else:
        (totals,) = take(1)
    if backward:
        own_b, *gots_b = take(1 + steps)
    if forward:
        (send,) = take(1)
    if backward:
        (send_b,) = take(1)
    uppers = uppers_of(steps)
    reached = []
    for b in range(batches):
        rows = slice(b * n, (b + 1) * n)
        if forward:
            total = join_total(own[batches * n :], b)
            mine = own[rows].astype(F32)
        else:
            total = totals[b : b + 1]
        if backward:
            mine_b = own_b[rows].astype(F32)
        for k, upper in enumerate(uppers):
            if forward:
                their_total = join_total(gots[k][batches * n :], b)
                mine = merge(
                    at, upper, mine, gots[k][rows].astype(F32), total, their_total, False
                )
            else:
                their_total = totals[(k + 1) * batches + b : (k + 1) * batches + b + 1]
            if backward:
                mine_b = merge(
                    at, upper, mine_b, gots_b[k][rows].astype(F32), total, their_total, True
                )
            total = total + their_total
        if forward:
            send[rows] = mine.astype(BF16)
        if backward:
            send_b[rows] = mine_b.astype(BF16)
        reached.append(total)
    if forward:
        send[batches * n :] = split_total(reached)


def prepare(step, marks, conv, seff, x):
    seff[...] = step + marks * STOP
    x[...] = step * conv.astype(F32)


def end_kernel(
    batches, span, width, rank, n, steps,
    gate, conv, proj, marks, vec, low_w, rows, gain, gain_before,
    own_out, other_out, own_in, other_in, own_send, *refs,
):
    gots, refs = refs[:steps], refs[steps:]
    (
        scanned_o, gated_t_o, rows_o, normed_before_o, normed_o, inner_o, gate_o, before_o,
        totals_o, tail_o, seff, x, bx, cx, out_w, in_w, sems,
    ) = refs

    arrivals = [
        fetch(0, own_out, other_out, out_w, sems.at[0]),
        fetch(1, own_in, other_in, in_w, sems.at[1]),
    ]
    blocks = width // BLOCK
    at = vec.at[0:n]
    ready(rows, gain_before, proj, low_w, vec, marks, conv)
    normed_before_o[...] = norm_rows(rows[...].astype(F32), gain_before[...]).astype(BF16)
    leave(normed_before_o)
    step = softplus(step_sum(proj[...], low_w, vec, rank, n))
    prepare(step, marks[:, 0:1], conv[...], seff, x)
    table = proj[...].astype(F32).T
    spread_columns(table, rank, bx)
    spread_columns(table, rank + n, cx)
    ready(own_send, *gots)
    uppers = uppers_of(steps)
    for b in range(batches):
        totals_o[b : b + 1] = join_total(own_send[batches * n :], b)
        theirs = [join_total(got[batches * n :], b) for got in gots]
        for k, their in enumerate(theirs):
            totals_o[(k + 1) * batches + b : (k + 1) * batches + b + 1] = their
        before_o[b] = reach(at[...], n, b, uppers, gots, theirs, False)
    leave(before_o, totals_o)
    row_ids = lax.broadcasted_iota(jnp.int32, (8, LANES), 0)

    def over_block(i, carry):
        rate = [at[:, tile_at(i, lt)] for lt in range(TILES)]

        def chunk(tc, states):
            states = list(states)
            for b in range(batches):
                rows8 = pl.ds(pl.multiple_of(b * span + tc * 8, 8), 8)
                for lt in range(TILES):
                    s8 = seff[rows8, tile_at(i, lt)]
                    x8 = x[rows8, tile_at(i, lt)]
                    h = states[b * TILES + lt]
                    parts = []
                    for j in range(8):
                        t = b * span + tc * 8 + j
                        decay = jnp.exp2(s8[j : j + 1] * rate[lt])
                        h = decay * h + x8[j : j + 1] * bx[t]
                        parts.append(halves(h * cx[t]))
                    states[b * TILES + lt] = h
                    scanned_o[rows8, tile_at(i, lt)] = fold_rows(parts, row_ids)
            return tuple(states)

        start = tuple(
            before_o[b, :, tile_at(i, lt)] for b in range(batches) for lt in range(TILES)
        )
        lax.fori_loop(0, span // 8, chunk, start)
        return carry

    lax.fori_loop(0, blocks, over_block, 0)
    scanned = scanned_o[...] + vec[n + 6 : n + 7] * conv[...].astype(F32)
    scanned_o[...] = scanned
    leave(scanned_o)
    ready(gate)
    gated_f = scanned * jax.nn.silu(gate[...].astype(F32))
    gated = gated_f.astype(BF16)
    gated_t_o[...] = gated_f.T.astype(BF16)
    leave(gated_t_o)
    arrivals[0].wait()
    result = (rows[...].astype(F32) + dot(gated, out_w[...])).astype(BF16)
    rows_o[...] = result
    leave(rows_o)
    ready(gain)
    normed_o[...] = norm_rows(result.astype(F32), gain[...]).astype(BF16)
    leave(normed_o)
    arrivals[1].wait()
    for first, target in ((0, inner_o), (width, gate_o)):
        for c in range(0, width, 512):
            mixed = dot(normed_o[...], in_w[:, first + c : first + c + 512])
            target[:, c : c + 512] = mixed.astype(BF16)
            if not first:
                for b in range(batches):
                    last = (b + 1) * span
                    tail_o[b, :, c : c + 512] = mixed[last - 3 : last].astype(BF16).astype(F32)
        leave(target, tail_o)


def back_kernel(
    batches, span, width, rank, n, x_width, steps, with_out,
    *refs,
):
    refs = list(refs)
    take = lambda k: [refs.pop(0) for _ in range(k)]
    gg, conv, inner, gate, rim, marks, vec, low_w, proj = take(9)
    if with_out:
        rows, own_out, other_out = take(3)
        gots = take(steps)
    else:
        before, totals = take(2)
    gots_b = take(steps)
    inner_o, tail_o, spill_o, small_o = take(4)
    if with_out:
        gate_o, gated_t_o, out_o = take(3)
    seff, x, hist, decays, drive, zsum, acc_b, acc_c, ext, sg, vec_o, bx, cx, pre_grad = take(14)
    state_in, grad_in = take(2)
    if with_out:
        scanned_ref, gg_s, out_w, sem = take(4)
        arrival = fetch(1, own_out, other_out, out_w, sem)
    blocks = width // BLOCK
    rows_n = batches * span
    chunks = span // 8
    ready(proj, low_w, vec, marks, conv)
    m = marks[...]
    at = vec.at[0:n]
    spre = step_sum(proj[...], low_w, vec, rank, n)
    prepare(softplus(spre), m[:, 0:1], conv[...], seff, x)
    table = proj[...].astype(F32).T
    spread_columns(table, rank, bx)
    spread_columns(table, rank + n, cx)
    ready(gg, gate)
    if with_out:
        arrival.wait()
        gg_s[...] = against(gg[...], out_w[...])
        gg = gg_s
    sg[...] = gg[...] * jax.nn.silu(gate[...].astype(F32))
    if with_out:
        ready(*gots)
    else:
        ready(before, totals)
    ready(*gots_b)
    uppers = uppers_of(steps)
    for b in range(batches):
        if with_out:
            theirs = [join_total(got[batches * n :], b) for got in gots]
            state_in[b] = reach(at[...], n, b, uppers, gots, theirs, False)
        else:
            theirs = [
                totals[(k + 1) * batches + b : (k + 1) * batches + b + 1] for k in range(steps)
            ]
            state_in[b] = before[b]
        grad_in[b] = reach(at[...], n, b, uppers, gots_b, theirs, True)
    acc_b[...] = jnp.zeros_like(acc_b)
    acc_c[...] = jnp.zeros_like(acc_c)
    vec_o[...] = jnp.zeros_like(vec_o)
    row_ids = lax.broadcasted_iota(jnp.int32, (8, LANES), 0)

    def over_block(i, carry):
        rate = [at[:, tile_at(i, lt)] for lt in range(TILES)]

        def again(tc, states):
            states = list(states)
            for b in range(batches):
                rows8 = pl.ds(pl.multiple_of(b * span + tc * 8, 8), 8)
                for lt in range(TILES):
                    s8 = seff[rows8, tile_at(i, lt)]
                    x8 = x[rows8, tile_at(i, lt)]
                    h = states[b * TILES + lt]
                    lanes = pl.ds(lt * LANES, LANES)
                    parts = []
                    for j in range(8):
                        t = tc * 8 + j
                        decay = jnp.exp2(s8[j : j + 1] * rate[lt])
                        h = decay * h + x8[j : j + 1] * bx[b * span + t]
                        decays[b, t, :, lanes] = decay
                        hist[b, t + 1, :, lanes] = h
                        if with_out:
                            parts.append(halves(h * cx[b * span + t]))
                    states[b * TILES + lt] = h
                    if with_out:
                        scanned_ref[rows8, tile_at(i, lt)] = fold_rows(parts, row_ids)
            return tuple(states)

        for b in range(batches):
            hist[b, 0] = state_in[b, :, block_at(i)]
        start = tuple(
            state_in[b, :, tile_at(i, lt)] for b in range(batches) for lt in range(TILES)
        )
        lax.fori_loop(0, chunks, again, start)

        sums = tuple(jnp.zeros((n, LANES), F32) for _ in range(TILES))
        for b in range(batches):

            def chunk(k, held):
                held = list(held)
                tc = chunks - 1 - k
                rows8 = pl.ds(pl.multiple_of(b * span + tc * 8, 8), 8)
                s8, x8, g8 = [], [], []
                for lt in range(TILES):
                    s8.append(seff[rows8, tile_at(i, lt)])
                    x8.append(x[rows8, tile_at(i, lt)])
                    g8.append(sg[rows8, tile_at(i, lt)])
                drives = [[None] * 8 for _ in range(TILES)]
                zs = [[None] * 8 for _ in range(TILES)]
                for j in range(7, -1, -1):
                    t = tc * 8 + j
                    part_b, part_c = [], []
                    for lt in range(TILES):
                        lanes = pl.ds(lt * LANES, LANES)
                        total = held[lt] + g8[lt][j : j + 1] * cx[b * span + t]
                        q = decays[b, t, :, lanes] * total
                        log_grad = q * hist[b, t, :, lanes]
                        held[TILES + lt] = held[TILES + lt] + log_grad * s8[lt][j : j + 1]
                        zs[lt][j] = halves(log_grad * rate[lt])
                        drives[lt][j] = halves(total * bx[b * span + t])
                        part_b.append(total * x8[lt][j : j + 1])
                        part_c.append(g8[lt][j : j + 1] * hist[b, t + 1, :, lanes])
                        held[lt] = q
                    acc_b[b * span + t] += sum(part_b[1:], part_b[0])
                    acc_c[b * span + t] += sum(part_c[1:], part_c[0])
                for lt in range(TILES):
                    drive[rows8, tile_at(i, lt)] = fold_rows(drives[lt], row_ids)
                    zsum[rows8, tile_at(i, lt)] = fold_rows(zs[lt], row_ids)
                return tuple(held)

            start = tuple(grad_in[b, :, tile_at(i, lt)] for lt in range(TILES)) + sums
            sums = lax.fori_loop(0, chunks, chunk, start)[TILES:]
        for lt in range(TILES):
            vec_o[0:n, tile_at(i, lt)] = -sums[lt]
        return carry

    lax.fori_loop(0, blocks, over_block, 0)

    conv_f = conv[...].astype(F32)
    if with_out:
        ready(rows)
        gate = gate[...].astype(F32)
        scanned = scanned_ref[...] + vec[n + 6 : n + 7] * conv_f
        gated_f = scanned * jax.nn.silu(gate)
        gated_t_o[...] = gated_f.T.astype(BF16)
        out_o[...] = (rows[...].astype(F32) + dot(gated_f.astype(BF16), out_w[...])).astype(BF16)
        gate_o[...] = (gg_s[...] * scanned * silu_slope(gate)).astype(BF16)
        leave(gate_o, gated_t_o, out_o)

    column_ids = lax.broadcasted_iota(jnp.int32, (n, rows_n), 1)

    def gather_column(t, pair):
        now = []
        for held, acc in zip(pair, (acc_b, acc_c)):
            column = jnp.sum(acc[t], axis=1, keepdims=True)
            now.append(jnp.where(column_ids == t, column, held))
        return tuple(now)

    zero = jnp.zeros((n, rows_n), F32)
    b_grad, c_grad = lax.fori_loop(0, rows_n, gather_column, (zero, zero), unroll=8)
    rest = LANES - rank - 2 * n
    placed = jnp.concatenate(
        [jnp.zeros((rank, rows_n), F32), b_grad, c_grad, jnp.zeros((rest, rows_n), F32)], 0
    ).T
    spre = step_sum(proj[...], low_w, vec, rank, n)
    step = softplus(spre)
    step_grad = zsum[...] * (1.0 / LOG2E) + drive[...] * conv_f
    pre_g = step_grad * jax.nn.sigmoid(spre)
    low = pre_g.astype(BF16)
    low_grad = against(low, low_w[rank + 2 * n :])
    pgrad = (
        jnp.concatenate([low_grad, jnp.zeros((rows_n, LANES - rank), F32)], 1) + placed
    ).astype(BF16)
    small = dot(conv_f.T.astype(BF16), pgrad)
    lows = pltpu.roll(dot(pre_g.T.astype(BF16), proj[...]), x_width, 1)
    columns = lax.broadcasted_iota(jnp.int32, (1, LANES), 1)
    small_o[:, :LANES] = jnp.where(columns < x_width, small, lows).astype(BF16)
    conv_grad = (
        sg[...] * vec[n + 6 : n + 7] + step * drive[...]
        + dot(pgrad[:, : rank + 2 * n], low_w[: rank + 2 * n])
    )
    pre_grad[...] = conv_grad
    vec_o[n + 5 : n + 6] = jnp.sum(pre_g, axis=0, keepdims=True)
    vec_o[n + 6 : n + 7] = jnp.sum(sg[...] * conv_f, axis=0, keepdims=True)
    ready(inner, rim)
    taps = [jnp.zeros((1, width), F32) for _ in range(4)]
    bias = jnp.zeros((1, width), F32)
    for b in range(batches):
        lo, hi = b * span, (b + 1) * span
        tap_rows(ext, rim[b], inner[lo:hi], width, span)
        grad_b = pre_grad[lo:hi] * silu_slope(conv_sum(ext, m[lo:hi], vec, n, span))
        bias = bias + jnp.sum(grad_b, axis=0, keepdims=True)
        taps[3] = taps[3] + jnp.sum(grad_b * ext[8 : 8 + span], axis=0, keepdims=True)
        for k in (1, 2, 3):
            taps[3 - k] = taps[3 - k] + jnp.sum(
                grad_b * (m[lo:hi, k : k + 1] * ext[8 - k : 8 - k + span]),
                axis=0, keepdims=True,
            )
        back = vec[n + 3 : n + 4] * grad_b
        spill = jnp.zeros((8, width), F32)
        for k in (1, 2, 3):
            ext[0:8] = jnp.zeros((8, width), F32)
            ext[8 : 8 + span] = vec[n + 3 - k : n + 4 - k] * (m[lo:hi, k : k + 1] * grad_b)
            ext[8 + span : 16 + span] = jnp.zeros((8, width), F32)
            back = back + ext[8 + k : 8 + k + span]
            spill = spill + ext[k : 8 + k]
        inner_o[lo:hi] = back.astype(BF16)
        tail_o[b] = back[span - 16 :]
        spill_o[b] = spill[5:8]
    leave(spill_o, inner_o, tail_o)
    for k in range(4):
        vec_o[n + k : n + k + 1] = taps[k]
    vec_o[n + 4 : n + 5] = bias
    small_o[:, LANES:] = vec_o[...].T.astype(BF16)


def norm_back(source, gain, grad):
    scale = lax.rsqrt(jnp.mean(source * source, axis=-1, keepdims=True) + EPS)
    unit = source * scale
    scaled = grad * gain
    along = jnp.mean(scaled * unit, axis=-1, keepdims=True)
    return scale * (scaled - unit * along), jnp.sum(grad * unit, axis=0, keepdims=True)


def turn_kernel(
    batches, span, width, rank, n, targets, layer,
    *refs,
):
    refs = list(refs)
    take = lambda k: [refs.pop(0) for _ in range(k)]
    inner, tail, spill, gate_grad, rows, gain, g, own_in, other_in = take(9)
    if layer:
        own_out, other_out, gate, proj, marks, low_w, vec, scanned = take(8)
    else:
        (gain_above,) = take(1)
    grad_o, g_o = take(2)
    if layer:
        gain_o, gg_o, send_o, gate_o = take(4)
    in_w, sem_in, mixed_grad = take(3)
    rows_n = batches * span
    if layer:
        seff, sg, cx, first, out_w, sem_out = take(6)
    arrival = fetch(layer, own_in, other_in, in_w, sem_in)
    if layer:
        arrival_out = fetch(0, own_out, other_out, out_w, sem_out)
    ready(tail, inner, spill)
    mixed_grad[:, :width] = inner[...]
    for b in range(batches):
        tail[b, 13:16] = tail[b, 13:16] + spill[b]
        hi = (b + 1) * span
        mixed_grad[hi - 16 : hi, :width] = tail[b].astype(BF16)
    ready(gate_grad)
    mixed_grad[:, width:] = gate_grad[...]
    block = 2 * width // targets
    turned = mixed_grad[...].astype(F32).T
    if layer:
        grad_o[...] = turned.astype(BF16)
        leave(grad_o)
    else:
        for j in range(targets):
            grad_o[j, :block] = turned[j * block : (j + 1) * block].astype(BF16)
    arrival.wait()
    normed_grad = against(mixed_grad[...], in_w[...])
    ready(rows, g, gain)
    input_grad, gain_grad = norm_back(rows[...].astype(F32), gain[...], normed_grad)
    if layer:
        gain_o[...] = gain_grad
        leave(gain_o)
    else:
        ready(gain_above)
        part = gain_grad.shape[1] // targets
        spot = lax.broadcasted_iota(jnp.int32, (16, LANES), 1)
        row = lax.broadcasted_iota(jnp.int32, (16, LANES), 0)
        pair = jnp.where(
            lax.broadcasted_iota(jnp.int32, (16, gain_grad.shape[1]), 0) == 0,
            gain_grad, gain_above[...],
        )
        for j in range(targets):
            moved = pltpu.roll(pair, (gain_grad.shape[1] - j * part) % gain_grad.shape[1], 1)
            grad_o[j, grad_o.held.shape[1] - 16 :] = jnp.where(
                (row < 2) & (spot < part), moved[:, :LANES], 0.0
            ).astype(BF16)
        leave(grad_o)
    g_new = (g[...].astype(F32) + input_grad).astype(BF16)
    g_o[...] = g_new
    leave(g_o)
    if layer:
        arrival_out.wait()
        gg = against(g_new, out_w[...])
        gg_o[...] = gg
        leave(gg_o)
        ready(gate, proj, low_w, vec, marks)
        gate = gate[...].astype(F32)
        sg[...] = gg * jax.nn.silu(gate)
        step = softplus(step_sum(proj[...], low_w, vec, rank, n))
        seff[...] = step + marks[:, 0:1] * STOP
        spread_columns(proj[...].astype(F32).T, rank + n, cx)
        ready(scanned)
        gate_o[...] = (gg * scanned[...] * silu_slope(gate)).astype(BF16)
        leave(gate_o)
        back_scan(batches, span, width // BLOCK, seff, sg, cx, vec.at[0:n], first)
        for b in range(batches):
            send_o[b * n : (b + 1) * n] = first[b].astype(BF16)


DMA = pltpu.SemaphoreType.DMA


def expected(us):
    return pl.CostEstimate(
        flops=int(us * 1e9), bytes_accessed=int(us * 3e6), transcendentals=0
    )


def run(kernel, us, outs, scratch, args, far, far_out, elsewhere=(), others=()):
    others = dict(others)
    whole_args = list(args) + list(others.values())
    far = tuple(far) + tuple(i for i in range(len(args)) if i not in far and i not in elsewhere)
    passing = [(args[i].shape, args[i].dtype) for i in far] + [outs[i] for i in far_out]
    count = len(passing)

    def whole(*refs):
        refs = list(refs)
        ins, refs = refs[: len(args)], refs[len(args) :]
        second, refs = dict(zip(others, refs)), refs[len(others) :]
        results, rest = refs[: len(outs)], refs[len(outs) :]
        own, buffers, sems = rest[: len(scratch)], rest[len(scratch) : -1], rest[-1]
        for k, i in enumerate(far):
            ins[i] = Arriving(ins[i], buffers[k], sems.at[k], second.get(i))
        for k, i in enumerate(far_out, len(far)):
            results[i] = Leaving(results[i], buffers[k], sems.at[k])
        kernel(*ins, *results, *own)
        ready(*ins)
        leave(*results)
        for ref in results:
            if isinstance(ref, Leaving):
                ref.copy.wait()

    return pl.pallas_call(
        whole,
        out_shape=[jax.ShapeDtypeStruct(*o) for o in outs],
        in_specs=[pl.BlockSpec(memory_space=pl.ANY)] * len(whole_args),
        out_specs=[
            pl.BlockSpec(memory_space=pl.ANY if i in far_out else pltpu.VMEM)
            for i in range(len(outs))
        ],
        scratch_shapes=[s if not isinstance(s, tuple) else pltpu.VMEM(*s) for s in scratch]
        + [pltpu.VMEM(*p) for p in passing]
        + [DMA((count,))],
        compiler_params=pltpu.CompilerParams(vmem_limit_bytes=VMEM_LIMIT),
        cost_estimate=expected(us),
    )(*whole_args)


def hop(batches, n, steps, at, own=(), own_b=(), totals=None):
    args = [at] + list(own) + ([] if own else [totals]) + list(own_b)
    outs = [jax.ShapeDtypeStruct(m[0].shape, BF16) for m in (own, own_b) if m]
    return pl.pallas_call(
        functools.partial(hop_kernel, batches, n, steps, bool(own), bool(own_b)),
        out_shape=outs,
        in_specs=[pl.BlockSpec(memory_space=pltpu.VMEM)] * len(args),
        out_specs=[pl.BlockSpec(memory_space=pltpu.VMEM)] * len(outs),
        compiler_params=pltpu.CompilerParams(vmem_limit_bytes=HOP_LIMIT),
        cost_estimate=expected(1),
    )(*args)


def flip(array, axis, bit):
    count = lax.axis_size(axis)
    return lax.ppermute(array, axis, [(i, i ^ bit) for i in range(count)])


def shifted(array, by):
    count = lax.axis_size("seq")
    pairs = [(i, i + by) for i in range(count) if 0 <= i + by < count]
    return lax.ppermute(array, "seq", pairs)


def tie(*arrays):
    return lax.optimization_barrier(arrays)


def bits_of(count):
    bits = [1 << k for k in range(count.bit_length() - 1)]
    assert 1 << len(bits) == count
    return bits


def pick(array, index, axis):
    return lax.dynamic_index_in_dim(array, index, axis, keepdims=False)


def local(
    tokens, starts, norm_gain, in_weight, conv_weight, conv_bias, xproj_weight,
    dtproj_weight, dt_bias, decay_rate, skip_gain, out_weight, cotangent,
):
    core = lax.axis_index("section")
    place = lax.axis_index("seq")
    cores = lax.axis_size("section")
    count = lax.axis_size("seq")
    bits = bits_of(count)
    batch_count, span, model = tokens.shape
    width = conv_weight.shape[2]
    n = decay_rate.shape[2]
    rank = dtproj_weight.shape[1]
    x_width = xproj_weight.shape[2]
    batches = batch_count // cores
    rows_n = batches * span
    half_model = model // 2
    low_core = core == 0
    steps = len(bits)

    def mine(array):
        return lax.dynamic_slice_in_dim(array, core * batches, batches, 0).reshape(
            (rows_n,) + array.shape[2:]
        )

    rows0 = mine(tokens)
    top = mine(cotangent)
    r = lax.dynamic_slice_in_dim(starts, core * batches, batches, 0).astype(F32)
    r_ext = jnp.concatenate([shifted(r[:, -3:].astype(BF16), 1).astype(F32), r], 1)
    free = 1.0 - r_ext
    m1 = free[:, 3:]
    m2 = m1 * free[:, 2:-1]
    m3 = m2 * free[:, 1:-2]
    marks = jnp.stack([r, m1, m2, m3], -1).reshape(rows_n, 4)

    tall = ((rows_n, width), F32)
    low_tall = ((rows_n, width), BF16)
    rim_s = ((batches, 3, width), F32)
    own_gain = norm_gain[0][None]
    in_own, out_own = in_weight[0], out_weight[0]

    vec_own = jnp.concatenate(
        [
            decay_rate[0].T * -LOG2E, conv_weight[0], conv_bias[0][None], dt_bias[0][None],
            skip_gain[0][None], jnp.pad(own_gain, ((0, 0), (0, width - model))),
        ],
        0,
    )
    low_own = jnp.concatenate([xproj_weight[0].T, dtproj_weight[0]], 0)
    all_rows0 = lax.all_gather(rows0, "seq")
    vec_other, low_other = flip(vec_own, "section", 1), flip(low_own, "section", 1)

    in_a, in_b, gate_a, gate_b, tail_a, tail_b = run(
        functools.partial(enter_kernel, batches, span, width), 5,
        [low_tall] * 4 + [rim_s] * 2,
        [((cores * rows_n, model), BF16), ((4, model, 2 * width // 4), BF16), DMA((4,))],
        [tokens.reshape(batch_count * span, model), own_gain, in_own],
        far=(0, 1), far_out=range(6), elsewhere=(2,),
    )
    in_a, in_b, gate_a, gate_b, tail_a, tail_b, vec_other, low_other, marks = tie(
        in_a, in_b, gate_a, gate_b, tail_a, tail_b, vec_other, low_other, marks
    )
    in_got = lax.ppermute(in_b, "section", [(0, 1)])
    everywhere = ("section", "seq")
    rim_a = lax.ppermute(tail_a, everywhere, [(i, i + 1) for i in range(count - 1)])
    rim_b = lax.ppermute(tail_b, everywhere, [(i, count + i + 1) for i in range(count - 1)])
    gate_got = lax.ppermute(gate_b, "section", [(0, 1)])

    out_now, in_now, _, _, _ = tie(out_own, in_own, in_got, rim_a, rim_b)
    out_other, in_other = flip(out_now, "section", 1), flip(in_now, "section", 1)
    vecs = [jnp.where(low_core == (l == 0), vec_own, vec_other) for l in range(2)]
    lows = [jnp.where(low_core == (l == 0), low_own, low_other) for l in range(2)]
    gains = [v[n + 7 :, :model] for v in vecs]
    in0, gate0 = jnp.where(low_core, in_a, in_got), jnp.where(low_core, gate_a, gate_got)
    rim0 = jnp.where(low_core, rim_a, rim_b)

    spread = ((rows_n, n, LANES), F32)
    state = ((batches, n, width), F32)
    flat_in = ((model, 2 * width), BF16)
    flat_out = ((width, model), BF16)
    send_s = ((batches * n + 16, width), BF16)
    send_back_s = ((batches * n, width), BF16)
    tall_t = ((width, rows_n), BF16)
    narrow = ((rows_n, model), BF16)

    totals_s = ((-(-batches * (steps + 1) // 8) * 8, width), F32)

    def front(layer, inner, rim, vec, low, *rest, others=()):
        outs = [low_tall, ((rows_n, LANES), BF16), send_s]
        scratch = [((span + 8, width), F32), tall, tall, spread, spread, state]
        args = [inner, rim, marks, vec, low, *rest]
        if layer:
            outs += [send_back_s]
            scratch += [tall, flat_out, DMA]
        return run(
            functools.partial(front_kernel, batches, span, width, rank, n, bool(layer)),
            10 if layer else 6, outs, scratch, args, far=(2, 3, 1, 0, 4),
            far_out=range(len(outs)), elsewhere=(7, 8) if layer else (), others=others,
        )

    conv0, proj0, send = front(
        0, in_a, rim_a, vec_own, low_own,
        others=((0, in_got), (1, rim_b), (3, vec_other), (4, low_other)),
    )
    at0, at1 = vecs[0][:n], vecs[1][:n]
    own = [send]
    for k, bit in enumerate(bits):
        own.append(flip(send, "seq", bit))
        if k < steps - 1:
            (send,) = hop(batches, n, k + 1, at0, own)
    scanned0, gated_t0, rows1, normed0, normed1, in1, gate1, before0, totals0, tail1 = run(
        functools.partial(end_kernel, batches, span, width, rank, n, steps), 10,
        [tall, tall_t, narrow, narrow, narrow, low_tall, low_tall, state, totals_s, rim_s],
        [tall, tall, spread, spread, flat_out, flat_in, DMA((2,))],
        [gate0, conv0, proj0, marks, vecs[0], lows[0], rows0, gains[1], gains[0],
         out_own, out_other, in_own, in_other, *own],
        far=(6, 8, 2, 5, 4, 3, 1, *range(13, 14 + steps), 0), far_out=range(10),
        elsewhere=(9, 10, 11, 12),
    )

    rim1 = shifted(tail1, 1)
    conv1, proj1, send, send_b = front(
        1, in1, rim1, vecs[1], lows[1], gate1, top, out_own, out_other
    )
    send, send_b, all_rows0 = tie(send, send_b, all_rows0)
    own, own_b = [send], [send_b]
    for k, bit in enumerate(bits):
        own.append(flip(send, "seq", bit))
        own_b.append(flip(send_b, "seq", bit))
        if k < steps - 1:
            send, send_b = hop(batches, n, k + 1, at1, own, own_b)

    def back(layer, gg, conv, inner, gate, rim, proj, *rest):
        outs = [
            low_tall, ((batches, 16, width), F32), ((batches, 3, width), F32),
            ((width, 2 * LANES), BF16),
        ]
        scratch = [
            tall, tall, ((batches, span + 1, n, BLOCK), F32), ((batches, span, n, BLOCK), F32),
            tall, tall, spread, spread, ((span + 16, width), F32), tall,
            ((LANES, width), F32), spread, spread, tall, state, state,
        ]
        if layer:
            outs += [low_tall, tall_t, narrow]
            scratch += [tall, tall, flat_out, DMA]
            far = (8, 7, 6, 5, 1, 0, 3, *range(12, 12 + 2 * steps))
        else:
            far = (8, 7, 6, 5, 1, 0, 3, *range(9, 11 + steps))
        return run(
            functools.partial(
                back_kernel, batches, span, width, rank, n, x_width, steps, bool(layer)
            ),
            22 if layer else 19, outs, scratch,
            [gg, conv, inner, gate, rim, marks, vecs[layer], lows[layer], proj, *rest],
            far=far, far_out=range(len(outs)),
            elsewhere=(10, 11) if layer else (),
        )

    inner1, last1, spill1, small1, gate_grad1, gated_t1, out1 = back(
        1, top, conv1, in1, gate1, rim1, proj1, rows1, out_own, out_other, *own[1:], *own_b[1:]
    )
    got1 = shifted(spill1, -1)

    def turn(layer, inner, tail, spill, gate_grad, rows, g, *rest):
        block = 2 * width // count
        outs = [((count, -(-block // 16) * 16 + 16, rows_n), BF16), narrow]
        if layer:
            outs[0] = ((2 * width, rows_n), BF16)
        scratch = [flat_in, DMA, ((rows_n, 2 * width), BF16)]
        args = [
            inner, tail, spill, gate_grad, rows, gains[layer], g, in_own, in_other, *rest
        ]
        elsewhere, far, far_out = [7, 8], [1, 2, 0, 3, 4, 6], [0, 1]
        if layer:
            outs += [((1, model), F32), tall, send_back_s, low_tall]
            scratch += [tall, tall, spread, state, flat_out, DMA]
            elsewhere += [9, 10]
            far += [11, 12, 16]
            far_out += [2, 3, 4, 5]
        return run(
            functools.partial(turn_kernel, batches, span, width, rank, n, count, layer),
            11 if layer else 4, outs, scratch, args, far=far, far_out=far_out,
            elsewhere=elsewhere,
        )

    grad_t1, g0, gain1, gg0, send_b, gate_grad0 = turn(
        1, inner1, last1, got1, gate_grad1, rows1, top, out_own, out_other, gate0, proj0,
        marks, lows[0], vecs[0], scanned0,
    )

    def half(array, which):
        return lax.dynamic_slice_in_dim(array, which * half_model, half_model, 1)

    def together(left, left_got, right, right_got):
        return dot(
            jnp.concatenate([left, left_got], 1), jnp.concatenate([right, right_got], 0)
        ).astype(BF16)

    normed_got = flip(half(normed1, 1 - core), "section", 1)
    gated_got = flip(jnp.where(low_core, gated_t1, gated_t0), "section", 1)
    gated_own = jnp.where(low_core, gated_t0, gated_t1)
    g_got = flip(jnp.where(low_core, top, g0), "section", 1)
    grad_got = flip(grad_t1, "section", 1)

    def add(kept, got):
        return kept + got.astype(F32)

    def part(total, bit, order):
        axis = len(order) - 1 - sorted(order).index(bit)
        total = total.reshape((2,) * len(order) + (-1, total.shape[-1]))
        mine = (place // bit) % 2
        return pick(total, 1 - mine, axis).astype(BF16), pick(total, mine, axis)

    def halve(total, bit, order):
        goes, stays = part(total, bit, order)
        return add(stays, flip(goes, "seq", bit))

    x_bit, y_bit = bits[0], bits[1]
    own_b = [send_b]
    for k, bit in enumerate(bits):
        got_b = flip(send_b, "seq", bit)
        if k == 1:
            a = together(grad_t1, grad_got, half(normed1, core), normed_got)
            b = together(gated_own, gated_got, jnp.where(low_core, g0, top), g_got)
            a_goes, a_stays = part(a, x_bit, bits)
            b_goes, b_stays = part(b, y_bit, bits)
            got_b, a_goes, b_goes = tie(got_b, a_goes, b_goes)
            a_got, b_got = flip(a_goes, "seq", x_bit), flip(b_goes, "seq", y_bit)
        own_b.append(got_b)
        if k < steps - 1:
            (send_b,) = hop(batches, n, k + 1, at0, (), own_b, totals0)
    inner0, tail0, spill0, small0 = back(
        0, gg0, conv0, in0, gate0, rim0, proj0, before0, totals0, *own_b[1:]
    )
    inner0, tail0, spill0, small0, a_got, b_got = tie(
        inner0, tail0, spill0, small0, a_got, b_got
    )
    got0 = shifted(spill0, -1)
    a_rest, b_rest = bits[1:], [x_bit] + bits[2:]
    a_goes, a_stays = part(add(a_stays, a_got), y_bit, a_rest)
    b_goes, b_stays = part(add(b_stays, b_got), x_bit, b_rest)
    a_got, b_got = flip(a_goes, "seq", y_bit), flip(b_goes, "seq", x_bit)
    blocks0, dx = turn(0, inner0, tail0, got0, gate_grad0, rows0, g0, gain1)
    blocks0, small0, small1, a_got, b_got = tie(blocks0, small0, small1, a_got, b_got)
    came0 = lax.all_to_all(blocks0, "seq", 0, 0, tiled=True)
    small_got = flip(jnp.where(low_core, small1, small0), "section", 1)
    small = add(jnp.where(low_core, small0, small1).astype(F32), small_got)
    a, b = add(a_stays, a_got), add(b_stays, b_got)
    for bit in bits[2:-1]:
        order = [k for k in bits[2:] if k >= bit]
        a, b = halve(a, bit, order), halve(b, bit, order)
    for bit in b_rest[:-1]:
        small = halve(small, bit, [k for k in b_rest if k >= bit]) if bit != x_bit else halve(
            halve(small, y_bit, bits), x_bit, b_rest
        )
    came0, a, b, small = tie(came0, a, b, small)
    all_normed0 = norm_rows(all_rows0.astype(F32), gains[0]).astype(BF16)
    block = 2 * width // count
    riding = jnp.sum(came0[:, -16:, : model // count].astype(F32), 0)
    in_sum0 = lax.dot_general(
        came0[:, :block], all_normed0, (((0, 2), (0, 1)), ((), ())),
        preferred_element_type=F32,
    )
    in_sum1 = halve(a, bits[-1], bits[-1:])
    out_sum = halve(b, bits[-1], bits[-1:])
    small = halve(small, bits[-1], bits[-1:])

    got0 = lax.ppermute(in_sum0.astype(BF16), "section", [(1, 0)])
    got1 = lax.ppermute(in_sum1.astype(BF16), "section", [(0, 1)])
    grad_in = jnp.where(
        low_core, add(in_sum0, got0), jnp.concatenate([got1.astype(F32), in_sum1], 1)
    )
    gain = jnp.where(low_core, riding[:1], riding[1:2])
    sent = jnp.where(low_core, riding[1:2], riding[:1])
    gain = gain + flip(sent, "section", 1)

    got = flip(jnp.where(low_core, out1, dx), "section", 1)
    boundary = jnp.where(
        low_core, jnp.concatenate([dx, got], 0), jnp.concatenate([got, out1], 0)
    ).reshape(1, batch_count, span, model)
    vec_sum = small[:, LANES:]
    return (
        boundary,
        gain,
        grad_in.T[None],
        vec_sum[:, n : n + 4].T[None],
        vec_sum[:, n + 4][None],
        small[:, :x_width][None],
        small[:, x_width:LANES].T[None],
        vec_sum[:, n + 5][None],
        vec_sum[:, :n][None],
        vec_sum[:, n + 6][None],
        out_sum[None],
    )


def solution(mesh):
    in_specs = (
        P(None, "seq", None), P(None, "seq"), P("section", None), P("section", None, None),
        P("section", None, None), P("section", None), P("section", None, None),
        P("section", None, None), P("section", None), P("section", None, None),
        P("section", None), P("section", None, None), P(None, "seq", None),
    )
    out_specs = (
        P("section", None, "seq", None), P("section", "seq"), P("section", None, "seq"),
        P("section", None, "seq"), P("section", "seq"), P("section", "seq", None),
        P("section", None, "seq"), P("section", "seq"), P("section", "seq", None),
        P("section", "seq"), P("section", "seq", None),
    )
    return jax.shard_map(local, mesh=mesh, in_specs=in_specs, out_specs=out_specs, check_vma=False)
```

```python
import functools
import jax
import jax.numpy as jnp
from jax import lax
from jax.experimental import pallas as pl
from jax.experimental.pallas import tpu as pltpu
from jax.sharding import PartitionSpec as P

EPS = 1e-05
LOG2E = 1.4426950408889634
STOP = 1e7
LANES = 128
BLOCK = 256
TILES = BLOCK // LANES
F32 = jnp.float32
BF16 = jnp.bfloat16
VMEM_LIMIT = 58 * 1024 * 1024
HOP_LIMIT = 6 * 1024 * 1024


def dot(left, right):
    return jnp.dot(left, right, preferred_element_type=F32)


def across(left, right):
    return lax.dot_general(left, right, (((0,), (0,)), ((), ())), preferred_element_type=F32)


def against(left, right):
    return lax.dot_general(left, right, (((1,), (1,)), ((), ())), preferred_element_type=F32)


def norm_rows(source, gain_row):
    return source * lax.rsqrt(jnp.mean(source * source, axis=-1, keepdims=True) + EPS) * gain_row


def softplus(v):
    return jnp.maximum(v, 0.0) + jnp.log1p(jnp.exp(-jnp.abs(v)))


def silu_slope(v):
    gate = jax.nn.sigmoid(v)
    return gate * (1.0 + v * (1.0 - gate))


def pair_up(left, right, row_ids, width):
    mask = (row_ids % (2 * width)) < width
    kept = jnp.where(mask, left, right)
    moved = jnp.where(mask, right, left)
    return kept + pltpu.roll(moved, 8 - width, 0)


def fold_rows(parts, row_ids):
    width = 1
    while len(parts) > 1:
        parts = [
            pair_up(parts[i], parts[i + 1], row_ids, width) for i in range(0, len(parts), 2)
        ]
        width *= 2
    return parts[0]


def halves(v):
    return v[:8] + v[8:]


def spread_columns(table, first, target):
    width = target.shape[1]
    for t in range(target.shape[0]):
        column = table[first : first + width, t : t + 1]
        target[t] = jnp.broadcast_to(column, (width, LANES))


def block_at(i):
    return pl.ds(pl.multiple_of(i * BLOCK, BLOCK), BLOCK)


def tile_at(i, lt):
    return pl.ds(pl.multiple_of(i * BLOCK + lt * LANES, LANES), LANES)


def local_scan(batches, span, blocks, seff, x, bx, at, final):
    def over_block(i, carry):
        rate = [at[:, tile_at(i, lt)] for lt in range(TILES)]

        def chunk(tc, states):
            states = list(states)
            for b in range(batches):
                rows = pl.ds(pl.multiple_of(b * span + tc * 8, 8), 8)
                for lt in range(TILES):
                    s8 = seff[rows, tile_at(i, lt)]
                    x8 = x[rows, tile_at(i, lt)]
                    h = states[b * TILES + lt]
                    for j in range(8):
                        decay = jnp.exp2(s8[j : j + 1] * rate[lt])
                        h = decay * h + x8[j : j + 1] * bx[b * span + tc * 8 + j]
                    states[b * TILES + lt] = h
            return tuple(states)

        zero = jnp.zeros((at.shape[0], LANES), F32)
        states = lax.fori_loop(0, span // 8, chunk, (zero,) * (batches * TILES))
        for b in range(batches):
            for lt in range(TILES):
                final[b, :, tile_at(i, lt)] = states[b * TILES + lt]
        return carry

    lax.fori_loop(0, blocks, over_block, 0)


def back_scan(batches, span, blocks, seff, sg, cx, at, first):
    chunks = span // 8

    def over_block(i, carry):
        rate = [at[:, tile_at(i, lt)] for lt in range(TILES)]

        def chunk(k, states):
            states = list(states)
            tc = chunks - 1 - k
            for b in range(batches):
                rows = pl.ds(pl.multiple_of(b * span + tc * 8, 8), 8)
                for lt in range(TILES):
                    s8 = seff[rows, tile_at(i, lt)]
                    g8 = sg[rows, tile_at(i, lt)]
                    q = states[b * TILES + lt]
                    for j in range(7, -1, -1):
                        decay = jnp.exp2(s8[j : j + 1] * rate[lt])
                        q = decay * (q + g8[j : j + 1] * cx[b * span + tc * 8 + j])
                    states[b * TILES + lt] = q
            return tuple(states)

        zero = jnp.zeros((at.shape[0], LANES), F32)
        states = lax.fori_loop(0, chunks, chunk, (zero,) * (batches * TILES))
        for b in range(batches):
            for lt in range(TILES):
                first[b, :, tile_at(i, lt)] = states[b * TILES + lt]
        return carry

    lax.fori_loop(0, blocks, over_block, 0)


class Arriving:
    def __init__(self, source, held, sem, other=None):
        self.held, self.waited = held, False
        if other is None:
            self.copy = pltpu.make_async_copy(source, held, sem)
            self.copy.start()
        else:
            self.copy = fetch(0, source, other, held, sem)

    def __getitem__(self, where):
        assert self.waited
        return self.held[where]

    def __setitem__(self, where, value):
        assert self.waited
        self.held[where] = value

    @property
    def at(self):
        return self.held.at


class Leaving:
    def __init__(self, target, held, sem):
        self.copy, self.held, self.started = pltpu.make_async_copy(held, target, sem), held, False

    def __getitem__(self, where):
        return self.held[where]

    def __setitem__(self, where, value):
        self.held[where] = value


def uppers_of(steps):
    place = lax.axis_index("seq")
    return [(place // (1 << k)) % 2 != 0 for k in range(steps)]


def ready(*refs):
    for ref in refs:
        if isinstance(ref, Arriving) and not ref.waited:
            ref.copy.wait()
            ref.waited = True


def leave(*refs):
    for ref in refs:
        if isinstance(ref, Leaving) and not ref.started:
            ref.copy.start()
            ref.started = True


def fetch(layer, own, other, held, sem):
    mine = lax.axis_index("section") == layer

    @pl.when(mine)
    def _():
        pltpu.make_async_copy(own, held, sem).start()

    @pl.when(jnp.logical_not(mine))
    def _():
        pltpu.make_async_copy(other, held, sem).start()

    return pltpu.make_async_copy(own, held, sem)


def split_total(totals):
    width = totals[0].shape[1]
    row_ids = lax.broadcasted_iota(jnp.int32, (16, width), 0)
    block = jnp.zeros((16, width), F32)
    for b, total in enumerate(totals):
        rest = total
        for k in range(3):
            part = rest.astype(BF16).astype(F32)
            block = jnp.where(row_ids == 3 * b + k, part, block)
            rest = rest - part
    return block.astype(BF16)


def join_total(block, b):
    block = block.astype(F32)
    return block[3 * b : 3 * b + 1] + block[3 * b + 1 : 3 * b + 2] + block[3 * b + 2 : 3 * b + 3]


def enter_kernel(
    batches, span, width,
    rows, gain, in_w,
    in_a_o, in_b_o, gate_a_o, gate_b_o, tail_a_o, tail_b_o,
    normed, held, sems,
):
    chunk = held.shape[2]
    copies = [
        pltpu.make_async_copy(in_w.at[:, pl.ds(c * chunk, chunk)], held.at[c], sems.at[c])
        for c in range(held.shape[0])
    ]
    for copy in copies:
        copy.start()
    ready(rows, gain)
    normed[...] = norm_rows(rows[...].astype(F32), gain[...]).astype(BF16)
    half = batches * span
    for c, copy in enumerate(copies):
        copy.wait()
        mixed = dot(normed[...], held[c])
        outs = (in_a_o, in_b_o) if c * chunk < width else (gate_a_o, gate_b_o)
        lanes = slice(c * chunk % width, c * chunk % width + chunk)
        for k, out in enumerate(outs):
            out[:, lanes] = mixed[k * half : (k + 1) * half].astype(BF16)
        if c * chunk < width:
            for k, tail in enumerate((tail_a_o, tail_b_o)):
                for b in range(batches):
                    last = k * half + (b + 1) * span
                    tail[b, :, lanes] = mixed[last - 3 : last].astype(BF16).astype(F32)
        if (c + 1) * chunk == width:
            leave(in_a_o, in_b_o, tail_a_o, tail_b_o)


def tap_rows(ext, rim, mixed, width, span):
    ext[5:8] = rim
    ext[8 : 8 + span] = mixed.astype(F32)


def conv_sum(ext, m, vec, n, span):
    v = vec[n + 4 : n + 5] + vec[n + 3 : n + 4] * ext[8 : 8 + span]
    for k in (1, 2, 3):
        v = v + vec[n + 3 - k : n + 4 - k] * (m[:, k : k + 1] * ext[8 - k : 8 - k + span])
    return v


def step_sum(proj, low_w, vec, rank, n):
    return dot(proj[:, :rank], low_w[rank + 2 * n :]) + vec[n + 5 : n + 6]


def front_kernel(
    batches, span, width, rank, states_n, with_back,
    *refs,
):
    refs = list(refs)
    mixed, rim, marks, vec, low_w = refs[:5]
    del refs[:5]
    if with_back:
        gate, g, own_w, other_w = refs[:4]
        del refs[:4]
    conv_o, proj_o, send_o = refs[:3]
    del refs[:3]
    if with_back:
        (send_back_o,) = refs[:1]
        del refs[:1]
    ext, seff, x, bx, cx, final = refs[:6]
    if with_back:
        sg, out_w, sem = refs[6:]
        arrival = fetch(1, own_w, other_w, out_w, sem)
    n = states_n
    ready(rim, marks, vec)
    m = marks[...]
    at = vec.at[0:n]
    ready(mixed)
    for b in range(batches):
        lo, hi = b * span, (b + 1) * span
        tap_rows(ext, rim[b], mixed[lo:hi], width, span)
        x[lo:hi] = jax.nn.silu(conv_sum(ext, m[lo:hi], vec, n, span))
    conv = x[...].astype(BF16)
    conv_o[...] = conv
    leave(conv_o)
    ready(low_w)
    proj = against(conv, low_w[...]).astype(BF16)
    proj_o[...] = proj
    leave(proj_o)
    step = softplus(step_sum(proj, low_w, vec, rank, n))
    seff[...] = step + m[:, 0:1] * STOP
    x[...] = step * conv.astype(F32)
    totals = [
        jnp.sum(seff[b * span : (b + 1) * span], axis=0, keepdims=True) for b in range(batches)
    ]
    send_o[batches * n :] = split_total(totals)
    table = proj.astype(F32).T
    spread_columns(table, rank, bx)
    local_scan(batches, span, width // BLOCK, seff, x, bx, at, final)
    for b in range(batches):
        send_o[b * n : (b + 1) * n] = final[b].astype(BF16)
    leave(send_o)
    if with_back:
        arrival.wait()
        spread_columns(table, rank + n, cx)
        ready(g, gate)
        gg = against(g[...], out_w[...])
        sg[...] = gg * jax.nn.silu(gate[...].astype(F32))
        back_scan(batches, span, width // BLOCK, seff, sg, cx, at, final)
        for b in range(batches):
            send_back_o[b * n : (b + 1) * n] = final[b].astype(BF16)


def merge(at, upper, mine, theirs, mine_total, their_total, backward):
    early, late = jnp.where(upper, theirs, mine), jnp.where(upper, mine, theirs)
    if backward:
        return jnp.exp2(jnp.where(upper, their_total, mine_total) * at) * late + early
    return jnp.exp2(jnp.where(upper, mine_total, their_total) * at) * early + late


def reach(at, n, b, uppers, gots, totals, backward):
    carry = jnp.zeros(at.shape, F32)
    span = jnp.zeros((1, at.shape[1]), F32)
    for upper, got, their_total in zip(uppers, gots, totals):
        comes = jnp.logical_not(upper) if backward else upper
        theirs = got[b * n : (b + 1) * n].astype(F32)
        carry = jnp.where(comes, jnp.exp2(span * at) * theirs + carry, carry)
        span = jnp.where(comes, span + their_total, span)
    return carry


def hop_kernel(batches, n, steps, forward, backward, *refs):
    refs = list(refs)
    take = lambda k: [refs.pop(0) for _ in range(k)]
    (at,) = take(1)
    at = at[...]
    if forward:
        own, *gots = take(1 + steps)
    else:
        (totals,) = take(1)
    if backward:
        own_b, *gots_b = take(1 + steps)
    if forward:
        (send,) = take(1)
    if backward:
        (send_b,) = take(1)
    uppers = uppers_of(steps)
    reached = []
    for b in range(batches):
        rows = slice(b * n, (b + 1) * n)
        if forward:
            total = join_total(own[batches * n :], b)
            mine = own[rows].astype(F32)
        else:
            total = totals[b : b + 1]
        if backward:
            mine_b = own_b[rows].astype(F32)
        for k, upper in enumerate(uppers):
            if forward:
                their_total = join_total(gots[k][batches * n :], b)
                mine = merge(
                    at, upper, mine, gots[k][rows].astype(F32), total, their_total, False
                )
            else:
                their_total = totals[(k + 1) * batches + b : (k + 1) * batches + b + 1]
            if backward:
                mine_b = merge(
                    at, upper, mine_b, gots_b[k][rows].astype(F32), total, their_total, True
                )
            total = total + their_total
        if forward:
            send[rows] = mine.astype(BF16)
        if backward:
            send_b[rows] = mine_b.astype(BF16)
        reached.append(total)
    if forward:
        send[batches * n :] = split_total(reached)


def prepare(step, marks, conv, seff, x):
    seff[...] = step + marks * STOP
    x[...] = step * conv.astype(F32)


def end_kernel(
    batches, span, width, rank, n, steps,
    gate, conv, proj, marks, vec, low_w, rows, gain, gain_before,
    own_out, other_out, own_in, other_in, own_send, *refs,
):
    gots, refs = refs[:steps], refs[steps:]
    (
        scanned_o, gated_t_o, rows_o, normed_before_o, normed_o, inner_o, gate_o, before_o,
        totals_o, tail_o, seff, x, bx, cx, out_w, in_w, sems,
    ) = refs

    arrivals = [
        fetch(0, own_out, other_out, out_w, sems.at[0]),
        fetch(1, own_in, other_in, in_w, sems.at[1]),
    ]
    blocks = width // BLOCK
    at = vec.at[0:n]
    ready(rows, gain_before, proj, low_w, vec, marks, conv)
    normed_before_o[...] = norm_rows(rows[...].astype(F32), gain_before[...]).astype(BF16)
    leave(normed_before_o)
    step = softplus(step_sum(proj[...], low_w, vec, rank, n))
    prepare(step, marks[:, 0:1], conv[...], seff, x)
    table = proj[...].astype(F32).T
    spread_columns(table, rank, bx)
    spread_columns(table, rank + n, cx)
    ready(own_send, *gots)
    uppers = uppers_of(steps)
    for b in range(batches):
        totals_o[b : b + 1] = join_total(own_send[batches * n :], b)
        theirs = [join_total(got[batches * n :], b) for got in gots]
        for k, their in enumerate(theirs):
            totals_o[(k + 1) * batches + b : (k + 1) * batches + b + 1] = their
        before_o[b] = reach(at[...], n, b, uppers, gots, theirs, False)
    leave(before_o, totals_o)
    row_ids = lax.broadcasted_iota(jnp.int32, (8, LANES), 0)

    def over_block(i, carry):
        rate = [at[:, tile_at(i, lt)] for lt in range(TILES)]

        def chunk(tc, states):
            states = list(states)
            for b in range(batches):
                rows8 = pl.ds(pl.multiple_of(b * span + tc * 8, 8), 8)
                for lt in range(TILES):
                    s8 = seff[rows8, tile_at(i, lt)]
                    x8 = x[rows8, tile_at(i, lt)]
                    h = states[b * TILES + lt]
                    parts = []
                    for j in range(8):
                        t = b * span + tc * 8 + j
                        decay = jnp.exp2(s8[j : j + 1] * rate[lt])
                        h = decay * h + x8[j : j + 1] * bx[t]
                        parts.append(halves(h * cx[t]))
                    states[b * TILES + lt] = h
                    scanned_o[rows8, tile_at(i, lt)] = fold_rows(parts, row_ids)
            return tuple(states)

        start = tuple(
            before_o[b, :, tile_at(i, lt)] for b in range(batches) for lt in range(TILES)
        )
        lax.fori_loop(0, span // 8, chunk, start)
        return carry

    lax.fori_loop(0, blocks, over_block, 0)
    scanned = scanned_o[...] + vec[n + 6 : n + 7] * conv[...].astype(F32)
    scanned_o[...] = scanned
    leave(scanned_o)
    ready(gate)
    gated_f = scanned * jax.nn.silu(gate[...].astype(F32))
    gated = gated_f.astype(BF16)
    gated_t_o[...] = gated_f.T.astype(BF16)
    leave(gated_t_o)
    arrivals[0].wait()
    result = (rows[...].astype(F32) + dot(gated, out_w[...])).astype(BF16)
    rows_o[...] = result
    leave(rows_o)
    ready(gain)
    normed_o[...] = norm_rows(result.astype(F32), gain[...]).astype(BF16)
    leave(normed_o)
    arrivals[1].wait()
    for first, target in ((0, inner_o), (width, gate_o)):
        for c in range(0, width, 512):
            mixed = dot(normed_o[...], in_w[:, first + c : first + c + 512])
            target[:, c : c + 512] = mixed.astype(BF16)
            if not first:
                for b in range(batches):
                    last = (b + 1) * span
                    tail_o[b, :, c : c + 512] = mixed[last - 3 : last].astype(BF16).astype(F32)
        leave(target, tail_o)


def back_kernel(
    batches, span, width, rank, n, x_width, steps, with_out,
    *refs,
):
    refs = list(refs)
    take = lambda k: [refs.pop(0) for _ in range(k)]
    gg, conv, inner, gate, rim, marks, vec, low_w, proj = take(9)
    if with_out:
        rows, own_out, other_out = take(3)
        gots = take(steps)
    else:
        before, totals = take(2)
    gots_b = take(steps)
    inner_o, tail_o, spill_o, pair_o, vec_o = take(5)
    if with_out:
        gate_o, gated_t_o, out_o = take(3)
    seff, x, hist, decays, drive, zsum, acc_b, acc_c, ext, sg, bx, cx, pre_grad = take(13)
    state_in, grad_in = take(2)
    if with_out:
        scanned_ref, gg_s, out_w, sem = take(4)
        arrival = fetch(1, own_out, other_out, out_w, sem)
    blocks = width // BLOCK
    rows_n = batches * span
    chunks = span // 8
    ready(proj, low_w, vec, marks, conv)
    m = marks[...]
    at = vec.at[0:n]
    spre = step_sum(proj[...], low_w, vec, rank, n)
    prepare(softplus(spre), m[:, 0:1], conv[...], seff, x)
    table = proj[...].astype(F32).T
    spread_columns(table, rank, bx)
    spread_columns(table, rank + n, cx)
    ready(gg, gate)
    if with_out:
        arrival.wait()
        gg_s[...] = against(gg[...], out_w[...])
        gg = gg_s
    sg[...] = gg[...] * jax.nn.silu(gate[...].astype(F32))
    if with_out:
        ready(*gots)
    else:
        ready(before, totals)
    ready(*gots_b)
    uppers = uppers_of(steps)
    for b in range(batches):
        if with_out:
            theirs = [join_total(got[batches * n :], b) for got in gots]
            state_in[b] = reach(at[...], n, b, uppers, gots, theirs, False)
        else:
            theirs = [
                totals[(k + 1) * batches + b : (k + 1) * batches + b + 1] for k in range(steps)
            ]
            state_in[b] = before[b]
        grad_in[b] = reach(at[...], n, b, uppers, gots_b, theirs, True)
    acc_b[...] = jnp.zeros_like(acc_b)
    acc_c[...] = jnp.zeros_like(acc_c)
    vec_o[...] = jnp.zeros((n + 8, width), F32)
    row_ids = lax.broadcasted_iota(jnp.int32, (8, LANES), 0)

    def over_block(i, carry):
        rate = [at[:, tile_at(i, lt)] for lt in range(TILES)]

        def again(tc, states):
            states = list(states)
            for b in range(batches):
                rows8 = pl.ds(pl.multiple_of(b * span + tc * 8, 8), 8)
                for lt in range(TILES):
                    s8 = seff[rows8, tile_at(i, lt)]
                    x8 = x[rows8, tile_at(i, lt)]
                    h = states[b * TILES + lt]
                    lanes = pl.ds(lt * LANES, LANES)
                    parts = []
                    for j in range(8):
                        t = tc * 8 + j
                        decay = jnp.exp2(s8[j : j + 1] * rate[lt])
                        h = decay * h + x8[j : j + 1] * bx[b * span + t]
                        decays[b, t, :, lanes] = decay
                        hist[b, t + 1, :, lanes] = h
                        if with_out:
                            parts.append(halves(h * cx[b * span + t]))
                    states[b * TILES + lt] = h
                    if with_out:
                        scanned_ref[rows8, tile_at(i, lt)] = fold_rows(parts, row_ids)
            return tuple(states)

        for b in range(batches):
            hist[b, 0] = state_in[b, :, block_at(i)]
        start = tuple(
            state_in[b, :, tile_at(i, lt)] for b in range(batches) for lt in range(TILES)
        )
        lax.fori_loop(0, chunks, again, start)

        sums = tuple(jnp.zeros((n, LANES), F32) for _ in range(TILES))
        for b in range(batches):

            def chunk(k, held):
                held = list(held)
                tc = chunks - 1 - k
                rows8 = pl.ds(pl.multiple_of(b * span + tc * 8, 8), 8)
                s8, x8, g8 = [], [], []
                for lt in range(TILES):
                    s8.append(seff[rows8, tile_at(i, lt)])
                    x8.append(x[rows8, tile_at(i, lt)])
                    g8.append(sg[rows8, tile_at(i, lt)])
                drives = [[None] * 8 for _ in range(TILES)]
                zs = [[None] * 8 for _ in range(TILES)]
                for j in range(7, -1, -1):
                    t = tc * 8 + j
                    part_b, part_c = [], []
                    for lt in range(TILES):
                        lanes = pl.ds(lt * LANES, LANES)
                        total = held[lt] + g8[lt][j : j + 1] * cx[b * span + t]
                        q = decays[b, t, :, lanes] * total
                        log_grad = q * hist[b, t, :, lanes]
                        held[TILES + lt] = held[TILES + lt] + log_grad * s8[lt][j : j + 1]
                        zs[lt][j] = halves(log_grad * rate[lt])
                        drives[lt][j] = halves(total * bx[b * span + t])
                        part_b.append(total * x8[lt][j : j + 1])
                        part_c.append(g8[lt][j : j + 1] * hist[b, t + 1, :, lanes])
                        held[lt] = q
                    acc_b[b * span + t] += sum(part_b[1:], part_b[0])
                    acc_c[b * span + t] += sum(part_c[1:], part_c[0])
                for lt in range(TILES):
                    drive[rows8, tile_at(i, lt)] = fold_rows(drives[lt], row_ids)
                    zsum[rows8, tile_at(i, lt)] = fold_rows(zs[lt], row_ids)
                return tuple(held)

            start = tuple(grad_in[b, :, tile_at(i, lt)] for lt in range(TILES)) + sums
            sums = lax.fori_loop(0, chunks, chunk, start)[TILES:]
        for lt in range(TILES):
            vec_o[0:n, tile_at(i, lt)] = -sums[lt]
        return carry

    lax.fori_loop(0, blocks, over_block, 0)

    conv_f = conv[...].astype(F32)
    if with_out:
        ready(rows)
        gate = gate[...].astype(F32)
        scanned = scanned_ref[...] + vec[n + 6 : n + 7] * conv_f
        gated_f = scanned * jax.nn.silu(gate)
        gated_t_o[...] = gated_f.T.astype(BF16)
        out_o[...] = (rows[...].astype(F32) + dot(gated_f.astype(BF16), out_w[...])).astype(BF16)
        gate_o[...] = (gg_s[...] * scanned * silu_slope(gate)).astype(BF16)
        leave(gate_o, gated_t_o, out_o)

    column_ids = lax.broadcasted_iota(jnp.int32, (n, rows_n), 1)

    def gather_column(t, pair):
        now = []
        for held, acc in zip(pair, (acc_b, acc_c)):
            column = jnp.sum(acc[t], axis=1, keepdims=True)
            now.append(jnp.where(column_ids == t, column, held))
        return tuple(now)

    zero = jnp.zeros((n, rows_n), F32)
    b_grad, c_grad = lax.fori_loop(0, rows_n, gather_column, (zero, zero), unroll=8)
    rest = LANES - rank - 2 * n
    placed = jnp.concatenate(
        [jnp.zeros((rank, rows_n), F32), b_grad, c_grad, jnp.zeros((rest, rows_n), F32)], 0
    ).T
    spre = step_sum(proj[...], low_w, vec, rank, n)
    step = softplus(spre)
    step_grad = zsum[...] * (1.0 / LOG2E) + drive[...] * conv_f
    pre_g = step_grad * jax.nn.sigmoid(spre)
    low = pre_g.astype(BF16)
    low_grad = against(low, low_w[rank + 2 * n :])
    pgrad = (
        jnp.concatenate([low_grad, jnp.zeros((rows_n, LANES - rank), F32)], 1) + placed
    ).astype(BF16)
    small = dot(conv_f.T.astype(BF16), pgrad)
    lows = pltpu.roll(dot(pre_g.T.astype(BF16), proj[...]), x_width, 1)
    columns = lax.broadcasted_iota(jnp.int32, (1, LANES), 1)
    pair_o[...] = jnp.where(columns < x_width, small, lows).astype(BF16)
    leave(pair_o)
    conv_grad = (
        sg[...] * vec[n + 6 : n + 7] + step * drive[...]
        + dot(pgrad[:, : rank + 2 * n], low_w[: rank + 2 * n])
    )
    pre_grad[...] = conv_grad
    vec_o[n + 5 : n + 6] = jnp.sum(pre_g, axis=0, keepdims=True)
    vec_o[n + 6 : n + 7] = jnp.sum(sg[...] * conv_f, axis=0, keepdims=True)
    ready(inner, rim)
    taps = [jnp.zeros((1, width), F32) for _ in range(4)]
    bias = jnp.zeros((1, width), F32)
    for b in range(batches):
        lo, hi = b * span, (b + 1) * span
        tap_rows(ext, rim[b], inner[lo:hi], width, span)
        grad_b = pre_grad[lo:hi] * silu_slope(conv_sum(ext, m[lo:hi], vec, n, span))
        bias = bias + jnp.sum(grad_b, axis=0, keepdims=True)
        taps[3] = taps[3] + jnp.sum(grad_b * ext[8 : 8 + span], axis=0, keepdims=True)
        for k in (1, 2, 3):
            taps[3 - k] = taps[3 - k] + jnp.sum(
                grad_b * (m[lo:hi, k : k + 1] * ext[8 - k : 8 - k + span]),
                axis=0, keepdims=True,
            )
        back = vec[n + 3 : n + 4] * grad_b
        spill = jnp.zeros((8, width), F32)
        for k in (1, 2, 3):
            ext[0:8] = jnp.zeros((8, width), F32)
            ext[8 : 8 + span] = vec[n + 3 - k : n + 4 - k] * (m[lo:hi, k : k + 1] * grad_b)
            ext[8 + span : 16 + span] = jnp.zeros((8, width), F32)
            back = back + ext[8 + k : 8 + k + span]
            spill = spill + ext[k : 8 + k]
        inner_o[lo:hi] = back.astype(BF16)
        tail_o[b] = back[span - 16 :]
        spill_o[b] = spill[5:8]
    leave(spill_o, inner_o, tail_o)
    for k in range(4):
        vec_o[n + k : n + k + 1] = taps[k]
    vec_o[n + 4 : n + 5] = bias


def norm_back(source, gain, grad):
    scale = lax.rsqrt(jnp.mean(source * source, axis=-1, keepdims=True) + EPS)
    unit = source * scale
    scaled = grad * gain
    along = jnp.mean(scaled * unit, axis=-1, keepdims=True)
    return scale * (scaled - unit * along), grad * unit


def turn_kernel(
    batches, span, width, rank, n, targets, layer,
    *refs,
):
    refs = list(refs)
    take = lambda k: [refs.pop(0) for _ in range(k)]
    inner, tail, spill, gate_grad, rows, gain, g, pair, vgrad, own_in, other_in = take(11)
    if layer:
        own_out, other_out, gate, proj, marks, low_w, vec, scanned = take(8)
    grad_o, g_o, small_o = take(3)
    if layer:
        gg_o, send_o, gate_o, gate_t_o = take(4)
    in_w, sem_in, mixed_grad, column = take(4)
    rows_n = batches * span
    if layer:
        seff, sg, cx, first, out_w, sem_out = take(6)
    arrival = fetch(layer, own_in, other_in, in_w, sem_in)
    if layer:
        arrival_out = fetch(0, own_out, other_out, out_w, sem_out)
    ready(tail, inner, spill)
    mixed_grad[:, :width] = inner[...]
    for b in range(batches):
        tail[b, 13:16] = tail[b, 13:16] + spill[b]
        hi = (b + 1) * span
        mixed_grad[hi - 16 : hi, :width] = tail[b].astype(BF16)
    ready(gate_grad)
    mixed_grad[:, width:] = gate_grad[...]
    wide = 2 * width if layer else width
    grad_o[...] = mixed_grad[:, :wide].astype(F32).T.astype(BF16)
    leave(grad_o)
    ready(pair, vgrad)
    small_o[:, :LANES] = pair[...]
    arrival.wait()
    normed_grad = against(mixed_grad[...], in_w[...])
    ready(rows, g, gain)
    input_grad, terms = norm_back(rows[...].astype(F32), gain[...], normed_grad)
    g_new = (g[...].astype(F32) + input_grad).astype(BF16)
    g_o[...] = g_new
    leave(g_o)
    column[...] = jnp.concatenate(
        [vgrad[...], jnp.zeros((LANES - vgrad.held.shape[0], width), F32)], 0
    ).T
    sums = jnp.sum(terms.T, axis=1, keepdims=True)
    spot = lax.broadcasted_iota(jnp.int32, (1, LANES), 1) == n + 7
    part, block = sums.shape[0] // targets, width // targets
    for j in range(targets):
        rows_j = slice(j * block, j * block + part)
        column[rows_j] = jnp.where(spot, sums[j * part : (j + 1) * part], column[rows_j])
    small_o[:, LANES:] = column[...].astype(BF16)
    leave(small_o)
    if layer:
        arrival_out.wait()
        gg = against(g_new, out_w[...])
        gg_o[...] = gg
        leave(gg_o)
        ready(gate, proj, low_w, vec, marks)
        gate = gate[...].astype(F32)
        sg[...] = gg * jax.nn.silu(gate)
        step = softplus(step_sum(proj[...], low_w, vec, rank, n))
        seff[...] = step + marks[:, 0:1] * STOP
        spread_columns(proj[...].astype(F32).T, rank + n, cx)
        ready(scanned)
        gate_new = gg * scanned[...] * silu_slope(gate)
        gate_o[...] = gate_new.astype(BF16)
        gate_t_o[...] = gate_new.T.astype(BF16)
        leave(gate_o, gate_t_o)
        back_scan(batches, span, width // BLOCK, seff, sg, cx, vec.at[0:n], first)
        for b in range(batches):
            send_o[b * n : (b + 1) * n] = first[b].astype(BF16)


DMA = pltpu.SemaphoreType.DMA


def expected(us):
    return pl.CostEstimate(
        flops=int(us * 1e9), bytes_accessed=int(us * 3e6), transcendentals=0
    )


def run(kernel, us, outs, scratch, args, far, far_out, elsewhere=(), others=()):
    others = dict(others)
    whole_args = list(args) + list(others.values())
    far = tuple(far) + tuple(i for i in range(len(args)) if i not in far and i not in elsewhere)
    passing = [(args[i].shape, args[i].dtype) for i in far] + [outs[i] for i in far_out]
    count = len(passing)

    def whole(*refs):
        refs = list(refs)
        ins, refs = refs[: len(args)], refs[len(args) :]
        second, refs = dict(zip(others, refs)), refs[len(others) :]
        results, rest = refs[: len(outs)], refs[len(outs) :]
        own, buffers, sems = rest[: len(scratch)], rest[len(scratch) : -1], rest[-1]
        for k, i in enumerate(far):
            ins[i] = Arriving(ins[i], buffers[k], sems.at[k], second.get(i))
        for k, i in enumerate(far_out, len(far)):
            results[i] = Leaving(results[i], buffers[k], sems.at[k])
        kernel(*ins, *results, *own)
        ready(*ins)
        leave(*results)
        for ref in results:
            if isinstance(ref, Leaving):
                ref.copy.wait()

    return pl.pallas_call(
        whole,
        out_shape=[jax.ShapeDtypeStruct(*o) for o in outs],
        in_specs=[pl.BlockSpec(memory_space=pl.ANY)] * len(whole_args),
        out_specs=[
            pl.BlockSpec(memory_space=pl.ANY if i in far_out else pltpu.VMEM)
            for i in range(len(outs))
        ],
        scratch_shapes=[s if not isinstance(s, tuple) else pltpu.VMEM(*s) for s in scratch]
        + [pltpu.VMEM(*p) for p in passing]
        + [DMA((count,))],
        compiler_params=pltpu.CompilerParams(vmem_limit_bytes=VMEM_LIMIT),
        cost_estimate=expected(us),
    )(*whole_args)


def hop(batches, n, steps, at, own=(), own_b=(), totals=None):
    args = [at] + list(own) + ([] if own else [totals]) + list(own_b)
    outs = [jax.ShapeDtypeStruct(m[0].shape, BF16) for m in (own, own_b) if m]
    return pl.pallas_call(
        functools.partial(hop_kernel, batches, n, steps, bool(own), bool(own_b)),
        out_shape=outs,
        in_specs=[pl.BlockSpec(memory_space=pltpu.VMEM)] * len(args),
        out_specs=[pl.BlockSpec(memory_space=pltpu.VMEM)] * len(outs),
        compiler_params=pltpu.CompilerParams(vmem_limit_bytes=HOP_LIMIT),
        cost_estimate=expected(1),
    )(*args)


def flip(array, axis, bit):
    count = lax.axis_size(axis)
    return lax.ppermute(array, axis, [(i, i ^ bit) for i in range(count)])


def shifted(array, by):
    count = lax.axis_size("seq")
    pairs = [(i, i + by) for i in range(count) if 0 <= i + by < count]
    return lax.ppermute(array, "seq", pairs)


def tie(*arrays):
    return lax.optimization_barrier(arrays)


def bits_of(count):
    bits = [1 << k for k in range(count.bit_length() - 1)]
    assert 1 << len(bits) == count
    return bits


def swapped(bits):
    return [bits[1], bits[0]] + list(bits[2:]) if len(bits) > 1 else list(bits)


def pick(array, index, axis):
    return lax.dynamic_index_in_dim(array, index, axis, keepdims=False)


def local(
    tokens, starts, norm_gain, in_weight, conv_weight, conv_bias, xproj_weight,
    dtproj_weight, dt_bias, decay_rate, skip_gain, out_weight, cotangent,
):
    core = lax.axis_index("section")
    place = lax.axis_index("seq")
    cores = lax.axis_size("section")
    count = lax.axis_size("seq")
    bits = bits_of(count)
    batch_count, span, model = tokens.shape
    width = conv_weight.shape[2]
    n = decay_rate.shape[2]
    rank = dtproj_weight.shape[1]
    x_width = xproj_weight.shape[2]
    batches = batch_count // cores
    rows_n = batches * span
    half_model = model // 2
    low_core = core == 0
    steps = len(bits)

    def mine(array):
        return lax.dynamic_slice_in_dim(array, core * batches, batches, 0).reshape(
            (rows_n,) + array.shape[2:]
        )

    rows0 = mine(tokens)
    top = mine(cotangent)
    r = lax.dynamic_slice_in_dim(starts, core * batches, batches, 0).astype(F32)
    r_ext = jnp.concatenate([shifted(r[:, -3:].astype(BF16), 1).astype(F32), r], 1)
    free = 1.0 - r_ext
    m1 = free[:, 3:]
    m2 = m1 * free[:, 2:-1]
    m3 = m2 * free[:, 1:-2]
    marks = jnp.stack([r, m1, m2, m3], -1).reshape(rows_n, 4)

    tall = ((rows_n, width), F32)
    low_tall = ((rows_n, width), BF16)
    rim_s = ((batches, 3, width), F32)
    own_gain = norm_gain[0][None]
    in_own, out_own = in_weight[0], out_weight[0]

    vec_own = jnp.concatenate(
        [
            decay_rate[0].T * -LOG2E, conv_weight[0], conv_bias[0][None], dt_bias[0][None],
            skip_gain[0][None], jnp.pad(own_gain, ((0, 0), (0, width - model))),
        ],
        0,
    )
    low_own = jnp.concatenate([xproj_weight[0].T, dtproj_weight[0]], 0)
    vec_other, low_other = flip(vec_own, "section", 1), flip(low_own, "section", 1)

    in_a, in_b, gate_a, gate_b, tail_a, tail_b = run(
        functools.partial(enter_kernel, batches, span, width), 5,
        [low_tall] * 4 + [rim_s] * 2,
        [((cores * rows_n, model), BF16), ((4, model, 2 * width // 4), BF16), DMA((4,))],
        [tokens.reshape(batch_count * span, model), own_gain, in_own],
        far=(0, 1), far_out=range(6), elsewhere=(2,),
    )
    in_a, in_b, gate_a, gate_b, tail_a, tail_b, vec_other, low_other, marks = tie(
        in_a, in_b, gate_a, gate_b, tail_a, tail_b, vec_other, low_other, marks
    )
    in_got = lax.ppermute(in_b, "section", [(0, 1)])
    everywhere = ("section", "seq")
    rim_a = lax.ppermute(tail_a, everywhere, [(i, i + 1) for i in range(count - 1)])
    rim_b = lax.ppermute(tail_b, everywhere, [(i, count + i + 1) for i in range(count - 1)])
    gate_got = lax.ppermute(gate_b, "section", [(0, 1)])

    out_now, in_now, _, _, _ = tie(out_own, in_own, in_got, rim_a, rim_b)
    out_other, in_other = flip(out_now, "section", 1), flip(in_now, "section", 1)
    vecs = [jnp.where(low_core == (l == 0), vec_own, vec_other) for l in range(2)]
    lows = [jnp.where(low_core == (l == 0), low_own, low_other) for l in range(2)]
    gains = [v[n + 7 :, :model] for v in vecs]
    in0, gate0 = jnp.where(low_core, in_a, in_got), jnp.where(low_core, gate_a, gate_got)
    rim0 = jnp.where(low_core, rim_a, rim_b)

    spread = ((rows_n, n, LANES), F32)
    state = ((batches, n, width), F32)
    flat_in = ((model, 2 * width), BF16)
    flat_out = ((width, model), BF16)
    send_s = ((batches * n + 16, width), BF16)
    send_back_s = ((batches * n, width), BF16)
    tall_t = ((width, rows_n), BF16)
    narrow = ((rows_n, model), BF16)

    totals_s = ((-(-batches * (steps + 1) // 8) * 8, width), F32)

    def front(layer, inner, rim, vec, low, *rest, others=()):
        outs = [low_tall, ((rows_n, LANES), BF16), send_s]
        scratch = [((span + 8, width), F32), tall, tall, spread, spread, state]
        args = [inner, rim, marks, vec, low, *rest]
        if layer:
            outs += [send_back_s]
            scratch += [tall, flat_out, DMA]
        return run(
            functools.partial(front_kernel, batches, span, width, rank, n, bool(layer)),
            10 if layer else 6, outs, scratch, args, far=(2, 3, 1, 0, 4),
            far_out=range(len(outs)), elsewhere=(7, 8) if layer else (), others=others,
        )

    conv0, proj0, send = front(
        0, in_a, rim_a, vec_own, low_own,
        others=((0, in_got), (1, rim_b), (3, vec_other), (4, low_other)),
    )
    at0, at1 = vecs[0][:n], vecs[1][:n]
    own = [send]
    for k, bit in enumerate(bits):
        own.append(flip(send, "seq", bit))
        if k < steps - 1:
            (send,) = hop(batches, n, k + 1, at0, own)
    scanned0, gated_t0, rows1, normed0, normed1, in1, gate1, before0, totals0, tail1 = run(
        functools.partial(end_kernel, batches, span, width, rank, n, steps), 10,
        [tall, tall_t, narrow, narrow, narrow, low_tall, low_tall, state, totals_s, rim_s],
        [tall, tall, spread, spread, flat_out, flat_in, DMA((2,))],
        [gate0, conv0, proj0, marks, vecs[0], lows[0], rows0, gains[1], gains[0],
         out_own, out_other, in_own, in_other, *own],
        far=(6, 8, 2, 5, 4, 3, 1, *range(13, 14 + steps), 0), far_out=range(10),
        elsewhere=(9, 10, 11, 12),
    )

    rim1 = shifted(tail1, 1)
    conv1, proj1, send, send_b = front(
        1, in1, rim1, vecs[1], lows[1], gate1, top, out_own, out_other
    )
    own, own_b = [send], [send_b]
    for k, bit in enumerate(bits):
        own.append(flip(send, "seq", bit))
        own_b.append(flip(send_b, "seq", bit))
        if k < steps - 1:
            send, send_b = hop(batches, n, k + 1, at1, own, own_b)

    def back(layer, gg, conv, inner, gate, rim, proj, *rest):
        outs = [
            low_tall, ((batches, 16, width), F32), ((batches, 3, width), F32),
            ((width, LANES), BF16), ((n + 8, width), F32),
        ]
        scratch = [
            tall, tall, ((batches, span + 1, n, BLOCK), F32), ((batches, span, n, BLOCK), F32),
            tall, tall, spread, spread, ((span + 16, width), F32), tall,
            spread, spread, tall, state, state,
        ]
        if layer:
            outs += [low_tall, tall_t, narrow]
            scratch += [tall, tall, flat_out, DMA]
            far = (8, 7, 6, 5, 1, 0, 3, *range(12, 12 + 2 * steps))
        else:
            far = (8, 7, 6, 5, 1, 0, 3, *range(9, 11 + steps))
        return run(
            functools.partial(
                back_kernel, batches, span, width, rank, n, x_width, steps, bool(layer)
            ),
            22 if layer else 19, outs, scratch,
            [gg, conv, inner, gate, rim, marks, vecs[layer], lows[layer], proj, *rest],
            far=far, far_out=range(len(outs)),
            elsewhere=(10, 11) if layer else (),
        )

    inner1, last1, spill1, pair1, vgrad1, gate_grad1, gated_t1, out1 = back(
        1, top, conv1, in1, gate1, rim1, proj1, rows1, out_own, out_other, *own[1:], *own_b[1:]
    )
    got1 = shifted(spill1, -1)

    def turn(layer, inner, tail, spill, gate_grad, rows, g, pair, vgrad, *rest):
        outs = [
            ((2 * width if layer else width, rows_n), BF16), narrow, ((width, 2 * LANES), BF16)
        ]
        scratch = [
            flat_in, DMA, ((rows_n, 2 * width), BF16), ((width, LANES), F32),
        ]
        args = [
            inner, tail, spill, gate_grad, rows, gains[layer], g, pair, vgrad, in_own, in_other,
            *rest,
        ]
        elsewhere, far, far_out = [9, 10], [1, 2, 0, 3, 4, 6], [0, 1, 2]
        if layer:
            outs += [tall, send_back_s, low_tall, tall_t]
            scratch += [tall, tall, spread, state, flat_out, DMA]
            elsewhere += [11, 12]
            far += [13, 14, 18]
            far_out += [3, 4, 5, 6]
        return run(
            functools.partial(turn_kernel, batches, span, width, rank, n, count, layer),
            11 if layer else 4, outs, scratch, args, far=far, far_out=far_out,
            elsewhere=elsewhere,
        )

    grad_t1, g0, small1, gg0, send_b, gate_grad0, gate_t0 = turn(
        1, inner1, last1, got1, gate_grad1, rows1, top, pair1, vgrad1, out_own, out_other,
        gate0, proj0, marks, lows[0], vecs[0], scanned0,
    )

    def half(array, which):
        return lax.dynamic_slice_in_dim(array, which * half_model, half_model, 1)

    def together(left, left_got, right, right_got):
        return dot(
            jnp.concatenate([left, left_got], 1), jnp.concatenate([right, right_got], 0)
        ).astype(BF16)

    normed_got = flip(half(normed1, 1 - core), "section", 1)
    normed_got0 = flip(half(normed0, 1 - core), "section", 1)
    gated_got = flip(jnp.where(low_core, gated_t1, gated_t0), "section", 1)
    gated_own = jnp.where(low_core, gated_t0, gated_t1)
    g_got = flip(jnp.where(low_core, top, g0), "section", 1)
    grad_got = flip(grad_t1, "section", 1)
    gate_got0 = flip(gate_t0, "section", 1)

    def add(kept, got):
        return kept + got.astype(F32)

    def part(total, bit, order):
        axis = len(order) - 1 - sorted(order).index(bit)
        total = total.reshape((2,) * len(order) + (-1, total.shape[-1]))
        mine = (place // bit) % 2
        return pick(total, 1 - mine, axis).astype(BF16), pick(total, mine, axis)

    def halve(total, bit, order):
        goes, stays = part(total, bit, order)
        return add(stays, flip(goes, "seq", bit))

    x_bit, y_bit, z_bit = bits[0], bits[1], bits[-2]
    own_b = [send_b]
    for k, bit in enumerate(bits):
        got_b = flip(send_b, "seq", bit)
        if k == 1:
            a = together(grad_t1, grad_got, half(normed1, core), normed_got)
            b = together(gated_own, gated_got, jnp.where(low_core, g0, top), g_got)
            c = together(gate_t0, gate_got0, half(normed0, core), normed_got0)
            a_goes, a_stays = part(a, x_bit, bits)
            b_goes, b_stays = part(b, y_bit, bits)
            c_goes, c_stays = part(c, z_bit, bits[:-1])
            got_b, a_goes, b_goes, c_goes = tie(got_b, a_goes, b_goes, c_goes)
            a_got, b_got = flip(a_goes, "seq", x_bit), flip(b_goes, "seq", y_bit)
            c_got = flip(c_goes, "seq", z_bit)
        own_b.append(got_b)
        if k < steps - 1:
            (send_b,) = hop(batches, n, k + 1, at0, (), own_b, totals0)
    inner0, tail0, spill0, pair0, vgrad0 = back(
        0, gg0, conv0, in0, gate0, rim0, proj0, before0, totals0, *own_b[1:]
    )
    inner0, tail0, spill0, pair0, vgrad0, a_got, b_got, c_got = tie(
        inner0, tail0, spill0, pair0, vgrad0, a_got, b_got, c_got
    )
    got0 = shifted(spill0, -1)
    a_rest, b_rest = bits[1:], [x_bit] + bits[2:]
    a_goes, a_stays = part(add(a_stays, a_got), y_bit, a_rest)
    b_goes, b_stays = part(add(b_stays, b_got), x_bit, b_rest)
    a_got, b_got = flip(a_goes, "seq", y_bit), flip(b_goes, "seq", x_bit)
    grad_t0, dx, small0 = turn(
        0, inner0, tail0, got0, gate_grad0, rows0, g0, pair0, vgrad0
    )
    grad_t0, dx, small0, a_got, b_got = tie(grad_t0, dx, small0, a_got, b_got)

    grad_got0 = flip(grad_t0, "section", 1)
    small_got = flip(jnp.where(low_core, small1, small0), "section", 1)
    d = together(grad_t0, grad_got0, half(normed0, core), normed_got0)
    d_goes, d_stays = part(d, x_bit, bits[:-1])
    d_got = flip(d_goes, "seq", x_bit)
    small = add(jnp.where(low_core, small0, small1).astype(F32), small_got)
    streams = {
        "a": (add(a_stays, a_got), bits[2:], bits[2:]),
        "b": (add(b_stays, b_got), bits[2:], bits[2:]),
        "c": (add(c_stays, c_got), bits[:-2], swapped(bits[:-2])),
        "d": (None, bits[1:-1], bits[1:-1]),
        "small": (small, bits, swapped(bits)),
    }
    while any(todo for _, _, todo in streams.values()):
        sent = {}
        for name in ("d", "small", "c", "a", "b"):
            total, left, todo = streams[name]
            if name == "d" and total is None:
                sent[name] = (d_got, d_stays, left, todo)
            elif todo:
                goes, stays = part(total, todo[0], left)
                left = [k for k in left if k != todo[0]]
                sent[name] = (flip(goes, "seq", todo[0]), stays, left, todo[1:])
        gots = tie(*(got for got, _, _, _ in sent.values()))
        for got, (name, (_, stays, left, todo)) in zip(gots, sent.items()):
            streams[name] = (add(stays, got), left, todo)
    c, d = streams["c"][0].astype(BF16), streams["d"][0].astype(BF16)
    top_half = place >= count // 2
    got = flip(jnp.where(top_half, d, c), "seq", bits[-1])
    in_sum0 = add(jnp.where(top_half, c, d).astype(F32), got).reshape(-1, half_model)
    in_sum1, out_sum, small = (streams[k][0] for k in ("a", "b", "small"))

    got = flip(jnp.where(low_core, in_sum1, in_sum0).astype(BF16), "section", 1).astype(F32)
    grad_in = jnp.where(
        low_core, jnp.concatenate([in_sum0, got], 1), jnp.concatenate([got, in_sum1], 1)
    )
    got = flip(jnp.where(low_core, out1, dx), "section", 1)
    boundary = jnp.where(
        low_core, jnp.concatenate([dx, got], 0), jnp.concatenate([got, out1], 0)
    ).reshape(1, batch_count, span, model)
    vec_sum = small[:, LANES:]
    gain = vec_sum[: model // count, n + 7][None]
    return (
        boundary,
        gain,
        grad_in.T[None],
        vec_sum[:, n : n + 4].T[None],
        vec_sum[:, n + 4][None],
        small[:, :x_width][None],
        small[:, x_width:LANES].T[None],
        vec_sum[:, n + 5][None],
        vec_sum[:, :n][None],
        vec_sum[:, n + 6][None],
        out_sum[None],
    )


def solution(mesh):
    in_specs = (
        P(None, "seq", None), P(None, "seq"), P("section", None), P("section", None, None),
        P("section", None, None), P("section", None), P("section", None, None),
        P("section", None, None), P("section", None), P("section", None, None),
        P("section", None), P("section", None, None), P(None, "seq", None),
    )
    out_specs = (
        P("section", None, "seq", None), P("section", "seq"), P("section", None, "seq"),
        P("section", None, "seq"), P("section", "seq"), P("section", "seq", None),
        P("section", None, "seq"), P("section", "seq"), P("section", "seq", None),
        P("section", "seq"), P("section", "seq", None),
    )
    return jax.shard_map(local, mesh=mesh, in_specs=in_specs, out_specs=out_specs, check_vma=False)
```

```python
import functools
import jax
import jax.numpy as jnp
from jax import lax
from jax.experimental import pallas as pl
from jax.experimental.pallas import tpu as pltpu
from jax.sharding import PartitionSpec as P

EPS = 1e-05
LOG2E = 1.4426950408889634
STOP = 1e7
LANES = 128
BLOCK = 512
TILES = BLOCK // LANES
F32 = jnp.float32
BF16 = jnp.bfloat16
VMEM_LIMIT = 58 * 1024 * 1024
HOP_LIMIT = 6 * 1024 * 1024
NEAR_LIMIT = 24 * 1024 * 1024
TURN_LIMIT = 58 * 1024 * 1024


def dot(left, right):
    return jnp.dot(left, right, preferred_element_type=F32)


def across(left, right):
    return lax.dot_general(left, right, (((0,), (0,)), ((), ())), preferred_element_type=F32)


def against(left, right):
    return lax.dot_general(left, right, (((1,), (1,)), ((), ())), preferred_element_type=F32)


def norm_rows(source, gain_row):
    return source * lax.rsqrt(jnp.mean(source * source, axis=-1, keepdims=True) + EPS) * gain_row


def softplus(v):
    return jnp.maximum(v, 0.0) + jnp.log1p(jnp.exp(-jnp.abs(v)))


def silu_slope(v):
    gate = jax.nn.sigmoid(v)
    return gate * (1.0 + v * (1.0 - gate))


def pair_up(left, right, row_ids, width):
    mask = (row_ids % (2 * width)) < width
    kept = jnp.where(mask, left, right)
    moved = jnp.where(mask, right, left)
    return kept + pltpu.roll(moved, 8 - width, 0)


def fold_rows(parts, row_ids):
    width = 1
    while len(parts) > 1:
        parts = [
            pair_up(parts[i], parts[i + 1], row_ids, width) for i in range(0, len(parts), 2)
        ]
        width *= 2
    return parts[0]


def halves(v):
    return v[:8] + v[8:]


def spread_columns(table, first, target):
    width = target.shape[1]
    for t in range(target.shape[0]):
        column = table[first : first + width, t : t + 1]
        target[t] = jnp.broadcast_to(column, (width, LANES))


def block_at(i):
    return pl.ds(pl.multiple_of(i * BLOCK, BLOCK), BLOCK)


def tile_at(i, lt):
    return pl.ds(pl.multiple_of(i * BLOCK + lt * LANES, LANES), LANES)


def local_scan(batches, span, blocks, seff, x, bx, at, final):
    def over_block(i, carry):
        rate = [at[:, tile_at(i, lt)] for lt in range(TILES)]

        def chunk(tc, states):
            states = list(states)
            for b in range(batches):
                rows = pl.ds(pl.multiple_of(b * span + tc * 8, 8), 8)
                for lt in range(TILES):
                    s8 = seff[rows, tile_at(i, lt)]
                    x8 = x[rows, tile_at(i, lt)]
                    h = states[b * TILES + lt]
                    for j in range(8):
                        decay = jnp.exp2(s8[j : j + 1] * rate[lt])
                        h = decay * h + x8[j : j + 1] * bx[b * span + tc * 8 + j]
                    states[b * TILES + lt] = h
            return tuple(states)

        zero = jnp.zeros((at.shape[0], LANES), F32)
        states = lax.fori_loop(0, span // 8, chunk, (zero,) * (batches * TILES))
        for b in range(batches):
            for lt in range(TILES):
                final[b, :, tile_at(i, lt)] = states[b * TILES + lt]
        return carry

    lax.fori_loop(0, blocks, over_block, 0)


def back_scan(batches, span, blocks, seff, sg, cx, at, first):
    chunks = span // 8

    def over_block(i, carry):
        rate = [at[:, tile_at(i, lt)] for lt in range(TILES)]

        def chunk(k, states):
            states = list(states)
            tc = chunks - 1 - k
            for b in range(batches):
                rows = pl.ds(pl.multiple_of(b * span + tc * 8, 8), 8)
                for lt in range(TILES):
                    s8 = seff[rows, tile_at(i, lt)]
                    g8 = sg[rows, tile_at(i, lt)]
                    q = states[b * TILES + lt]
                    for j in range(7, -1, -1):
                        decay = jnp.exp2(s8[j : j + 1] * rate[lt])
                        q = decay * (q + g8[j : j + 1] * cx[b * span + tc * 8 + j])
                    states[b * TILES + lt] = q
            return tuple(states)

        zero = jnp.zeros((at.shape[0], LANES), F32)
        states = lax.fori_loop(0, chunks, chunk, (zero,) * (batches * TILES))
        for b in range(batches):
            for lt in range(TILES):
                first[b, :, tile_at(i, lt)] = states[b * TILES + lt]
        return carry

    lax.fori_loop(0, blocks, over_block, 0)


class Arriving:
    def __init__(self, source, held, sem, other=None):
        self.held, self.waited = held, False
        if other is None:
            self.copy = pltpu.make_async_copy(source, held, sem)
            self.copy.start()
        else:
            self.copy = fetch(0, source, other, held, sem)

    def __getitem__(self, where):
        assert self.waited
        return self.held[where]

    def __setitem__(self, where, value):
        assert self.waited
        self.held[where] = value

    @property
    def at(self):
        return self.held.at


class Leaving:
    def __init__(self, target, held, sem):
        self.copy, self.held, self.started = pltpu.make_async_copy(held, target, sem), held, False

    def __getitem__(self, where):
        return self.held[where]

    def __setitem__(self, where, value):
        self.held[where] = value


def uppers_of(steps):
    place = lax.axis_index("seq")
    return [(place // (1 << k)) % 2 != 0 for k in range(steps)]


def ready(*refs):
    for ref in refs:
        if isinstance(ref, Arriving) and not ref.waited:
            ref.copy.wait()
            ref.waited = True


def leave(*refs):
    for ref in refs:
        if isinstance(ref, Leaving) and not ref.started:
            ref.copy.start()
            ref.started = True


def fetch(layer, own, other, held, sem):
    mine = lax.axis_index("section") == layer

    @pl.when(mine)
    def _():
        pltpu.make_async_copy(own, held, sem).start()

    @pl.when(jnp.logical_not(mine))
    def _():
        pltpu.make_async_copy(other, held, sem).start()

    return pltpu.make_async_copy(own, held, sem)


def split_total(totals):
    width = totals[0].shape[1]
    row_ids = lax.broadcasted_iota(jnp.int32, (16, width), 0)
    block = jnp.zeros((16, width), F32)
    for b, total in enumerate(totals):
        rest = total
        for k in range(3):
            part = rest.astype(BF16).astype(F32)
            block = jnp.where(row_ids == 3 * b + k, part, block)
            rest = rest - part
    return block.astype(BF16)


def join_total(block, b):
    block = block.astype(F32)
    return block[3 * b : 3 * b + 1] + block[3 * b + 1 : 3 * b + 2] + block[3 * b + 2 : 3 * b + 3]


def enter_kernel(
    batches, span, width,
    rows, gain, in_w,
    in_a_o, in_b_o, gate_a_o, gate_b_o, tail_a_o, tail_b_o,
    normed, held, sems,
):
    chunk = held.shape[2]
    copies = [
        pltpu.make_async_copy(in_w.at[:, pl.ds(c * chunk, chunk)], held.at[c], sems.at[c])
        for c in range(held.shape[0])
    ]
    for copy in copies:
        copy.start()
    ready(rows, gain)
    normed[...] = norm_rows(rows[...].astype(F32), gain[...]).astype(BF16)
    half = batches * span
    for c, copy in enumerate(copies):
        copy.wait()
        mixed = dot(normed[...], held[c])
        outs = (in_a_o, in_b_o) if c * chunk < width else (gate_a_o, gate_b_o)
        lanes = slice(c * chunk % width, c * chunk % width + chunk)
        for k, out in enumerate(outs):
            out[:, lanes] = mixed[k * half : (k + 1) * half].astype(BF16)
        if c * chunk < width:
            for k, tail in enumerate((tail_a_o, tail_b_o)):
                for b in range(batches):
                    last = k * half + (b + 1) * span
                    tail[b, :, lanes] = mixed[last - 3 : last].astype(BF16).astype(F32)
        if (c + 1) * chunk == width:
            leave(in_a_o, in_b_o, tail_a_o, tail_b_o)


def tap_rows(ext, rim, mixed, width, span):
    ext[5:8] = rim
    ext[8 : 8 + span] = mixed.astype(F32)


def conv_sum(ext, m, vec, n, span):
    v = vec[n + 4 : n + 5] + vec[n + 3 : n + 4] * ext[8 : 8 + span]
    for k in (1, 2, 3):
        v = v + vec[n + 3 - k : n + 4 - k] * (m[:, k : k + 1] * ext[8 - k : 8 - k + span])
    return v


def step_sum(proj, low_w, vec, rank, n):
    return dot(proj[:, :rank], low_w[rank + 2 * n :]) + vec[n + 5 : n + 6]


def front_kernel(
    batches, span, width, rank, states_n, with_back,
    *refs,
):
    refs = list(refs)
    mixed, rim, marks, vec, low_w = refs[:5]
    del refs[:5]
    if with_back:
        gate, g, own_w, other_w = refs[:4]
        del refs[:4]
    conv_o, proj_o, send_o = refs[:3]
    del refs[:3]
    if with_back:
        (send_back_o,) = refs[:1]
        del refs[:1]
    ext, seff, x, bx, cx, final = refs[:6]
    if with_back:
        sg, out_w, sem = refs[6:]
        arrival = fetch(1, own_w, other_w, out_w, sem)
    n = states_n
    ready(rim, marks, vec)
    m = marks[...]
    at = vec.at[0:n]
    ready(mixed)
    for b in range(batches):
        lo, hi = b * span, (b + 1) * span
        tap_rows(ext, rim[b], mixed[lo:hi], width, span)
        x[lo:hi] = jax.nn.silu(conv_sum(ext, m[lo:hi], vec, n, span))
    conv = x[...].astype(BF16)
    conv_o[...] = conv
    leave(conv_o)
    ready(low_w)
    proj = against(conv, low_w[...]).astype(BF16)
    proj_o[...] = proj
    leave(proj_o)
    step = softplus(step_sum(proj, low_w, vec, rank, n))
    seff[...] = step + m[:, 0:1] * STOP
    x[...] = step * conv.astype(F32)
    totals = [
        jnp.sum(seff[b * span : (b + 1) * span], axis=0, keepdims=True) for b in range(batches)
    ]
    send_o[batches * n :] = split_total(totals)
    table = proj.astype(F32).T
    spread_columns(table, rank, bx)
    local_scan(batches, span, width // BLOCK, seff, x, bx, at, final)
    for b in range(batches):
        send_o[b * n : (b + 1) * n] = final[b].astype(BF16)
    leave(send_o)
    if with_back:
        arrival.wait()
        spread_columns(table, rank + n, cx)
        ready(g, gate)
        gg = against(g[...], out_w[...])
        sg[...] = gg * jax.nn.silu(gate[...].astype(F32))
        back_scan(batches, span, width // BLOCK, seff, sg, cx, at, final)
        for b in range(batches):
            send_back_o[b * n : (b + 1) * n] = final[b].astype(BF16)


def merge(at, upper, mine, theirs, mine_total, their_total, backward):
    early, late = jnp.where(upper, theirs, mine), jnp.where(upper, mine, theirs)
    if backward:
        return jnp.exp2(jnp.where(upper, their_total, mine_total) * at) * late + early
    return jnp.exp2(jnp.where(upper, mine_total, their_total) * at) * early + late


def reach(at, n, b, uppers, gots, totals, backward):
    carry = jnp.zeros(at.shape, F32)
    span = jnp.zeros((1, at.shape[1]), F32)
    for upper, got, their_total in zip(uppers, gots, totals):
        comes = jnp.logical_not(upper) if backward else upper
        theirs = got[b * n : (b + 1) * n].astype(F32)
        carry = jnp.where(comes, jnp.exp2(span * at) * theirs + carry, carry)
        span = jnp.where(comes, span + their_total, span)
    return carry


def hop_kernel(batches, n, steps, forward, backward, *refs):
    refs = list(refs)
    take = lambda k: [refs.pop(0) for _ in range(k)]
    (at,) = take(1)
    at = at[...]
    if forward:
        own, *gots = take(1 + steps)
    else:
        (totals,) = take(1)
    if backward:
        own_b, *gots_b = take(1 + steps)
    if forward:
        (send,) = take(1)
    if backward:
        (send_b,) = take(1)
    uppers = uppers_of(steps)
    reached = []
    for b in range(batches):
        rows = slice(b * n, (b + 1) * n)
        if forward:
            total = join_total(own[batches * n :], b)
            mine = own[rows].astype(F32)
        else:
            total = totals[b : b + 1]
        if backward:
            mine_b = own_b[rows].astype(F32)
        for k, upper in enumerate(uppers):
            if forward:
                their_total = join_total(gots[k][batches * n :], b)
                mine = merge(
                    at, upper, mine, gots[k][rows].astype(F32), total, their_total, False
                )
            else:
                their_total = totals[(k + 1) * batches + b : (k + 1) * batches + b + 1]
            if backward:
                mine_b = merge(
                    at, upper, mine_b, gots_b[k][rows].astype(F32), total, their_total, True
                )
            total = total + their_total
        if forward:
            send[rows] = mine.astype(BF16)
        if backward:
            send_b[rows] = mine_b.astype(BF16)
        reached.append(total)
    if forward:
        send[batches * n :] = split_total(reached)


def prepare(step, marks, conv, seff, x):
    seff[...] = step + marks * STOP
    x[...] = step * conv.astype(F32)


def end_kernel(
    batches, span, width, rank, n, steps,
    gate, conv, proj, marks, vec, low_w, rows, gain, gain_before,
    own_out, other_out, own_in, other_in, own_send, *refs,
):
    gots, refs = refs[:steps], refs[steps:]
    (
        scanned_o, gated_t_o, rows_o, normed_before_o, normed_o, inner_o, gate_o, before_o,
        totals_o, tail_o, seff, x, bx, cx, out_w, in_w, sems,
    ) = refs

    arrivals = [
        fetch(0, own_out, other_out, out_w, sems.at[0]),
        fetch(1, own_in, other_in, in_w, sems.at[1]),
    ]
    blocks = width // BLOCK
    at = vec.at[0:n]
    ready(rows, gain_before, proj, low_w, vec, marks, conv)
    normed_before_o[...] = norm_rows(rows[...].astype(F32), gain_before[...]).astype(BF16)
    leave(normed_before_o)
    tail_o[...] = jnp.zeros((batches, 6, width), F32)
    for b in range(batches):
        last = normed_before_o[(b + 1) * span - 16 : (b + 1) * span].astype(F32)
        tail_o[b, 3:6, : last.shape[1]] = last[13:]
    step = softplus(step_sum(proj[...], low_w, vec, rank, n))
    prepare(step, marks[:, 0:1], conv[...], seff, x)
    table = proj[...].astype(F32).T
    spread_columns(table, rank, bx)
    spread_columns(table, rank + n, cx)
    ready(own_send, *gots)
    uppers = uppers_of(steps)
    for b in range(batches):
        totals_o[b : b + 1] = join_total(own_send[batches * n :], b)
        theirs = [join_total(got[batches * n :], b) for got in gots]
        for k, their in enumerate(theirs):
            totals_o[(k + 1) * batches + b : (k + 1) * batches + b + 1] = their
        before_o[b] = reach(at[...], n, b, uppers, gots, theirs, False)
    leave(before_o, totals_o)
    row_ids = lax.broadcasted_iota(jnp.int32, (8, LANES), 0)

    def over_block(i, carry):
        rate = [at[:, tile_at(i, lt)] for lt in range(TILES)]

        def chunk(tc, states):
            states = list(states)
            for b in range(batches):
                rows8 = pl.ds(pl.multiple_of(b * span + tc * 8, 8), 8)
                for lt in range(TILES):
                    s8 = seff[rows8, tile_at(i, lt)]
                    x8 = x[rows8, tile_at(i, lt)]
                    h = states[b * TILES + lt]
                    parts = []
                    for j in range(8):
                        t = b * span + tc * 8 + j
                        decay = jnp.exp2(s8[j : j + 1] * rate[lt])
                        h = decay * h + x8[j : j + 1] * bx[t]
                        parts.append(halves(h * cx[t]))
                    states[b * TILES + lt] = h
                    scanned_o[rows8, tile_at(i, lt)] = fold_rows(parts, row_ids)
            return tuple(states)

        start = tuple(
            before_o[b, :, tile_at(i, lt)] for b in range(batches) for lt in range(TILES)
        )
        lax.fori_loop(0, span // 8, chunk, start)
        return carry

    lax.fori_loop(0, blocks, over_block, 0)
    scanned = scanned_o[...] + vec[n + 6 : n + 7] * conv[...].astype(F32)
    scanned_o[...] = scanned
    leave(scanned_o)
    ready(gate)
    gated_f = scanned * jax.nn.silu(gate[...].astype(F32))
    gated = gated_f.astype(BF16)
    gated_t_o[...] = gated_f.T.astype(BF16)
    leave(gated_t_o)
    arrivals[0].wait()
    result = (rows[...].astype(F32) + dot(gated, out_w[...])).astype(BF16)
    rows_o[...] = result
    leave(rows_o)
    ready(gain)
    normed_o[...] = norm_rows(result.astype(F32), gain[...]).astype(BF16)
    leave(normed_o)
    arrivals[1].wait()
    for first, target in ((0, inner_o), (width, gate_o)):
        for c in range(0, width, 512):
            mixed = dot(normed_o[...], in_w[:, first + c : first + c + 512])
            target[:, c : c + 512] = mixed.astype(BF16)
            if not first:
                for b in range(batches):
                    last = (b + 1) * span
                    tail_o[b, 0:3, c : c + 512] = mixed[last - 3 : last].astype(BF16).astype(F32)
        leave(target, tail_o)


def back_kernel(
    batches, span, width, rank, n, x_width, steps, with_out,
    *refs,
):
    refs = list(refs)
    take = lambda k: [refs.pop(0) for _ in range(k)]
    gg, conv, inner, gate, rim, marks, vec, low_w, proj = take(9)
    if with_out:
        rows, own_out, other_out = take(3)
        gots = take(steps)
    else:
        before, totals = take(2)
    gots_b = take(steps)
    inner_o, tail_o, spill_o, pair_o, vec_o = take(5)
    if with_out:
        gate_o, gated_t_o, out_o = take(3)
    else:
        (turned_o,) = take(1)
    seff, x, hist, decays, drive, zsum, acc_b, acc_c, ext, sg, bx, cx, pre_grad = take(13)
    state_in, grad_in = take(2)
    if with_out:
        scanned_ref, gg_s, out_w, sem = take(4)
        arrival = fetch(1, own_out, other_out, out_w, sem)
    blocks = width // BLOCK
    rows_n = batches * span
    chunks = span // 8
    ready(proj, low_w, vec, marks, conv)
    m = marks[...]
    at = vec.at[0:n]
    spre = step_sum(proj[...], low_w, vec, rank, n)
    prepare(softplus(spre), m[:, 0:1], conv[...], seff, x)
    table = proj[...].astype(F32).T
    spread_columns(table, rank, bx)
    spread_columns(table, rank + n, cx)
    ready(gg, gate)
    if with_out:
        arrival.wait()
        gg_s[...] = against(gg[...], out_w[...])
        gg = gg_s
    sg[...] = gg[...] * jax.nn.silu(gate[...].astype(F32))
    if with_out:
        ready(*gots)
    else:
        ready(before, totals)
    ready(*gots_b)
    uppers = uppers_of(steps)
    for b in range(batches):
        if with_out:
            theirs = [join_total(got[batches * n :], b) for got in gots]
            state_in[b] = reach(at[...], n, b, uppers, gots, theirs, False)
        else:
            theirs = [
                totals[(k + 1) * batches + b : (k + 1) * batches + b + 1] for k in range(steps)
            ]
            state_in[b] = before[b]
        grad_in[b] = reach(at[...], n, b, uppers, gots_b, theirs, True)
    acc_b[...] = jnp.zeros_like(acc_b)
    acc_c[...] = jnp.zeros_like(acc_c)
    vec_o[...] = jnp.zeros((n + 8, width), F32)
    row_ids = lax.broadcasted_iota(jnp.int32, (8, LANES), 0)

    def over_block(i, carry):
        rate = [at[:, tile_at(i, lt)] for lt in range(TILES)]

        def again(tc, states):
            states = list(states)
            for b in range(batches):
                rows8 = pl.ds(pl.multiple_of(b * span + tc * 8, 8), 8)
                for lt in range(TILES):
                    s8 = seff[rows8, tile_at(i, lt)]
                    x8 = x[rows8, tile_at(i, lt)]
                    h = states[b * TILES + lt]
                    lanes = pl.ds(lt * LANES, LANES)
                    parts = []
                    for j in range(8):
                        t = tc * 8 + j
                        decay = jnp.exp2(s8[j : j + 1] * rate[lt])
                        h = decay * h + x8[j : j + 1] * bx[b * span + t]
                        decays[b, t, :, lanes] = decay
                        hist[b, t + 1, :, lanes] = h
                        if with_out:
                            parts.append(halves(h * cx[b * span + t]))
                    states[b * TILES + lt] = h
                    if with_out:
                        scanned_ref[rows8, tile_at(i, lt)] = fold_rows(parts, row_ids)
            return tuple(states)

        for b in range(batches):
            hist[b, 0] = state_in[b, :, block_at(i)]
        start = tuple(
            state_in[b, :, tile_at(i, lt)] for b in range(batches) for lt in range(TILES)
        )
        lax.fori_loop(0, chunks, again, start)

        sums = tuple(jnp.zeros((n, LANES), F32) for _ in range(TILES))
        for b in range(batches):

            def chunk(k, held):
                held = list(held)
                tc = chunks - 1 - k
                rows8 = pl.ds(pl.multiple_of(b * span + tc * 8, 8), 8)
                s8, x8, g8 = [], [], []
                for lt in range(TILES):
                    s8.append(seff[rows8, tile_at(i, lt)])
                    x8.append(x[rows8, tile_at(i, lt)])
                    g8.append(sg[rows8, tile_at(i, lt)])
                drives = [[None] * 8 for _ in range(TILES)]
                zs = [[None] * 8 for _ in range(TILES)]
                for j in range(7, -1, -1):
                    t = tc * 8 + j
                    part_b, part_c = [], []
                    for lt in range(TILES):
                        lanes = pl.ds(lt * LANES, LANES)
                        total = held[lt] + g8[lt][j : j + 1] * cx[b * span + t]
                        q = decays[b, t, :, lanes] * total
                        log_grad = q * hist[b, t, :, lanes]
                        held[TILES + lt] = held[TILES + lt] + log_grad * s8[lt][j : j + 1]
                        zs[lt][j] = halves(log_grad * rate[lt])
                        drives[lt][j] = halves(total * bx[b * span + t])
                        part_b.append(total * x8[lt][j : j + 1])
                        part_c.append(g8[lt][j : j + 1] * hist[b, t + 1, :, lanes])
                        held[lt] = q
                    acc_b[b * span + t] += sum(part_b[1:], part_b[0])
                    acc_c[b * span + t] += sum(part_c[1:], part_c[0])
                for lt in range(TILES):
                    drive[rows8, tile_at(i, lt)] = fold_rows(drives[lt], row_ids)
                    zsum[rows8, tile_at(i, lt)] = fold_rows(zs[lt], row_ids)
                return tuple(held)

            start = tuple(grad_in[b, :, tile_at(i, lt)] for lt in range(TILES)) + sums
            sums = lax.fori_loop(0, chunks, chunk, start)[TILES:]
        for lt in range(TILES):
            vec_o[0:n, tile_at(i, lt)] = -sums[lt]
        return carry

    lax.fori_loop(0, blocks, over_block, 0)

    conv_f = conv[...].astype(F32)
    if with_out:
        ready(rows)
        gate = gate[...].astype(F32)
        scanned = scanned_ref[...] + vec[n + 6 : n + 7] * conv_f
        gated_f = scanned * jax.nn.silu(gate)
        gated_t_o[...] = gated_f.T.astype(BF16)
        out_o[...] = (rows[...].astype(F32) + dot(gated_f.astype(BF16), out_w[...])).astype(BF16)
        gate_o[...] = (gg_s[...] * scanned * silu_slope(gate)).astype(BF16)
        leave(gate_o, gated_t_o, out_o)

    column_ids = lax.broadcasted_iota(jnp.int32, (n, rows_n), 1)

    def gather_column(t, pair):
        now = []
        for held, acc in zip(pair, (acc_b, acc_c)):
            column = jnp.sum(acc[t], axis=1, keepdims=True)
            now.append(jnp.where(column_ids == t, column, held))
        return tuple(now)

    zero = jnp.zeros((n, rows_n), F32)
    b_grad, c_grad = lax.fori_loop(0, rows_n, gather_column, (zero, zero), unroll=8)
    rest = LANES - rank - 2 * n
    placed = jnp.concatenate(
        [jnp.zeros((rank, rows_n), F32), b_grad, c_grad, jnp.zeros((rest, rows_n), F32)], 0
    ).T
    spre = step_sum(proj[...], low_w, vec, rank, n)
    step = softplus(spre)
    step_grad = zsum[...] * (1.0 / LOG2E) + drive[...] * conv_f
    pre_g = step_grad * jax.nn.sigmoid(spre)
    low = pre_g.astype(BF16)
    low_grad = against(low, low_w[rank + 2 * n :])
    pgrad = (
        jnp.concatenate([low_grad, jnp.zeros((rows_n, LANES - rank), F32)], 1) + placed
    ).astype(BF16)
    small = dot(conv_f.T.astype(BF16), pgrad)
    lows = pltpu.roll(dot(pre_g.T.astype(BF16), proj[...]), x_width, 1)
    columns = lax.broadcasted_iota(jnp.int32, (1, LANES), 1)
    pair_o[...] = jnp.where(columns < x_width, small, lows).astype(BF16)
    leave(pair_o)
    conv_grad = (
        sg[...] * vec[n + 6 : n + 7] + step * drive[...]
        + dot(pgrad[:, : rank + 2 * n], low_w[: rank + 2 * n])
    )
    pre_grad[...] = conv_grad
    vec_o[n + 5 : n + 6] = jnp.sum(pre_g, axis=0, keepdims=True)
    vec_o[n + 6 : n + 7] = jnp.sum(sg[...] * conv_f, axis=0, keepdims=True)
    ready(inner, rim)
    taps = [jnp.zeros((1, width), F32) for _ in range(4)]
    bias = jnp.zeros((1, width), F32)
    spilled = []
    for b in range(batches):
        lo, hi = b * span, (b + 1) * span
        tap_rows(ext, rim[b], inner[lo:hi], width, span)
        grad_b = pre_grad[lo:hi] * silu_slope(conv_sum(ext, m[lo:hi], vec, n, span))
        bias = bias + jnp.sum(grad_b, axis=0, keepdims=True)
        taps[3] = taps[3] + jnp.sum(grad_b * ext[8 : 8 + span], axis=0, keepdims=True)
        for k in (1, 2, 3):
            taps[3 - k] = taps[3 - k] + jnp.sum(
                grad_b * (m[lo:hi, k : k + 1] * ext[8 - k : 8 - k + span]),
                axis=0, keepdims=True,
            )
        back = vec[n + 3 : n + 4] * grad_b
        spill = jnp.zeros((8, width), F32)
        for k in (1, 2, 3):
            ext[0:8] = jnp.zeros((8, width), F32)
            ext[8 : 8 + span] = vec[n + 3 - k : n + 4 - k] * (m[lo:hi, k : k + 1] * grad_b)
            ext[8 + span : 16 + span] = jnp.zeros((8, width), F32)
            back = back + ext[8 + k : 8 + k + span]
            spill = spill + ext[k : 8 + k]
        inner_o[lo:hi] = back.astype(BF16)
        tail_o[b] = back[span - 16 :]
        spill_o[b] = spill[5:8]
        if not with_out:
            pre_grad[lo:hi] = back
            spilled.append(
                jnp.where(lax.broadcasted_iota(jnp.int32, (8, width), 0) < 5, 0.0, spill)
            )
    leave(spill_o, inner_o, tail_o)
    if not with_out:
        turned_o[:, :rows_n] = pre_grad[...].T.astype(BF16)
        for b in range(batches):
            pre_grad[8 * b : 8 * b + 8] = spilled[b]
        pre_grad[8 * batches : rows_n] = jnp.zeros((rows_n - 8 * batches, width), F32)
        turned_o[:, rows_n:] = pre_grad[...].T.astype(BF16)
        leave(turned_o)
    for k in range(4):
        vec_o[n + k : n + k + 1] = taps[k]
    vec_o[n + 4 : n + 5] = bias


def norm_back(source, gain, grad):
    scale = lax.rsqrt(jnp.mean(source * source, axis=-1, keepdims=True) + EPS)
    unit = source * scale
    scaled = grad * gain
    along = jnp.mean(scaled * unit, axis=-1, keepdims=True)
    return scale * (scaled - unit * along), grad * unit


def turn_kernel(
    batches, span, width, rank, n, targets, layer,
    *refs,
):
    refs = list(refs)
    take = lambda k: [refs.pop(0) for _ in range(k)]
    inner, tail, spill, gate_grad, rows, gain, g, pair, vgrad, own_in, other_in = take(11)
    if layer:
        own_out, other_out, gate, proj, marks, low_w, vec, scanned = take(8)
    g_o, small_o = take(2)
    if layer:
        grad_o, gg_o, send_o, gate_o, gate_t_o = take(5)
    in_w, sem_in, mixed_grad, column = take(4)
    rows_n = batches * span
    if layer:
        seff, sg, cx, first, out_w, sem_out = take(6)
    arrival = fetch(layer, own_in, other_in, in_w, sem_in)
    if layer:
        arrival_out = fetch(0, own_out, other_out, out_w, sem_out)
    ready(tail, inner, spill)
    mixed_grad[:, :width] = inner[...]
    for b in range(batches):
        tail[b, 13:16] = tail[b, 13:16] + spill[b]
        hi = (b + 1) * span
        mixed_grad[hi - 16 : hi, :width] = tail[b].astype(BF16)
    ready(gate_grad)
    mixed_grad[:, width:] = gate_grad[...]
    if layer:
        grad_o[...] = mixed_grad[...].astype(F32).T.astype(BF16)
        leave(grad_o)
    ready(pair, vgrad)
    small_o[:, :LANES] = pair[...]
    arrival.wait()
    normed_grad = against(mixed_grad[...], in_w[...])
    ready(rows, g, gain)
    input_grad, terms = norm_back(rows[...].astype(F32), gain[...], normed_grad)
    g_new = (g[...].astype(F32) + input_grad).astype(BF16)
    g_o[...] = g_new
    leave(g_o)
    column[...] = jnp.concatenate(
        [vgrad[...], jnp.zeros((LANES - vgrad.held.shape[0], width), F32)], 0
    ).T
    sums = jnp.sum(terms.T, axis=1, keepdims=True)
    spot = lax.broadcasted_iota(jnp.int32, (1, LANES), 1) == n + 7
    part, block = sums.shape[0] // targets, width // targets
    for j in range(targets):
        rows_j = slice(j * block, j * block + part)
        column[rows_j] = jnp.where(spot, sums[j * part : (j + 1) * part], column[rows_j])
    small_o[:, LANES:] = column[...].astype(BF16)
    leave(small_o)
    if layer:
        arrival_out.wait()
        gg = against(g_new, out_w[...])
        gg_o[...] = gg
        leave(gg_o)
        ready(gate, proj, low_w, vec, marks)
        gate = gate[...].astype(F32)
        sg[...] = gg * jax.nn.silu(gate)
        step = softplus(step_sum(proj[...], low_w, vec, rank, n))
        seff[...] = step + marks[:, 0:1] * STOP
        spread_columns(proj[...].astype(F32).T, rank + n, cx)
        ready(scanned)
        gate_new = gg * scanned[...] * silu_slope(gate)
        gate_o[...] = gate_new.astype(BF16)
        gate_t_o[...] = gate_new.T.astype(BF16)
        leave(gate_o, gate_t_o)
        back_scan(batches, span, width // BLOCK, seff, sg, cx, vec.at[0:n], first)
        for b in range(batches):
            send_o[b * n : (b + 1) * n] = first[b].astype(BF16)


def by_core(groups, emit):
    if len(groups) == 1:
        emit(groups[0])
    else:
        for core, group in enumerate(groups):
            pl.when(lax.axis_index("section") == core)(functools.partial(emit, group))


def meet_kernel(groups, bit, lanes, *refs):
    goes, stays = refs[-2:]
    low, pairs = min(bit, goes.shape[0]), goes.shape[0]
    place = lax.axis_index("seq") // bit % 2

    def emit(group):
        left, left_got, right, right_got = group
        depth = left.shape[-1]
        first = 0 if lanes == right.shape[1] else lax.axis_index("section") * lanes
        columns = pl.ds(pl.multiple_of(first, LANES), lanes) if lanes != right.shape[1] else ...
        own = right[:depth, columns] if columns is not ... else right[:depth]
        got = right_got[:depth, columns] if columns is not ... else right_got[:depth]
        for which, out in ((1 - place, goes), (place, stays)):
            for k in range(pairs):
                source = (k // low * 2 + which) * low + k % low
                out[k] = (dot(left[source], own) + dot(left_got[source], got)).astype(BF16)

    by_core([refs[4 * i : 4 * i + 4] for i in range(groups)], emit)


def advance_kernel(plan, *refs):
    refs = list(refs)
    take = lambda k: [refs.pop(0) for _ in range(k)]
    ins = [[take(2) for _ in range(groups)] for groups, _ in plan]
    for groups, (_, bits) in zip(ins, plan):
        outs = take(2 if bits else 1)

        def emit(group, outs=outs, bits=bits):
            stayed, came = group
            if not bits:
                outs[0][...] = stayed[0].astype(F32) + came[0].astype(F32)
                return
            low = 1 << sorted(bits).index(bits[0])
            place = lax.axis_index("seq") // bits[0] % 2
            for which, out in ((1 - place, outs[0]), (place, outs[1])):
                for k in range(out.shape[0]):
                    source = (k // low * 2 + which) * low + k % low
                    out[k] = (stayed[source].astype(F32) + came[source].astype(F32)).astype(BF16)

        by_core(groups, emit)


DMA = pltpu.SemaphoreType.DMA


def expected(us):
    return pl.CostEstimate(
        flops=int(us * 3e8), bytes_accessed=int(us * 1e6), transcendentals=0
    )


def run(kernel, us, outs, scratch, args, far, far_out, elsewhere=(), others=(), limit=None):
    others = dict(others)
    whole_args = list(args) + list(others.values())
    far = tuple(far) + tuple(i for i in range(len(args)) if i not in far and i not in elsewhere)
    passing = [(args[i].shape, args[i].dtype) for i in far] + [outs[i] for i in far_out]
    count = len(passing)

    def whole(*refs):
        refs = list(refs)
        ins, refs = refs[: len(args)], refs[len(args) :]
        second, refs = dict(zip(others, refs)), refs[len(others) :]
        results, rest = refs[: len(outs)], refs[len(outs) :]
        own, buffers, sems = rest[: len(scratch)], rest[len(scratch) : -1], rest[-1]
        for k, i in enumerate(far):
            ins[i] = Arriving(ins[i], buffers[k], sems.at[k], second.get(i))
        for k, i in enumerate(far_out, len(far)):
            results[i] = Leaving(results[i], buffers[k], sems.at[k])
        kernel(*ins, *results, *own)
        ready(*ins)
        leave(*results)
        for ref in results:
            if isinstance(ref, Leaving):
                ref.copy.wait()

    return pl.pallas_call(
        whole,
        out_shape=[jax.ShapeDtypeStruct(*o) for o in outs],
        in_specs=[pl.BlockSpec(memory_space=pl.ANY)] * len(whole_args),
        out_specs=[
            pl.BlockSpec(memory_space=pl.ANY if i in far_out else pltpu.VMEM)
            for i in range(len(outs))
        ],
        scratch_shapes=[s if not isinstance(s, tuple) else pltpu.VMEM(*s) for s in scratch]
        + [pltpu.VMEM(*p) for p in passing]
        + [DMA((count,))],
        compiler_params=pltpu.CompilerParams(vmem_limit_bytes=limit or VMEM_LIMIT),
        cost_estimate=expected(us),
    )(*whole_args)


def hop(batches, n, steps, at, own=(), own_b=(), totals=None):
    args = [at] + list(own) + ([] if own else [totals]) + list(own_b)
    outs = [jax.ShapeDtypeStruct(m[0].shape, BF16) for m in (own, own_b) if m]
    return pl.pallas_call(
        functools.partial(hop_kernel, batches, n, steps, bool(own), bool(own_b)),
        out_shape=outs,
        in_specs=[pl.BlockSpec(memory_space=pltpu.VMEM)] * len(args),
        out_specs=[pl.BlockSpec(memory_space=pltpu.VMEM)] * len(outs),
        compiler_params=pltpu.CompilerParams(vmem_limit_bytes=HOP_LIMIT),
        cost_estimate=expected(1),
    )(*args)


def near(kernel, us, outs, args):
    return pl.pallas_call(
        kernel,
        out_shape=[jax.ShapeDtypeStruct(*o) for o in outs],
        in_specs=[pl.BlockSpec(memory_space=pltpu.VMEM)] * len(args),
        out_specs=[pl.BlockSpec(memory_space=pltpu.VMEM)] * len(outs),
        compiler_params=pltpu.CompilerParams(vmem_limit_bytes=NEAR_LIMIT),
        cost_estimate=expected(us),
    )(*args)


def meet(groups, bit, targets, lanes):
    args = []
    for left, left_got, right, right_got in groups:
        shape = (targets, left.shape[0] // targets, left.shape[1])
        args += [left.reshape(shape), left_got.reshape(shape), right, right_got]
    out = ((targets // 2, args[0].shape[1], lanes), BF16)
    return near(functools.partial(meet_kernel, len(groups), bit, lanes), 3, [out] * 2, args)


def advance(streams):
    outs, args, plan = [], [], []
    for groups, bits in streams:
        for group in groups:
            args += group
        count, *block = groups[0][0].shape
        outs += [((count // 2, *block), BF16)] * 2 if bits else [(tuple(block), F32)]
        plan.append((len(groups), tuple(bits)))
    results = list(near(functools.partial(advance_kernel, plan), 2, outs, args))
    return [tuple(results.pop(0) for _ in range(2 if bits else 1)) for _, bits in streams]


def flip(array, axis, bit):
    count = lax.axis_size(axis)
    return lax.ppermute(array, axis, [(i, i ^ bit) for i in range(count)])


def shifted(array, by):
    count = lax.axis_size("seq")
    pairs = [(i, i + by) for i in range(count) if 0 <= i + by < count]
    return lax.ppermute(array, "seq", pairs)


def tie(*arrays):
    return lax.optimization_barrier(arrays)


def bits_of(count):
    bits = [1 << k for k in range(count.bit_length() - 1)]
    assert 1 << len(bits) == count
    return bits


def swapped(bits):
    return [bits[1], bits[0]] + list(bits[2:]) if len(bits) > 1 else list(bits)


def pick(array, index, axis):
    return lax.dynamic_index_in_dim(array, index, axis, keepdims=False)


def local(
    tokens, starts, norm_gain, in_weight, conv_weight, conv_bias, xproj_weight,
    dtproj_weight, dt_bias, decay_rate, skip_gain, out_weight, cotangent,
):
    core = lax.axis_index("section")
    place = lax.axis_index("seq")
    cores = lax.axis_size("section")
    count = lax.axis_size("seq")
    bits = bits_of(count)
    batch_count, span, model = tokens.shape
    width = conv_weight.shape[2]
    n = decay_rate.shape[2]
    rank = dtproj_weight.shape[1]
    x_width = xproj_weight.shape[2]
    batches = batch_count // cores
    rows_n = batches * span
    half_model = model // 2
    low_core = core == 0
    steps = len(bits)

    def mine(array):
        return lax.dynamic_slice_in_dim(array, core * batches, batches, 0).reshape(
            (rows_n,) + array.shape[2:]
        )

    rows0 = mine(tokens)
    top = mine(cotangent)
    r = lax.dynamic_slice_in_dim(starts, core * batches, batches, 0).astype(F32)
    r_ext = jnp.concatenate([shifted(r[:, -3:].astype(BF16), 1).astype(F32), r], 1)
    free = 1.0 - r_ext
    m1 = free[:, 3:]
    m2 = m1 * free[:, 2:-1]
    m3 = m2 * free[:, 1:-2]
    marks = jnp.stack([r, m1, m2, m3], -1).reshape(rows_n, 4)

    tall = ((rows_n, width), F32)
    low_tall = ((rows_n, width), BF16)
    rim_s = ((batches, 3, width), F32)
    own_gain = norm_gain[0][None]
    in_own, out_own = in_weight[0], out_weight[0]

    vec_own = jnp.concatenate(
        [
            decay_rate[0].T * -LOG2E, conv_weight[0], conv_bias[0][None], dt_bias[0][None],
            skip_gain[0][None], jnp.pad(own_gain, ((0, 0), (0, width - model))),
        ],
        0,
    )
    low_own = jnp.concatenate([xproj_weight[0].T, dtproj_weight[0]], 0)
    vec_other, low_other = flip(vec_own, "section", 1), flip(low_own, "section", 1)

    in_a, in_b, gate_a, gate_b, tail_a, tail_b = run(
        functools.partial(enter_kernel, batches, span, width), 5,
        [low_tall] * 4 + [rim_s] * 2,
        [((cores * rows_n, model), BF16), ((4, model, 2 * width // 4), BF16), DMA((4,))],
        [tokens.reshape(batch_count * span, model), own_gain, in_own],
        far=(0, 1), far_out=range(6), elsewhere=(2,),
    )
    in_a, in_b, gate_a, gate_b, tail_a, tail_b, vec_other, low_other, marks = tie(
        in_a, in_b, gate_a, gate_b, tail_a, tail_b, vec_other, low_other, marks
    )
    in_got = lax.ppermute(in_b, "section", [(0, 1)])
    everywhere = ("section", "seq")
    rim_a = lax.ppermute(tail_a, everywhere, [(i, i + 1) for i in range(count - 1)])
    rim_b = lax.ppermute(tail_b, everywhere, [(i, count + i + 1) for i in range(count - 1)])
    gate_got = lax.ppermute(gate_b, "section", [(0, 1)])

    out_now, in_now, _, _, _ = tie(out_own, in_own, in_got, rim_a, rim_b)
    out_other, in_other = flip(out_now, "section", 1), flip(in_now, "section", 1)
    vecs = [jnp.where(low_core == (l == 0), vec_own, vec_other) for l in range(2)]
    lows = [jnp.where(low_core == (l == 0), low_own, low_other) for l in range(2)]
    gains = [v[n + 7 :, :model] for v in vecs]
    in0, gate0 = jnp.where(low_core, in_a, in_got), jnp.where(low_core, gate_a, gate_got)
    rim0 = jnp.where(low_core, rim_a, rim_b)

    spread = ((rows_n, n, LANES), F32)
    state = ((batches, n, width), F32)
    flat_in = ((model, 2 * width), BF16)
    flat_out = ((width, model), BF16)
    send_s = ((batches * n + 16, width), BF16)
    send_back_s = ((batches * n, width), BF16)
    tall_t = ((width, rows_n), BF16)
    narrow = ((rows_n, model), BF16)

    totals_s = ((-(-batches * (steps + 1) // 8) * 8, width), F32)

    def front(layer, inner, rim, vec, low, *rest, others=()):
        outs = [low_tall, ((rows_n, LANES), BF16), send_s]
        scratch = [((span + 8, width), F32), tall, tall, spread, spread, state]
        args = [inner, rim, marks, vec, low, *rest]
        if layer:
            outs += [send_back_s]
            scratch += [tall, flat_out, DMA]
        return run(
            functools.partial(front_kernel, batches, span, width, rank, n, bool(layer)),
            10 if layer else 6, outs, scratch, args, far=(2, 3, 1, 0, 4),
            far_out=range(len(outs)), elsewhere=(7, 8) if layer else (), others=others,
        )

    conv0, proj0, send = front(
        0, in_a, rim_a, vec_own, low_own,
        others=((0, in_got), (1, rim_b), (3, vec_other), (4, low_other)),
    )
    at0, at1 = vecs[0][:n], vecs[1][:n]
    own = [send]
    for k, bit in enumerate(bits):
        own.append(flip(send, "seq", bit))
        if k < steps - 1:
            (send,) = hop(batches, n, k + 1, at0, own)
    scanned0, gated_t0, rows1, normed0, normed1, in1, gate1, before0, totals0, tail1 = run(
        functools.partial(end_kernel, batches, span, width, rank, n, steps), 10,
        [tall, tall_t, narrow, narrow, narrow, low_tall, low_tall, state, totals_s, ((batches, 6, width), F32)],
        [tall, tall, spread, spread, flat_out, flat_in, DMA((2,))],
        [gate0, conv0, proj0, marks, vecs[0], lows[0], rows0, gains[1], gains[0],
         out_own, out_other, in_own, in_other, *own],
        far=(6, 8, 2, 5, 4, 3, 1, *range(13, 14 + steps), 0), far_out=range(10),
        elsewhere=(9, 10, 11, 12),
    )

    rims = shifted(tail1, 1)
    rim1 = rims[:, :3]
    conv1, proj1, send, send_b = front(
        1, in1, rim1, vecs[1], lows[1], gate1, top, out_own, out_other
    )
    rim = rims[:, 3:, :model].astype(BF16)
    rim = jnp.pad(rim, ((0, 0), (5, 0), (0, 0))).reshape(8 * batches, model)
    normed_ext = jnp.concatenate(
        [normed0, rim, jnp.zeros((rows_n - 8 * batches, model), BF16)], 0
    )
    ext_got, normed_got = flip(normed_ext, "section", 1), flip(normed1, "section", 1)
    own, own_b = [send], [send_b]
    for k, bit in enumerate(bits):
        own.append(flip(send, "seq", bit))
        own_b.append(flip(send_b, "seq", bit))
        if k < steps - 1:
            send, send_b = hop(batches, n, k + 1, at1, own, own_b)

    def back(layer, gg, conv, inner, gate, rim, proj, *rest):
        outs = [
            low_tall, ((batches, 16, width), F32), ((batches, 3, width), F32),
            ((width, LANES), BF16), ((n + 8, width), F32),
        ]
        scratch = [
            tall, tall, ((batches, span + 1, n, BLOCK), F32), ((batches, span, n, BLOCK), F32),
            tall, tall, spread, spread, ((span + 16, width), F32), tall,
            spread, spread, tall, state, state,
        ]
        if layer:
            outs += [low_tall, tall_t, narrow]
            scratch += [tall, tall, flat_out, DMA]
            far = (8, 7, 6, 5, 1, 0, 3, *range(12, 12 + 2 * steps))
        else:
            outs += [((width, 2 * rows_n), BF16)]
            far = (8, 7, 6, 5, 1, 0, 3, *range(9, 11 + steps))
        return run(
            functools.partial(
                back_kernel, batches, span, width, rank, n, x_width, steps, bool(layer)
            ),
            22 if layer else 19, outs, scratch,
            [gg, conv, inner, gate, rim, marks, vecs[layer], lows[layer], proj, *rest],
            far=far, far_out=range(len(outs)),
            elsewhere=(10, 11) if layer else (),
        )

    inner1, last1, spill1, pair1, vgrad1, gate_grad1, gated_t1, out1 = back(
        1, top, conv1, in1, gate1, rim1, proj1, rows1, out_own, out_other, *own[1:], *own_b[1:]
    )
    got1 = shifted(spill1, -1)

    def turn(layer, inner, tail, spill, gate_grad, rows, g, pair, vgrad, *rest):
        outs = [narrow, ((width, 2 * LANES), BF16)]
        scratch = [flat_in, DMA, ((rows_n, 2 * width), BF16), ((width, LANES), F32)]
        args = [
            inner, tail, spill, gate_grad, rows, gains[layer], g, pair, vgrad, in_own, in_other,
            *rest,
        ]
        elsewhere, far, far_out = [9, 10], [1, 2, 0, 3, 4, 6], [0, 1]
        if layer:
            outs += [((2 * width, rows_n), BF16), tall, send_back_s, low_tall, tall_t]
            scratch += [tall, tall, spread, state, flat_out, DMA]
            elsewhere += [11, 12]
            far += [13, 14, 18]
            far_out += [2, 3, 4, 5, 6]
        return run(
            functools.partial(turn_kernel, batches, span, width, rank, n, count, layer),
            11 if layer else 5, outs, scratch, args, far=far, far_out=far_out,
            elsewhere=elsewhere, limit=None if layer else TURN_LIMIT,
        )

    g0, small1, grad_t1, gg0, send_b, gate_grad0, gate_t0 = turn(
        1, inner1, last1, got1, gate_grad1, rows1, top, pair1, vgrad1, out_own, out_other,
        gate0, proj0,
        marks, lows[0], vecs[0], scanned0,
    )

    first_b = flip(send_b, "seq", bits[0])
    first_b, grad_t1, gate_t0, g0, gated_t0, gated_t1 = tie(
        first_b, grad_t1, gate_t0, g0, gated_t0, gated_t1
    )

    x_bit, y_bit, z_bit = bits[0], bits[1], bits[-2]
    one_way = lambda array, a, b: lax.ppermute(array, "section", [(a, b)])
    def half(array, which):
        return lax.dynamic_slice_in_dim(array, which * half_model, half_model, 1)

    def together(left, left_got, right, right_got):
        return dot(
            jnp.concatenate([left, left_got], 1), jnp.concatenate([right, right_got], 0)
        ).astype(BF16)

    def part(total, bit, order):
        axis = len(order) - 1 - sorted(order).index(bit)
        total = total.reshape((2,) * len(order) + (-1, total.shape[-1]))
        mine = (place // bit) % 2
        block = (total.shape[-2], total.shape[-1])
        return (
            pick(total, 1 - mine, axis).reshape((-1, *block)),
            pick(total, mine, axis).reshape((-1, *block)),
        )

    gated_got = flip(jnp.where(low_core, gated_t1, gated_t0), "section", 1)
    gated_own = jnp.where(low_core, gated_t0, gated_t1)
    g_got = flip(jnp.where(low_core, top, g0), "section", 1)
    grad_got, gate_got0 = flip(grad_t1, "section", 1), flip(gate_t0, "section", 1)

    own_b = [send_b]
    for k, bit in enumerate(bits):
        got_b = flip(send_b, "seq", bit) if k else first_b
        if k == 1:
            a = together(grad_t1, grad_got, half(normed1, core), half(normed_got, core))
            b = together(gated_own, gated_got, jnp.where(low_core, g0, top), g_got)
            c = together(
                gate_t0, gate_got0, half(normed0, core), half(ext_got[:rows_n], core)
            )
            a_goes, a_stays = part(a, x_bit, bits)
            b_goes, b_stays = part(b, y_bit, bits)
            c_goes, c_stays = part(c, z_bit, bits[:-1])
            got_b, a_goes, b_goes = tie(got_b, a_goes, b_goes)
        if k == steps - 1:
            got_b, a_goes, b_goes, c_goes = tie(got_b, a_goes, b_goes, c_goes)
            a_got, b_got = flip(a_goes, "seq", x_bit), flip(b_goes, "seq", y_bit)
            c_got = flip(c_goes, "seq", z_bit)
            small_up = one_way(small1, 0, 1)
        own_b.append(got_b)
        if k < steps - 1:
            (send_b,) = hop(batches, n, k + 1, at0, (), own_b, totals0)
    inner0, tail0, spill0, pair0, vgrad0, turned0 = back(
        0, gg0, conv0, in0, gate0, rim0, proj0, before0, totals0, *own_b[1:]
    )
    inner0, tail0, spill0, pair0, vgrad0, turned0, a_got, b_got, c_got, small_up = tie(
        inner0, tail0, spill0, pair0, vgrad0, turned0, a_got, b_got, c_got, small_up
    )
    got0 = shifted(spill0, -1)
    turned_got = flip(turned0, "section", 1)

    middle = bits[2:-2]
    blocks = lambda array: array.reshape(count, -1, array.shape[-1])
    held = {"a": [(a_stays, a_got)], "b": [(b_stays, b_got)], "c": [(c_stays, c_got)]}
    todo = {
        "d": [x_bit, y_bit, *middle, z_bit],
        "a": [y_bit, *middle, z_bit, bits[-1]],
        "b": [z_bit, x_bit, *middle, bits[-1]],
        "c": [x_bit, y_bit, *middle],
    }
    parts = dict(zip("ab", advance([(held[k], todo[k]) for k in "ab"])))
    parts["d"] = meet(
        [(turned0, turned_got, normed_ext, ext_got)], x_bit, count // 2, half_model
    )
    first = [parts[k][0] for k in "dab"]
    got0, inner0, tail0, pair0, vgrad0, *first = tie(got0, inner0, tail0, pair0, vgrad0, *first)
    gots = [flip(goes, "seq", todo[k][0]) for k, goes in zip("dab", first)]
    dx, small0 = turn(0, inner0, tail0, got0, gate_grad0, rows0, g0, pair0, vgrad0)
    *gots, dx, small0 = tie(*gots, dx, small0)
    for k, got in zip("dab", gots):
        held[k] = [(parts[k][1], got)]
        todo[k] = todo[k][1:]
    small_down = one_way(small0, 1, 0)
    late = {
        "small": (
            [(blocks(small0), blocks(small_down)), (blocks(small1), blocks(small_up))],
            [y_bit, x_bit, *middle, z_bit, bits[-1]],
        )
    }
    while any(todo.values()):
        names = [k for k in todo if todo[k]]
        parts = dict(zip(names, advance([(held[k], todo[k]) for k in names])))
        gots = [flip(parts[k][0], "seq", todo[k][0]) for k in names]
        for k in late:
            held[k], todo[k] = late[k]
            parts.update(zip([k], advance([late[k]])))
            names.append(k)
            gots.append(flip(parts[k][0], "seq", todo[k][0]))
        late = {}
        gots = tie(*gots)
        for k, got in zip(names, gots):
            held[k] = [(parts[k][1], got)]
            todo[k] = todo[k][1:]
        if not todo["d"] and not todo["c"] and "d" in parts:
            c, d = (t.astype(BF16) for (t,) in advance([(held[k], []) for k in "cd"]))
            top_half = place >= count // 2
            swap_sent = jnp.where(top_half, d, c)
            swap_got = flip(swap_sent, "seq", bits[-1])
    in_sum1, out_sum, small = (
        total for (total,) in advance([(held[k], []) for k in ("a", "b", "small")])
    )
    in_sum0 = jnp.where(top_half, c, d).astype(F32) + swap_got.astype(F32)

    got = flip(jnp.where(low_core, in_sum1, in_sum0).astype(BF16), "section", 1).astype(F32)
    grad_in = jnp.where(
        low_core, jnp.concatenate([in_sum0, got], 1), jnp.concatenate([got, in_sum1], 1)
    )
    got = flip(jnp.where(low_core, out1, dx), "section", 1)
    boundary = jnp.where(
        low_core, jnp.concatenate([dx, got], 0), jnp.concatenate([got, out1], 0)
    ).reshape(1, batch_count, span, model)
    vec_sum = small[:, LANES : LANES + n + 8].T
    gain = vec_sum[n + 7 :, : model // count]
    return (
        boundary,
        gain,
        grad_in.T[None],
        vec_sum[n : n + 4][None],
        vec_sum[n + 4 : n + 5],
        small[:, :x_width][None],
        small[:, x_width:LANES].T[None],
        vec_sum[n + 5 : n + 6],
        small[:, LANES : LANES + n][None],
        vec_sum[n + 6 : n + 7],
        out_sum[None],
    )


def solution(mesh):
    in_specs = (
        P(None, "seq", None), P(None, "seq"), P("section", None), P("section", None, None),
        P("section", None, None), P("section", None), P("section", None, None),
        P("section", None, None), P("section", None), P("section", None, None),
        P("section", None), P("section", None, None), P(None, "seq", None),
    )
    out_specs = (
        P("section", None, "seq", None), P("section", "seq"), P("section", None, "seq"),
        P("section", None, "seq"), P("section", "seq"), P("section", "seq", None),
        P("section", None, "seq"), P("section", "seq"), P("section", "seq", None),
        P("section", "seq"), P("section", "seq", None),
    )
    return jax.shard_map(local, mesh=mesh, in_specs=in_specs, out_specs=out_specs, check_vma=False)
```

```python
import functools
import jax
import jax.numpy as jnp
from jax import lax
from jax.experimental import pallas as pl
from jax.experimental.pallas import tpu as pltpu
from jax.sharding import PartitionSpec as P

EPS = 1e-05
LOG2E = 1.4426950408889634
STOP = 1e7
LANES = 128
BLOCK = 512
TILES = BLOCK // LANES
F32 = jnp.float32
BF16 = jnp.bfloat16
VMEM_LIMIT = 58 * 1024 * 1024
HOP_LIMIT = 6 * 1024 * 1024
NEAR_LIMIT = 24 * 1024 * 1024
TURN_LIMIT = 58 * 1024 * 1024


def dot(left, right):
    return jnp.dot(left, right, preferred_element_type=F32)


def across(left, right):
    return lax.dot_general(left, right, (((0,), (0,)), ((), ())), preferred_element_type=F32)


def against(left, right):
    return lax.dot_general(left, right, (((1,), (1,)), ((), ())), preferred_element_type=F32)


def norm_rows(source, gain_row):
    return source * lax.rsqrt(jnp.mean(source * source, axis=-1, keepdims=True) + EPS) * gain_row


def softplus(v):
    return jnp.maximum(v, 0.0) + jnp.log1p(jnp.exp(-jnp.abs(v)))


def silu_slope(v):
    gate = jax.nn.sigmoid(v)
    return gate * (1.0 + v * (1.0 - gate))


def pair_up(left, right, row_ids, width):
    mask = (row_ids % (2 * width)) < width
    kept = jnp.where(mask, left, right)
    moved = jnp.where(mask, right, left)
    return kept + pltpu.roll(moved, 8 - width, 0)


def fold_rows(parts, row_ids):
    width = 1
    while len(parts) > 1:
        parts = [
            pair_up(parts[i], parts[i + 1], row_ids, width) for i in range(0, len(parts), 2)
        ]
        width *= 2
    return parts[0]


def halves(v):
    return v[:8] + v[8:]


def spread_columns(table, first, target):
    width = target.shape[1]
    for t in range(target.shape[0]):
        column = table[first : first + width, t : t + 1]
        target[t] = jnp.broadcast_to(column, (width, LANES))


def block_at(i):
    return pl.ds(pl.multiple_of(i * BLOCK, BLOCK), BLOCK)


def tile_at(i, lt):
    return pl.ds(pl.multiple_of(i * BLOCK + lt * LANES, LANES), LANES)


def local_scan(batches, span, blocks, seff, x, bx, at, final):
    def over_block(i, carry):
        rate = [at[:, tile_at(i, lt)] for lt in range(TILES)]

        def chunk(tc, states):
            states = list(states)
            for b in range(batches):
                rows = pl.ds(pl.multiple_of(b * span + tc * 8, 8), 8)
                for lt in range(TILES):
                    s8 = seff[rows, tile_at(i, lt)]
                    x8 = x[rows, tile_at(i, lt)]
                    h = states[b * TILES + lt]
                    for j in range(8):
                        decay = jnp.exp2(s8[j : j + 1] * rate[lt])
                        h = decay * h + x8[j : j + 1] * bx[b * span + tc * 8 + j]
                    states[b * TILES + lt] = h
            return tuple(states)

        zero = jnp.zeros((at.shape[0], LANES), F32)
        states = lax.fori_loop(0, span // 8, chunk, (zero,) * (batches * TILES))
        for b in range(batches):
            for lt in range(TILES):
                final[b, :, tile_at(i, lt)] = states[b * TILES + lt]
        return carry

    lax.fori_loop(0, blocks, over_block, 0)


def back_scan(batches, span, blocks, seff, sg, cx, at, first):
    chunks = span // 8

    def over_block(i, carry):
        rate = [at[:, tile_at(i, lt)] for lt in range(TILES)]

        def chunk(k, states):
            states = list(states)
            tc = chunks - 1 - k
            for b in range(batches):
                rows = pl.ds(pl.multiple_of(b * span + tc * 8, 8), 8)
                for lt in range(TILES):
                    s8 = seff[rows, tile_at(i, lt)]
                    g8 = sg[rows, tile_at(i, lt)]
                    q = states[b * TILES + lt]
                    for j in range(7, -1, -1):
                        decay = jnp.exp2(s8[j : j + 1] * rate[lt])
                        q = decay * (q + g8[j : j + 1] * cx[b * span + tc * 8 + j])
                    states[b * TILES + lt] = q
            return tuple(states)

        zero = jnp.zeros((at.shape[0], LANES), F32)
        states = lax.fori_loop(0, chunks, chunk, (zero,) * (batches * TILES))
        for b in range(batches):
            for lt in range(TILES):
                first[b, :, tile_at(i, lt)] = states[b * TILES + lt]
        return carry

    lax.fori_loop(0, blocks, over_block, 0)


class Arriving:
    def __init__(self, source, held, sem, other=None):
        self.held, self.waited = held, False
        if other is None:
            self.copy = pltpu.make_async_copy(source, held, sem)
            self.copy.start()
        else:
            self.copy = fetch(0, source, other, held, sem)

    def __getitem__(self, where):
        assert self.waited
        return self.held[where]

    def __setitem__(self, where, value):
        assert self.waited
        self.held[where] = value

    @property
    def at(self):
        return self.held.at


class Leaving:
    def __init__(self, target, held, sem):
        self.copy, self.held, self.started = pltpu.make_async_copy(held, target, sem), held, False

    def __getitem__(self, where):
        return self.held[where]

    def __setitem__(self, where, value):
        self.held[where] = value


def uppers_of(steps):
    place = lax.axis_index("seq")
    return [(place // (1 << k)) % 2 != 0 for k in range(steps)]


def ready(*refs):
    for ref in refs:
        if isinstance(ref, Arriving) and not ref.waited:
            ref.copy.wait()
            ref.waited = True


def leave(*refs):
    for ref in refs:
        if isinstance(ref, Leaving) and not ref.started:
            ref.copy.start()
            ref.started = True


def fetch(layer, own, other, held, sem):
    mine = lax.axis_index("section") == layer

    @pl.when(mine)
    def _():
        pltpu.make_async_copy(own, held, sem).start()

    @pl.when(jnp.logical_not(mine))
    def _():
        pltpu.make_async_copy(other, held, sem).start()

    return pltpu.make_async_copy(own, held, sem)


def split_total(totals):
    width = totals[0].shape[1]
    row_ids = lax.broadcasted_iota(jnp.int32, (16, width), 0)
    block = jnp.zeros((16, width), F32)
    for b, total in enumerate(totals):
        rest = total
        for k in range(3):
            part = rest.astype(BF16).astype(F32)
            block = jnp.where(row_ids == 3 * b + k, part, block)
            rest = rest - part
    return block.astype(BF16)


def join_total(block, b):
    block = block.astype(F32)
    return block[3 * b : 3 * b + 1] + block[3 * b + 1 : 3 * b + 2] + block[3 * b + 2 : 3 * b + 3]


def enter_kernel(
    batches, span, width,
    rows, gain, in_w,
    in_a_o, in_b_o, gate_a_o, gate_b_o, tail_a_o, tail_b_o,
    normed, held, sems,
):
    chunk = held.shape[2]
    copies = [
        pltpu.make_async_copy(in_w.at[:, pl.ds(c * chunk, chunk)], held.at[c], sems.at[c])
        for c in range(held.shape[0])
    ]
    for copy in copies:
        copy.start()
    ready(rows, gain)
    normed[...] = norm_rows(rows[...].astype(F32), gain[...]).astype(BF16)
    half = batches * span
    for c, copy in enumerate(copies):
        copy.wait()
        mixed = dot(normed[...], held[c])
        outs = (in_a_o, in_b_o) if c * chunk < width else (gate_a_o, gate_b_o)
        lanes = slice(c * chunk % width, c * chunk % width + chunk)
        for k, out in enumerate(outs):
            out[:, lanes] = mixed[k * half : (k + 1) * half].astype(BF16)
        if c * chunk < width:
            for k, tail in enumerate((tail_a_o, tail_b_o)):
                for b in range(batches):
                    last = k * half + (b + 1) * span
                    tail[b, :, lanes] = mixed[last - 3 : last].astype(BF16).astype(F32)
        if (c + 1) * chunk == width:
            leave(in_a_o, in_b_o, tail_a_o, tail_b_o)


def tap_rows(ext, rim, mixed, width, span):
    ext[5:8] = rim
    ext[8 : 8 + span] = mixed.astype(F32)


def conv_sum(ext, m, vec, n, span):
    v = vec[n + 4 : n + 5] + vec[n + 3 : n + 4] * ext[8 : 8 + span]
    for k in (1, 2, 3):
        v = v + vec[n + 3 - k : n + 4 - k] * (m[:, k : k + 1] * ext[8 - k : 8 - k + span])
    return v


def step_sum(proj, low_w, vec, rank, n):
    return dot(proj[:, :rank], low_w[rank + 2 * n :]) + vec[n + 5 : n + 6]


def front_kernel(
    batches, span, width, rank, states_n, with_back,
    *refs,
):
    refs = list(refs)
    mixed, rim, marks, vec, low_w = refs[:5]
    del refs[:5]
    if with_back:
        gate, g, own_w, other_w = refs[:4]
        del refs[:4]
    conv_o, proj_o, send_o = refs[:3]
    del refs[:3]
    if with_back:
        first = batches * states_n + 16
    ext, seff, x, bx, cx, final = refs[:6]
    if with_back:
        sg, out_w, sem = refs[6:]
        arrival = fetch(1, own_w, other_w, out_w, sem)
    n = states_n
    ready(rim, marks, vec)
    m = marks[...]
    at = vec.at[0:n]
    ready(mixed)
    for b in range(batches):
        lo, hi = b * span, (b + 1) * span
        tap_rows(ext, rim[b], mixed[lo:hi], width, span)
        x[lo:hi] = jax.nn.silu(conv_sum(ext, m[lo:hi], vec, n, span))
    conv = x[...].astype(BF16)
    conv_o[...] = conv
    leave(conv_o)
    ready(low_w)
    proj = against(conv, low_w[...]).astype(BF16)
    proj_o[...] = proj
    leave(proj_o)
    step = softplus(step_sum(proj, low_w, vec, rank, n))
    seff[...] = step + m[:, 0:1] * STOP
    x[...] = step * conv.astype(F32)
    totals = [
        jnp.sum(seff[b * span : (b + 1) * span], axis=0, keepdims=True) for b in range(batches)
    ]
    send_o[batches * n : batches * n + 16] = split_total(totals)
    table = proj.astype(F32).T
    spread_columns(table, rank, bx)
    local_scan(batches, span, width // BLOCK, seff, x, bx, at, final)
    for b in range(batches):
        send_o[b * n : (b + 1) * n] = final[b].astype(BF16)
    if not with_back:
        leave(send_o)
    if with_back:
        arrival.wait()
        spread_columns(table, rank + n, cx)
        ready(g, gate)
        gg = against(g[...], out_w[...])
        sg[...] = gg * jax.nn.silu(gate[...].astype(F32))
        back_scan(batches, span, width // BLOCK, seff, sg, cx, at, final)
        for b in range(batches):
            send_o[first + b * n : first + (b + 1) * n] = final[b].astype(BF16)


def merge(at, upper, mine, theirs, mine_total, their_total, backward):
    early, late = jnp.where(upper, theirs, mine), jnp.where(upper, mine, theirs)
    if backward:
        return jnp.exp2(jnp.where(upper, their_total, mine_total) * at) * late + early
    return jnp.exp2(jnp.where(upper, mine_total, their_total) * at) * early + late


def reach(at, n, b, uppers, gots, totals, backward, first=0):
    carry = jnp.zeros(at.shape, F32)
    span = jnp.zeros((1, at.shape[1]), F32)
    for upper, got, their_total in zip(uppers, gots, totals):
        comes = jnp.logical_not(upper) if backward else upper
        theirs = got[first + b * n : first + (b + 1) * n].astype(F32)
        carry = jnp.where(comes, jnp.exp2(span * at) * theirs + carry, carry)
        span = jnp.where(comes, span + their_total, span)
    return carry


def hop_kernel(batches, n, steps, forward, backward, *refs):
    refs = list(refs)
    take = lambda k: [refs.pop(0) for _ in range(k)]
    (at,) = take(1)
    at = at[...]
    if forward:
        own, *gots = take(1 + steps)
    else:
        (totals,) = take(1)
    first = 0
    if forward and backward:
        own_b, gots_b, first = own, gots, batches * n + 16
    elif backward:
        own_b, *gots_b = take(1 + steps)
    (send,) = take(1)
    uppers = uppers_of(steps)
    reached = []
    for b in range(batches):
        rows = slice(b * n, (b + 1) * n)
        if forward:
            total = join_total(own[batches * n : batches * n + 16], b)
            mine = own[rows].astype(F32)
        else:
            total = totals[b : b + 1]
        if backward:
            rows_b = slice(first + b * n, first + (b + 1) * n)
            mine_b = own_b[rows_b].astype(F32)
        for k, upper in enumerate(uppers):
            if forward:
                their_total = join_total(gots[k][batches * n : batches * n + 16], b)
                mine = merge(
                    at, upper, mine, gots[k][rows].astype(F32), total, their_total, False
                )
            else:
                their_total = totals[(k + 1) * batches + b : (k + 1) * batches + b + 1]
            if backward:
                mine_b = merge(
                    at, upper, mine_b, gots_b[k][rows_b].astype(F32), total, their_total, True
                )
            total = total + their_total
        if forward:
            send[rows] = mine.astype(BF16)
        if backward:
            send[rows_b] = mine_b.astype(BF16)
        reached.append(total)
    if forward:
        send[batches * n : batches * n + 16] = split_total(reached)


def prepare(step, marks, conv, seff, x):
    seff[...] = step + marks * STOP
    x[...] = step * conv.astype(F32)


def end_kernel(
    batches, span, width, rank, n, steps,
    gate, conv, proj, marks, vec, low_w, rows, gain, gain_before,
    own_out, other_out, own_in, other_in, own_send, *refs,
):
    gots, refs = refs[:steps], refs[steps:]
    (
        scanned_o, gated_t_o, rows_o, normed_before_o, normed_o, inner_o, gate_o, before_o,
        totals_o, tail_o, seff, x, bx, cx, out_w, in_w, sems,
    ) = refs

    arrivals = [
        fetch(0, own_out, other_out, out_w, sems.at[0]),
        fetch(1, own_in, other_in, in_w, sems.at[1]),
    ]
    blocks = width // BLOCK
    at = vec.at[0:n]
    ready(rows, gain_before, proj, low_w, vec, marks, conv)
    normed_before_o[...] = norm_rows(rows[...].astype(F32), gain_before[...]).astype(BF16)
    leave(normed_before_o)
    tail_o[...] = jnp.zeros((batches, 6, width), F32)
    for b in range(batches):
        last = normed_before_o[(b + 1) * span - 16 : (b + 1) * span].astype(F32)
        tail_o[b, 3:6, : last.shape[1]] = last[13:]
    step = softplus(step_sum(proj[...], low_w, vec, rank, n))
    prepare(step, marks[:, 0:1], conv[...], seff, x)
    table = proj[...].astype(F32).T
    spread_columns(table, rank, bx)
    spread_columns(table, rank + n, cx)
    ready(own_send, *gots)
    uppers = uppers_of(steps)
    for b in range(batches):
        totals_o[b : b + 1] = join_total(own_send[batches * n : batches * n + 16], b)
        theirs = [join_total(got[batches * n : batches * n + 16], b) for got in gots]
        for k, their in enumerate(theirs):
            totals_o[(k + 1) * batches + b : (k + 1) * batches + b + 1] = their
        before_o[b] = reach(at[...], n, b, uppers, gots, theirs, False)
    leave(before_o, totals_o)
    row_ids = lax.broadcasted_iota(jnp.int32, (8, LANES), 0)

    def over_block(i, carry):
        rate = [at[:, tile_at(i, lt)] for lt in range(TILES)]

        def chunk(tc, states):
            states = list(states)
            for b in range(batches):
                rows8 = pl.ds(pl.multiple_of(b * span + tc * 8, 8), 8)
                for lt in range(TILES):
                    s8 = seff[rows8, tile_at(i, lt)]
                    x8 = x[rows8, tile_at(i, lt)]
                    h = states[b * TILES + lt]
                    parts = []
                    for j in range(8):
                        t = b * span + tc * 8 + j
                        decay = jnp.exp2(s8[j : j + 1] * rate[lt])
                        h = decay * h + x8[j : j + 1] * bx[t]
                        parts.append(halves(h * cx[t]))
                    states[b * TILES + lt] = h
                    scanned_o[rows8, tile_at(i, lt)] = fold_rows(parts, row_ids)
            return tuple(states)

        start = tuple(
            before_o[b, :, tile_at(i, lt)] for b in range(batches) for lt in range(TILES)
        )
        lax.fori_loop(0, span // 8, chunk, start)
        return carry

    lax.fori_loop(0, blocks, over_block, 0)
    scanned = scanned_o[...] + vec[n + 6 : n + 7] * conv[...].astype(F32)
    scanned_o[...] = scanned
    leave(scanned_o)
    ready(gate)
    gated_f = scanned * jax.nn.silu(gate[...].astype(F32))
    gated = gated_f.astype(BF16)
    gated_t_o[...] = gated_f.T.astype(BF16)
    leave(gated_t_o)
    arrivals[0].wait()
    result = (rows[...].astype(F32) + dot(gated, out_w[...])).astype(BF16)
    rows_o[...] = result
    leave(rows_o)
    ready(gain)
    normed_o[...] = norm_rows(result.astype(F32), gain[...]).astype(BF16)
    leave(normed_o)
    arrivals[1].wait()
    for first, target in ((0, inner_o), (width, gate_o)):
        for c in range(0, width, 512):
            mixed = dot(normed_o[...], in_w[:, first + c : first + c + 512])
            target[:, c : c + 512] = mixed.astype(BF16)
            if not first:
                for b in range(batches):
                    last = (b + 1) * span
                    tail_o[b, 0:3, c : c + 512] = mixed[last - 3 : last].astype(BF16).astype(F32)
        leave(target, tail_o)


def back_kernel(
    batches, span, width, rank, n, x_width, steps, with_out,
    *refs,
):
    refs = list(refs)
    take = lambda k: [refs.pop(0) for _ in range(k)]
    gg, conv, inner, gate, rim, marks, vec, low_w, proj = take(9)
    if with_out:
        rows, own_out, other_out = take(3)
        gots = gots_b = take(steps)
    else:
        before, totals = take(2)
        gots_b = take(steps)
    inner_o, tail_o, spill_o, pair_o, vec_o = take(5)
    if with_out:
        gate_o, gated_t_o, out_o = take(3)
    else:
        (turned_o,) = take(1)
    seff, x, hist, decays, drive, zsum, acc_b, acc_c, ext, sg, bx, cx, pre_grad = take(13)
    state_in, grad_in = take(2)
    if with_out:
        scanned_ref, gg_s, out_w, sem = take(4)
        arrival = fetch(1, own_out, other_out, out_w, sem)
    blocks = width // BLOCK
    rows_n = batches * span
    chunks = span // 8
    ready(proj, low_w, vec, marks, conv)
    m = marks[...]
    at = vec.at[0:n]
    spre = step_sum(proj[...], low_w, vec, rank, n)
    prepare(softplus(spre), m[:, 0:1], conv[...], seff, x)
    table = proj[...].astype(F32).T
    spread_columns(table, rank, bx)
    spread_columns(table, rank + n, cx)
    ready(gg, gate)
    if with_out:
        arrival.wait()
        gg_s[...] = against(gg[...], out_w[...])
        gg = gg_s
    sg[...] = gg[...] * jax.nn.silu(gate[...].astype(F32))
    if with_out:
        ready(*gots)
    else:
        ready(before, totals)
    ready(*gots_b)
    uppers = uppers_of(steps)
    for b in range(batches):
        if with_out:
            theirs = [join_total(got[batches * n : batches * n + 16], b) for got in gots]
            state_in[b] = reach(at[...], n, b, uppers, gots, theirs, False)
        else:
            theirs = [
                totals[(k + 1) * batches + b : (k + 1) * batches + b + 1] for k in range(steps)
            ]
            state_in[b] = before[b]
        first = batches * n + 16 if with_out else 0
        grad_in[b] = reach(at[...], n, b, uppers, gots_b, theirs, True, first)
    acc_b[...] = jnp.zeros_like(acc_b)
    acc_c[...] = jnp.zeros_like(acc_c)
    vec_o[...] = jnp.zeros((n + 8, width), F32)
    row_ids = lax.broadcasted_iota(jnp.int32, (8, LANES), 0)

    def over_block(i, carry):
        rate = [at[:, tile_at(i, lt)] for lt in range(TILES)]

        def again(tc, states):
            states = list(states)
            for b in range(batches):
                rows8 = pl.ds(pl.multiple_of(b * span + tc * 8, 8), 8)
                for lt in range(TILES):
                    s8 = seff[rows8, tile_at(i, lt)]
                    x8 = x[rows8, tile_at(i, lt)]
                    h = states[b * TILES + lt]
                    lanes = pl.ds(lt * LANES, LANES)
                    parts = []
                    for j in range(8):
                        t = tc * 8 + j
                        decay = jnp.exp2(s8[j : j + 1] * rate[lt])
                        h = decay * h + x8[j : j + 1] * bx[b * span + t]
                        decays[b, t, :, lanes] = decay
                        hist[b, t + 1, :, lanes] = h
                        if with_out:
                            parts.append(halves(h * cx[b * span + t]))
                    states[b * TILES + lt] = h
                    if with_out:
                        scanned_ref[rows8, tile_at(i, lt)] = fold_rows(parts, row_ids)
            return tuple(states)

        for b in range(batches):
            hist[b, 0] = state_in[b, :, block_at(i)]
        start = tuple(
            state_in[b, :, tile_at(i, lt)] for b in range(batches) for lt in range(TILES)
        )
        lax.fori_loop(0, chunks, again, start)

        sums = tuple(jnp.zeros((n, LANES), F32) for _ in range(TILES))
        for b in range(batches):

            def chunk(k, held):
                held = list(held)
                tc = chunks - 1 - k
                rows8 = pl.ds(pl.multiple_of(b * span + tc * 8, 8), 8)
                s8, x8, g8 = [], [], []
                for lt in range(TILES):
                    s8.append(seff[rows8, tile_at(i, lt)])
                    x8.append(x[rows8, tile_at(i, lt)])
                    g8.append(sg[rows8, tile_at(i, lt)])
                drives = [[None] * 8 for _ in range(TILES)]
                zs = [[None] * 8 for _ in range(TILES)]
                for j in range(7, -1, -1):
                    t = tc * 8 + j
                    part_b, part_c = [], []
                    for lt in range(TILES):
                        lanes = pl.ds(lt * LANES, LANES)
                        total = held[lt] + g8[lt][j : j + 1] * cx[b * span + t]
                        q = decays[b, t, :, lanes] * total
                        log_grad = q * hist[b, t, :, lanes]
                        held[TILES + lt] = held[TILES + lt] + log_grad * s8[lt][j : j + 1]
                        zs[lt][j] = halves(log_grad * rate[lt])
                        drives[lt][j] = halves(total * bx[b * span + t])
                        part_b.append(total * x8[lt][j : j + 1])
                        part_c.append(g8[lt][j : j + 1] * hist[b, t + 1, :, lanes])
                        held[lt] = q
                    acc_b[b * span + t] += sum(part_b[1:], part_b[0])
                    acc_c[b * span + t] += sum(part_c[1:], part_c[0])
                for lt in range(TILES):
                    drive[rows8, tile_at(i, lt)] = fold_rows(drives[lt], row_ids)
                    zsum[rows8, tile_at(i, lt)] = fold_rows(zs[lt], row_ids)
                return tuple(held)

            start = tuple(grad_in[b, :, tile_at(i, lt)] for lt in range(TILES)) + sums
            sums = lax.fori_loop(0, chunks, chunk, start)[TILES:]
        for lt in range(TILES):
            vec_o[0:n, tile_at(i, lt)] = -sums[lt]
        return carry

    lax.fori_loop(0, blocks, over_block, 0)

    conv_f = conv[...].astype(F32)
    if with_out:
        ready(rows)
        gate = gate[...].astype(F32)
        scanned = scanned_ref[...] + vec[n + 6 : n + 7] * conv_f
        gated_f = scanned * jax.nn.silu(gate)
        gated_t_o[...] = gated_f.T.astype(BF16)
        out_o[...] = (rows[...].astype(F32) + dot(gated_f.astype(BF16), out_w[...])).astype(BF16)
        gate_o[...] = (gg_s[...] * scanned * silu_slope(gate)).astype(BF16)
        leave(gate_o, gated_t_o, out_o)

    ones = jnp.ones((LANES, LANES), BF16)
    table = (rows_n * n, LANES)
    at_n = lax.broadcasted_iota(jnp.int32, table, 0) % n
    lane = lax.broadcasted_iota(jnp.int32, table, 1)
    sums_b, sums_c = (
        dot(acc[...].reshape(table).astype(BF16), ones) for acc in (acc_b, acc_c)
    )
    placed = jnp.where(lane == rank + at_n, sums_b, 0.0)
    placed = placed + jnp.where(lane == rank + n + at_n, sums_c, 0.0)
    placed = jnp.sum(placed.reshape(rows_n, n, LANES), axis=1)
    spre = step_sum(proj[...], low_w, vec, rank, n)
    step = softplus(spre)
    step_grad = zsum[...] * (1.0 / LOG2E) + drive[...] * conv_f
    pre_g = step_grad * jax.nn.sigmoid(spre)
    low = pre_g.astype(BF16)
    low_grad = against(low, low_w[rank + 2 * n :])
    pgrad = (
        jnp.concatenate([low_grad, jnp.zeros((rows_n, LANES - rank), F32)], 1) + placed
    ).astype(BF16)
    small = dot(conv_f.T.astype(BF16), pgrad)
    lows = pltpu.roll(dot(pre_g.T.astype(BF16), proj[...]), x_width, 1)
    columns = lax.broadcasted_iota(jnp.int32, (1, LANES), 1)
    pair_o[...] = jnp.where(columns < x_width, small, lows).astype(BF16)
    leave(pair_o)
    conv_grad = (
        sg[...] * vec[n + 6 : n + 7] + step * drive[...]
        + dot(pgrad[:, : rank + 2 * n], low_w[: rank + 2 * n])
    )
    pre_grad[...] = conv_grad
    vec_o[n + 5 : n + 6] = jnp.sum(pre_g, axis=0, keepdims=True)
    vec_o[n + 6 : n + 7] = jnp.sum(sg[...] * conv_f, axis=0, keepdims=True)
    ready(inner, rim)
    taps = [jnp.zeros((1, width), F32) for _ in range(4)]
    bias = jnp.zeros((1, width), F32)
    spilled = []
    for b in range(batches):
        lo, hi = b * span, (b + 1) * span
        tap_rows(ext, rim[b], inner[lo:hi], width, span)
        grad_b = pre_grad[lo:hi] * silu_slope(conv_sum(ext, m[lo:hi], vec, n, span))
        bias = bias + jnp.sum(grad_b, axis=0, keepdims=True)
        taps[3] = taps[3] + jnp.sum(grad_b * ext[8 : 8 + span], axis=0, keepdims=True)
        for k in (1, 2, 3):
            taps[3 - k] = taps[3 - k] + jnp.sum(
                grad_b * (m[lo:hi, k : k + 1] * ext[8 - k : 8 - k + span]),
                axis=0, keepdims=True,
            )
        back = vec[n + 3 : n + 4] * grad_b
        spill = jnp.zeros((8, width), F32)
        for k in (1, 2, 3):
            ext[0:8] = jnp.zeros((8, width), F32)
            ext[8 : 8 + span] = vec[n + 3 - k : n + 4 - k] * (m[lo:hi, k : k + 1] * grad_b)
            ext[8 + span : 16 + span] = jnp.zeros((8, width), F32)
            back = back + ext[8 + k : 8 + k + span]
            spill = spill + ext[k : 8 + k]
        inner_o[lo:hi] = back.astype(BF16)
        tail_o[b] = back[span - 16 :]
        spill_o[b] = spill[5:8]
        if not with_out:
            pre_grad[lo:hi] = back
            spilled.append(
                jnp.where(lax.broadcasted_iota(jnp.int32, (8, width), 0) < 5, 0.0, spill)
            )
    leave(spill_o, inner_o, tail_o)
    if not with_out:
        turned_o[:, :rows_n] = pre_grad[...].T.astype(BF16)
        for b in range(batches):
            pre_grad[8 * b : 8 * b + 8] = spilled[b]
        pre_grad[8 * batches : rows_n] = jnp.zeros((rows_n - 8 * batches, width), F32)
        turned_o[:, rows_n:] = pre_grad[...].T.astype(BF16)
        leave(turned_o)
    for k in range(4):
        vec_o[n + k : n + k + 1] = taps[k]
    vec_o[n + 4 : n + 5] = bias


def norm_back(source, gain, grad):
    scale = lax.rsqrt(jnp.mean(source * source, axis=-1, keepdims=True) + EPS)
    unit = source * scale
    scaled = grad * gain
    along = jnp.mean(scaled * unit, axis=-1, keepdims=True)
    return scale * (scaled - unit * along), grad * unit


def turn_kernel(
    batches, span, width, rank, n, targets, layer,
    *refs,
):
    refs = list(refs)
    take = lambda k: [refs.pop(0) for _ in range(k)]
    inner, tail, spill, gate_grad, rows, gain, g, pair, vgrad, own_in, other_in = take(11)
    if layer:
        own_out, other_out, gate, proj, marks, low_w, vec, scanned = take(8)
    g_o, small_o = take(2)
    if layer:
        grad_o, gg_o, send_o, gate_o, gate_t_o = take(5)
    in_w, sem_in, mixed_grad, column = take(4)
    rows_n = batches * span
    if layer:
        seff, sg, cx, first, out_w, sem_out = take(6)
    arrival = fetch(layer, own_in, other_in, in_w, sem_in)
    if layer:
        arrival_out = fetch(0, own_out, other_out, out_w, sem_out)
    ready(tail, inner, spill)
    mixed_grad[:, :width] = inner[...]
    for b in range(batches):
        tail[b, 13:16] = tail[b, 13:16] + spill[b]
        hi = (b + 1) * span
        mixed_grad[hi - 16 : hi, :width] = tail[b].astype(BF16)
    ready(gate_grad)
    mixed_grad[:, width:] = gate_grad[...]
    if layer:
        grad_o[...] = mixed_grad[...].astype(F32).T.astype(BF16)
        leave(grad_o)
    ready(pair, vgrad)
    small_o[:, :LANES] = pair[...]
    arrival.wait()
    normed_grad = against(mixed_grad[...], in_w[...])
    ready(rows, g, gain)
    input_grad, terms = norm_back(rows[...].astype(F32), gain[...], normed_grad)
    g_new = (g[...].astype(F32) + input_grad).astype(BF16)
    g_o[...] = g_new
    leave(g_o)
    column[...] = jnp.concatenate(
        [vgrad[...], jnp.zeros((LANES - vgrad.held.shape[0], width), F32)], 0
    ).T
    sums = jnp.sum(terms.T, axis=1, keepdims=True)
    spot = lax.broadcasted_iota(jnp.int32, (1, LANES), 1) == n + 7
    part, block = sums.shape[0] // targets, width // targets
    for j in range(targets):
        rows_j = slice(j * block, j * block + part)
        column[rows_j] = jnp.where(spot, sums[j * part : (j + 1) * part], column[rows_j])
    small_o[:, LANES:] = column[...].astype(BF16)
    leave(small_o)
    if layer:
        arrival_out.wait()
        gg = against(g_new, out_w[...])
        gg_o[...] = gg
        leave(gg_o)
        ready(gate, proj, low_w, vec, marks)
        gate = gate[...].astype(F32)
        sg[...] = gg * jax.nn.silu(gate)
        step = softplus(step_sum(proj[...], low_w, vec, rank, n))
        seff[...] = step + marks[:, 0:1] * STOP
        spread_columns(proj[...].astype(F32).T, rank + n, cx)
        ready(scanned)
        gate_new = gg * scanned[...] * silu_slope(gate)
        gate_o[...] = gate_new.astype(BF16)
        gate_t_o[...] = gate_new.T.astype(BF16)
        leave(gate_o, gate_t_o)
        back_scan(batches, span, width // BLOCK, seff, sg, cx, vec.at[0:n], first)
        for b in range(batches):
            send_o[b * n : (b + 1) * n] = first[b].astype(BF16)


def by_core(groups, emit):
    if len(groups) == 1:
        emit(groups[0])
    else:
        for core, group in enumerate(groups):
            pl.when(lax.axis_index("section") == core)(functools.partial(emit, group))


def meet_kernel(groups, bit, lanes, *refs):
    goes, stays = refs[-2:]
    low, pairs = min(bit, goes.shape[0]), goes.shape[0]
    place = lax.axis_index("seq") // bit % 2

    def emit(group):
        left, left_got, right, right_got = group
        depth = left.shape[-1]
        first = 0 if lanes == right.shape[1] else lax.axis_index("section") * lanes
        columns = pl.ds(pl.multiple_of(first, LANES), lanes) if lanes != right.shape[1] else ...
        own = right[:depth, columns] if columns is not ... else right[:depth]
        got = right_got[:depth, columns] if columns is not ... else right_got[:depth]
        for which, out in ((1 - place, goes), (place, stays)):
            for k in range(pairs):
                source = (k // low * 2 + which) * low + k % low
                out[k] = (dot(left[source], own) + dot(left_got[source], got)).astype(BF16)

    by_core([refs[4 * i : 4 * i + 4] for i in range(groups)], emit)


def advance_kernel(plan, *refs):
    refs = list(refs)
    take = lambda k: [refs.pop(0) for _ in range(k)]
    ins = [[take(2) for _ in range(groups)] for groups, _ in plan]
    for groups, (_, bits) in zip(ins, plan):
        outs = take(2 if bits else 1)

        def emit(group, outs=outs, bits=bits):
            stayed, came = group
            if not bits:
                outs[0][...] = stayed[0].astype(F32) + came[0].astype(F32)
                return
            low = 1 << sorted(bits).index(bits[0])
            place = lax.axis_index("seq") // bits[0] % 2
            for which, out in ((1 - place, outs[0]), (place, outs[1])):
                for k in range(out.shape[0]):
                    source = (k // low * 2 + which) * low + k % low
                    out[k] = (stayed[source].astype(F32) + came[source].astype(F32)).astype(BF16)

        by_core(groups, emit)


DMA = pltpu.SemaphoreType.DMA


def expected(us):
    return pl.CostEstimate(
        flops=int(us * 3e8), bytes_accessed=int(us * 1e6), transcendentals=0
    )


def run(kernel, us, outs, scratch, args, far, far_out, elsewhere=(), others=(), limit=None):
    others = dict(others)
    whole_args = list(args) + list(others.values())
    far = tuple(far) + tuple(i for i in range(len(args)) if i not in far and i not in elsewhere)
    passing = [(args[i].shape, args[i].dtype) for i in far] + [outs[i] for i in far_out]
    count = len(passing)

    def whole(*refs):
        refs = list(refs)
        ins, refs = refs[: len(args)], refs[len(args) :]
        second, refs = dict(zip(others, refs)), refs[len(others) :]
        results, rest = refs[: len(outs)], refs[len(outs) :]
        own, buffers, sems = rest[: len(scratch)], rest[len(scratch) : -1], rest[-1]
        for k, i in enumerate(far):
            ins[i] = Arriving(ins[i], buffers[k], sems.at[k], second.get(i))
        for k, i in enumerate(far_out, len(far)):
            results[i] = Leaving(results[i], buffers[k], sems.at[k])
        kernel(*ins, *results, *own)
        ready(*ins)
        leave(*results)
        for ref in results:
            if isinstance(ref, Leaving):
                ref.copy.wait()

    return pl.pallas_call(
        whole,
        out_shape=[jax.ShapeDtypeStruct(*o) for o in outs],
        in_specs=[pl.BlockSpec(memory_space=pl.ANY)] * len(whole_args),
        out_specs=[
            pl.BlockSpec(memory_space=pl.ANY if i in far_out else pltpu.VMEM)
            for i in range(len(outs))
        ],
        scratch_shapes=[s if not isinstance(s, tuple) else pltpu.VMEM(*s) for s in scratch]
        + [pltpu.VMEM(*p) for p in passing]
        + [DMA((count,))],
        compiler_params=pltpu.CompilerParams(vmem_limit_bytes=limit or VMEM_LIMIT),
        cost_estimate=expected(us),
    )(*whole_args)


def hop(batches, n, steps, at, own=(), own_b=(), totals=None, both=False):
    messages = list(own) + list(own_b)
    args = [at] + ([] if own else [totals]) + messages
    return pl.pallas_call(
        functools.partial(hop_kernel, batches, n, steps, bool(own), both or bool(own_b)),
        out_shape=jax.ShapeDtypeStruct(messages[0].shape, BF16),
        in_specs=[pl.BlockSpec(memory_space=pltpu.VMEM)] * len(args),
        out_specs=pl.BlockSpec(memory_space=pltpu.VMEM),
        compiler_params=pltpu.CompilerParams(vmem_limit_bytes=HOP_LIMIT),
        cost_estimate=expected(1),
    )(*args)


def near(kernel, us, outs, args):
    return pl.pallas_call(
        kernel,
        out_shape=[jax.ShapeDtypeStruct(*o) for o in outs],
        in_specs=[pl.BlockSpec(memory_space=pltpu.VMEM)] * len(args),
        out_specs=[pl.BlockSpec(memory_space=pltpu.VMEM)] * len(outs),
        compiler_params=pltpu.CompilerParams(vmem_limit_bytes=NEAR_LIMIT),
        cost_estimate=expected(us),
    )(*args)


def meet(groups, bit, targets, lanes):
    args = []
    for left, left_got, right, right_got in groups:
        shape = (targets, left.shape[0] // targets, left.shape[1])
        args += [left.reshape(shape), left_got.reshape(shape), right, right_got]
    out = ((targets // 2, args[0].shape[1], lanes), BF16)
    return near(functools.partial(meet_kernel, len(groups), bit, lanes), 3, [out] * 2, args)


def advance(streams):
    outs, args, plan = [], [], []
    for groups, bits in streams:
        for group in groups:
            args += group
        count, *block = groups[0][0].shape
        outs += [((count // 2, *block), BF16)] * 2 if bits else [(tuple(block), F32)]
        plan.append((len(groups), tuple(bits)))
    results = list(near(functools.partial(advance_kernel, plan), 2, outs, args))
    return [tuple(results.pop(0) for _ in range(2 if bits else 1)) for _, bits in streams]


def flip(array, axis, bit):
    count = lax.axis_size(axis)
    return lax.ppermute(array, axis, [(i, i ^ bit) for i in range(count)])


def shifted(array, by):
    count = lax.axis_size("seq")
    pairs = [(i, i + by) for i in range(count) if 0 <= i + by < count]
    return lax.ppermute(array, "seq", pairs)


def tie(*arrays):
    return lax.optimization_barrier(arrays)


def bits_of(count):
    bits = [1 << k for k in range(count.bit_length() - 1)]
    assert 1 << len(bits) == count
    return bits


def swapped(bits):
    return [bits[1], bits[0]] + list(bits[2:]) if len(bits) > 1 else list(bits)


def pick(array, index, axis):
    return lax.dynamic_index_in_dim(array, index, axis, keepdims=False)


def local(
    tokens, starts, norm_gain, in_weight, conv_weight, conv_bias, xproj_weight,
    dtproj_weight, dt_bias, decay_rate, skip_gain, out_weight, cotangent,
):
    core = lax.axis_index("section")
    place = lax.axis_index("seq")
    cores = lax.axis_size("section")
    count = lax.axis_size("seq")
    bits = bits_of(count)
    batch_count, span, model = tokens.shape
    width = conv_weight.shape[2]
    n = decay_rate.shape[2]
    rank = dtproj_weight.shape[1]
    x_width = xproj_weight.shape[2]
    batches = batch_count // cores
    rows_n = batches * span
    half_model = model // 2
    low_core = core == 0
    steps = len(bits)

    def mine(array):
        return lax.dynamic_slice_in_dim(array, core * batches, batches, 0).reshape(
            (rows_n,) + array.shape[2:]
        )

    rows0 = mine(tokens)
    top = mine(cotangent)
    r = lax.dynamic_slice_in_dim(starts, core * batches, batches, 0).astype(F32)
    r_ext = jnp.concatenate([shifted(r[:, -3:].astype(BF16), 1).astype(F32), r], 1)
    free = 1.0 - r_ext
    m1 = free[:, 3:]
    m2 = m1 * free[:, 2:-1]
    m3 = m2 * free[:, 1:-2]
    marks = jnp.stack([r, m1, m2, m3], -1).reshape(rows_n, 4)

    tall = ((rows_n, width), F32)
    low_tall = ((rows_n, width), BF16)
    rim_s = ((batches, 3, width), F32)
    own_gain = norm_gain[0][None]
    in_own, out_own = in_weight[0], out_weight[0]

    vec_own = jnp.concatenate(
        [
            decay_rate[0].T * -LOG2E, conv_weight[0], conv_bias[0][None], dt_bias[0][None],
            skip_gain[0][None], jnp.pad(own_gain, ((0, 0), (0, width - model))),
        ],
        0,
    )
    low_own = jnp.concatenate([xproj_weight[0].T, dtproj_weight[0]], 0)
    vec_other, low_other = flip(vec_own, "section", 1), flip(low_own, "section", 1)

    in_a, in_b, gate_a, gate_b, tail_a, tail_b = run(
        functools.partial(enter_kernel, batches, span, width), 5,
        [low_tall] * 4 + [rim_s] * 2,
        [((cores * rows_n, model), BF16), ((4, model, 2 * width // 4), BF16), DMA((4,))],
        [tokens.reshape(batch_count * span, model), own_gain, in_own],
        far=(0, 1), far_out=range(6), elsewhere=(2,),
    )
    in_a, in_b, gate_a, gate_b, tail_a, tail_b, vec_other, low_other, marks = tie(
        in_a, in_b, gate_a, gate_b, tail_a, tail_b, vec_other, low_other, marks
    )
    in_got = lax.ppermute(in_b, "section", [(0, 1)])
    everywhere = ("section", "seq")
    rim_a = lax.ppermute(tail_a, everywhere, [(i, i + 1) for i in range(count - 1)])
    rim_b = lax.ppermute(tail_b, everywhere, [(i, count + i + 1) for i in range(count - 1)])
    gate_got = lax.ppermute(gate_b, "section", [(0, 1)])

    out_now, in_now, _, _, _ = tie(out_own, in_own, in_got, rim_a, rim_b)
    out_other, in_other = flip(out_now, "section", 1), flip(in_now, "section", 1)
    vecs = [jnp.where(low_core == (l == 0), vec_own, vec_other) for l in range(2)]
    lows = [jnp.where(low_core == (l == 0), low_own, low_other) for l in range(2)]
    gains = [v[n + 7 :, :model] for v in vecs]
    in0, gate0 = jnp.where(low_core, in_a, in_got), jnp.where(low_core, gate_a, gate_got)
    rim0 = jnp.where(low_core, rim_a, rim_b)

    spread = ((rows_n, n, LANES), F32)
    state = ((batches, n, width), F32)
    flat_in = ((model, 2 * width), BF16)
    flat_out = ((width, model), BF16)
    send_s = ((batches * n + 16, width), BF16)
    send_back_s = ((batches * n, width), BF16)
    both_s = ((2 * batches * n + 16, width), BF16)
    tall_t = ((width, rows_n), BF16)
    narrow = ((rows_n, model), BF16)

    totals_s = ((-(-batches * (steps + 1) // 8) * 8, width), F32)

    def front(layer, inner, rim, vec, low, *rest, others=()):
        outs = [low_tall, ((rows_n, LANES), BF16), both_s if layer else send_s]
        scratch = [((span + 8, width), F32), tall, tall, spread, spread, state]
        args = [inner, rim, marks, vec, low, *rest]
        if layer:
            scratch += [tall, flat_out, DMA]
        return run(
            functools.partial(front_kernel, batches, span, width, rank, n, bool(layer)),
            10 if layer else 6, outs, scratch, args, far=(2, 3, 1, 0, 4),
            far_out=range(len(outs)), elsewhere=(7, 8) if layer else (), others=others,
        )

    conv0, proj0, send = front(
        0, in_a, rim_a, vec_own, low_own,
        others=((0, in_got), (1, rim_b), (3, vec_other), (4, low_other)),
    )
    at0, at1 = vecs[0][:n], vecs[1][:n]
    own = [send]
    for k, bit in enumerate(bits):
        own.append(flip(send, "seq", bit))
        if k < steps - 1:
            send = hop(batches, n, k + 1, at0, own)
    scanned0, gated_t0, rows1, normed0, normed1, in1, gate1, before0, totals0, tail1 = run(
        functools.partial(end_kernel, batches, span, width, rank, n, steps), 10,
        [tall, tall_t, narrow, narrow, narrow, low_tall, low_tall, state, totals_s, ((batches, 6, width), F32)],
        [tall, tall, spread, spread, flat_out, flat_in, DMA((2,))],
        [gate0, conv0, proj0, marks, vecs[0], lows[0], rows0, gains[1], gains[0],
         out_own, out_other, in_own, in_other, *own],
        far=(6, 8, 2, 5, 4, 3, 1, *range(13, 14 + steps), 0), far_out=range(10),
        elsewhere=(9, 10, 11, 12),
    )

    rims = shifted(tail1, 1)
    rim1 = rims[:, :3]
    conv1, proj1, send = front(
        1, in1, rim1, vecs[1], lows[1], gate1, top, out_own, out_other
    )
    rim = rims[:, 3:, :model].astype(BF16)
    rim = jnp.pad(rim, ((0, 0), (5, 0), (0, 0))).reshape(8 * batches, model)
    normed_ext = jnp.concatenate(
        [normed0, rim, jnp.zeros((rows_n - 8 * batches, model), BF16)], 0
    )
    ext_got, normed_got = flip(normed_ext, "section", 1), flip(normed1, "section", 1)
    own = [send]
    for k, bit in enumerate(bits):
        own.append(flip(send, "seq", bit))
        if k < steps - 1:
            send = hop(batches, n, k + 1, at1, own, both=True)

    def back(layer, gg, conv, inner, gate, rim, proj, *rest):
        outs = [
            low_tall, ((batches, 16, width), F32), ((batches, 3, width), F32),
            ((width, LANES), BF16), ((n + 8, width), F32),
        ]
        scratch = [
            tall, tall, ((batches, span + 1, n, BLOCK), F32), ((batches, span, n, BLOCK), F32),
            tall, tall, spread, spread, ((span + 16, width), F32), tall,
            spread, spread, tall, state, state,
        ]
        if layer:
            outs += [low_tall, tall_t, narrow]
            scratch += [tall, tall, flat_out, DMA]
            far = (8, 7, 6, 5, 1, 0, 3, *range(12, 12 + steps))
        else:
            outs += [((width, 2 * rows_n), BF16)]
            far = (8, 7, 6, 5, 1, 0, 3, *range(9, 11 + steps))
        return run(
            functools.partial(
                back_kernel, batches, span, width, rank, n, x_width, steps, bool(layer)
            ),
            22 if layer else 19, outs, scratch,
            [gg, conv, inner, gate, rim, marks, vecs[layer], lows[layer], proj, *rest],
            far=far, far_out=range(len(outs)),
            elsewhere=(10, 11) if layer else (),
        )

    inner1, last1, spill1, pair1, vgrad1, gate_grad1, gated_t1, out1 = back(
        1, top, conv1, in1, gate1, rim1, proj1, rows1, out_own, out_other, *own[1:]
    )
    got1 = shifted(spill1, -1)

    def turn(layer, inner, tail, spill, gate_grad, rows, g, pair, vgrad, *rest):
        outs = [narrow, ((width, 2 * LANES), BF16)]
        scratch = [flat_in, DMA, ((rows_n, 2 * width), BF16), ((width, LANES), F32)]
        args = [
            inner, tail, spill, gate_grad, rows, gains[layer], g, pair, vgrad, in_own, in_other,
            *rest,
        ]
        elsewhere, far, far_out = [9, 10], [1, 2, 0, 3, 4, 6], [0, 1]
        if layer:
            outs += [((2 * width, rows_n), BF16), tall, send_back_s, low_tall, tall_t]
            scratch += [tall, tall, spread, state, flat_out, DMA]
            elsewhere += [11, 12]
            far += [13, 14, 18]
            far_out += [2, 3, 4, 5, 6]
        return run(
            functools.partial(turn_kernel, batches, span, width, rank, n, count, layer),
            11 if layer else 5, outs, scratch, args, far=far, far_out=far_out,
            elsewhere=elsewhere, limit=None if layer else TURN_LIMIT,
        )

    g0, small1, grad_t1, gg0, send_b, gate_grad0, gate_t0 = turn(
        1, inner1, last1, got1, gate_grad1, rows1, top, pair1, vgrad1, out_own, out_other,
        gate0, proj0,
        marks, lows[0], vecs[0], scanned0,
    )

    first_b = flip(send_b, "seq", bits[0])
    first_b, grad_t1, gate_t0, g0, gated_t0, gated_t1 = tie(
        first_b, grad_t1, gate_t0, g0, gated_t0, gated_t1
    )

    x_bit, y_bit, z_bit = bits[0], bits[1], bits[-2]
    one_way = lambda array, a, b: lax.ppermute(array, "section", [(a, b)])
    def half(array, which):
        return lax.dynamic_slice_in_dim(array, which * half_model, half_model, 1)

    def together(left, left_got, right, right_got):
        return dot(
            jnp.concatenate([left, left_got], 1), jnp.concatenate([right, right_got], 0)
        ).astype(BF16)

    def part(total, bit, order):
        axis = len(order) - 1 - sorted(order).index(bit)
        total = total.reshape((2,) * len(order) + (-1, total.shape[-1]))
        mine = (place // bit) % 2
        block = (total.shape[-2], total.shape[-1])
        return (
            pick(total, 1 - mine, axis).reshape((-1, *block)),
            pick(total, mine, axis).reshape((-1, *block)),
        )

    gated_got = flip(jnp.where(low_core, gated_t1, gated_t0), "section", 1)
    gated_own = jnp.where(low_core, gated_t0, gated_t1)
    g_got = flip(jnp.where(low_core, top, g0), "section", 1)
    grad_got, gate_got0 = flip(grad_t1, "section", 1), flip(gate_t0, "section", 1)

    own_b = [send_b]
    for k, bit in enumerate(bits):
        got_b = flip(send_b, "seq", bit) if k else first_b
        if k == 1:
            a = together(grad_t1, grad_got, half(normed1, core), half(normed_got, core))
            b = together(gated_own, gated_got, jnp.where(low_core, g0, top), g_got)
            c = together(
                gate_t0, gate_got0, half(normed0, core), half(ext_got[:rows_n], core)
            )
            a_goes, a_stays = part(a, x_bit, bits)
            b_goes, b_stays = part(b, y_bit, bits)
            c_goes, c_stays = part(c, z_bit, bits[:-1])
            got_b, a_goes, b_goes = tie(got_b, a_goes, b_goes)
        if k == steps - 1:
            got_b, a_goes, b_goes, c_goes = tie(got_b, a_goes, b_goes, c_goes)
            a_got, b_got = flip(a_goes, "seq", x_bit), flip(b_goes, "seq", y_bit)
            c_got = flip(c_goes, "seq", z_bit)
            small_up = one_way(small1, 0, 1)
        own_b.append(got_b)
        if k < steps - 1:
            send_b = hop(batches, n, k + 1, at0, (), own_b, totals0)
    inner0, tail0, spill0, pair0, vgrad0, turned0 = back(
        0, gg0, conv0, in0, gate0, rim0, proj0, before0, totals0, *own_b[1:]
    )
    inner0, tail0, spill0, pair0, vgrad0, turned0, a_got, b_got, c_got, small_up = tie(
        inner0, tail0, spill0, pair0, vgrad0, turned0, a_got, b_got, c_got, small_up
    )
    got0 = shifted(spill0, -1)
    turned_got = flip(turned0, "section", 1)

    middle = bits[2:-2]
    blocks = lambda array: array.reshape(count, -1, array.shape[-1])
    held = {"a": [(a_stays, a_got)], "b": [(b_stays, b_got)], "c": [(c_stays, c_got)]}
    todo = {
        "d": [x_bit, y_bit, *middle, z_bit],
        "a": [y_bit, *middle, z_bit, bits[-1]],
        "b": [z_bit, x_bit, *middle, bits[-1]],
        "c": [x_bit, y_bit, *middle],
    }
    parts = dict(zip("ab", advance([(held[k], todo[k]) for k in "ab"])))
    parts["d"] = meet(
        [(turned0, turned_got, normed_ext, ext_got)], x_bit, count // 2, half_model
    )
    first = [parts[k][0] for k in "dab"]
    got0, inner0, tail0, pair0, vgrad0, *first = tie(got0, inner0, tail0, pair0, vgrad0, *first)
    gots = [flip(goes, "seq", todo[k][0]) for k, goes in zip("dab", first)]
    dx, small0 = turn(0, inner0, tail0, got0, gate_grad0, rows0, g0, pair0, vgrad0)
    *gots, dx, small0 = tie(*gots, dx, small0)
    for k, got in zip("dab", gots):
        held[k] = [(parts[k][1], got)]
        todo[k] = todo[k][1:]
    small_down = one_way(small0, 1, 0)
    late = {
        "small": (
            [(blocks(small0), blocks(small_down)), (blocks(small1), blocks(small_up))],
            [y_bit, x_bit, *middle, z_bit, bits[-1]],
        )
    }
    while any(todo.values()):
        names = [k for k in todo if todo[k]]
        parts = dict(zip(names, advance([(held[k], todo[k]) for k in names])))
        gots = [flip(parts[k][0], "seq", todo[k][0]) for k in names]
        for k in late:
            held[k], todo[k] = late[k]
            parts.update(zip([k], advance([late[k]])))
            names.append(k)
            gots.append(flip(parts[k][0], "seq", todo[k][0]))
        late = {}
        gots = tie(*gots)
        for k, got in zip(names, gots):
            held[k] = [(parts[k][1], got)]
            todo[k] = todo[k][1:]
        if not todo["d"] and not todo["c"] and "d" in parts:
            c, d = (t.astype(BF16) for (t,) in advance([(held[k], []) for k in "cd"]))
            top_half = place >= count // 2
            swap_sent = jnp.where(top_half, d, c)
            swap_got = flip(swap_sent, "seq", bits[-1])
    in_sum1, out_sum, small = (
        total for (total,) in advance([(held[k], []) for k in ("a", "b", "small")])
    )
    in_sum0 = jnp.where(top_half, c, d).astype(F32) + swap_got.astype(F32)

    got = flip(jnp.where(low_core, in_sum1, in_sum0).astype(BF16), "section", 1).astype(F32)
    grad_in = jnp.where(
        low_core, jnp.concatenate([in_sum0, got], 1), jnp.concatenate([got, in_sum1], 1)
    )
    got = flip(jnp.where(low_core, out1, dx), "section", 1)
    boundary = jnp.where(
        low_core, jnp.concatenate([dx, got], 0), jnp.concatenate([got, out1], 0)
    ).reshape(1, batch_count, span, model)
    vec_sum = small[:, LANES : LANES + n + 8].T
    gain = vec_sum[n + 7 :, : model // count]
    return (
        boundary,
        gain,
        grad_in.T[None],
        vec_sum[n : n + 4][None],
        vec_sum[n + 4 : n + 5],
        small[:, :x_width][None],
        small[:, x_width:LANES].T[None],
        vec_sum[n + 5 : n + 6],
        small[:, LANES : LANES + n][None],
        vec_sum[n + 6 : n + 7],
        out_sum[None],
    )


def solution(mesh):
    in_specs = (
        P(None, "seq", None), P(None, "seq"), P("section", None), P("section", None, None),
        P("section", None, None), P("section", None), P("section", None, None),
        P("section", None, None), P("section", None), P("section", None, None),
        P("section", None), P("section", None, None), P(None, "seq", None),
    )
    out_specs = (
        P("section", None, "seq", None), P("section", "seq"), P("section", None, "seq"),
        P("section", None, "seq"), P("section", "seq"), P("section", "seq", None),
        P("section", None, "seq"), P("section", "seq"), P("section", "seq", None),
        P("section", "seq"), P("section", "seq", None),
    )
    return jax.shard_map(local, mesh=mesh, in_specs=in_specs, out_specs=out_specs, check_vma=False)
```

```python
import functools
import jax
import jax.numpy as jnp
from jax import lax
from jax.experimental import pallas as pl
from jax.experimental.pallas import tpu as pltpu
from jax.sharding import PartitionSpec as P

EPS = 1e-05
LOG2E = 1.4426950408889634
STOP = 1e7
LANES = 128
BLOCK = 512
TILES = BLOCK // LANES
F32 = jnp.float32
BF16 = jnp.bfloat16
VMEM_LIMIT = 58 * 1024 * 1024
HOP_LIMIT = 6 * 1024 * 1024
NEAR_LIMIT = 24 * 1024 * 1024
TURN_LIMIT = 58 * 1024 * 1024


def dot(left, right):
    return jnp.dot(left, right, preferred_element_type=F32)


def across(left, right):
    return lax.dot_general(left, right, (((0,), (0,)), ((), ())), preferred_element_type=F32)


def against(left, right):
    return lax.dot_general(left, right, (((1,), (1,)), ((), ())), preferred_element_type=F32)


def norm_rows(source, gain_row):
    return source * lax.rsqrt(jnp.mean(source * source, axis=-1, keepdims=True) + EPS) * gain_row


def softplus(v):
    return jnp.maximum(v, 0.0) + jnp.log1p(jnp.exp(-jnp.abs(v)))


def silu_slope(v):
    gate = jax.nn.sigmoid(v)
    return gate * (1.0 + v * (1.0 - gate))


def pair_up(left, right, row_ids, width):
    mask = (row_ids % (2 * width)) < width
    kept = jnp.where(mask, left, right)
    moved = jnp.where(mask, right, left)
    return kept + pltpu.roll(moved, 8 - width, 0)


def fold_rows(parts, row_ids):
    width = 1
    while len(parts) > 1:
        parts = [
            pair_up(parts[i], parts[i + 1], row_ids, width) for i in range(0, len(parts), 2)
        ]
        width *= 2
    return parts[0]


def halves(v):
    return v[:8] + v[8:]


def spread_columns(table, first, target):
    width = target.shape[1]
    for t in range(target.shape[0]):
        column = table[first : first + width, t : t + 1]
        target[t] = jnp.broadcast_to(column, (width, LANES))


def block_at(i):
    return pl.ds(pl.multiple_of(i * BLOCK, BLOCK), BLOCK)


def tile_at(i, lt):
    return pl.ds(pl.multiple_of(i * BLOCK + lt * LANES, LANES), LANES)


def local_scan(batches, span, blocks, seff, x, bx, at, final):
    def over_block(i, carry):
        rate = [at[:, tile_at(i, lt)] for lt in range(TILES)]

        def chunk(tc, states):
            states = list(states)
            for b in range(batches):
                rows = pl.ds(pl.multiple_of(b * span + tc * 8, 8), 8)
                for lt in range(TILES):
                    s8 = seff[rows, tile_at(i, lt)]
                    x8 = x[rows, tile_at(i, lt)]
                    h = states[b * TILES + lt]
                    for j in range(8):
                        decay = jnp.exp2(s8[j : j + 1] * rate[lt])
                        h = decay * h + x8[j : j + 1] * bx[b * span + tc * 8 + j]
                    states[b * TILES + lt] = h
            return tuple(states)

        zero = jnp.zeros((at.shape[0], LANES), F32)
        states = lax.fori_loop(0, span // 8, chunk, (zero,) * (batches * TILES))
        for b in range(batches):
            for lt in range(TILES):
                final[b, :, tile_at(i, lt)] = states[b * TILES + lt]
        return carry

    lax.fori_loop(0, blocks, over_block, 0)


def back_scan(batches, span, blocks, seff, sg, cx, at, first):
    chunks = span // 8

    def over_block(i, carry):
        rate = [at[:, tile_at(i, lt)] for lt in range(TILES)]

        def chunk(k, states):
            states = list(states)
            tc = chunks - 1 - k
            for b in range(batches):
                rows = pl.ds(pl.multiple_of(b * span + tc * 8, 8), 8)
                for lt in range(TILES):
                    s8 = seff[rows, tile_at(i, lt)]
                    g8 = sg[rows, tile_at(i, lt)]
                    q = states[b * TILES + lt]
                    for j in range(7, -1, -1):
                        decay = jnp.exp2(s8[j : j + 1] * rate[lt])
                        q = decay * (q + g8[j : j + 1] * cx[b * span + tc * 8 + j])
                    states[b * TILES + lt] = q
            return tuple(states)

        zero = jnp.zeros((at.shape[0], LANES), F32)
        states = lax.fori_loop(0, chunks, chunk, (zero,) * (batches * TILES))
        for b in range(batches):
            for lt in range(TILES):
                first[b, :, tile_at(i, lt)] = states[b * TILES + lt]
        return carry

    lax.fori_loop(0, blocks, over_block, 0)


class Arriving:
    def __init__(self, source, held, sem, other=None):
        self.held, self.waited = held, False
        if other is None:
            self.copy = pltpu.make_async_copy(source, held, sem)
            self.copy.start()
        else:
            self.copy = fetch(0, source, other, held, sem)

    def __getitem__(self, where):
        assert self.waited
        return self.held[where]

    def __setitem__(self, where, value):
        assert self.waited
        self.held[where] = value

    @property
    def at(self):
        return self.held.at


class Leaving:
    def __init__(self, target, held, sem):
        self.copy, self.held, self.started = pltpu.make_async_copy(held, target, sem), held, False

    def __getitem__(self, where):
        return self.held[where]

    def __setitem__(self, where, value):
        self.held[where] = value


def uppers_of(steps):
    place = lax.axis_index("seq")
    return [(place // (1 << k)) % 2 != 0 for k in range(steps)]


def ready(*refs):
    for ref in refs:
        if isinstance(ref, Arriving) and not ref.waited:
            ref.copy.wait()
            ref.waited = True


def leave(*refs):
    for ref in refs:
        if isinstance(ref, Leaving) and not ref.started:
            ref.copy.start()
            ref.started = True


def fetch(layer, own, other, held, sem):
    mine = lax.axis_index("section") == layer

    @pl.when(mine)
    def _():
        pltpu.make_async_copy(own, held, sem).start()

    @pl.when(jnp.logical_not(mine))
    def _():
        pltpu.make_async_copy(other, held, sem).start()

    return pltpu.make_async_copy(own, held, sem)


def split_total(totals):
    width = totals[0].shape[1]
    row_ids = lax.broadcasted_iota(jnp.int32, (16, width), 0)
    block = jnp.zeros((16, width), F32)
    for b, total in enumerate(totals):
        rest = total
        for k in range(3):
            part = rest.astype(BF16).astype(F32)
            block = jnp.where(row_ids == 3 * b + k, part, block)
            rest = rest - part
    return block.astype(BF16)


def join_total(block, b):
    block = block.astype(F32)
    return block[3 * b : 3 * b + 1] + block[3 * b + 1 : 3 * b + 2] + block[3 * b + 2 : 3 * b + 3]


def enter_kernel(
    batches, span, width,
    rows, gain, in_w,
    in_a_o, in_b_o, gate_a_o, gate_b_o, tail_a_o, tail_b_o,
    normed, held, sems,
):
    chunk = held.shape[2]
    copies = [
        pltpu.make_async_copy(in_w.at[:, pl.ds(c * chunk, chunk)], held.at[c], sems.at[c])
        for c in range(held.shape[0])
    ]
    for copy in copies:
        copy.start()
    ready(rows, gain)
    normed[...] = norm_rows(rows[...].astype(F32), gain[...]).astype(BF16)
    half = batches * span
    for c, copy in enumerate(copies):
        copy.wait()
        mixed = dot(normed[...], held[c])
        outs = (in_a_o, in_b_o) if c * chunk < width else (gate_a_o, gate_b_o)
        lanes = slice(c * chunk % width, c * chunk % width + chunk)
        for k, out in enumerate(outs):
            out[:, lanes] = mixed[k * half : (k + 1) * half].astype(BF16)
        if c * chunk < width:
            for k, tail in enumerate((tail_a_o, tail_b_o)):
                for b in range(batches):
                    last = k * half + (b + 1) * span
                    tail[b, :, lanes] = mixed[last - 3 : last].astype(BF16).astype(F32)
        if (c + 1) * chunk == width:
            leave(in_a_o, in_b_o, tail_a_o, tail_b_o)


def tap_rows(ext, rim, mixed, width, span):
    ext[5:8] = rim
    ext[8 : 8 + span] = mixed.astype(F32)


def conv_sum(ext, m, vec, n, span):
    v = vec[n + 4 : n + 5] + vec[n + 3 : n + 4] * ext[8 : 8 + span]
    for k in (1, 2, 3):
        v = v + vec[n + 3 - k : n + 4 - k] * (m[:, k : k + 1] * ext[8 - k : 8 - k + span])
    return v


def step_sum(proj, low_w, vec, rank, n):
    return dot(proj[:, :rank], low_w[rank + 2 * n :]) + vec[n + 5 : n + 6]


def front_kernel(
    batches, span, width, rank, states_n, with_back,
    *refs,
):
    refs = list(refs)
    mixed, rim, marks, vec, low_w = refs[:5]
    del refs[:5]
    if with_back:
        gate, g, own_w, other_w = refs[:4]
        del refs[:4]
    conv_o, proj_o, send_o = refs[:3]
    del refs[:3]
    if with_back:
        first = batches * states_n + 16
    ext, seff, x, bx, cx, final = refs[:6]
    if with_back:
        sg, out_w, sem = refs[6:]
        arrival = fetch(1, own_w, other_w, out_w, sem)
    n = states_n
    ready(rim, marks, vec)
    m = marks[...]
    at = vec.at[0:n]
    ready(mixed)
    for b in range(batches):
        lo, hi = b * span, (b + 1) * span
        tap_rows(ext, rim[b], mixed[lo:hi], width, span)
        x[lo:hi] = jax.nn.silu(conv_sum(ext, m[lo:hi], vec, n, span))
    conv = x[...].astype(BF16)
    conv_o[...] = conv
    leave(conv_o)
    ready(low_w)
    proj = against(conv, low_w[...]).astype(BF16)
    proj_o[...] = proj
    leave(proj_o)
    step = softplus(step_sum(proj, low_w, vec, rank, n))
    seff[...] = step + m[:, 0:1] * STOP
    x[...] = step * conv.astype(F32)
    totals = [
        jnp.sum(seff[b * span : (b + 1) * span], axis=0, keepdims=True) for b in range(batches)
    ]
    send_o[batches * n : batches * n + 16] = split_total(totals)
    table = proj.astype(F32).T
    spread_columns(table, rank, bx)
    local_scan(batches, span, width // BLOCK, seff, x, bx, at, final)
    for b in range(batches):
        send_o[b * n : (b + 1) * n] = final[b].astype(BF16)
    if not with_back:
        leave(send_o)
    if with_back:
        arrival.wait()
        spread_columns(table, rank + n, cx)
        ready(g, gate)
        gg = against(g[...], out_w[...])
        sg[...] = gg * jax.nn.silu(gate[...].astype(F32))
        back_scan(batches, span, width // BLOCK, seff, sg, cx, at, final)
        for b in range(batches):
            send_o[first + b * n : first + (b + 1) * n] = final[b].astype(BF16)


def merge(at, upper, mine, theirs, mine_total, their_total, backward):
    early, late = jnp.where(upper, theirs, mine), jnp.where(upper, mine, theirs)
    if backward:
        return jnp.exp2(jnp.where(upper, their_total, mine_total) * at) * late + early
    return jnp.exp2(jnp.where(upper, mine_total, their_total) * at) * early + late


def reach(at, n, b, uppers, gots, totals, backward, first=0):
    carry = jnp.zeros(at.shape, F32)
    span = jnp.zeros((1, at.shape[1]), F32)
    for upper, got, their_total in zip(uppers, gots, totals):
        comes = jnp.logical_not(upper) if backward else upper
        theirs = got[first + b * n : first + (b + 1) * n].astype(F32)
        carry = jnp.where(comes, jnp.exp2(span * at) * theirs + carry, carry)
        span = jnp.where(comes, span + their_total, span)
    return carry


def hop_kernel(batches, n, steps, forward, backward, *refs):
    refs = list(refs)
    take = lambda k: [refs.pop(0) for _ in range(k)]
    (at,) = take(1)
    at = at[...]
    if forward:
        own, *gots = take(1 + steps)
    else:
        (totals,) = take(1)
    first = 0
    if forward and backward:
        own_b, gots_b, first = own, gots, batches * n + 16
    elif backward:
        own_b, *gots_b = take(1 + steps)
    (send,) = take(1)
    uppers = uppers_of(steps)
    reached = []
    for b in range(batches):
        rows = slice(b * n, (b + 1) * n)
        if forward:
            total = join_total(own[batches * n : batches * n + 16], b)
            mine = own[rows].astype(F32)
        else:
            total = totals[b : b + 1]
        if backward:
            rows_b = slice(first + b * n, first + (b + 1) * n)
            mine_b = own_b[rows_b].astype(F32)
        for k, upper in enumerate(uppers):
            if forward:
                their_total = join_total(gots[k][batches * n : batches * n + 16], b)
                mine = merge(
                    at, upper, mine, gots[k][rows].astype(F32), total, their_total, False
                )
            else:
                their_total = totals[(k + 1) * batches + b : (k + 1) * batches + b + 1]
            if backward:
                mine_b = merge(
                    at, upper, mine_b, gots_b[k][rows_b].astype(F32), total, their_total, True
                )
            total = total + their_total
        if forward:
            send[rows] = mine.astype(BF16)
        if backward:
            send[rows_b] = mine_b.astype(BF16)
        reached.append(total)
    if forward:
        send[batches * n : batches * n + 16] = split_total(reached)


def prepare(step, marks, conv, seff, x):
    seff[...] = step + marks * STOP
    x[...] = step * conv.astype(F32)


def end_kernel(
    batches, span, width, rank, n, steps,
    gate, conv, proj, marks, vec, low_w, rows, gain, gain_before,
    own_out, other_out, own_in, other_in, own_send, *refs,
):
    gots, refs = refs[:steps], refs[steps:]
    (
        scanned_o, gated_t_o, rows_o, normed_before_o, normed_o, inner_o, gate_o, before_o,
        totals_o, tail_o, seff, x, bx, cx, out_w, in_w, sems,
    ) = refs

    arrivals = [
        fetch(0, own_out, other_out, out_w, sems.at[0]),
        fetch(1, own_in, other_in, in_w, sems.at[1]),
    ]
    blocks = width // BLOCK
    at = vec.at[0:n]
    ready(rows, gain_before, proj, low_w, vec, marks, conv)
    normed_before_o[...] = norm_rows(rows[...].astype(F32), gain_before[...]).astype(BF16)
    leave(normed_before_o)
    tail_o[...] = jnp.zeros((batches, 6, width), F32)
    for b in range(batches):
        last = normed_before_o[(b + 1) * span - 16 : (b + 1) * span].astype(F32)
        tail_o[b, 3:6, : last.shape[1]] = last[13:]
    step = softplus(step_sum(proj[...], low_w, vec, rank, n))
    prepare(step, marks[:, 0:1], conv[...], seff, x)
    table = proj[...].astype(F32).T
    spread_columns(table, rank, bx)
    spread_columns(table, rank + n, cx)
    ready(own_send, *gots)
    uppers = uppers_of(steps)
    for b in range(batches):
        totals_o[b : b + 1] = join_total(own_send[batches * n : batches * n + 16], b)
        theirs = [join_total(got[batches * n : batches * n + 16], b) for got in gots]
        for k, their in enumerate(theirs):
            totals_o[(k + 1) * batches + b : (k + 1) * batches + b + 1] = their
        before_o[b] = reach(at[...], n, b, uppers, gots, theirs, False)
    leave(before_o, totals_o)
    row_ids = lax.broadcasted_iota(jnp.int32, (8, LANES), 0)

    def over_block(i, carry):
        rate = [at[:, tile_at(i, lt)] for lt in range(TILES)]

        def chunk(tc, states):
            states = list(states)
            for b in range(batches):
                rows8 = pl.ds(pl.multiple_of(b * span + tc * 8, 8), 8)
                for lt in range(TILES):
                    s8 = seff[rows8, tile_at(i, lt)]
                    x8 = x[rows8, tile_at(i, lt)]
                    h = states[b * TILES + lt]
                    parts = []
                    for j in range(8):
                        t = b * span + tc * 8 + j
                        decay = jnp.exp2(s8[j : j + 1] * rate[lt])
                        h = decay * h + x8[j : j + 1] * bx[t]
                        parts.append(halves(h * cx[t]))
                    states[b * TILES + lt] = h
                    scanned_o[rows8, tile_at(i, lt)] = fold_rows(parts, row_ids)
            return tuple(states)

        start = tuple(
            before_o[b, :, tile_at(i, lt)] for b in range(batches) for lt in range(TILES)
        )
        lax.fori_loop(0, span // 8, chunk, start)
        return carry

    lax.fori_loop(0, blocks, over_block, 0)
    scanned = scanned_o[...] + vec[n + 6 : n + 7] * conv[...].astype(F32)
    scanned_o[...] = scanned
    leave(scanned_o)
    ready(gate)
    gated_f = scanned * jax.nn.silu(gate[...].astype(F32))
    gated = gated_f.astype(BF16)
    gated_t_o[...] = gated_f.T.astype(BF16)
    leave(gated_t_o)
    arrivals[0].wait()
    result = (rows[...].astype(F32) + dot(gated, out_w[...])).astype(BF16)
    rows_o[...] = result
    leave(rows_o)
    ready(gain)
    normed_o[...] = norm_rows(result.astype(F32), gain[...]).astype(BF16)
    leave(normed_o)
    arrivals[1].wait()
    for first, target in ((0, inner_o), (width, gate_o)):
        for c in range(0, width, 512):
            mixed = dot(normed_o[...], in_w[:, first + c : first + c + 512])
            target[:, c : c + 512] = mixed.astype(BF16)
            if not first:
                for b in range(batches):
                    last = (b + 1) * span
                    tail_o[b, 0:3, c : c + 512] = mixed[last - 3 : last].astype(BF16).astype(F32)
        leave(target, tail_o)


def back_kernel(
    batches, span, width, rank, n, x_width, steps, with_out,
    *refs,
):
    refs = list(refs)
    take = lambda k: [refs.pop(0) for _ in range(k)]
    gg, conv, inner, gate, rim, marks, vec, low_w, proj = take(9)
    if with_out:
        rows, own_out, other_out = take(3)
        gots = gots_b = take(steps)
    else:
        before, totals = take(2)
        gots_b = take(steps)
    inner_o, tail_o, spill_o, pair_o, vec_o = take(5)
    if with_out:
        gate_o, gated_t_o, out_o = take(3)
    else:
        (turned_o,) = take(1)
    seff, x, hist, decays, drive, zsum, acc_b, acc_c, ext, sg, bx, cx, pre_grad = take(13)
    state_in, grad_in = take(2)
    if with_out:
        scanned_ref, gg_s, out_w, sem = take(4)
        arrival = fetch(1, own_out, other_out, out_w, sem)
    blocks = width // BLOCK
    rows_n = batches * span
    chunks = span // 8
    ready(proj, low_w, vec, marks, conv)
    m = marks[...]
    at = vec.at[0:n]
    spre = step_sum(proj[...], low_w, vec, rank, n)
    prepare(softplus(spre), m[:, 0:1], conv[...], seff, x)
    table = proj[...].astype(F32).T
    spread_columns(table, rank, bx)
    spread_columns(table, rank + n, cx)
    ready(gg, gate)
    if with_out:
        arrival.wait()
        gg_s[...] = against(gg[...], out_w[...])
        gg = gg_s
    sg[...] = gg[...] * jax.nn.silu(gate[...].astype(F32))
    if with_out:
        ready(*gots)
    else:
        ready(before, totals)
    ready(*gots_b)
    uppers = uppers_of(steps)
    for b in range(batches):
        if with_out:
            theirs = [join_total(got[batches * n : batches * n + 16], b) for got in gots]
            state_in[b] = reach(at[...], n, b, uppers, gots, theirs, False)
        else:
            theirs = [
                totals[(k + 1) * batches + b : (k + 1) * batches + b + 1] for k in range(steps)
            ]
            state_in[b] = before[b]
        first = batches * n + 16 if with_out else 0
        grad_in[b] = reach(at[...], n, b, uppers, gots_b, theirs, True, first)
    acc_b[...] = jnp.zeros_like(acc_b)
    acc_c[...] = jnp.zeros_like(acc_c)
    vec_o[...] = jnp.zeros((n + 8, width), F32)
    row_ids = lax.broadcasted_iota(jnp.int32, (8, LANES), 0)

    def over_block(i, carry):
        rate = [at[:, tile_at(i, lt)] for lt in range(TILES)]

        def again(tc, states):
            states = list(states)
            for b in range(batches):
                rows8 = pl.ds(pl.multiple_of(b * span + tc * 8, 8), 8)
                for lt in range(TILES):
                    s8 = seff[rows8, tile_at(i, lt)]
                    x8 = x[rows8, tile_at(i, lt)]
                    h = states[b * TILES + lt]
                    lanes = pl.ds(lt * LANES, LANES)
                    parts = []
                    for j in range(8):
                        t = tc * 8 + j
                        decay = jnp.exp2(s8[j : j + 1] * rate[lt])
                        h = decay * h + x8[j : j + 1] * bx[b * span + t]
                        decays[b, t, :, lanes] = decay
                        hist[b, t + 1, :, lanes] = h
                        if with_out:
                            parts.append(halves(h * cx[b * span + t]))
                    states[b * TILES + lt] = h
                    if with_out:
                        scanned_ref[rows8, tile_at(i, lt)] = fold_rows(parts, row_ids)
            return tuple(states)

        for b in range(batches):
            hist[b, 0] = state_in[b, :, block_at(i)]
        start = tuple(
            state_in[b, :, tile_at(i, lt)] for b in range(batches) for lt in range(TILES)
        )
        lax.fori_loop(0, chunks, again, start)

        sums = tuple(jnp.zeros((n, LANES), F32) for _ in range(TILES))
        for b in range(batches):

            def chunk(k, held):
                held = list(held)
                tc = chunks - 1 - k
                rows8 = pl.ds(pl.multiple_of(b * span + tc * 8, 8), 8)
                s8, x8, g8 = [], [], []
                for lt in range(TILES):
                    s8.append(seff[rows8, tile_at(i, lt)])
                    x8.append(x[rows8, tile_at(i, lt)])
                    g8.append(sg[rows8, tile_at(i, lt)])
                drives = [[None] * 8 for _ in range(TILES)]
                zs = [[None] * 8 for _ in range(TILES)]
                for j in range(7, -1, -1):
                    t = tc * 8 + j
                    part_b, part_c = [], []
                    for lt in range(TILES):
                        lanes = pl.ds(lt * LANES, LANES)
                        total = held[lt] + g8[lt][j : j + 1] * cx[b * span + t]
                        q = decays[b, t, :, lanes] * total
                        log_grad = q * hist[b, t, :, lanes]
                        held[TILES + lt] = held[TILES + lt] + log_grad * s8[lt][j : j + 1]
                        zs[lt][j] = halves(log_grad * rate[lt])
                        drives[lt][j] = halves(total * bx[b * span + t])
                        part_b.append(total * x8[lt][j : j + 1])
                        part_c.append(g8[lt][j : j + 1] * hist[b, t + 1, :, lanes])
                        held[lt] = q
                    acc_b[b * span + t] += sum(part_b[1:], part_b[0])
                    acc_c[b * span + t] += sum(part_c[1:], part_c[0])
                for lt in range(TILES):
                    drive[rows8, tile_at(i, lt)] = fold_rows(drives[lt], row_ids)
                    zsum[rows8, tile_at(i, lt)] = fold_rows(zs[lt], row_ids)
                return tuple(held)

            start = tuple(grad_in[b, :, tile_at(i, lt)] for lt in range(TILES)) + sums
            sums = lax.fori_loop(0, chunks, chunk, start)[TILES:]
        for lt in range(TILES):
            vec_o[0:n, tile_at(i, lt)] = -sums[lt]
        return carry

    lax.fori_loop(0, blocks, over_block, 0)

    conv_f = conv[...].astype(F32)
    if with_out:
        ready(rows)
        gate = gate[...].astype(F32)
        scanned = scanned_ref[...] + vec[n + 6 : n + 7] * conv_f
        gated_f = scanned * jax.nn.silu(gate)
        gated_t_o[...] = gated_f.T.astype(BF16)
        out_o[...] = (rows[...].astype(F32) + dot(gated_f.astype(BF16), out_w[...])).astype(BF16)
        gate_o[...] = (gg_s[...] * scanned * silu_slope(gate)).astype(BF16)
        leave(gate_o, gated_t_o, out_o)

    ones = jnp.ones((LANES, LANES), BF16)
    table = (rows_n * n, LANES)
    at_n = lax.broadcasted_iota(jnp.int32, table, 0) % n
    lane = lax.broadcasted_iota(jnp.int32, table, 1)
    sums_b, sums_c = (
        dot(acc[...].reshape(table).astype(BF16), ones) for acc in (acc_b, acc_c)
    )
    placed = jnp.where(lane == rank + at_n, sums_b, 0.0)
    placed = placed + jnp.where(lane == rank + n + at_n, sums_c, 0.0)
    placed = jnp.sum(placed.reshape(rows_n, n, LANES), axis=1)
    spre = step_sum(proj[...], low_w, vec, rank, n)
    step = softplus(spre)
    step_grad = zsum[...] * (1.0 / LOG2E) + drive[...] * conv_f
    pre_g = step_grad * jax.nn.sigmoid(spre)
    low = pre_g.astype(BF16)
    low_grad = against(low, low_w[rank + 2 * n :])
    pgrad = (
        jnp.concatenate([low_grad, jnp.zeros((rows_n, LANES - rank), F32)], 1) + placed
    ).astype(BF16)
    small = dot(conv_f.T.astype(BF16), pgrad)
    lows = pltpu.roll(dot(pre_g.T.astype(BF16), proj[...]), x_width, 1)
    columns = lax.broadcasted_iota(jnp.int32, (1, LANES), 1)
    pair_o[...] = jnp.where(columns < x_width, small, lows).astype(BF16)
    leave(pair_o)
    conv_grad = (
        sg[...] * vec[n + 6 : n + 7] + step * drive[...]
        + dot(pgrad[:, : rank + 2 * n], low_w[: rank + 2 * n])
    )
    pre_grad[...] = conv_grad
    vec_o[n + 5 : n + 6] = jnp.sum(pre_g, axis=0, keepdims=True)
    vec_o[n + 6 : n + 7] = jnp.sum(sg[...] * conv_f, axis=0, keepdims=True)
    ready(inner, rim)
    taps = [jnp.zeros((1, width), F32) for _ in range(4)]
    bias = jnp.zeros((1, width), F32)
    spilled = []
    for b in range(batches):
        lo, hi = b * span, (b + 1) * span
        tap_rows(ext, rim[b], inner[lo:hi], width, span)
        grad_b = pre_grad[lo:hi] * silu_slope(conv_sum(ext, m[lo:hi], vec, n, span))
        bias = bias + jnp.sum(grad_b, axis=0, keepdims=True)
        taps[3] = taps[3] + jnp.sum(grad_b * ext[8 : 8 + span], axis=0, keepdims=True)
        for k in (1, 2, 3):
            taps[3 - k] = taps[3 - k] + jnp.sum(
                grad_b * (m[lo:hi, k : k + 1] * ext[8 - k : 8 - k + span]),
                axis=0, keepdims=True,
            )
        back = vec[n + 3 : n + 4] * grad_b
        spill = jnp.zeros((8, width), F32)
        for k in (1, 2, 3):
            ext[0:8] = jnp.zeros((8, width), F32)
            ext[8 : 8 + span] = vec[n + 3 - k : n + 4 - k] * (m[lo:hi, k : k + 1] * grad_b)
            ext[8 + span : 16 + span] = jnp.zeros((8, width), F32)
            back = back + ext[8 + k : 8 + k + span]
            spill = spill + ext[k : 8 + k]
        inner_o[lo:hi] = back.astype(BF16)
        tail_o[b] = back[span - 16 :]
        spill_o[b] = spill[5:8]
        if not with_out:
            pre_grad[lo:hi] = back
            spilled.append(
                jnp.where(lax.broadcasted_iota(jnp.int32, (8, width), 0) < 5, 0.0, spill)
            )
    leave(spill_o, inner_o, tail_o)
    if not with_out:
        turned_o[:, :rows_n] = pre_grad[...].T.astype(BF16)
        for b in range(batches):
            pre_grad[8 * b : 8 * b + 8] = spilled[b]
        pre_grad[8 * batches : rows_n] = jnp.zeros((rows_n - 8 * batches, width), F32)
        turned_o[:, rows_n:] = pre_grad[...].T.astype(BF16)
        leave(turned_o)
    for k in range(4):
        vec_o[n + k : n + k + 1] = taps[k]
    vec_o[n + 4 : n + 5] = bias


def norm_back(source, gain, grad):
    scale = lax.rsqrt(jnp.mean(source * source, axis=-1, keepdims=True) + EPS)
    unit = source * scale
    scaled = grad * gain
    along = jnp.mean(scaled * unit, axis=-1, keepdims=True)
    return scale * (scaled - unit * along), grad * unit


def turn_kernel(
    batches, span, width, rank, n, targets, layer,
    *refs,
):
    refs = list(refs)
    take = lambda k: [refs.pop(0) for _ in range(k)]
    inner, tail, spill, gate_grad, rows, gain, g, pair, vgrad, own_in, other_in = take(11)
    if layer:
        own_out, other_out, gate, proj, marks, low_w, vec, scanned = take(8)
    g_o, small_o = take(2)
    if layer:
        grad_o, gg_o, send_o, gate_o, gate_t_o = take(5)
    in_w, sem_in, mixed_grad, column = take(4)
    rows_n = batches * span
    if layer:
        seff, sg, cx, first, out_w, sem_out = take(6)
    arrival = fetch(layer, own_in, other_in, in_w, sem_in)
    if layer:
        arrival_out = fetch(0, own_out, other_out, out_w, sem_out)
    ready(tail, inner, spill)
    mixed_grad[:, :width] = inner[...]
    for b in range(batches):
        tail[b, 13:16] = tail[b, 13:16] + spill[b]
        hi = (b + 1) * span
        mixed_grad[hi - 16 : hi, :width] = tail[b].astype(BF16)
    ready(gate_grad)
    mixed_grad[:, width:] = gate_grad[...]
    if layer:
        grad_o[...] = mixed_grad[...].astype(F32).T.astype(BF16)
        leave(grad_o)
    ready(pair, vgrad)
    small_o[:, :LANES] = pair[...]
    arrival.wait()
    normed_grad = against(mixed_grad[...], in_w[...])
    ready(rows, g, gain)
    input_grad, terms = norm_back(rows[...].astype(F32), gain[...], normed_grad)
    g_new = (g[...].astype(F32) + input_grad).astype(BF16)
    g_o[...] = g_new
    leave(g_o)
    column[...] = jnp.concatenate(
        [vgrad[...], jnp.zeros((LANES - vgrad.held.shape[0], width), F32)], 0
    ).T
    sums = jnp.sum(terms.T, axis=1, keepdims=True)
    spot = lax.broadcasted_iota(jnp.int32, (1, LANES), 1) == n + 7
    part, block = sums.shape[0] // targets, width // targets
    for j in range(targets):
        rows_j = slice(j * block, j * block + part)
        column[rows_j] = jnp.where(spot, sums[j * part : (j + 1) * part], column[rows_j])
    small_o[:, LANES:] = column[...].astype(BF16)
    leave(small_o)
    if layer:
        arrival_out.wait()
        gg = against(g_new, out_w[...])
        gg_o[...] = gg
        leave(gg_o)
        ready(gate, proj, low_w, vec, marks)
        gate = gate[...].astype(F32)
        sg[...] = gg * jax.nn.silu(gate)
        step = softplus(step_sum(proj[...], low_w, vec, rank, n))
        seff[...] = step + marks[:, 0:1] * STOP
        spread_columns(proj[...].astype(F32).T, rank + n, cx)
        ready(scanned)
        gate_new = gg * scanned[...] * silu_slope(gate)
        gate_o[...] = gate_new.astype(BF16)
        gate_t_o[...] = gate_new.T.astype(BF16)
        leave(gate_o, gate_t_o)
        back_scan(batches, span, width // BLOCK, seff, sg, cx, vec.at[0:n], first)
        for b in range(batches):
            send_o[b * n : (b + 1) * n] = first[b].astype(BF16)


def by_core(groups, emit):
    if len(groups) == 1:
        emit(groups[0])
    else:
        for core, group in enumerate(groups):
            pl.when(lax.axis_index("section") == core)(functools.partial(emit, group))


def meet_kernel(groups, bit, lanes, *refs):
    goes, stays = refs[-2:]
    low, pairs = min(bit, goes.shape[0]), goes.shape[0]
    place = lax.axis_index("seq") // bit % 2

    def emit(group):
        left, left_got, right, right_got = group
        depth = left.shape[-1]
        first = 0 if lanes == right.shape[1] else lax.axis_index("section") * lanes
        columns = pl.ds(pl.multiple_of(first, LANES), lanes) if lanes != right.shape[1] else ...
        own = right[:depth, columns] if columns is not ... else right[:depth]
        got = right_got[:depth, columns] if columns is not ... else right_got[:depth]
        for which, out in ((1 - place, goes), (place, stays)):
            for k in range(pairs):
                source = (k // low * 2 + which) * low + k % low
                out[k] = (dot(left[source], own) + dot(left_got[source], got)).astype(BF16)

    by_core([refs[4 * i : 4 * i + 4] for i in range(groups)], emit)


def advance_kernel(plan, *refs):
    refs = list(refs)
    take = lambda k: [refs.pop(0) for _ in range(k)]
    ins = [[take(2) for _ in range(groups)] for groups, _ in plan]
    for groups, (_, bits) in zip(ins, plan):
        outs = take(2 if bits else 1)

        def emit(group, outs=outs, bits=bits):
            stayed, came = group
            if not bits:
                outs[0][...] = stayed[0].astype(F32) + came[0].astype(F32)
                return
            low = 1 << sorted(bits).index(bits[0])
            place = lax.axis_index("seq") // bits[0] % 2
            for which, out in ((1 - place, outs[0]), (place, outs[1])):
                for k in range(out.shape[0]):
                    source = (k // low * 2 + which) * low + k % low
                    out[k] = (stayed[source].astype(F32) + came[source].astype(F32)).astype(BF16)

        by_core(groups, emit)


DMA = pltpu.SemaphoreType.DMA


def expected(us):
    return pl.CostEstimate(
        flops=int(us * 3e8), bytes_accessed=int(us * 1e6), transcendentals=0
    )


def run(kernel, us, outs, scratch, args, far, far_out, elsewhere=(), others=(), limit=None):
    others = dict(others)
    whole_args = list(args) + list(others.values())
    far = tuple(far) + tuple(i for i in range(len(args)) if i not in far and i not in elsewhere)
    passing = [(args[i].shape, args[i].dtype) for i in far] + [outs[i] for i in far_out]
    count = len(passing)

    def whole(*refs):
        refs = list(refs)
        ins, refs = refs[: len(args)], refs[len(args) :]
        second, refs = dict(zip(others, refs)), refs[len(others) :]
        results, rest = refs[: len(outs)], refs[len(outs) :]
        own, buffers, sems = rest[: len(scratch)], rest[len(scratch) : -1], rest[-1]
        for k, i in enumerate(far):
            ins[i] = Arriving(ins[i], buffers[k], sems.at[k], second.get(i))
        for k, i in enumerate(far_out, len(far)):
            results[i] = Leaving(results[i], buffers[k], sems.at[k])
        kernel(*ins, *results, *own)
        ready(*ins)
        leave(*results)
        for ref in results:
            if isinstance(ref, Leaving):
                ref.copy.wait()

    return pl.pallas_call(
        whole,
        out_shape=[jax.ShapeDtypeStruct(*o) for o in outs],
        in_specs=[pl.BlockSpec(memory_space=pl.ANY)] * len(whole_args),
        out_specs=[
            pl.BlockSpec(memory_space=pl.ANY if i in far_out else pltpu.VMEM)
            for i in range(len(outs))
        ],
        scratch_shapes=[s if not isinstance(s, tuple) else pltpu.VMEM(*s) for s in scratch]
        + [pltpu.VMEM(*p) for p in passing]
        + [DMA((count,))],
        compiler_params=pltpu.CompilerParams(vmem_limit_bytes=limit or VMEM_LIMIT),
        cost_estimate=expected(us),
    )(*whole_args)


def hop(batches, n, steps, at, own=(), own_b=(), totals=None, both=False):
    messages = list(own) + list(own_b)
    args = [at] + ([] if own else [totals]) + messages
    return pl.pallas_call(
        functools.partial(hop_kernel, batches, n, steps, bool(own), both or bool(own_b)),
        out_shape=jax.ShapeDtypeStruct(messages[0].shape, BF16),
        in_specs=[pl.BlockSpec(memory_space=pltpu.VMEM)] * len(args),
        out_specs=pl.BlockSpec(memory_space=pltpu.VMEM),
        compiler_params=pltpu.CompilerParams(vmem_limit_bytes=HOP_LIMIT),
        cost_estimate=expected(1),
    )(*args)


def near(kernel, us, outs, args):
    return pl.pallas_call(
        kernel,
        out_shape=[jax.ShapeDtypeStruct(*o) for o in outs],
        in_specs=[pl.BlockSpec(memory_space=pltpu.VMEM)] * len(args),
        out_specs=[pl.BlockSpec(memory_space=pltpu.VMEM)] * len(outs),
        compiler_params=pltpu.CompilerParams(vmem_limit_bytes=NEAR_LIMIT),
        cost_estimate=expected(us),
    )(*args)


def meet(groups, bit, targets, lanes):
    args = []
    for left, left_got, right, right_got in groups:
        shape = (targets, left.shape[0] // targets, left.shape[1])
        args += [left.reshape(shape), left_got.reshape(shape), right, right_got]
    out = ((targets // 2, args[0].shape[1], lanes), BF16)
    return near(functools.partial(meet_kernel, len(groups), bit, lanes), 3, [out] * 2, args)


def advance(streams):
    outs, args, plan = [], [], []
    for groups, bits in streams:
        for group in groups:
            args += group
        count, *block = groups[0][0].shape
        outs += [((count // 2, *block), BF16)] * 2 if bits else [(tuple(block), F32)]
        plan.append((len(groups), tuple(bits)))
    results = list(near(functools.partial(advance_kernel, plan), 2, outs, args))
    return [tuple(results.pop(0) for _ in range(2 if bits else 1)) for _, bits in streams]


def flip(array, axis, bit):
    count = lax.axis_size(axis)
    return lax.ppermute(array, axis, [(i, i ^ bit) for i in range(count)])


def shifted(array, by):
    count = lax.axis_size("seq")
    pairs = [(i, i + by) for i in range(count) if 0 <= i + by < count]
    return lax.ppermute(array, "seq", pairs)


def tie(*arrays):
    return lax.optimization_barrier(arrays)


def bits_of(count):
    bits = [1 << k for k in range(count.bit_length() - 1)]
    assert 1 << len(bits) == count
    return bits


def swapped(bits):
    return [bits[1], bits[0]] + list(bits[2:]) if len(bits) > 1 else list(bits)


def pick(array, index, axis):
    return lax.dynamic_index_in_dim(array, index, axis, keepdims=False)


def local(
    tokens, starts, norm_gain, in_weight, conv_weight, conv_bias, xproj_weight,
    dtproj_weight, dt_bias, decay_rate, skip_gain, out_weight, cotangent,
):
    core = lax.axis_index("section")
    place = lax.axis_index("seq")
    cores = lax.axis_size("section")
    count = lax.axis_size("seq")
    bits = bits_of(count)
    batch_count, span, model = tokens.shape
    width = conv_weight.shape[2]
    n = decay_rate.shape[2]
    rank = dtproj_weight.shape[1]
    x_width = xproj_weight.shape[2]
    batches = batch_count // cores
    rows_n = batches * span
    half_model = model // 2
    low_core = core == 0
    steps = len(bits)

    def mine(array):
        return lax.dynamic_slice_in_dim(array, core * batches, batches, 0).reshape(
            (rows_n,) + array.shape[2:]
        )

    rows0 = mine(tokens)
    top = mine(cotangent)
    r = lax.dynamic_slice_in_dim(starts, core * batches, batches, 0).astype(F32)
    r_ext = jnp.concatenate([shifted(r[:, -3:].astype(BF16), 1).astype(F32), r], 1)
    free = 1.0 - r_ext
    m1 = free[:, 3:]
    m2 = m1 * free[:, 2:-1]
    m3 = m2 * free[:, 1:-2]
    marks = jnp.stack([r, m1, m2, m3], -1).reshape(rows_n, 4)

    tall = ((rows_n, width), F32)
    low_tall = ((rows_n, width), BF16)
    rim_s = ((batches, 3, width), F32)
    own_gain = norm_gain[0][None]
    in_own, out_own = in_weight[0], out_weight[0]

    vec_own = jnp.concatenate(
        [
            decay_rate[0].T * -LOG2E, conv_weight[0], conv_bias[0][None], dt_bias[0][None],
            skip_gain[0][None], jnp.pad(own_gain, ((0, 0), (0, width - model))),
        ],
        0,
    )
    low_own = jnp.concatenate([xproj_weight[0].T, dtproj_weight[0]], 0)
    vec_other, low_other = flip(vec_own, "section", 1), flip(low_own, "section", 1)

    in_a, in_b, gate_a, gate_b, tail_a, tail_b = run(
        functools.partial(enter_kernel, batches, span, width), 5,
        [low_tall] * 4 + [rim_s] * 2,
        [((cores * rows_n, model), BF16), ((4, model, 2 * width // 4), BF16), DMA((4,))],
        [tokens.reshape(batch_count * span, model), own_gain, in_own],
        far=(0, 1), far_out=range(6), elsewhere=(2,),
    )
    in_a, in_b, gate_a, gate_b, tail_a, tail_b, vec_other, low_other, marks = tie(
        in_a, in_b, gate_a, gate_b, tail_a, tail_b, vec_other, low_other, marks
    )
    in_got = lax.ppermute(in_b, "section", [(0, 1)])
    everywhere = ("section", "seq")
    rim_a = lax.ppermute(tail_a, everywhere, [(i, i + 1) for i in range(count - 1)])
    rim_b = lax.ppermute(tail_b, everywhere, [(i, count + i + 1) for i in range(count - 1)])
    gate_got = lax.ppermute(gate_b, "section", [(0, 1)])

    out_now, in_now, _, _, _ = tie(out_own, in_own, in_got, rim_a, rim_b)
    out_other, in_other = flip(out_now, "section", 1), flip(in_now, "section", 1)
    vecs = [jnp.where(low_core == (l == 0), vec_own, vec_other) for l in range(2)]
    lows = [jnp.where(low_core == (l == 0), low_own, low_other) for l in range(2)]
    gains = [v[n + 7 :, :model] for v in vecs]
    in0, gate0 = jnp.where(low_core, in_a, in_got), jnp.where(low_core, gate_a, gate_got)
    rim0 = jnp.where(low_core, rim_a, rim_b)

    spread = ((rows_n, n, LANES), F32)
    state = ((batches, n, width), F32)
    flat_in = ((model, 2 * width), BF16)
    flat_out = ((width, model), BF16)
    send_s = ((batches * n + 16, width), BF16)
    send_back_s = ((batches * n, width), BF16)
    both_s = ((2 * batches * n + 16, width), BF16)
    tall_t = ((width, rows_n), BF16)
    narrow = ((rows_n, model), BF16)

    totals_s = ((-(-batches * (steps + 1) // 8) * 8, width), F32)

    def front(layer, inner, rim, vec, low, *rest, others=()):
        outs = [low_tall, ((rows_n, LANES), BF16), both_s if layer else send_s]
        scratch = [((span + 8, width), F32), tall, tall, spread, spread, state]
        args = [inner, rim, marks, vec, low, *rest]
        if layer:
            scratch += [tall, flat_out, DMA]
        return run(
            functools.partial(front_kernel, batches, span, width, rank, n, bool(layer)),
            10 if layer else 6, outs, scratch, args, far=(2, 3, 1, 0, 4),
            far_out=range(len(outs)), elsewhere=(7, 8) if layer else (), others=others,
        )

    conv0, proj0, send = front(
        0, in_a, rim_a, vec_own, low_own,
        others=((0, in_got), (1, rim_b), (3, vec_other), (4, low_other)),
    )
    at0, at1 = vecs[0][:n], vecs[1][:n]
    own = [send]
    for k, bit in enumerate(bits):
        own.append(flip(send, "seq", bit))
        if k < steps - 1:
            send = hop(batches, n, k + 1, at0, own)
    scanned0, gated_t0, rows1, normed0, normed1, in1, gate1, before0, totals0, tail1 = run(
        functools.partial(end_kernel, batches, span, width, rank, n, steps), 10,
        [tall, tall_t, narrow, narrow, narrow, low_tall, low_tall, state, totals_s, ((batches, 6, width), F32)],
        [tall, tall, spread, spread, flat_out, flat_in, DMA((2,))],
        [gate0, conv0, proj0, marks, vecs[0], lows[0], rows0, gains[1], gains[0],
         out_own, out_other, in_own, in_other, *own],
        far=(6, 8, 2, 5, 4, 3, 1, *range(13, 14 + steps), 0), far_out=range(10),
        elsewhere=(9, 10, 11, 12),
    )

    rims = shifted(tail1, 1)
    rim1 = rims[:, :3]
    conv1, proj1, send = front(
        1, in1, rim1, vecs[1], lows[1], gate1, top, out_own, out_other
    )
    rim = rims[:, 3:, :model].astype(BF16)
    rim = jnp.pad(rim, ((0, 0), (5, 0), (0, 0))).reshape(8 * batches, model)
    normed_ext = jnp.concatenate(
        [normed0, rim, jnp.zeros((rows_n - 8 * batches, model), BF16)], 0
    )
    ext_got, normed_got = flip(normed_ext, "section", 1), flip(normed1, "section", 1)
    own = [send]
    for k, bit in enumerate(bits):
        own.append(flip(send, "seq", bit))
        if k < steps - 1:
            send = hop(batches, n, k + 1, at1, own, both=True)

    def back(layer, gg, conv, inner, gate, rim, proj, *rest):
        outs = [
            low_tall, ((batches, 16, width), F32), ((batches, 3, width), F32),
            ((width, LANES), BF16), ((n + 8, width), F32),
        ]
        scratch = [
            tall, tall, ((batches, span + 1, n, BLOCK), F32), ((batches, span, n, BLOCK), F32),
            tall, tall, spread, spread, ((span + 16, width), F32), tall,
            spread, spread, tall, state, state,
        ]
        if layer:
            outs += [low_tall, tall_t, narrow]
            scratch += [tall, tall, flat_out, DMA]
            far = (8, 7, 6, 5, 1, 0, 3, *range(12, 12 + steps))
        else:
            outs += [((width, 2 * rows_n), BF16)]
            far = (8, 7, 6, 5, 1, 0, 3, *range(9, 11 + steps))
        return run(
            functools.partial(
                back_kernel, batches, span, width, rank, n, x_width, steps, bool(layer)
            ),
            22 if layer else 19, outs, scratch,
            [gg, conv, inner, gate, rim, marks, vecs[layer], lows[layer], proj, *rest],
            far=far, far_out=range(len(outs)),
            elsewhere=(10, 11) if layer else (),
        )

    inner1, last1, spill1, pair1, vgrad1, gate_grad1, gated_t1, out1 = back(
        1, top, conv1, in1, gate1, rim1, proj1, rows1, out_own, out_other, *own[1:]
    )
    got1 = shifted(spill1, -1)

    def turn(layer, inner, tail, spill, gate_grad, rows, g, pair, vgrad, *rest):
        outs = [narrow, ((width, 2 * LANES), BF16)]
        scratch = [flat_in, DMA, ((rows_n, 2 * width), BF16), ((width, LANES), F32)]
        args = [
            inner, tail, spill, gate_grad, rows, gains[layer], g, pair, vgrad, in_own, in_other,
            *rest,
        ]
        elsewhere, far, far_out = [9, 10], [1, 2, 0, 3, 4, 6], [0, 1]
        if layer:
            outs += [((2 * width, rows_n), BF16), tall, send_back_s, low_tall, tall_t]
            scratch += [tall, tall, spread, state, flat_out, DMA]
            elsewhere += [11, 12]
            far += [13, 14, 18]
            far_out += [2, 3, 4, 5, 6]
        return run(
            functools.partial(turn_kernel, batches, span, width, rank, n, count, layer),
            11 if layer else 5, outs, scratch, args, far=far, far_out=far_out,
            elsewhere=elsewhere, limit=None if layer else TURN_LIMIT,
        )

    g0, small1, grad_t1, gg0, send_b, gate_grad0, gate_t0 = turn(
        1, inner1, last1, got1, gate_grad1, rows1, top, pair1, vgrad1, out_own, out_other,
        gate0, proj0,
        marks, lows[0], vecs[0], scanned0,
    )

    first_b = flip(send_b, "seq", bits[0])
    first_b, grad_t1, gate_t0, g0, gated_t0, gated_t1 = tie(
        first_b, grad_t1, gate_t0, g0, gated_t0, gated_t1
    )

    x_bit, y_bit, z_bit = bits[0], bits[1], bits[-2]
    one_way = lambda array, a, b: lax.ppermute(array, "section", [(a, b)])
    def half(array, which):
        return lax.dynamic_slice_in_dim(array, which * half_model, half_model, 1)

    def together(left, left_got, right, right_got):
        return dot(
            jnp.concatenate([left, left_got], 1), jnp.concatenate([right, right_got], 0)
        ).astype(BF16)

    def part(total, bit, order):
        axis = len(order) - 1 - sorted(order).index(bit)
        total = total.reshape((2,) * len(order) + (-1, total.shape[-1]))
        mine = (place // bit) % 2
        block = (total.shape[-2], total.shape[-1])
        return (
            pick(total, 1 - mine, axis).reshape((-1, *block)),
            pick(total, mine, axis).reshape((-1, *block)),
        )

    gated_got = flip(jnp.where(low_core, gated_t1, gated_t0), "section", 1)
    gated_own = jnp.where(low_core, gated_t0, gated_t1)
    g_got = flip(jnp.where(low_core, top, g0), "section", 1)
    grad_got, gate_got0 = flip(grad_t1, "section", 1), flip(gate_t0, "section", 1)

    own_b = [send_b]
    for k, bit in enumerate(bits):
        got_b = flip(send_b, "seq", bit) if k else first_b
        if k == 2:
            a = together(grad_t1, grad_got, half(normed1, core), half(normed_got, core))
            b = together(gated_own, gated_got, jnp.where(low_core, g0, top), g_got)
            c = together(
                gate_t0, gate_got0, half(normed0, core), half(ext_got[:rows_n], core)
            )
            a_goes, a_stays = part(a, x_bit, bits)
            b_goes, b_stays = part(b, y_bit, bits)
            c_goes, c_stays = part(c, z_bit, bits[:-1])
            got_b, a_goes, b_goes = tie(got_b, a_goes, b_goes)
        if k == steps - 1:
            got_b, a_goes, b_goes, c_goes = tie(got_b, a_goes, b_goes, c_goes)
            a_got, b_got = flip(a_goes, "seq", x_bit), flip(b_goes, "seq", y_bit)
            c_got = flip(c_goes, "seq", z_bit)
            small_up = one_way(small1, 0, 1)
        own_b.append(got_b)
        if k < steps - 1:
            send_b = hop(batches, n, k + 1, at0, (), own_b, totals0)
    inner0, tail0, spill0, pair0, vgrad0, turned0 = back(
        0, gg0, conv0, in0, gate0, rim0, proj0, before0, totals0, *own_b[1:]
    )
    inner0, tail0, spill0, pair0, vgrad0, turned0, a_got, b_got, c_got, small_up = tie(
        inner0, tail0, spill0, pair0, vgrad0, turned0, a_got, b_got, c_got, small_up
    )
    got0 = shifted(spill0, -1)
    turned_got = flip(turned0, "section", 1)

    middle = bits[2:-2]
    blocks = lambda array: array.reshape(count, -1, array.shape[-1])
    held = {"a": [(a_stays, a_got)], "b": [(b_stays, b_got)], "c": [(c_stays, c_got)]}
    todo = {
        "d": [x_bit, y_bit, *middle, z_bit],
        "a": [y_bit, *middle, z_bit, bits[-1]],
        "b": [z_bit, x_bit, *middle, bits[-1]],
        "c": [x_bit, y_bit, *middle],
    }
    parts = dict(zip("ab", advance([(held[k], todo[k]) for k in "ab"])))
    parts["d"] = meet(
        [(turned0, turned_got, normed_ext, ext_got)], x_bit, count // 2, half_model
    )
    first = [parts[k][0] for k in "dab"]
    got0, inner0, tail0, pair0, vgrad0, *first = tie(got0, inner0, tail0, pair0, vgrad0, *first)
    gots = [flip(goes, "seq", todo[k][0]) for k, goes in zip("dab", first)]
    dx, small0 = turn(0, inner0, tail0, got0, gate_grad0, rows0, g0, pair0, vgrad0)
    *gots, dx, small0 = tie(*gots, dx, small0)
    for k, got in zip("dab", gots):
        held[k] = [(parts[k][1], got)]
        todo[k] = todo[k][1:]
    small_down = one_way(small0, 1, 0)
    late = {
        "small": (
            [(blocks(small0), blocks(small_down)), (blocks(small1), blocks(small_up))],
            [z_bit, y_bit, x_bit, *middle, bits[-1]],
        )
    }
    while any(todo.values()):
        names = [k for k in todo if todo[k]]
        parts = dict(zip(names, advance([(held[k], todo[k]) for k in names])))
        gots = [flip(parts[k][0], "seq", todo[k][0]) for k in names]
        for k in late:
            held[k], todo[k] = late[k]
            parts.update(zip([k], advance([late[k]])))
            names.append(k)
            gots.append(flip(parts[k][0], "seq", todo[k][0]))
        late = {}
        gots = tie(*gots)
        for k, got in zip(names, gots):
            held[k] = [(parts[k][1], got)]
            todo[k] = todo[k][1:]
        if not todo["d"] and not todo["c"] and "d" in parts:
            c, d = (t.astype(BF16) for (t,) in advance([(held[k], []) for k in "cd"]))
            top_half = place >= count // 2
            swap_sent = jnp.where(top_half, d, c)
            swap_got = flip(swap_sent, "seq", bits[-1])
    in_sum1, out_sum, small = (
        total for (total,) in advance([(held[k], []) for k in ("a", "b", "small")])
    )
    in_sum0 = jnp.where(top_half, c, d).astype(F32) + swap_got.astype(F32)

    got = flip(jnp.where(low_core, in_sum1, in_sum0).astype(BF16), "section", 1).astype(F32)
    grad_in = jnp.where(
        low_core, jnp.concatenate([in_sum0, got], 1), jnp.concatenate([got, in_sum1], 1)
    )
    got = flip(jnp.where(low_core, out1, dx), "section", 1)
    boundary = jnp.where(
        low_core, jnp.concatenate([dx, got], 0), jnp.concatenate([got, out1], 0)
    ).reshape(1, batch_count, span, model)
    vec_sum = small[:, LANES : LANES + n + 8].T
    gain = vec_sum[n + 7 :, : model // count]
    return (
        boundary,
        gain,
        grad_in.T[None],
        vec_sum[n : n + 4][None],
        vec_sum[n + 4 : n + 5],
        small[:, :x_width][None],
        small[:, x_width:LANES].T[None],
        vec_sum[n + 5 : n + 6],
        small[:, LANES : LANES + n][None],
        vec_sum[n + 6 : n + 7],
        out_sum[None],
    )


def solution(mesh):
    in_specs = (
        P(None, "seq", None), P(None, "seq"), P("section", None), P("section", None, None),
        P("section", None, None), P("section", None), P("section", None, None),
        P("section", None, None), P("section", None), P("section", None, None),
        P("section", None), P("section", None, None), P(None, "seq", None),
    )
    out_specs = (
        P("section", None, "seq", None), P("section", "seq"), P("section", None, "seq"),
        P("section", None, "seq"), P("section", "seq"), P("section", "seq", None),
        P("section", None, "seq"), P("section", "seq"), P("section", "seq", None),
        P("section", "seq"), P("section", "seq", None),
    )
    return jax.shard_map(local, mesh=mesh, in_specs=in_specs, out_specs=out_specs, check_vma=False)
```

```python
import functools
import jax
import jax.numpy as jnp
from jax import lax
from jax.experimental import pallas as pl
from jax.experimental.pallas import tpu as pltpu
from jax.sharding import PartitionSpec as P

EPS = 1e-05
LOG2E = 1.4426950408889634
STOP = 1e7
LANES = 128
BLOCK = 768
TILES = BLOCK // LANES
F32 = jnp.float32
BF16 = jnp.bfloat16
VMEM_LIMIT = 58 * 1024 * 1024
HOP_LIMIT = 6 * 1024 * 1024
NEAR_LIMIT = 24 * 1024 * 1024
TURN_LIMIT = 58 * 1024 * 1024


def dot(left, right):
    return jnp.dot(left, right, preferred_element_type=F32)


def across(left, right):
    return lax.dot_general(left, right, (((0,), (0,)), ((), ())), preferred_element_type=F32)


def against(left, right):
    return lax.dot_general(left, right, (((1,), (1,)), ((), ())), preferred_element_type=F32)


def norm_rows(source, gain_row):
    return source * lax.rsqrt(jnp.mean(source * source, axis=-1, keepdims=True) + EPS) * gain_row


def softplus(v):
    return jnp.maximum(v, 0.0) + jnp.log1p(jnp.exp(-jnp.abs(v)))


def silu_slope(v):
    gate = jax.nn.sigmoid(v)
    return gate * (1.0 + v * (1.0 - gate))


def pair_up(left, right, row_ids, width):
    mask = (row_ids % (2 * width)) < width
    kept = jnp.where(mask, left, right)
    moved = jnp.where(mask, right, left)
    return kept + pltpu.roll(moved, 8 - width, 0)


def fold_rows(parts, row_ids):
    width = 1
    while len(parts) > 1:
        parts = [
            pair_up(parts[i], parts[i + 1], row_ids, width) for i in range(0, len(parts), 2)
        ]
        width *= 2
    return parts[0]


def halves(v):
    return v[:8] + v[8:]


def spread_columns(table, first, target):
    width = target.shape[1]
    for t in range(target.shape[0]):
        column = table[first : first + width, t : t + 1]
        target[t] = jnp.broadcast_to(column, (width, LANES))


def block_at(i):
    return pl.ds(pl.multiple_of(i * BLOCK, BLOCK), BLOCK)


def tile_at(i, lt):
    return pl.ds(pl.multiple_of(i * BLOCK + lt * LANES, LANES), LANES)


def local_scan(batches, span, blocks, seff, x, bx, at, final):
    def over_block(i, carry):
        rate = [at[:, tile_at(i, lt)] for lt in range(TILES)]

        def chunk(tc, states):
            states = list(states)
            for b in range(batches):
                rows = pl.ds(pl.multiple_of(b * span + tc * 8, 8), 8)
                for lt in range(TILES):
                    s8 = seff[rows, tile_at(i, lt)]
                    x8 = x[rows, tile_at(i, lt)]
                    h = states[b * TILES + lt]
                    for j in range(8):
                        decay = jnp.exp2(s8[j : j + 1] * rate[lt])
                        h = decay * h + x8[j : j + 1] * bx[b * span + tc * 8 + j]
                    states[b * TILES + lt] = h
            return tuple(states)

        zero = jnp.zeros((at.shape[0], LANES), F32)
        states = lax.fori_loop(0, span // 8, chunk, (zero,) * (batches * TILES))
        for b in range(batches):
            for lt in range(TILES):
                final[b, :, tile_at(i, lt)] = states[b * TILES + lt]
        return carry

    lax.fori_loop(0, blocks, over_block, 0)


def back_scan(batches, span, blocks, seff, sg, cx, at, first):
    chunks = span // 8

    def over_block(i, carry):
        rate = [at[:, tile_at(i, lt)] for lt in range(TILES)]

        def chunk(k, states):
            states = list(states)
            tc = chunks - 1 - k
            for b in range(batches):
                rows = pl.ds(pl.multiple_of(b * span + tc * 8, 8), 8)
                for lt in range(TILES):
                    s8 = seff[rows, tile_at(i, lt)]
                    g8 = sg[rows, tile_at(i, lt)]
                    q = states[b * TILES + lt]
                    for j in range(7, -1, -1):
                        decay = jnp.exp2(s8[j : j + 1] * rate[lt])
                        q = decay * (q + g8[j : j + 1] * cx[b * span + tc * 8 + j])
                    states[b * TILES + lt] = q
            return tuple(states)

        zero = jnp.zeros((at.shape[0], LANES), F32)
        states = lax.fori_loop(0, chunks, chunk, (zero,) * (batches * TILES))
        for b in range(batches):
            for lt in range(TILES):
                first[b, :, tile_at(i, lt)] = states[b * TILES + lt]
        return carry

    lax.fori_loop(0, blocks, over_block, 0)


class Arriving:
    def __init__(self, source, held, sem, other=None):
        self.held, self.waited = held, False
        if other is None:
            self.copy = pltpu.make_async_copy(source, held, sem)
            self.copy.start()
        else:
            self.copy = fetch(0, source, other, held, sem)

    def __getitem__(self, where):
        assert self.waited
        return self.held[where]

    def __setitem__(self, where, value):
        assert self.waited
        self.held[where] = value

    @property
    def at(self):
        return self.held.at


class Leaving:
    def __init__(self, target, held, sem):
        self.copy, self.held, self.started = pltpu.make_async_copy(held, target, sem), held, False

    def __getitem__(self, where):
        return self.held[where]

    def __setitem__(self, where, value):
        self.held[where] = value


def uppers_of(steps):
    place = lax.axis_index("seq")
    return [(place // (1 << k)) % 2 != 0 for k in range(steps)]


def ready(*refs):
    for ref in refs:
        if isinstance(ref, Arriving) and not ref.waited:
            ref.copy.wait()
            ref.waited = True


def leave(*refs):
    for ref in refs:
        if isinstance(ref, Leaving) and not ref.started:
            ref.copy.start()
            ref.started = True


def fetch(layer, own, other, held, sem):
    mine = lax.axis_index("section") == layer

    @pl.when(mine)
    def _():
        pltpu.make_async_copy(own, held, sem).start()

    @pl.when(jnp.logical_not(mine))
    def _():
        pltpu.make_async_copy(other, held, sem).start()

    return pltpu.make_async_copy(own, held, sem)


def split_total(totals):
    width = totals[0].shape[1]
    row_ids = lax.broadcasted_iota(jnp.int32, (16, width), 0)
    block = jnp.zeros((16, width), F32)
    for b, total in enumerate(totals):
        rest = total
        for k in range(3):
            part = rest.astype(BF16).astype(F32)
            block = jnp.where(row_ids == 3 * b + k, part, block)
            rest = rest - part
    return block.astype(BF16)


def join_total(block, b):
    block = block.astype(F32)
    return block[3 * b : 3 * b + 1] + block[3 * b + 1 : 3 * b + 2] + block[3 * b + 2 : 3 * b + 3]


def enter_kernel(
    batches, span, width,
    rows, gain, in_w,
    in_a_o, in_b_o, gate_a_o, gate_b_o, tail_a_o, tail_b_o,
    normed, held, sems,
):
    chunk = held.shape[2]
    copies = [
        pltpu.make_async_copy(in_w.at[:, pl.ds(c * chunk, chunk)], held.at[c], sems.at[c])
        for c in range(held.shape[0])
    ]
    for copy in copies:
        copy.start()
    ready(rows, gain)
    normed[...] = norm_rows(rows[...].astype(F32), gain[...]).astype(BF16)
    half = batches * span
    for c, copy in enumerate(copies):
        copy.wait()
        mixed = dot(normed[...], held[c])
        outs = (in_a_o, in_b_o) if c * chunk < width else (gate_a_o, gate_b_o)
        lanes = slice(c * chunk % width, c * chunk % width + chunk)
        for k, out in enumerate(outs):
            out[:, lanes] = mixed[k * half : (k + 1) * half].astype(BF16)
        if c * chunk < width:
            for k, tail in enumerate((tail_a_o, tail_b_o)):
                for b in range(batches):
                    last = k * half + (b + 1) * span
                    tail[b, :, lanes] = mixed[last - 3 : last].astype(BF16).astype(F32)
        if (c + 1) * chunk == width:
            leave(in_a_o, in_b_o, tail_a_o, tail_b_o)


def tap_rows(ext, rim, mixed, width, span):
    ext[5:8] = rim
    ext[8 : 8 + span] = mixed.astype(F32)


def conv_sum(ext, m, vec, n, span):
    v = vec[n + 4 : n + 5] + vec[n + 3 : n + 4] * ext[8 : 8 + span]
    for k in (1, 2, 3):
        v = v + vec[n + 3 - k : n + 4 - k] * (m[:, k : k + 1] * ext[8 - k : 8 - k + span])
    return v


def step_sum(proj, low_w, vec, rank, n):
    return dot(proj[:, :rank], low_w[rank + 2 * n :]) + vec[n + 5 : n + 6]


def front_kernel(
    batches, span, width, rank, states_n, with_back,
    *refs,
):
    refs = list(refs)
    mixed, rim, marks, vec, low_w = refs[:5]
    del refs[:5]
    if with_back:
        gate, g, own_w, other_w = refs[:4]
        del refs[:4]
    conv_o, proj_o, send_o = refs[:3]
    del refs[:3]
    if with_back:
        first = batches * states_n + 16
    ext, seff, x, bx, cx, final = refs[:6]
    if with_back:
        sg, out_w, sem = refs[6:]
        arrival = fetch(1, own_w, other_w, out_w, sem)
    n = states_n
    ready(rim, marks, vec)
    m = marks[...]
    at = vec.at[0:n]
    ready(mixed)
    for b in range(batches):
        lo, hi = b * span, (b + 1) * span
        tap_rows(ext, rim[b], mixed[lo:hi], width, span)
        x[lo:hi] = jax.nn.silu(conv_sum(ext, m[lo:hi], vec, n, span))
    conv = x[...].astype(BF16)
    conv_o[...] = conv
    leave(conv_o)
    ready(low_w)
    proj = against(conv, low_w[...]).astype(BF16)
    proj_o[...] = proj
    leave(proj_o)
    step = softplus(step_sum(proj, low_w, vec, rank, n))
    seff[...] = step + m[:, 0:1] * STOP
    x[...] = step * conv.astype(F32)
    totals = [
        jnp.sum(seff[b * span : (b + 1) * span], axis=0, keepdims=True) for b in range(batches)
    ]
    send_o[batches * n : batches * n + 16] = split_total(totals)
    table = proj.astype(F32).T
    spread_columns(table, rank, bx)
    local_scan(batches, span, width // BLOCK, seff, x, bx, at, final)
    for b in range(batches):
        send_o[b * n : (b + 1) * n] = final[b].astype(BF16)
    if not with_back:
        leave(send_o)
    if with_back:
        arrival.wait()
        spread_columns(table, rank + n, cx)
        ready(g, gate)
        gg = against(g[...], out_w[...])
        sg[...] = gg * jax.nn.silu(gate[...].astype(F32))
        back_scan(batches, span, width // BLOCK, seff, sg, cx, at, final)
        for b in range(batches):
            send_o[first + b * n : first + (b + 1) * n] = final[b].astype(BF16)


def merge(at, upper, mine, theirs, mine_total, their_total, backward):
    early, late = jnp.where(upper, theirs, mine), jnp.where(upper, mine, theirs)
    if backward:
        return jnp.exp2(jnp.where(upper, their_total, mine_total) * at) * late + early
    return jnp.exp2(jnp.where(upper, mine_total, their_total) * at) * early + late


def reach(at, n, b, uppers, gots, totals, backward, first=0):
    carry = jnp.zeros(at.shape, F32)
    span = jnp.zeros((1, at.shape[1]), F32)
    for upper, got, their_total in zip(uppers, gots, totals):
        comes = jnp.logical_not(upper) if backward else upper
        theirs = got[first + b * n : first + (b + 1) * n].astype(F32)
        carry = jnp.where(comes, jnp.exp2(span * at) * theirs + carry, carry)
        span = jnp.where(comes, span + their_total, span)
    return carry


def hop_kernel(batches, n, steps, forward, backward, *refs):
    refs = list(refs)
    take = lambda k: [refs.pop(0) for _ in range(k)]
    (at,) = take(1)
    at = at[...]
    if forward:
        own, *gots = take(1 + steps)
    else:
        (totals,) = take(1)
    first = 0
    if forward and backward:
        own_b, gots_b, first = own, gots, batches * n + 16
    elif backward:
        own_b, *gots_b = take(1 + steps)
    (send,) = take(1)
    uppers = uppers_of(steps)
    reached = []
    for b in range(batches):
        rows = slice(b * n, (b + 1) * n)
        if forward:
            total = join_total(own[batches * n : batches * n + 16], b)
            mine = own[rows].astype(F32)
        else:
            total = totals[b : b + 1]
        if backward:
            rows_b = slice(first + b * n, first + (b + 1) * n)
            mine_b = own_b[rows_b].astype(F32)
        for k, upper in enumerate(uppers):
            if forward:
                their_total = join_total(gots[k][batches * n : batches * n + 16], b)
                mine = merge(
                    at, upper, mine, gots[k][rows].astype(F32), total, their_total, False
                )
            else:
                their_total = totals[(k + 1) * batches + b : (k + 1) * batches + b + 1]
            if backward:
                mine_b = merge(
                    at, upper, mine_b, gots_b[k][rows_b].astype(F32), total, their_total, True
                )
            total = total + their_total
        if forward:
            send[rows] = mine.astype(BF16)
        if backward:
            send[rows_b] = mine_b.astype(BF16)
        reached.append(total)
    if forward:
        send[batches * n : batches * n + 16] = split_total(reached)


def prepare(step, marks, conv, seff, x):
    seff[...] = step + marks * STOP
    x[...] = step * conv.astype(F32)


def end_kernel(
    batches, span, width, rank, n, steps,
    gate, conv, proj, marks, vec, low_w, rows, gain, gain_before,
    own_out, other_out, own_in, other_in, own_send, *refs,
):
    gots, refs = refs[:steps], refs[steps:]
    (
        scanned_o, gated_t_o, rows_o, normed_before_o, normed_o, inner_o, gate_o, before_o,
        totals_o, tail_o, seff, x, bx, cx, out_w, in_w, sems,
    ) = refs

    arrivals = [
        fetch(0, own_out, other_out, out_w, sems.at[0]),
        fetch(1, own_in, other_in, in_w, sems.at[1]),
    ]
    blocks = width // BLOCK
    at = vec.at[0:n]
    ready(rows, gain_before, proj, low_w, vec, marks, conv)
    normed_before_o[...] = norm_rows(rows[...].astype(F32), gain_before[...]).astype(BF16)
    leave(normed_before_o)
    tail_o[...] = jnp.zeros((batches, 6, width), F32)
    for b in range(batches):
        last = normed_before_o[(b + 1) * span - 16 : (b + 1) * span].astype(F32)
        tail_o[b, 3:6, : last.shape[1]] = last[13:]
    step = softplus(step_sum(proj[...], low_w, vec, rank, n))
    prepare(step, marks[:, 0:1], conv[...], seff, x)
    table = proj[...].astype(F32).T
    spread_columns(table, rank, bx)
    spread_columns(table, rank + n, cx)
    ready(own_send, *gots)
    uppers = uppers_of(steps)
    for b in range(batches):
        totals_o[b : b + 1] = join_total(own_send[batches * n : batches * n + 16], b)
        theirs = [join_total(got[batches * n : batches * n + 16], b) for got in gots]
        for k, their in enumerate(theirs):
            totals_o[(k + 1) * batches + b : (k + 1) * batches + b + 1] = their
        before_o[b] = reach(at[...], n, b, uppers, gots, theirs, False)
    leave(before_o, totals_o)
    row_ids = lax.broadcasted_iota(jnp.int32, (8, LANES), 0)

    def over_block(i, carry):
        rate = [at[:, tile_at(i, lt)] for lt in range(TILES)]

        def chunk(tc, states):
            states = list(states)
            for b in range(batches):
                rows8 = pl.ds(pl.multiple_of(b * span + tc * 8, 8), 8)
                for lt in range(TILES):
                    s8 = seff[rows8, tile_at(i, lt)]
                    x8 = x[rows8, tile_at(i, lt)]
                    h = states[b * TILES + lt]
                    parts = []
                    for j in range(8):
                        t = b * span + tc * 8 + j
                        decay = jnp.exp2(s8[j : j + 1] * rate[lt])
                        h = decay * h + x8[j : j + 1] * bx[t]
                        parts.append(halves(h * cx[t]))
                    states[b * TILES + lt] = h
                    scanned_o[rows8, tile_at(i, lt)] = fold_rows(parts, row_ids)
            return tuple(states)

        start = tuple(
            before_o[b, :, tile_at(i, lt)] for b in range(batches) for lt in range(TILES)
        )
        lax.fori_loop(0, span // 8, chunk, start)
        return carry

    lax.fori_loop(0, blocks, over_block, 0)
    scanned = scanned_o[...] + vec[n + 6 : n + 7] * conv[...].astype(F32)
    scanned_o[...] = scanned
    leave(scanned_o)
    ready(gate)
    gated_f = scanned * jax.nn.silu(gate[...].astype(F32))
    gated = gated_f.astype(BF16)
    gated_t_o[...] = gated_f.T.astype(BF16)
    leave(gated_t_o)
    arrivals[0].wait()
    result = (rows[...].astype(F32) + dot(gated, out_w[...])).astype(BF16)
    rows_o[...] = result
    leave(rows_o)
    ready(gain)
    normed_o[...] = norm_rows(result.astype(F32), gain[...]).astype(BF16)
    leave(normed_o)
    arrivals[1].wait()
    for first, target in ((0, inner_o), (width, gate_o)):
        for c in range(0, width, 512):
            mixed = dot(normed_o[...], in_w[:, first + c : first + c + 512])
            target[:, c : c + 512] = mixed.astype(BF16)
            if not first:
                for b in range(batches):
                    last = (b + 1) * span
                    tail_o[b, 0:3, c : c + 512] = mixed[last - 3 : last].astype(BF16).astype(F32)
        leave(target, tail_o)


def back_kernel(
    batches, span, width, rank, n, x_width, steps, with_out,
    *refs,
):
    refs = list(refs)
    take = lambda k: [refs.pop(0) for _ in range(k)]
    gg, conv, inner, gate, rim, marks, vec, low_w, proj = take(9)
    if with_out:
        rows, own_out, other_out = take(3)
        gots = gots_b = take(steps)
    else:
        before, totals = take(2)
        gots_b = take(steps)
    inner_o, tail_o, spill_o, pair_o, vec_o = take(5)
    if with_out:
        gate_o, gated_t_o, out_o = take(3)
    else:
        (turned_o,) = take(1)
    seff, x, hist, decays, drive, zsum, acc_b, acc_c, ext, sg, bx, cx, pre_grad = take(13)
    state_in, grad_in = take(2)
    if with_out:
        scanned_ref, gg_s, out_w, sem = take(4)
        arrival = fetch(1, own_out, other_out, out_w, sem)
    blocks = width // BLOCK
    rows_n = batches * span
    chunks = span // 8
    ready(proj, low_w, vec, marks, conv)
    m = marks[...]
    at = vec.at[0:n]
    spre = step_sum(proj[...], low_w, vec, rank, n)
    prepare(softplus(spre), m[:, 0:1], conv[...], seff, x)
    table = proj[...].astype(F32).T
    spread_columns(table, rank, bx)
    spread_columns(table, rank + n, cx)
    ready(gg, gate)
    if with_out:
        arrival.wait()
        gg_s[...] = against(gg[...], out_w[...])
        gg = gg_s
    sg[...] = gg[...] * jax.nn.silu(gate[...].astype(F32))
    if with_out:
        ready(*gots)
    else:
        ready(before, totals)
    ready(*gots_b)
    uppers = uppers_of(steps)
    for b in range(batches):
        if with_out:
            theirs = [join_total(got[batches * n : batches * n + 16], b) for got in gots]
            state_in[b] = reach(at[...], n, b, uppers, gots, theirs, False)
        else:
            theirs = [
                totals[(k + 1) * batches + b : (k + 1) * batches + b + 1] for k in range(steps)
            ]
            state_in[b] = before[b]
        first = batches * n + 16 if with_out else 0
        grad_in[b] = reach(at[...], n, b, uppers, gots_b, theirs, True, first)
    acc_b[...] = jnp.zeros_like(acc_b)
    acc_c[...] = jnp.zeros_like(acc_c)
    vec_o[...] = jnp.zeros((n + 8, width), F32)
    row_ids = lax.broadcasted_iota(jnp.int32, (8, LANES), 0)

    def over_block(i, carry):
        rate = [at[:, tile_at(i, lt)] for lt in range(TILES)]

        def again(tc, states):
            states = list(states)
            for b in range(batches):
                rows8 = pl.ds(pl.multiple_of(b * span + tc * 8, 8), 8)
                for lt in range(TILES):
                    s8 = seff[rows8, tile_at(i, lt)]
                    x8 = x[rows8, tile_at(i, lt)]
                    h = states[b * TILES + lt]
                    lanes = pl.ds(lt * LANES, LANES)
                    parts = []
                    for j in range(8):
                        t = tc * 8 + j
                        decay = jnp.exp2(s8[j : j + 1] * rate[lt])
                        h = decay * h + x8[j : j + 1] * bx[b * span + t]
                        decays[b, t, :, lanes] = decay
                        hist[b, t + 1, :, lanes] = h
                        if with_out:
                            parts.append(halves(h * cx[b * span + t]))
                    states[b * TILES + lt] = h
                    if with_out:
                        scanned_ref[rows8, tile_at(i, lt)] = fold_rows(parts, row_ids)
            return tuple(states)

        for b in range(batches):
            hist[b, 0] = state_in[b, :, block_at(i)]
        start = tuple(
            state_in[b, :, tile_at(i, lt)] for b in range(batches) for lt in range(TILES)
        )
        lax.fori_loop(0, chunks, again, start)

        sums = tuple(jnp.zeros((n, LANES), F32) for _ in range(TILES))
        for b in range(batches):

            def chunk(k, held):
                held = list(held)
                tc = chunks - 1 - k
                rows8 = pl.ds(pl.multiple_of(b * span + tc * 8, 8), 8)
                s8, x8, g8 = [], [], []
                for lt in range(TILES):
                    s8.append(seff[rows8, tile_at(i, lt)])
                    x8.append(x[rows8, tile_at(i, lt)])
                    g8.append(sg[rows8, tile_at(i, lt)])
                drives = [[None] * 8 for _ in range(TILES)]
                zs = [[None] * 8 for _ in range(TILES)]
                for j in range(7, -1, -1):
                    t = tc * 8 + j
                    part_b, part_c = [], []
                    for lt in range(TILES):
                        lanes = pl.ds(lt * LANES, LANES)
                        total = held[lt] + g8[lt][j : j + 1] * cx[b * span + t]
                        q = decays[b, t, :, lanes] * total
                        log_grad = q * hist[b, t, :, lanes]
                        held[TILES + lt] = held[TILES + lt] + log_grad * s8[lt][j : j + 1]
                        zs[lt][j] = halves(log_grad * rate[lt])
                        drives[lt][j] = halves(total * bx[b * span + t])
                        part_b.append(total * x8[lt][j : j + 1])
                        part_c.append(g8[lt][j : j + 1] * hist[b, t + 1, :, lanes])
                        held[lt] = q
                    acc_b[b * span + t] += sum(part_b[1:], part_b[0])
                    acc_c[b * span + t] += sum(part_c[1:], part_c[0])
                for lt in range(TILES):
                    drive[rows8, tile_at(i, lt)] = fold_rows(drives[lt], row_ids)
                    zsum[rows8, tile_at(i, lt)] = fold_rows(zs[lt], row_ids)
                return tuple(held)

            start = tuple(grad_in[b, :, tile_at(i, lt)] for lt in range(TILES)) + sums
            sums = lax.fori_loop(0, chunks, chunk, start)[TILES:]
        for lt in range(TILES):
            vec_o[0:n, tile_at(i, lt)] = -sums[lt]
        return carry

    lax.fori_loop(0, blocks, over_block, 0)

    conv_f = conv[...].astype(F32)
    if with_out:
        ready(rows)
        gate = gate[...].astype(F32)
        scanned = scanned_ref[...] + vec[n + 6 : n + 7] * conv_f
        gated_f = scanned * jax.nn.silu(gate)
        gated_t_o[...] = gated_f.T.astype(BF16)
        out_o[...] = (rows[...].astype(F32) + dot(gated_f.astype(BF16), out_w[...])).astype(BF16)
        gate_o[...] = (gg_s[...] * scanned * silu_slope(gate)).astype(BF16)
        leave(gate_o, gated_t_o, out_o)

    ones = jnp.ones((LANES, LANES), BF16)
    table = (rows_n * n, LANES)
    at_n = lax.broadcasted_iota(jnp.int32, table, 0) % n
    lane = lax.broadcasted_iota(jnp.int32, table, 1)
    sums_b, sums_c = (
        dot(acc[...].reshape(table).astype(BF16), ones) for acc in (acc_b, acc_c)
    )
    placed = jnp.where(lane == rank + at_n, sums_b, 0.0)
    placed = placed + jnp.where(lane == rank + n + at_n, sums_c, 0.0)
    placed = jnp.sum(placed.reshape(rows_n, n, LANES), axis=1)
    spre = step_sum(proj[...], low_w, vec, rank, n)
    step = softplus(spre)
    step_grad = zsum[...] * (1.0 / LOG2E) + drive[...] * conv_f
    pre_g = step_grad * jax.nn.sigmoid(spre)
    low = pre_g.astype(BF16)
    low_grad = against(low, low_w[rank + 2 * n :])
    pgrad = (
        jnp.concatenate([low_grad, jnp.zeros((rows_n, LANES - rank), F32)], 1) + placed
    ).astype(BF16)
    small = dot(conv_f.T.astype(BF16), pgrad)
    lows = pltpu.roll(dot(pre_g.T.astype(BF16), proj[...]), x_width, 1)
    columns = lax.broadcasted_iota(jnp.int32, (1, LANES), 1)
    pair_o[...] = jnp.where(columns < x_width, small, lows).astype(BF16)
    leave(pair_o)
    conv_grad = (
        sg[...] * vec[n + 6 : n + 7] + step * drive[...]
        + dot(pgrad[:, : rank + 2 * n], low_w[: rank + 2 * n])
    )
    pre_grad[...] = conv_grad
    vec_o[n + 5 : n + 6] = jnp.sum(pre_g, axis=0, keepdims=True)
    vec_o[n + 6 : n + 7] = jnp.sum(sg[...] * conv_f, axis=0, keepdims=True)
    ready(inner, rim)
    taps = [jnp.zeros((1, width), F32) for _ in range(4)]
    bias = jnp.zeros((1, width), F32)
    spilled = []
    for b in range(batches):
        lo, hi = b * span, (b + 1) * span
        tap_rows(ext, rim[b], inner[lo:hi], width, span)
        grad_b = pre_grad[lo:hi] * silu_slope(conv_sum(ext, m[lo:hi], vec, n, span))
        bias = bias + jnp.sum(grad_b, axis=0, keepdims=True)
        taps[3] = taps[3] + jnp.sum(grad_b * ext[8 : 8 + span], axis=0, keepdims=True)
        for k in (1, 2, 3):
            taps[3 - k] = taps[3 - k] + jnp.sum(
                grad_b * (m[lo:hi, k : k + 1] * ext[8 - k : 8 - k + span]),
                axis=0, keepdims=True,
            )
        back = vec[n + 3 : n + 4] * grad_b
        spill = jnp.zeros((8, width), F32)
        for k in (1, 2, 3):
            ext[0:8] = jnp.zeros((8, width), F32)
            ext[8 : 8 + span] = vec[n + 3 - k : n + 4 - k] * (m[lo:hi, k : k + 1] * grad_b)
            ext[8 + span : 16 + span] = jnp.zeros((8, width), F32)
            back = back + ext[8 + k : 8 + k + span]
            spill = spill + ext[k : 8 + k]
        inner_o[lo:hi] = back.astype(BF16)
        tail_o[b] = back[span - 16 :]
        spill_o[b] = spill[5:8]
        if not with_out:
            pre_grad[lo:hi] = back
            spilled.append(
                jnp.where(lax.broadcasted_iota(jnp.int32, (8, width), 0) < 5, 0.0, spill)
            )
    leave(spill_o, inner_o, tail_o)
    if not with_out:
        turned_o[:, :rows_n] = pre_grad[...].T.astype(BF16)
        for b in range(batches):
            pre_grad[8 * b : 8 * b + 8] = spilled[b]
        pre_grad[8 * batches : rows_n] = jnp.zeros((rows_n - 8 * batches, width), F32)
        turned_o[:, rows_n:] = pre_grad[...].T.astype(BF16)
        leave(turned_o)
    for k in range(4):
        vec_o[n + k : n + k + 1] = taps[k]
    vec_o[n + 4 : n + 5] = bias


def norm_back(source, gain, grad):
    scale = lax.rsqrt(jnp.mean(source * source, axis=-1, keepdims=True) + EPS)
    unit = source * scale
    scaled = grad * gain
    along = jnp.mean(scaled * unit, axis=-1, keepdims=True)
    return scale * (scaled - unit * along), grad * unit


def turn_kernel(
    batches, span, width, rank, n, targets, layer,
    *refs,
):
    refs = list(refs)
    take = lambda k: [refs.pop(0) for _ in range(k)]
    inner, tail, spill, gate_grad, rows, gain, g, pair, vgrad, own_in, other_in = take(11)
    if layer:
        own_out, other_out, gate, proj, marks, low_w, vec, scanned = take(8)
    g_o, small_o = take(2)
    if layer:
        grad_o, gg_o, send_o, gate_o, gate_t_o = take(5)
    in_w, sem_in, mixed_grad, column = take(4)
    rows_n = batches * span
    if layer:
        seff, sg, cx, first, out_w, sem_out = take(6)
    arrival = fetch(layer, own_in, other_in, in_w, sem_in)
    if layer:
        arrival_out = fetch(0, own_out, other_out, out_w, sem_out)
    ready(tail, inner, spill)
    mixed_grad[:, :width] = inner[...]
    for b in range(batches):
        tail[b, 13:16] = tail[b, 13:16] + spill[b]
        hi = (b + 1) * span
        mixed_grad[hi - 16 : hi, :width] = tail[b].astype(BF16)
    ready(gate_grad)
    mixed_grad[:, width:] = gate_grad[...]
    if layer:
        grad_o[...] = mixed_grad[...].astype(F32).T.astype(BF16)
        leave(grad_o)
    ready(pair, vgrad)
    small_o[:, :LANES] = pair[...]
    arrival.wait()
    normed_grad = against(mixed_grad[...], in_w[...])
    ready(rows, g, gain)
    input_grad, terms = norm_back(rows[...].astype(F32), gain[...], normed_grad)
    g_new = (g[...].astype(F32) + input_grad).astype(BF16)
    g_o[...] = g_new
    leave(g_o)
    column[...] = jnp.concatenate(
        [vgrad[...], jnp.zeros((LANES - vgrad.held.shape[0], width), F32)], 0
    ).T
    sums = jnp.sum(terms.T, axis=1, keepdims=True)
    spot = lax.broadcasted_iota(jnp.int32, (1, LANES), 1) == n + 7
    part, block = sums.shape[0] // targets, width // targets
    for j in range(targets):
        rows_j = slice(j * block, j * block + part)
        column[rows_j] = jnp.where(spot, sums[j * part : (j + 1) * part], column[rows_j])
    small_o[:, LANES:] = column[...].astype(BF16)
    leave(small_o)
    if layer:
        arrival_out.wait()
        gg = against(g_new, out_w[...])
        gg_o[...] = gg
        leave(gg_o)
        ready(gate, proj, low_w, vec, marks)
        gate = gate[...].astype(F32)
        sg[...] = gg * jax.nn.silu(gate)
        step = softplus(step_sum(proj[...], low_w, vec, rank, n))
        seff[...] = step + marks[:, 0:1] * STOP
        spread_columns(proj[...].astype(F32).T, rank + n, cx)
        ready(scanned)
        gate_new = gg * scanned[...] * silu_slope(gate)
        gate_o[...] = gate_new.astype(BF16)
        gate_t_o[...] = gate_new.T.astype(BF16)
        leave(gate_o, gate_t_o)
        back_scan(batches, span, width // BLOCK, seff, sg, cx, vec.at[0:n], first)
        for b in range(batches):
            send_o[b * n : (b + 1) * n] = first[b].astype(BF16)


def by_core(groups, emit):
    if len(groups) == 1:
        emit(groups[0])
    else:
        for core, group in enumerate(groups):
            pl.when(lax.axis_index("section") == core)(functools.partial(emit, group))


def meet_kernel(groups, bit, lanes, *refs):
    goes, stays = refs[-2:]
    low, pairs = min(bit, goes.shape[0]), goes.shape[0]
    place = lax.axis_index("seq") // bit % 2

    def emit(group):
        left, left_got, right, right_got = group
        depth = left.shape[-1]
        first = 0 if lanes == right.shape[1] else lax.axis_index("section") * lanes
        columns = pl.ds(pl.multiple_of(first, LANES), lanes) if lanes != right.shape[1] else ...
        own = right[:depth, columns] if columns is not ... else right[:depth]
        got = right_got[:depth, columns] if columns is not ... else right_got[:depth]
        for which, out in ((1 - place, goes), (place, stays)):
            for k in range(pairs):
                source = (k // low * 2 + which) * low + k % low
                out[k] = (dot(left[source], own) + dot(left_got[source], got)).astype(BF16)

    by_core([refs[4 * i : 4 * i + 4] for i in range(groups)], emit)


def advance_kernel(plan, *refs):
    refs = list(refs)
    take = lambda k: [refs.pop(0) for _ in range(k)]
    ins = [[take(2) for _ in range(groups)] for groups, _ in plan]
    for groups, (_, bits) in zip(ins, plan):
        outs = take(2 if bits else 1)

        def emit(group, outs=outs, bits=bits):
            stayed, came = group
            if not bits:
                outs[0][...] = stayed[0].astype(F32) + came[0].astype(F32)
                return
            low = 1 << sorted(bits).index(bits[0])
            place = lax.axis_index("seq") // bits[0] % 2
            for which, out in ((1 - place, outs[0]), (place, outs[1])):
                for k in range(out.shape[0]):
                    source = (k // low * 2 + which) * low + k % low
                    out[k] = (stayed[source].astype(F32) + came[source].astype(F32)).astype(BF16)

        by_core(groups, emit)


DMA = pltpu.SemaphoreType.DMA


def expected(us):
    return pl.CostEstimate(
        flops=int(us * 3e8), bytes_accessed=int(us * 1e6), transcendentals=0
    )


def run(kernel, us, outs, scratch, args, far, far_out, elsewhere=(), others=(), limit=None):
    others = dict(others)
    whole_args = list(args) + list(others.values())
    far = tuple(far) + tuple(i for i in range(len(args)) if i not in far and i not in elsewhere)
    passing = [(args[i].shape, args[i].dtype) for i in far] + [outs[i] for i in far_out]
    count = len(passing)

    def whole(*refs):
        refs = list(refs)
        ins, refs = refs[: len(args)], refs[len(args) :]
        second, refs = dict(zip(others, refs)), refs[len(others) :]
        results, rest = refs[: len(outs)], refs[len(outs) :]
        own, buffers, sems = rest[: len(scratch)], rest[len(scratch) : -1], rest[-1]
        for k, i in enumerate(far):
            ins[i] = Arriving(ins[i], buffers[k], sems.at[k], second.get(i))
        for k, i in enumerate(far_out, len(far)):
            results[i] = Leaving(results[i], buffers[k], sems.at[k])
        kernel(*ins, *results, *own)
        ready(*ins)
        leave(*results)
        for ref in results:
            if isinstance(ref, Leaving):
                ref.copy.wait()

    return pl.pallas_call(
        whole,
        out_shape=[jax.ShapeDtypeStruct(*o) for o in outs],
        in_specs=[pl.BlockSpec(memory_space=pl.ANY)] * len(whole_args),
        out_specs=[
            pl.BlockSpec(memory_space=pl.ANY if i in far_out else pltpu.VMEM)
            for i in range(len(outs))
        ],
        scratch_shapes=[s if not isinstance(s, tuple) else pltpu.VMEM(*s) for s in scratch]
        + [pltpu.VMEM(*p) for p in passing]
        + [DMA((count,))],
        compiler_params=pltpu.CompilerParams(vmem_limit_bytes=limit or VMEM_LIMIT),
        cost_estimate=expected(us),
    )(*whole_args)


def hop(batches, n, steps, at, own=(), own_b=(), totals=None, both=False):
    messages = list(own) + list(own_b)
    args = [at] + ([] if own else [totals]) + messages
    return pl.pallas_call(
        functools.partial(hop_kernel, batches, n, steps, bool(own), both or bool(own_b)),
        out_shape=jax.ShapeDtypeStruct(messages[0].shape, BF16),
        in_specs=[pl.BlockSpec(memory_space=pltpu.VMEM)] * len(args),
        out_specs=pl.BlockSpec(memory_space=pltpu.VMEM),
        compiler_params=pltpu.CompilerParams(vmem_limit_bytes=HOP_LIMIT),
        cost_estimate=expected(1),
    )(*args)


def near(kernel, us, outs, args):
    return pl.pallas_call(
        kernel,
        out_shape=[jax.ShapeDtypeStruct(*o) for o in outs],
        in_specs=[pl.BlockSpec(memory_space=pltpu.VMEM)] * len(args),
        out_specs=[pl.BlockSpec(memory_space=pltpu.VMEM)] * len(outs),
        compiler_params=pltpu.CompilerParams(vmem_limit_bytes=NEAR_LIMIT),
        cost_estimate=expected(us),
    )(*args)


def meet(groups, bit, targets, lanes):
    args = []
    for left, left_got, right, right_got in groups:
        shape = (targets, left.shape[0] // targets, left.shape[1])
        args += [left.reshape(shape), left_got.reshape(shape), right, right_got]
    out = ((targets // 2, args[0].shape[1], lanes), BF16)
    return near(functools.partial(meet_kernel, len(groups), bit, lanes), 3, [out] * 2, args)


def advance(streams):
    outs, args, plan = [], [], []
    for groups, bits in streams:
        for group in groups:
            args += group
        count, *block = groups[0][0].shape
        outs += [((count // 2, *block), BF16)] * 2 if bits else [(tuple(block), F32)]
        plan.append((len(groups), tuple(bits)))
    results = list(near(functools.partial(advance_kernel, plan), 2, outs, args))
    return [tuple(results.pop(0) for _ in range(2 if bits else 1)) for _, bits in streams]


def flip(array, axis, bit):
    count = lax.axis_size(axis)
    return lax.ppermute(array, axis, [(i, i ^ bit) for i in range(count)])


def shifted(array, by):
    count = lax.axis_size("seq")
    pairs = [(i, i + by) for i in range(count) if 0 <= i + by < count]
    return lax.ppermute(array, "seq", pairs)


def tie(*arrays):
    return lax.optimization_barrier(arrays)


def bits_of(count):
    bits = [1 << k for k in range(count.bit_length() - 1)]
    assert 1 << len(bits) == count
    return bits


def swapped(bits):
    return [bits[1], bits[0]] + list(bits[2:]) if len(bits) > 1 else list(bits)


def pick(array, index, axis):
    return lax.dynamic_index_in_dim(array, index, axis, keepdims=False)


def local(
    tokens, starts, norm_gain, in_weight, conv_weight, conv_bias, xproj_weight,
    dtproj_weight, dt_bias, decay_rate, skip_gain, out_weight, cotangent,
):
    core = lax.axis_index("section")
    place = lax.axis_index("seq")
    cores = lax.axis_size("section")
    count = lax.axis_size("seq")
    bits = bits_of(count)
    batch_count, span, model = tokens.shape
    width = conv_weight.shape[2]
    n = decay_rate.shape[2]
    rank = dtproj_weight.shape[1]
    x_width = xproj_weight.shape[2]
    batches = batch_count // cores
    rows_n = batches * span
    half_model = model // 2
    low_core = core == 0
    steps = len(bits)

    def mine(array):
        return lax.dynamic_slice_in_dim(array, core * batches, batches, 0).reshape(
            (rows_n,) + array.shape[2:]
        )

    rows0 = mine(tokens)
    top = mine(cotangent)
    r = lax.dynamic_slice_in_dim(starts, core * batches, batches, 0).astype(F32)
    r_ext = jnp.concatenate([shifted(r[:, -3:].astype(BF16), 1).astype(F32), r], 1)
    free = 1.0 - r_ext
    m1 = free[:, 3:]
    m2 = m1 * free[:, 2:-1]
    m3 = m2 * free[:, 1:-2]
    marks = jnp.stack([r, m1, m2, m3], -1).reshape(rows_n, 4)

    tall = ((rows_n, width), F32)
    low_tall = ((rows_n, width), BF16)
    rim_s = ((batches, 3, width), F32)
    own_gain = norm_gain[0][None]
    in_own, out_own = in_weight[0], out_weight[0]

    vec_own = jnp.concatenate(
        [
            decay_rate[0].T * -LOG2E, conv_weight[0], conv_bias[0][None], dt_bias[0][None],
            skip_gain[0][None], jnp.pad(own_gain, ((0, 0), (0, width - model))),
        ],
        0,
    )
    low_own = jnp.concatenate([xproj_weight[0].T, dtproj_weight[0]], 0)
    vec_other, low_other = flip(vec_own, "section", 1), flip(low_own, "section", 1)

    in_a, in_b, gate_a, gate_b, tail_a, tail_b = run(
        functools.partial(enter_kernel, batches, span, width), 5,
        [low_tall] * 4 + [rim_s] * 2,
        [((cores * rows_n, model), BF16), ((4, model, 2 * width // 4), BF16), DMA((4,))],
        [tokens.reshape(batch_count * span, model), own_gain, in_own],
        far=(0, 1), far_out=range(6), elsewhere=(2,),
    )
    in_a, in_b, gate_a, gate_b, tail_a, tail_b, vec_other, low_other, marks = tie(
        in_a, in_b, gate_a, gate_b, tail_a, tail_b, vec_other, low_other, marks
    )
    in_got = lax.ppermute(in_b, "section", [(0, 1)])
    everywhere = ("section", "seq")
    rim_a = lax.ppermute(tail_a, everywhere, [(i, i + 1) for i in range(count - 1)])
    rim_b = lax.ppermute(tail_b, everywhere, [(i, count + i + 1) for i in range(count - 1)])
    gate_got = lax.ppermute(gate_b, "section", [(0, 1)])

    out_now, in_now, _, _, _ = tie(out_own, in_own, in_got, rim_a, rim_b)
    out_other, in_other = flip(out_now, "section", 1), flip(in_now, "section", 1)
    vecs = [jnp.where(low_core == (l == 0), vec_own, vec_other) for l in range(2)]
    lows = [jnp.where(low_core == (l == 0), low_own, low_other) for l in range(2)]
    gains = [v[n + 7 :, :model] for v in vecs]
    in0, gate0 = jnp.where(low_core, in_a, in_got), jnp.where(low_core, gate_a, gate_got)
    rim0 = jnp.where(low_core, rim_a, rim_b)

    spread = ((rows_n, n, LANES), F32)
    state = ((batches, n, width), F32)
    flat_in = ((model, 2 * width), BF16)
    flat_out = ((width, model), BF16)
    send_s = ((batches * n + 16, width), BF16)
    send_back_s = ((batches * n, width), BF16)
    both_s = ((2 * batches * n + 16, width), BF16)
    tall_t = ((width, rows_n), BF16)
    narrow = ((rows_n, model), BF16)

    totals_s = ((-(-batches * (steps + 1) // 8) * 8, width), F32)

    def front(layer, inner, rim, vec, low, *rest, others=()):
        outs = [low_tall, ((rows_n, LANES), BF16), both_s if layer else send_s]
        scratch = [((span + 8, width), F32), tall, tall, spread, spread, state]
        args = [inner, rim, marks, vec, low, *rest]
        if layer:
            scratch += [tall, flat_out, DMA]
        return run(
            functools.partial(front_kernel, batches, span, width, rank, n, bool(layer)),
            10 if layer else 6, outs, scratch, args, far=(2, 3, 1, 0, 4),
            far_out=range(len(outs)), elsewhere=(7, 8) if layer else (), others=others,
        )

    conv0, proj0, send = front(
        0, in_a, rim_a, vec_own, low_own,
        others=((0, in_got), (1, rim_b), (3, vec_other), (4, low_other)),
    )
    at0, at1 = vecs[0][:n], vecs[1][:n]
    own = [send]
    for k, bit in enumerate(bits):
        own.append(flip(send, "seq", bit))
        if k < steps - 1:
            send = hop(batches, n, k + 1, at0, own)
    scanned0, gated_t0, rows1, normed0, normed1, in1, gate1, before0, totals0, tail1 = run(
        functools.partial(end_kernel, batches, span, width, rank, n, steps), 10,
        [tall, tall_t, narrow, narrow, narrow, low_tall, low_tall, state, totals_s, ((batches, 6, width), F32)],
        [tall, tall, spread, spread, flat_out, flat_in, DMA((2,))],
        [gate0, conv0, proj0, marks, vecs[0], lows[0], rows0, gains[1], gains[0],
         out_own, out_other, in_own, in_other, *own],
        far=(6, 8, 2, 5, 4, 3, 1, *range(13, 14 + steps), 0), far_out=range(10),
        elsewhere=(9, 10, 11, 12),
    )

    rims = shifted(tail1, 1)
    rim1 = rims[:, :3]
    conv1, proj1, send = front(
        1, in1, rim1, vecs[1], lows[1], gate1, top, out_own, out_other
    )
    rim = rims[:, 3:, :model].astype(BF16)
    rim = jnp.pad(rim, ((0, 0), (5, 0), (0, 0))).reshape(8 * batches, model)
    normed_ext = jnp.concatenate(
        [normed0, rim, jnp.zeros((rows_n - 8 * batches, model), BF16)], 0
    )
    ext_got, normed_got = flip(normed_ext, "section", 1), flip(normed1, "section", 1)
    own = [send]
    for k, bit in enumerate(bits):
        own.append(flip(send, "seq", bit))
        if k < steps - 1:
            send = hop(batches, n, k + 1, at1, own, both=True)

    def back(layer, gg, conv, inner, gate, rim, proj, *rest):
        outs = [
            low_tall, ((batches, 16, width), F32), ((batches, 3, width), F32),
            ((width, LANES), BF16), ((n + 8, width), F32),
        ]
        scratch = [
            tall, tall, ((batches, span + 1, n, BLOCK), F32), ((batches, span, n, BLOCK), F32),
            tall, tall, spread, spread, ((span + 16, width), F32), tall,
            spread, spread, tall, state, state,
        ]
        if layer:
            outs += [low_tall, tall_t, narrow]
            scratch += [tall, tall, flat_out, DMA]
            far = (8, 7, 6, 5, 1, 0, 3, *range(12, 12 + steps))
        else:
            outs += [((width, 2 * rows_n), BF16)]
            far = (8, 7, 6, 5, 1, 0, 3, *range(9, 11 + steps))
        return run(
            functools.partial(
                back_kernel, batches, span, width, rank, n, x_width, steps, bool(layer)
            ),
            22 if layer else 19, outs, scratch,
            [gg, conv, inner, gate, rim, marks, vecs[layer], lows[layer], proj, *rest],
            far=far, far_out=range(len(outs)),
            elsewhere=(10, 11) if layer else (),
        )

    inner1, last1, spill1, pair1, vgrad1, gate_grad1, gated_t1, out1 = back(
        1, top, conv1, in1, gate1, rim1, proj1, rows1, out_own, out_other, *own[1:]
    )
    got1 = shifted(spill1, -1)

    def turn(layer, inner, tail, spill, gate_grad, rows, g, pair, vgrad, *rest):
        outs = [narrow, ((width, 2 * LANES), BF16)]
        scratch = [flat_in, DMA, ((rows_n, 2 * width), BF16), ((width, LANES), F32)]
        args = [
            inner, tail, spill, gate_grad, rows, gains[layer], g, pair, vgrad, in_own, in_other,
            *rest,
        ]
        elsewhere, far, far_out = [9, 10], [1, 2, 0, 3, 4, 6], [0, 1]
        if layer:
            outs += [((2 * width, rows_n), BF16), tall, send_back_s, low_tall, tall_t]
            scratch += [tall, tall, spread, state, flat_out, DMA]
            elsewhere += [11, 12]
            far += [13, 14, 18]
            far_out += [2, 3, 4, 5, 6]
        return run(
            functools.partial(turn_kernel, batches, span, width, rank, n, count, layer),
            11 if layer else 5, outs, scratch, args, far=far, far_out=far_out,
            elsewhere=elsewhere, limit=None if layer else TURN_LIMIT,
        )

    g0, small1, grad_t1, gg0, send_b, gate_grad0, gate_t0 = turn(
        1, inner1, last1, got1, gate_grad1, rows1, top, pair1, vgrad1, out_own, out_other,
        gate0, proj0,
        marks, lows[0], vecs[0], scanned0,
    )

    first_b = flip(send_b, "seq", bits[0])
    first_b, grad_t1, gate_t0, g0, gated_t0, gated_t1 = tie(
        first_b, grad_t1, gate_t0, g0, gated_t0, gated_t1
    )

    x_bit, y_bit, z_bit = bits[0], bits[1], bits[-2]
    one_way = lambda array, a, b: lax.ppermute(array, "section", [(a, b)])
    def half(array, which):
        return lax.dynamic_slice_in_dim(array, which * half_model, half_model, 1)

    def together(left, left_got, right, right_got):
        return dot(
            jnp.concatenate([left, left_got], 1), jnp.concatenate([right, right_got], 0)
        ).astype(BF16)

    def part(total, bit, order):
        axis = len(order) - 1 - sorted(order).index(bit)
        total = total.reshape((2,) * len(order) + (-1, total.shape[-1]))
        mine = (place // bit) % 2
        block = (total.shape[-2], total.shape[-1])
        return (
            pick(total, 1 - mine, axis).reshape((-1, *block)),
            pick(total, mine, axis).reshape((-1, *block)),
        )

    gated_got = flip(jnp.where(low_core, gated_t1, gated_t0), "section", 1)
    gated_own = jnp.where(low_core, gated_t0, gated_t1)
    g_got = flip(jnp.where(low_core, top, g0), "section", 1)
    grad_got, gate_got0 = flip(grad_t1, "section", 1), flip(gate_t0, "section", 1)

    own_b = [send_b]
    for k, bit in enumerate(bits):
        got_b = flip(send_b, "seq", bit) if k else first_b
        if k == 2:
            a = together(grad_t1, grad_got, half(normed1, core), half(normed_got, core))
            b = together(gated_own, gated_got, jnp.where(low_core, g0, top), g_got)
            c = together(
                gate_t0, gate_got0, half(normed0, core), half(ext_got[:rows_n], core)
            )
            a_goes, a_stays = part(a, x_bit, bits)
            b_goes, b_stays = part(b, y_bit, bits)
            c_goes, c_stays = part(c, z_bit, bits[:-1])
            got_b, a_goes, b_goes = tie(got_b, a_goes, b_goes)
        if k == steps - 1:
            got_b, a_goes, b_goes, c_goes = tie(got_b, a_goes, b_goes, c_goes)
            a_got, b_got = flip(a_goes, "seq", x_bit), flip(b_goes, "seq", y_bit)
            c_got = flip(c_goes, "seq", z_bit)
            small_up = one_way(small1, 0, 1)
        own_b.append(got_b)
        if k < steps - 1:
            send_b = hop(batches, n, k + 1, at0, (), own_b, totals0)
    inner0, tail0, spill0, pair0, vgrad0, turned0 = back(
        0, gg0, conv0, in0, gate0, rim0, proj0, before0, totals0, *own_b[1:]
    )
    inner0, tail0, spill0, pair0, vgrad0, turned0, a_got, b_got, c_got, small_up = tie(
        inner0, tail0, spill0, pair0, vgrad0, turned0, a_got, b_got, c_got, small_up
    )
    got0 = shifted(spill0, -1)
    turned_got = flip(turned0, "section", 1)

    middle = bits[2:-2]
    blocks = lambda array: array.reshape(count, -1, array.shape[-1])
    held = {"a": [(a_stays, a_got)], "b": [(b_stays, b_got)], "c": [(c_stays, c_got)]}
    todo = {
        "d": [x_bit, y_bit, *middle, z_bit],
        "a": [y_bit, *middle, z_bit, bits[-1]],
        "b": [z_bit, x_bit, *middle, bits[-1]],
        "c": [x_bit, y_bit, *middle],
    }
    parts = dict(zip("ab", advance([(held[k], todo[k]) for k in "ab"])))
    parts["d"] = meet(
        [(turned0, turned_got, normed_ext, ext_got)], x_bit, count // 2, half_model
    )
    first = [parts[k][0] for k in "dab"]
    got0, inner0, tail0, pair0, vgrad0, *first = tie(got0, inner0, tail0, pair0, vgrad0, *first)
    gots = [flip(goes, "seq", todo[k][0]) for k, goes in zip("dab", first)]
    dx, small0 = turn(0, inner0, tail0, got0, gate_grad0, rows0, g0, pair0, vgrad0)
    *gots, dx, small0 = tie(*gots, dx, small0)
    for k, got in zip("dab", gots):
        held[k] = [(parts[k][1], got)]
        todo[k] = todo[k][1:]
    small_down = one_way(small0, 1, 0)
    late = {
        "small": (
            [(blocks(small0), blocks(small_down)), (blocks(small1), blocks(small_up))],
            [z_bit, y_bit, x_bit, *middle, bits[-1]],
        )
    }
    while any(todo.values()):
        names = [k for k in todo if todo[k]]
        parts = dict(zip(names, advance([(held[k], todo[k]) for k in names])))
        gots = [flip(parts[k][0], "seq", todo[k][0]) for k in names]
        for k in late:
            held[k], todo[k] = late[k]
            parts.update(zip([k], advance([late[k]])))
            names.append(k)
            gots.append(flip(parts[k][0], "seq", todo[k][0]))
        late = {}
        gots = tie(*gots)
        for k, got in zip(names, gots):
            held[k] = [(parts[k][1], got)]
            todo[k] = todo[k][1:]
        if not todo["d"] and not todo["c"] and "d" in parts:
            c, d = (t.astype(BF16) for (t,) in advance([(held[k], []) for k in "cd"]))
            top_half = place >= count // 2
            swap_sent = jnp.where(top_half, d, c)
            swap_got = flip(swap_sent, "seq", bits[-1])
    in_sum1, out_sum, small = (
        total for (total,) in advance([(held[k], []) for k in ("a", "b", "small")])
    )
    in_sum0 = jnp.where(top_half, c, d).astype(F32) + swap_got.astype(F32)

    got = flip(jnp.where(low_core, in_sum1, in_sum0).astype(BF16), "section", 1).astype(F32)
    grad_in = jnp.where(
        low_core, jnp.concatenate([in_sum0, got], 1), jnp.concatenate([got, in_sum1], 1)
    )
    got = flip(jnp.where(low_core, out1, dx), "section", 1)
    boundary = jnp.where(
        low_core, jnp.concatenate([dx, got], 0), jnp.concatenate([got, out1], 0)
    ).reshape(1, batch_count, span, model)
    vec_sum = small[:, LANES : LANES + n + 8].T
    gain = vec_sum[n + 7 :, : model // count]
    return (
        boundary,
        gain,
        grad_in.T[None],
        vec_sum[n : n + 4][None],
        vec_sum[n + 4 : n + 5],
        small[:, :x_width][None],
        small[:, x_width:LANES].T[None],
        vec_sum[n + 5 : n + 6],
        small[:, LANES : LANES + n][None],
        vec_sum[n + 6 : n + 7],
        out_sum[None],
    )


def solution(mesh):
    in_specs = (
        P(None, "seq", None), P(None, "seq"), P("section", None), P("section", None, None),
        P("section", None, None), P("section", None), P("section", None, None),
        P("section", None, None), P("section", None), P("section", None, None),
        P("section", None), P("section", None, None), P(None, "seq", None),
    )
    out_specs = (
        P("section", None, "seq", None), P("section", "seq"), P("section", None, "seq"),
        P("section", None, "seq"), P("section", "seq"), P("section", "seq", None),
        P("section", None, "seq"), P("section", "seq"), P("section", "seq", None),
        P("section", "seq"), P("section", "seq", None),
    )
    return jax.shard_map(local, mesh=mesh, in_specs=in_specs, out_specs=out_specs, check_vma=False)
```
